32 devices in a mesh: dom: 4 (over x, core), shard: 8 (over z, y).
Axes of the slice: x: 2, y: 2, z: 4, core: 2. Of those that a mesh axis runs over, the one named last changes fastest.
Arguments:
- embeddings: float32 [2048, 400], P(('dom', 'shard')), may hold values from -3 to 3
- row_accum: float32 [2048], P(('dom', 'shard')), may hold values from 0.01 to 1
- relations: bfloat16 [160, 400], replicated, may hold values from -3 to 3
- relation_accum: float32 [160], P(('dom', 'shard')), may hold values from 0.01 to 1
- request_rows: int32 [2, 256, 2, 16], P(None, ('dom', 'shard')), may hold values from 0 to 63
- head_slots: int32 [2, 4096], P(None, ('dom', 'shard')), may hold values from 0 to 127
- tail_slots: int32 [2, 4096], P(None, ('dom', 'shard')), may hold values from 0 to 127
- relation_ids: int32 [2, 4096], P(None, ('dom', 'shard')), may hold values from 0 to 159
- own_negatives: int32 [2, 16384], P(None, ('dom', 'shard')), may hold values from 0 to 127
- far_negatives: int32 [2, 16384], P(None, ('dom', 'shard')), may hold values from 0 to 127
Outputs:
- new_embeddings: float32 [2048, 400], P(('dom', 'shard'))
- new_accum: float32 [2048], P(('dom', 'shard'))
- relation_step: float32 [160, 400], P(('dom', 'shard'))
- new_relation_accum: float32 [160], P(('dom', 'shard'))
The draws below stay inside these ranges and needn't reach their ends.
Inputs may be any that keep to these rules, and one draw needn't show every extreme that they name: `request_rows`: local row numbers within the owner's 64 rows. `head_slots`: slots of the 128 own-side touched rows. `tail_slots`: slots of the 128 partner-side touched rows. `own_negatives`: slots of the 128 own-side touched rows. `far_negatives`: slots of the 128 partner-side touched rows.
All inputs are finite; a program needn't handle non-finite values.
Results may differ from the reference program's by a relative error of at most 0.0049.
Values may be sent and summed in bfloat16 or wider, within the bound.
No kernel may reach another device: no remote copies, remote signals or barrier semaphores. Data moves between devices by JAX's collectives and lax.ppermute only.
A program may use at most 64 MiB of HBM per device.

```python
import math
import jax
import jax.numpy as jnp
from jax import lax

D = 400
NEG = 512
ROUNDS = 2
ROWS_DEV = 64
SLOT = 16
EDGES = 128
NREL = 160
TOUCH = 128
ENT = 2048
N_DOM = 4
N_SHARD = 8


def with_ends(result, rng, low, high):
    spot = [jax.random.randint(jax.random.fold_in(rng, axis), (), 0, length) for axis, length in enumerate(result.shape)]
    longest = result.shape.index(max(result.shape))
    neighbour = spot[:longest] + [(spot[longest] + 1) % result.shape[longest]] + spot[longest + 1:]
    return result.at[tuple(spot)].set(low).at[tuple(neighbour)].set(high)


def level_of(rng, shape, cuts, smallest, high):
    level, own = 1.0, jax.random.fold_in(rng, 6)
    for position, shards_of in cuts:
        steps = jnp.exp(jax.random.uniform(jax.random.fold_in(own, position), (shards_of,), jnp.float32, smallest / len(cuts), high / len(cuts)))
        level = level * jnp.repeat(steps, shape[position] // shards_of).reshape([-1 if axis == position else 1 for axis in range(len(shape))])
    return level


def normal_values(stream_key, shape, spread, most, shards=(), kind=jnp.bfloat16):
    values = spread * jax.random.normal(stream_key, shape, jnp.float32)
    if shards:
        values = values * level_of(stream_key, shape, shards, -0.22, 0.18)
    return jnp.clip(values, -most, most).astype(kind)


def setup_inputs(seed: int = 0) -> dict:
    arg_keys = jax.random.split(jax.random.key(seed), 11)
    embeddings = normal_values(arg_keys[0], (ENT, D), 0.5, 3.0, ((0, 32),), jnp.float32)
    row_accum = jnp.clip(jnp.exp(math.log(1.0) - 4.6051702 * jax.random.uniform(arg_keys[1], (ENT,), jnp.float32) ** level_of(arg_keys[1], (ENT,), ((0, 32),), -0.2, 0.2)), 0.01, 1.0)
    relations = normal_values(arg_keys[2], (NREL, D), 0.5, 3.0)
    relation_accum = jnp.clip(jnp.exp(math.log(1.0) - 4.6051702 * jax.random.uniform(arg_keys[3], (NREL,), jnp.float32) ** level_of(arg_keys[3], (NREL,), ((0, 32),), -0.2, 0.2)), 0.01, 1.0)
    request_rows = with_ends(jax.random.randint(arg_keys[4], (ROUNDS, N_DOM * N_SHARD * N_SHARD, 2, SLOT), 0, ROWS_DEV), jax.random.fold_in(arg_keys[4], 1), 0, ROWS_DEV - 1).astype(jnp.int32)
    head_slots = with_ends(jax.random.randint(arg_keys[5], (ROUNDS, EDGES * N_DOM * N_SHARD), 0, TOUCH), jax.random.fold_in(arg_keys[5], 1), 0, TOUCH - 1).astype(jnp.int32)
    tail_slots = with_ends(jax.random.randint(arg_keys[6], (ROUNDS, EDGES * N_DOM * N_SHARD), 0, TOUCH), jax.random.fold_in(arg_keys[6], 1), 0, TOUCH - 1).astype(jnp.int32)
    relation_ids = with_ends(jax.random.randint(arg_keys[7], (ROUNDS, EDGES * N_DOM * N_SHARD), 0, NREL), jax.random.fold_in(arg_keys[7], 1), 0, NREL - 1).astype(jnp.int32)
    own_negatives = with_ends(jax.random.randint(arg_keys[8], (ROUNDS, NEG * N_DOM * N_SHARD), 0, TOUCH), jax.random.fold_in(arg_keys[8], 1), 0, TOUCH - 1).astype(jnp.int32)
    far_negatives = with_ends(jax.random.randint(arg_keys[9], (ROUNDS, NEG * N_DOM * N_SHARD), 0, TOUCH), jax.random.fold_in(arg_keys[9], 1), 0, TOUCH - 1).astype(jnp.int32)
    return dict(embeddings=embeddings, row_accum=row_accum, relations=relations, relation_accum=relation_accum, request_rows=request_rows, head_slots=head_slots, tail_slots=tail_slots, relation_ids=relation_ids, own_negatives=own_negatives, far_negatives=far_negatives)


LEARN_RATE = 0.1

def edge_terms(own_touched, far_touched, head_slots, tail_slots, relation_ids, own_negatives, far_negatives, relations):
    neg_count = own_negatives.shape[0]
    head_vec = own_touched[head_slots].astype(jnp.float32)
    tail_vec = far_touched[tail_slots].astype(jnp.float32)
    rel_vec = relations[relation_ids].astype(jnp.float32)
    positive = lax.optimization_barrier(jnp.sum(head_vec * rel_vec * tail_vec, axis=-1))
    query_tail = (head_vec * rel_vec).astype(jnp.bfloat16)
    query_head = (tail_vec * rel_vec).astype(jnp.bfloat16)
    neg_tail = far_touched[far_negatives]
    neg_head = own_touched[own_negatives]
    contract_last = (((1,), (1,)), ((), ()))
    contract_first = (((0,), (0,)), ((), ()))
    score_tail = lax.dot_general(query_tail, neg_tail, contract_last, preferred_element_type=jnp.float32)
    score_head = lax.dot_general(query_head, neg_head, contract_last, preferred_element_type=jnp.float32)
    weight_tail = (jax.nn.sigmoid(score_tail) / neg_count).astype(jnp.bfloat16)
    weight_head = (jax.nn.sigmoid(score_head) / neg_count).astype(jnp.bfloat16)
    back_tail = jnp.dot(weight_tail, neg_tail, preferred_element_type=jnp.float32)
    back_head = jnp.dot(weight_head, neg_head, preferred_element_type=jnp.float32)
    coeff = -jax.nn.sigmoid(-positive)[:, None]
    grad_head = coeff * rel_vec * tail_vec + rel_vec * back_tail
    grad_tail = coeff * head_vec * rel_vec + rel_vec * back_head
    grad_rel = coeff * head_vec * tail_vec + head_vec * back_tail + tail_vec * back_head
    grad_negtail = lax.dot_general(weight_tail, query_tail, contract_first, preferred_element_type=jnp.float32)
    grad_neghead = lax.dot_general(weight_head, query_head, contract_first, preferred_element_type=jnp.float32)
    touch_rows = own_touched.shape[0]
    emb_width = own_touched.shape[1]
    own_grad = jnp.zeros((touch_rows, emb_width), jnp.float32).at[head_slots].add(grad_head).at[own_negatives].add(grad_neghead)
    far_grad = jnp.zeros((touch_rows, emb_width), jnp.float32).at[tail_slots].add(grad_tail).at[far_negatives].add(grad_negtail)
    return (own_grad.astype(jnp.bfloat16), far_grad.astype(jnp.bfloat16), grad_rel)

def pick_rows(table_piece, index_piece):
    return table_piece[index_piece]

def add_rows(index_piece, value_piece):
    flat_index = index_piece.reshape(-1)
    flat_value = value_piece.reshape(-1, D).astype(jnp.float32)
    return jnp.zeros((ROWS_DEV, D), jnp.float32).at[flat_index].add(flat_value)

def reference(embeddings, row_accum, relations, relation_accum, request_rows, head_slots, tail_slots, relation_ids, own_negatives, far_negatives):
    device_count = N_DOM * N_SHARD
    emb_table = embeddings.reshape(N_DOM, N_SHARD, ROWS_DEV, D)
    accum_now = row_accum.reshape(N_DOM, N_SHARD, ROWS_DEV)
    relation_grad = jnp.zeros((NREL, D), jnp.float32)
    group_index = jnp.arange(N_DOM, dtype=jnp.int32)
    for r in range(ROUNDS):
        partner = jnp.bitwise_xor(group_index, jnp.int32(1 << r))
        lowered = emb_table.astype(jnp.bfloat16)
        request_ids = request_rows[r].reshape(N_DOM, N_SHARD, N_SHARD, 2, SLOT)
        served = jax.vmap(jax.vmap(pick_rows))(lowered, request_ids)
        own_touched = served[:, :, :, 0].transpose(0, 2, 1, 3, 4).reshape(device_count, TOUCH, D)
        far_touched = served[:, :, :, 1].transpose(0, 2, 1, 3, 4)[partner].reshape(device_count, TOUCH, D)

        def device_step(carried, device_items):
            own_piece, far_piece, head_piece, tail_piece, rel_piece, own_neg, far_neg = device_items
            own_grad, far_grad, grad_rel = edge_terms(own_piece, far_piece, head_piece, tail_piece, rel_piece, own_neg, far_neg, relations)
            return (carried.at[rel_piece].add(grad_rel), (own_grad, far_grad))
        scanned = (own_touched, far_touched, head_slots[r].reshape(device_count, EDGES), tail_slots[r].reshape(device_count, EDGES), relation_ids[r].reshape(device_count, EDGES), own_negatives[r].reshape(device_count, NEG), far_negatives[r].reshape(device_count, NEG))
        relation_grad, (own_grads, far_grads) = lax.scan(device_step, relation_grad, scanned)
        own_vals = own_grads.reshape(N_DOM, N_SHARD, N_SHARD, SLOT, D).transpose(0, 2, 1, 3, 4)
        far_vals = far_grads.reshape(N_DOM, N_SHARD, N_SHARD, SLOT, D)[partner].transpose(0, 2, 1, 3, 4)
        stacked = jnp.stack([own_vals, far_vals], axis=3)
        row_grad = jax.vmap(jax.vmap(add_rows))(request_ids, stacked)
        accum_now = accum_now + lax.optimization_barrier(jnp.mean(row_grad * row_grad, axis=-1))
        emb_table = emb_table - LEARN_RATE * row_grad / jnp.sqrt(accum_now)[..., None]
    new_relation_accum = relation_accum + lax.optimization_barrier(jnp.mean(relation_grad * relation_grad, axis=-1))
    relation_step = -LEARN_RATE * relation_grad / jnp.sqrt(new_relation_accum)[:, None]
    return (emb_table.reshape(ENT, D), accum_now.reshape(ENT), relation_step, new_relation_accum)
```

```python
import functools

import jax
import jax.numpy as jnp
from jax import lax
from jax.experimental import pallas as pl
from jax.experimental.pallas import tpu as pltpu
from jax.sharding import PartitionSpec as P

LEARN_RATE = 0.1
LANES = 128
BF16 = jnp.bfloat16
F32 = jnp.float32
NATURAL = (((1,), (0,)), ((), ()))
LAST = (((1,), (1,)), ((), ()))
FIRST = (((0,), (0,)), ((), ()))


def dot(left, right, dims=NATURAL):
    return lax.dot_general(left, right, dims, preferred_element_type=F32)


def iota(shape, axis):
    return lax.broadcasted_iota(jnp.int32, shape, axis)


def one_hot_rows(row, count):
    return (iota((count, row.shape[1]), 0) == row).astype(BF16)


def to_column(row):
    n = row.shape[1]
    return jnp.sum(jnp.where(iota((n, n), 0) == iota((n, n), 1), row, 0), axis=1, keepdims=True)


def to_row(column):
    n = column.shape[0]
    return jnp.sum(jnp.where(iota((n, n), 0) == iota((n, n), 1), column, 0), axis=0, keepdims=True)


def request_one_hot(request_ref, r, rows):
    ids = jnp.concatenate([request_ref[r, :, 0, :], request_ref[r, :, 1, :]], axis=0)
    pieces, slots = ids.shape
    n = pieces * slots
    spread = (iota((n, pieces), 0) // slots == iota((n, pieces), 1)).astype(F32)
    rep = dot(spread, ids.astype(F32))
    column = jnp.sum(
        jnp.where(iota((n, slots), 0) % slots == iota((n, slots), 1), rep, 0.0), axis=1, keepdims=True
    )
    return (iota((n, rows), 1) == column.astype(jnp.int32)).astype(BF16)


def halves(r, shards):
    bit = (lax.axis_index("dom") >> r) & 1
    return pl.ds(bit * shards, shards), pl.ds((1 - bit) * shards, shards)


def serve(request_ref, r, table, out_ref):
    shards, slots = out_ref.shape[0] // 2, out_ref.shape[1]
    served = dot(request_one_hot(request_ref, r, table.shape[0]), table.astype(BF16)).astype(BF16)
    served = served.reshape(2, shards, slots, table.shape[1])
    own, far = halves(r, shards)
    out_ref[own] = served[0]
    out_ref[far] = served[1]


def row_update(request_ref, r, back_ref, table, accum_row):
    chunks, slots, width = back_ref.shape
    own, far = halves(r, chunks // 2)
    back = jnp.concatenate(
        [back_ref[own].reshape(chunks // 2 * slots, width), back_ref[far].reshape(chunks // 2 * slots, width)], axis=0
    )
    row_grad = dot(request_one_hot(request_ref, r, table.shape[0]), back, FIRST)
    accum = to_column(accum_row) + jnp.mean(row_grad * row_grad, axis=1, keepdims=True)
    return table - LEARN_RATE * row_grad / jnp.sqrt(accum), to_row(accum)


def serve_kernel(r, request_ref, table_ref, out_ref):
    serve(request_ref, r, table_ref[...], out_ref)


def update_serve_kernel(r, request_ref, back_ref, table_ref, accum_ref, table_out, accum_out, out_ref):
    table, accum = row_update(request_ref, r, back_ref, table_ref[...], accum_ref[...])
    table_out[...] = table
    accum_out[...] = accum
    serve(request_ref, r + 1, table, out_ref)


def update_kernel(r, request_ref, back_ref, table_ref, accum_ref, table_out, accum_out):
    table, accum = row_update(request_ref, r, back_ref, table_ref[...], accum_ref[...])
    table_out[...] = table
    accum_out[...] = accum


def packed_shape(per_device, width):
    full, rest = width // LANES, width % LANES
    beside = LANES // rest
    return full, rest, beside, per_device * full + pl.cdiv(per_device, beside)


def pack_relations(grad_rel, ids, devices, per_device, add):
    edges, width = grad_rel.shape
    full, rest, beside, rows = packed_shape(per_device, width)
    place = to_column(ids) % per_device
    tail = grad_rel[:, full * LANES :]
    tail = jnp.concatenate([tail] * beside, axis=1)
    tail = jnp.where(iota((edges, LANES), 1) // rest == place % beside, tail, 0.0)
    values = jnp.concatenate(
        [grad_rel[:, c * LANES : (c + 1) * LANES] for c in range(full)] + [tail], axis=0
    ).astype(BF16)
    owner, spot = ids // per_device, ids % per_device
    spots = jnp.concatenate(
        [owner * rows + c * per_device + spot for c in range(full)]
        + [owner * rows + full * per_device + spot // beside],
        axis=1,
    )
    step = min(devices, 32)
    for d in range(0, devices, step):
        add(pl.ds(d, step), dot(one_hot_rows(spots - d * rows, step * rows), values).reshape(step, rows, LANES))


def edge_kernel(
    r, devices, rec_ref, head_ref, tail_ref, rel_ref, own_neg_ref, far_neg_ref, relations_ref, *rest
):
    last = len(rest) == 3
    before_ref = rest[0] if last else None
    out_ref, rel_out = rest[-2:]
    chunks, slots, width = rec_ref.shape
    shards = chunks // 2
    touched = shards * slots
    negatives = own_neg_ref.shape[1]
    own_half, far_half = halves(r, shards)
    own = rec_ref[own_half].reshape(touched, width)
    far = rec_ref[far_half].reshape(touched, width)
    row = slice(r, r + 1)
    relations = relations_ref.shape[0]
    ids = rel_ref[row]
    hot_head = one_hot_rows(head_ref[row], touched)
    hot_tail = one_hot_rows(tail_ref[row], touched)
    head = dot(hot_head, own, FIRST)
    tail = dot(hot_tail, far, FIRST)
    rel = dot(one_hot_rows(ids, relations), relations_ref[...], FIRST)
    query_tail = (head * rel).astype(BF16)
    query_head = (tail * rel).astype(BF16)

    def counts(neg_ref):
        hit = iota((touched, negatives), 0) == neg_ref[row]
        return jnp.sum(jnp.where(hit, 1.0 / negatives, 0.0), axis=1, keepdims=True)

    weight_tail = (jax.nn.sigmoid(dot(far, query_tail, LAST)) * counts(far_neg_ref)).astype(BF16)
    weight_head = (jax.nn.sigmoid(dot(own, query_head, LAST)) * counts(own_neg_ref)).astype(BF16)
    positive = jnp.sum(head * rel * tail, axis=1, keepdims=True)
    coeff = -jax.nn.sigmoid(-positive)
    back_tail = dot(weight_tail, far, FIRST)
    back_head = dot(weight_head, own, FIRST)
    toward_head = coeff * tail + back_tail
    grad_head = (rel * toward_head).astype(BF16)
    grad_tail = (rel * (coeff * head + back_head)).astype(BF16)
    own_grad = dot(
        jnp.concatenate([hot_head, weight_head], axis=1), jnp.concatenate([grad_head, query_head], axis=0)
    )
    far_grad = dot(
        jnp.concatenate([hot_tail, weight_tail], axis=1), jnp.concatenate([grad_tail, query_tail], axis=0)
    )
    out_ref[own_half] = own_grad.astype(BF16).reshape(shards, slots, width)
    out_ref[far_half] = far_grad.astype(BF16).reshape(shards, slots, width)
    grad_rel = head * toward_head + tail * back_head

    def add(where, value):
        if last:
            value = value + before_ref[where]
        rel_out[where] = value.astype(rel_out.dtype)

    pack_relations(grad_rel, ids, devices, relations // devices, add)


def relation_kernel(parts_ref, accum_ref, step_out, accum_out):
    per_device, width = step_out.shape
    full, rest, beside, rows = packed_shape(per_device, width)
    total = jnp.sum(parts_ref[...].astype(F32), axis=0)
    tails = [
        total[full * per_device + i // beside :][:1, i % beside * rest : (i % beside + 1) * rest]
        for i in range(per_device)
    ]
    grad = jnp.concatenate(
        [total[c * per_device : (c + 1) * per_device] for c in range(full)] + [jnp.concatenate(tails, axis=0)], axis=1
    )
    accum = to_column(accum_ref[...]) + jnp.mean(grad * grad, axis=1, keepdims=True)
    step_out[...] = -LEARN_RATE * grad / jnp.sqrt(accum)
    accum_out[...] = to_row(accum)


def call(kernel, outs, *args):
    return pl.pallas_call(
        kernel,
        out_shape=[jax.ShapeDtypeStruct(shape, kind) for shape, kind in outs],
        compiler_params=pltpu.CompilerParams(vmem_limit_bytes=48 * 2**20),
    )(*args)


def swap_pair(value, r):
    doms, shards = lax.axis_size("dom"), lax.axis_size("shard")
    groups = [
        [g * shards + s for g in (low, low ^ (1 << r)) for s in range(shards)]
        for low in range(doms)
        if not low >> r & 1
    ]
    return lax.all_to_all(
        value, ("dom", "shard"), split_axis=0, concat_axis=0, axis_index_groups=groups, tiled=True
    )


def body(
    embeddings,
    row_accum,
    relations,
    relation_accum,
    request_rows,
    head_slots,
    tail_slots,
    relation_ids,
    own_negatives,
    far_negatives,
):
    rows, width = embeddings.shape
    shards = lax.axis_size("shard")
    devices = shards * lax.axis_size("dom")
    rounds, slots = request_rows.shape[0], request_rows.shape[-1]
    per_device = relation_accum.shape[0]
    packed = packed_shape(per_device, width)[3]
    chunks = ((2 * shards, slots, width), BF16)
    table, accum = embeddings, row_accum.reshape(1, rows)
    state = [((rows, width), F32), ((1, rows), F32)]
    (outgoing,) = call(functools.partial(serve_kernel, 0), [chunks], request_rows, table)
    before = []
    for r in range(rounds):
        last = r == rounds - 1
        received = swap_pair(outgoing, r)
        grads, rel_part = call(
            functools.partial(edge_kernel, r, devices),
            [chunks, ((devices, packed, LANES), BF16 if last else F32)],
            received,
            head_slots,
            tail_slots,
            relation_ids,
            own_negatives,
            far_negatives,
            relations,
            *before,
        )
        before = [rel_part]
        back = swap_pair(grads, r)
        if last:
            parts = lax.all_to_all(rel_part, ("dom", "shard"), split_axis=0, concat_axis=0, tiled=True)
            table, accum = call(functools.partial(update_kernel, r), state, request_rows, back, table, accum)
        else:
            table, accum, outgoing = call(
                functools.partial(update_serve_kernel, r), state + [chunks], request_rows, back, table, accum
            )
    step, rel_accum = call(
        relation_kernel,
        [((per_device, width), F32), ((1, per_device), F32)],
        parts,
        relation_accum.reshape(1, per_device),
    )
    return (table, accum.reshape(rows), step, rel_accum.reshape(per_device))


def solution(mesh):
    placed = (
        P(("dom", "shard"), None),
        P(("dom", "shard")),
        P(),
        P(("dom", "shard")),
        P(None, ("dom", "shard"), None, None),
        P(None, ("dom", "shard")),
        P(None, ("dom", "shard")),
        P(None, ("dom", "shard")),
        P(None, ("dom", "shard")),
        P(None, ("dom", "shard")),
    )
    return jax.shard_map(
        body,
        mesh=mesh,
        in_specs=placed,
        out_specs=(
            P(("dom", "shard"), None),
            P(("dom", "shard")),
            P(("dom", "shard"), None),
            P(("dom", "shard")),
        ),
        check_vma=False,
    )
```

```python
import functools

import jax
import jax.numpy as jnp
from jax import lax
from jax.experimental import pallas as pl
from jax.experimental.pallas import tpu as pltpu
from jax.sharding import PartitionSpec as P

LEARN_RATE = 0.1
LANES = 128
BF16 = jnp.bfloat16
F32 = jnp.float32
NATURAL = (((1,), (0,)), ((), ()))
LAST = (((1,), (1,)), ((), ()))
FIRST = (((0,), (0,)), ((), ()))


def dot(left, right, dims=NATURAL):
    return lax.dot_general(left, right, dims, preferred_element_type=F32)


def iota(shape, axis):
    return lax.broadcasted_iota(jnp.int32, shape, axis)


def one_hot_rows(row, count):
    return (iota((count, row.shape[1]), 0) == row).astype(BF16)


def to_column(row):
    n = row.shape[1]
    return jnp.sum(jnp.where(iota((n, n), 0) == iota((n, n), 1), row, 0), axis=1, keepdims=True)


def to_row(column):
    n = column.shape[0]
    return jnp.sum(jnp.where(iota((n, n), 0) == iota((n, n), 1), column, 0), axis=0, keepdims=True)


def request_one_hot(request_ref, r, rows):
    ids = jnp.concatenate([request_ref[r, :, 0, :], request_ref[r, :, 1, :]], axis=0)
    pieces, slots = ids.shape
    n = pieces * slots
    spread = (iota((n, pieces), 0) // slots == iota((n, pieces), 1)).astype(F32)
    rep = dot(spread, ids.astype(F32))
    column = jnp.sum(
        jnp.where(iota((n, slots), 0) % slots == iota((n, slots), 1), rep, 0.0), axis=1, keepdims=True
    )
    return (iota((n, rows), 1) == column.astype(jnp.int32)).astype(BF16)


def halves(r, shards):
    bit = (lax.axis_index("dom") >> r) & 1
    return pl.ds(bit * shards, shards), pl.ds((1 - bit) * shards, shards)


def serve(request_ref, r, table, out_ref):
    shards, slots = out_ref.shape[0] // 2, out_ref.shape[1]
    served = dot(request_one_hot(request_ref, r, table.shape[0]), table.astype(BF16)).astype(BF16)
    served = served.reshape(2, shards, slots, table.shape[1])
    own, far = halves(r, shards)
    out_ref[own] = served[0]
    out_ref[far] = served[1]


def row_update(request_ref, r, back_ref, table, accum_row):
    chunks, slots, _ = back_ref.shape
    width = table.shape[1]
    back = jnp.concatenate(
        [back_ref[half, :, :width].reshape(chunks // 2 * slots, width) for half in halves(r, chunks // 2)], axis=0
    )
    row_grad = dot(request_one_hot(request_ref, r, table.shape[0]), back, FIRST)
    accum = to_column(accum_row) + jnp.mean(row_grad * row_grad, axis=1, keepdims=True)
    return table - LEARN_RATE * row_grad / jnp.sqrt(accum), to_row(accum)


def serve_kernel(r, request_ref, table_ref, out_ref):
    serve(request_ref, r, table_ref[...], out_ref)


def update_serve_kernel(r, request_ref, back_ref, table_ref, accum_ref, table_out, accum_out, out_ref):
    table, accum = row_update(request_ref, r, back_ref, table_ref[...], accum_ref[...])
    table_out[...] = table
    accum_out[...] = accum
    serve(request_ref, r + 1, table, out_ref)


def update_kernel(r, request_ref, back_ref, table_ref, accum_ref, table_out, accum_out):
    table, accum = row_update(request_ref, r, back_ref, table_ref[...], accum_ref[...])
    table_out[...] = table
    accum_out[...] = accum


def padded(width):
    return pl.cdiv(width, LANES) * LANES


def packed_shape(per_device, width):
    full, rest = width // LANES, width % LANES
    beside = LANES // rest
    return full, rest, beside, per_device * full + pl.cdiv(per_device, beside)


def place_relations(ids, per_device, rows, shards, doms, bit):
    owner, spot = ids // per_device, ids % per_device
    away = (owner // shards) ^ (lax.axis_index("dom") & ~(1 << bit))
    part = (away & ((1 << bit) - 1)) | (away >> (bit + 1) << bit)
    chunk = (away >> bit & 1) * shards + owner % shards
    return part, chunk * rows, spot


def pack_relations(grad_rel, ids, per_device, shards, doms, bit):
    edges, width = grad_rel.shape
    full, rest, beside, rows = packed_shape(per_device, width)
    part, base, spot = place_relations(ids, per_device, rows, shards, doms, bit)
    tail = jnp.concatenate([grad_rel[:, full * LANES :]] * beside, axis=1)
    tail = jnp.where(iota((edges, LANES), 1) // rest == to_column(spot) % beside, tail, 0.0)
    values = jnp.concatenate(
        [grad_rel[:, c * LANES : (c + 1) * LANES] for c in range(full)] + [tail], axis=0
    ).astype(BF16)
    spots = jnp.concatenate(
        [base + c * per_device + spot for c in range(full)] + [base + full * per_device + spot // beside], axis=1
    )
    parts = jnp.concatenate([part] * (full + 1), axis=1)
    return [dot(one_hot_rows(jnp.where(parts == q, spots, -1), 2 * shards * rows), values) for q in range(doms // 2)]


def edge_kernel(
    r, bit, doms, per_device, rec_ref, head_ref, tail_ref, rel_ref, own_neg_ref, far_neg_ref, relations_ref, *rest
):
    last = r == bit
    out_ref = rest[-1] if last else rest[-2]
    chunks, slots, width = rec_ref.shape
    shards = chunks // 2
    touched = shards * slots
    negatives = own_neg_ref.shape[1]
    own_half, far_half = halves(r, shards)
    own = rec_ref[own_half].reshape(touched, width)
    far = rec_ref[far_half].reshape(touched, width)
    row = slice(r, r + 1)
    relations = relations_ref.shape[0]
    ids = rel_ref[row]
    hot_head = one_hot_rows(head_ref[row], touched)
    hot_tail = one_hot_rows(tail_ref[row], touched)
    head = dot(hot_head, own, FIRST)
    tail = dot(hot_tail, far, FIRST)
    rel = dot(one_hot_rows(ids, relations), relations_ref[...], FIRST)
    query_tail = (head * rel).astype(BF16)
    query_head = (tail * rel).astype(BF16)

    def counts(neg_ref):
        hit = iota((touched, negatives), 0) == neg_ref[row]
        return jnp.sum(jnp.where(hit, 1.0 / negatives, 0.0), axis=1, keepdims=True)

    weight_tail = (jax.nn.sigmoid(dot(far, query_tail, LAST)) * counts(far_neg_ref)).astype(BF16)
    weight_head = (jax.nn.sigmoid(dot(own, query_head, LAST)) * counts(own_neg_ref)).astype(BF16)
    positive = jnp.sum(head * rel * tail, axis=1, keepdims=True)
    coeff = -jax.nn.sigmoid(-positive)
    back_tail = dot(weight_tail, far, FIRST)
    back_head = dot(weight_head, own, FIRST)
    toward_head = coeff * tail + back_tail
    grad_head = (rel * toward_head).astype(BF16)
    grad_tail = (rel * (coeff * head + back_head)).astype(BF16)
    own_grad = dot(
        jnp.concatenate([hot_head, weight_head], axis=1), jnp.concatenate([grad_head, query_head], axis=0)
    )
    far_grad = dot(
        jnp.concatenate([hot_tail, weight_tail], axis=1), jnp.concatenate([grad_tail, query_tail], axis=0)
    )
    out_ref[own_half, :, :width] = own_grad.astype(BF16).reshape(shards, slots, width)
    out_ref[far_half, :, :width] = far_grad.astype(BF16).reshape(shards, slots, width)
    grad_rel = head * toward_head + tail * back_head

    sums = pack_relations(grad_rel, ids, per_device, shards, doms, bit)
    for q, value in enumerate(sums):
        if last:
            value = (value + rest[0][q]).astype(BF16).reshape(chunks, slots, LANES)
            out_ref[:, :, pl.ds(padded(width) + q * LANES, LANES)] = value
        else:
            rest[-1][q] = value


def relation_sum_kernel(parts_ref, out_ref):
    parts, rows, width = out_ref.shape
    for q in range(parts):
        value = parts_ref[:, :, pl.ds(parts_ref.shape[2] - (parts - q) * LANES, LANES)]
        out_ref[q] = jnp.sum(value.astype(F32), axis=0)


def relation_kernel(kept_ref, came_ref, accum_ref, step_out, accum_out):
    per_device, width = step_out.shape
    full, rest, beside, rows = packed_shape(per_device, width)
    total = kept_ref[0] + came_ref[0]
    tails = [
        total[full * per_device + i // beside :][:1, i % beside * rest : (i % beside + 1) * rest]
        for i in range(per_device)
    ]
    grad = jnp.concatenate(
        [total[c * per_device : (c + 1) * per_device] for c in range(full)] + [jnp.concatenate(tails, axis=0)], axis=1
    )
    accum = to_column(accum_ref[...]) + jnp.mean(grad * grad, axis=1, keepdims=True)
    step_out[...] = -LEARN_RATE * grad / jnp.sqrt(accum)
    accum_out[...] = to_row(accum)


def call(kernel, outs, *args):
    return pl.pallas_call(
        kernel,
        out_shape=[jax.ShapeDtypeStruct(shape, kind) for shape, kind in outs],
        compiler_params=pltpu.CompilerParams(vmem_limit_bytes=48 * 2**20),
    )(*args)


def swap_pair(value, r):
    doms, shards = lax.axis_size("dom"), lax.axis_size("shard")
    groups = [
        [g * shards + s for g in (low, low ^ (1 << r)) for s in range(shards)]
        for low in range(doms)
        if not low >> r & 1
    ]
    return lax.all_to_all(
        value, ("dom", "shard"), split_axis=0, concat_axis=0, axis_index_groups=groups, tiled=True
    )


def body(
    embeddings,
    row_accum,
    relations,
    relation_accum,
    request_rows,
    head_slots,
    tail_slots,
    relation_ids,
    own_negatives,
    far_negatives,
):
    rows, width = embeddings.shape
    doms, shards = lax.axis_size("dom"), lax.axis_size("shard")
    rounds, slots = request_rows.shape[0], request_rows.shape[-1]
    bit = rounds - 1
    per_device = relation_accum.shape[0]
    packed = packed_shape(per_device, width)[3]
    assert packed == slots
    chunks = ((2 * shards, slots, width), BF16)
    wide = ((2 * shards, slots, padded(width) + doms // 2 * LANES), BF16)
    sums = ((doms // 2, 2 * shards * packed, LANES), F32)
    table, accum = embeddings, row_accum.reshape(1, rows)
    state = [((rows, width), F32), ((1, rows), F32)]
    (outgoing,) = call(functools.partial(serve_kernel, 0), [chunks], request_rows, table)
    before = []
    for r in range(rounds):
        last = r == bit
        received = swap_pair(outgoing, r)
        grads, *before = call(
            functools.partial(edge_kernel, r, bit, doms, per_device),
            [wide] if last else [chunks, sums],
            received,
            head_slots,
            tail_slots,
            relation_ids,
            own_negatives,
            far_negatives,
            relations,
            *before,
        )
        back = swap_pair(grads, r)
        if not last:
            table, accum, outgoing = call(
                functools.partial(update_serve_kernel, r), state + [chunks], request_rows, back, table, accum
            )
    (kept,) = call(relation_sum_kernel, [((doms // 2, packed, LANES), F32)], back)
    came = jnp.zeros((1, packed, LANES), F32)
    for b in reversed([b for b in range(doms.bit_length() - 1) if b != bit]):
        half = kept.shape[0] // 2
        came = lax.ppermute(kept[half:], "dom", [(g, g ^ 1 << b) for g in range(doms)])
        kept = kept[:half] if half == 1 else kept[:half] + came
    table, accum = call(functools.partial(update_kernel, bit), state, request_rows, back, table, accum)
    step, rel_accum = call(
        relation_kernel,
        [((per_device, width), F32), ((1, per_device), F32)],
        kept,
        came,
        relation_accum.reshape(1, per_device),
    )
    return (table, accum.reshape(rows), step, rel_accum.reshape(per_device))


def solution(mesh):
    placed = (
        P(("dom", "shard"), None),
        P(("dom", "shard")),
        P(),
        P(("dom", "shard")),
        P(None, ("dom", "shard"), None, None),
        P(None, ("dom", "shard")),
        P(None, ("dom", "shard")),
        P(None, ("dom", "shard")),
        P(None, ("dom", "shard")),
        P(None, ("dom", "shard")),
    )
    return jax.shard_map(
        body,
        mesh=mesh,
        in_specs=placed,
        out_specs=(
            P(("dom", "shard"), None),
            P(("dom", "shard")),
            P(("dom", "shard"), None),
            P(("dom", "shard")),
        ),
        check_vma=False,
    )
```

```python
import functools

import jax
import jax.numpy as jnp
from jax import lax
from jax.experimental import pallas as pl
from jax.experimental.pallas import tpu as pltpu
from jax.sharding import PartitionSpec as P

LEARN_RATE = 0.1
LANES = 128
BF16 = jnp.bfloat16
F32 = jnp.float32
NATURAL = (((1,), (0,)), ((), ()))
LAST = (((1,), (1,)), ((), ()))
FIRST = (((0,), (0,)), ((), ()))


def dot(left, right, dims=NATURAL):
    return lax.dot_general(left, right, dims, preferred_element_type=F32)


def iota(shape, axis):
    return lax.broadcasted_iota(jnp.int32, shape, axis)


def one_hot_rows(row, count):
    return (iota((count, row.shape[1]), 0) == row).astype(BF16)


def to_column(row):
    n = row.shape[1]
    return jnp.sum(jnp.where(iota((n, n), 0) == iota((n, n), 1), row, 0), axis=1, keepdims=True)


def to_row(column):
    n = column.shape[0]
    return jnp.sum(jnp.where(iota((n, n), 0) == iota((n, n), 1), column, 0), axis=0, keepdims=True)


def request_one_hot(request_ref, r, rows):
    ids = jnp.concatenate([request_ref[r, :, 0, :], request_ref[r, :, 1, :]], axis=0)
    pieces, slots = ids.shape
    n = pieces * slots
    spread = ((iota((n, pieces), 0) // slots) ^ lax.axis_index("shard") == iota((n, pieces), 1)).astype(F32)
    rep = dot(spread, ids.astype(F32))
    column = jnp.sum(
        jnp.where(iota((n, slots), 0) % slots == iota((n, slots), 1), rep, 0.0), axis=1, keepdims=True
    )
    return (iota((n, rows), 1) == column.astype(jnp.int32)).astype(BF16)


def put(refs, value, first=0):
    slots = refs[0].shape[0]
    for i in range(value.shape[0] // slots):
        refs[first + i][:, : value.shape[1]] = value[i * slots : (i + 1) * slots]


def serve(request_ref, r, table, out_refs):
    put(out_refs, dot(request_one_hot(request_ref, r, table.shape[0]), table.astype(BF16)).astype(BF16))


def row_update(request_ref, r, back_refs, table, accum_row):
    back = jnp.concatenate([ref[:, : table.shape[1]] for ref in back_refs], axis=0)
    row_grad = dot(request_one_hot(request_ref, r, table.shape[0]), back, FIRST)
    accum = to_column(accum_row) + jnp.mean(row_grad * row_grad, axis=1, keepdims=True)
    return table - LEARN_RATE * row_grad / jnp.sqrt(accum), to_row(accum)


def serve_kernel(r, request_ref, table_ref, *out_refs):
    serve(request_ref, r, table_ref[...], out_refs)


def update_serve_kernel(r, request_ref, table_ref, accum_ref, *refs):
    pieces = (len(refs) - 2) // 2
    table, accum = row_update(request_ref, r, refs[:pieces], table_ref[...], accum_ref[...])
    table_out, accum_out = refs[pieces : pieces + 2]
    table_out[...] = table
    accum_out[...] = accum
    serve(request_ref, r + 1, table, refs[pieces + 2 :])


def update_kernel(r, request_ref, table_ref, accum_ref, *refs):
    table_out, accum_out = refs[-2:]
    table, accum = row_update(request_ref, r, refs[:-2], table_ref[...], accum_ref[...])
    table_out[...] = table
    accum_out[...] = accum


def padded(width):
    return pl.cdiv(width, LANES) * LANES


def packed_shape(per_device, width):
    full, rest = width // LANES, width % LANES
    beside = LANES // rest
    return full, rest, beside, per_device * full + pl.cdiv(per_device, beside)


def place_relations(ids, per_device, rows, shards, doms, bit):
    owner, spot = ids // per_device, ids % per_device
    away = (owner // shards) ^ lax.axis_index("dom")
    part = (away & ((1 << bit) - 1)) | (away >> (bit + 1) << bit)
    chunk = (away >> bit & 1) * shards + (owner % shards ^ lax.axis_index("shard"))
    return part, chunk * rows, spot


def pack_relations(grad_rel, ids, per_device, shards, doms, bit):
    edges, width = grad_rel.shape
    full, rest, beside, rows = packed_shape(per_device, width)
    part, base, spot = place_relations(ids, per_device, rows, shards, doms, bit)
    tail = jnp.concatenate([grad_rel[:, full * LANES :]] * beside, axis=1)
    tail = jnp.where(iota((edges, LANES), 1) // rest == to_column(spot) % beside, tail, 0.0)
    values = jnp.concatenate(
        [grad_rel[:, c * LANES : (c + 1) * LANES] for c in range(full)] + [tail], axis=0
    ).astype(BF16)
    spots = jnp.concatenate(
        [base + c * per_device + spot for c in range(full)] + [base + full * per_device + spot // beside], axis=1
    )
    parts = jnp.concatenate([part] * (full + 1), axis=1)
    return [dot(one_hot_rows(jnp.where(parts == q, spots, -1), 2 * shards * rows), values) for q in range(doms // 2)]


def edge_kernel(
    r, bit, doms, per_device, head_ref, tail_ref, rel_ref, own_neg_ref, far_neg_ref, relations_ref, *refs
):
    last = r == bit
    pieces = (len(refs) - 1) // 2
    rec_refs = refs[:pieces]
    out_refs, sum_ref = (refs[pieces + 1 :], refs[pieces]) if last else (refs[pieces:-1], refs[-1])
    shards = pieces // 2
    slots, width = rec_refs[0].shape
    touched = shards * slots
    negatives = own_neg_ref.shape[1]
    own = jnp.concatenate([ref[...] for ref in rec_refs[:shards]], axis=0)
    far = jnp.concatenate([ref[...] for ref in rec_refs[shards:]], axis=0)
    row = slice(r, r + 1)
    mine = lax.axis_index("shard") * slots
    ids = rel_ref[row]
    hot_head = one_hot_rows(head_ref[row] ^ mine, touched)
    hot_tail = one_hot_rows(tail_ref[row] ^ mine, touched)
    head = dot(hot_head, own, FIRST)
    tail = dot(hot_tail, far, FIRST)
    rel = dot(one_hot_rows(ids, relations_ref.shape[0]), relations_ref[...], FIRST)
    query_tail = (head * rel).astype(BF16)
    query_head = (tail * rel).astype(BF16)

    def counts(neg_ref):
        hit = iota((touched, negatives), 0) == neg_ref[row] ^ mine
        return jnp.sum(jnp.where(hit, 1.0 / negatives, 0.0), axis=1, keepdims=True)

    weight_tail = (jax.nn.sigmoid(dot(far, query_tail, LAST)) * counts(far_neg_ref)).astype(BF16)
    weight_head = (jax.nn.sigmoid(dot(own, query_head, LAST)) * counts(own_neg_ref)).astype(BF16)
    positive = jnp.sum(head * rel * tail, axis=1, keepdims=True)
    coeff = -jax.nn.sigmoid(-positive)
    back_tail = dot(weight_tail, far, FIRST)
    back_head = dot(weight_head, own, FIRST)
    toward_head = coeff * tail + back_tail
    grad_head = (rel * toward_head).astype(BF16)
    grad_tail = (rel * (coeff * head + back_head)).astype(BF16)
    own_grad = dot(
        jnp.concatenate([hot_head, weight_head], axis=1), jnp.concatenate([grad_head, query_head], axis=0)
    )
    far_grad = dot(
        jnp.concatenate([hot_tail, weight_tail], axis=1), jnp.concatenate([grad_tail, query_tail], axis=0)
    )
    put(out_refs, own_grad.astype(BF16))
    put(out_refs, far_grad.astype(BF16), shards)
    grad_rel = head * toward_head + tail * back_head

    sums = pack_relations(grad_rel, ids, per_device, shards, doms, bit)
    for q, value in enumerate(sums):
        if last:
            value = (value + sum_ref[q]).astype(BF16)
            for i in range(pieces):
                out_refs[i][:, pl.ds(padded(width) + q * LANES, LANES)] = value[i * slots : (i + 1) * slots]
        else:
            sum_ref[q] = value


def relation_sum_kernel(*refs):
    part_refs, (kept_out, sent_out) = refs[:-2], refs[-2:]
    for out, first in ((kept_out, 0), (sent_out, kept_out.shape[0])):
        for q in range(out.shape[0]):
            lane = part_refs[0].shape[1] - (2 * kept_out.shape[0] - first - q) * LANES
            out[q] = sum(ref[:, pl.ds(lane, LANES)].astype(F32) for ref in part_refs)


def relation_kernel(kept_ref, came_ref, accum_ref, step_out, accum_out):
    per_device, width = step_out.shape
    full, rest, beside, rows = packed_shape(per_device, width)
    total = kept_ref[0] + came_ref[0]
    tails = [
        total[full * per_device + i // beside :][:1, i % beside * rest : (i % beside + 1) * rest]
        for i in range(per_device)
    ]
    grad = jnp.concatenate(
        [total[c * per_device : (c + 1) * per_device] for c in range(full)] + [jnp.concatenate(tails, axis=0)], axis=1
    )
    accum = to_column(accum_ref[...]) + jnp.mean(grad * grad, axis=1, keepdims=True)
    step_out[...] = -LEARN_RATE * grad / jnp.sqrt(accum)
    accum_out[...] = to_row(accum)


def call(kernel, outs, *args):
    return pl.pallas_call(
        kernel,
        out_shape=[jax.ShapeDtypeStruct(shape, kind) for shape, kind in outs],
        compiler_params=pltpu.CompilerParams(vmem_limit_bytes=48 * 2**20),
    )(*args)


def exchange(pieces, r):
    doms, shards = lax.axis_size("dom"), lax.axis_size("shard")
    came = [pieces[0]]
    for i in range(1, len(pieces)):
        swap = i // shards << r, i % shards
        pairs = [
            (g * shards + s, (g ^ swap[0]) * shards + (s ^ swap[1])) for g in range(doms) for s in range(shards)
        ]
        came.append(lax.ppermute(pieces[i], ("dom", "shard"), pairs))
    return came


def body(
    embeddings,
    row_accum,
    relations,
    relation_accum,
    request_rows,
    head_slots,
    tail_slots,
    relation_ids,
    own_negatives,
    far_negatives,
):
    rows, width = embeddings.shape
    doms, shards = lax.axis_size("dom"), lax.axis_size("shard")
    rounds, slots = request_rows.shape[0], request_rows.shape[-1]
    bit = rounds - 1
    per_device = relation_accum.shape[0]
    packed = packed_shape(per_device, width)[3]
    assert packed == slots
    chunks = [((slots, width), BF16)] * (2 * shards)
    wide = [((slots, padded(width) + doms // 2 * LANES), BF16)] * (2 * shards)
    sums = ((doms // 2, 2 * shards * packed, LANES), F32)
    table, accum = embeddings, row_accum.reshape(1, rows)
    state = [((rows, width), F32), ((1, rows), F32)]
    outgoing = call(functools.partial(serve_kernel, 0), chunks, request_rows, table)
    edges = (head_slots, tail_slots, relation_ids, own_negatives, far_negatives, relations)
    before = []
    for r in range(rounds):
        last = r == bit
        received = exchange(outgoing, r)
        done = call(
            functools.partial(edge_kernel, r, bit, doms, per_device),
            wide if last else chunks + [sums],
            *edges,
            *received,
            *before,
        )
        grads, before = done[: 2 * shards], done[2 * shards :]
        back = exchange(grads, r)
        if not last:
            table, accum, *outgoing = call(
                functools.partial(update_serve_kernel, r), state + chunks, request_rows, table, accum, *back
            )
    kept, came = call(relation_sum_kernel, [((doms // 4, packed, LANES), F32)] * 2, *back)
    for b in reversed([b for b in range(doms.bit_length() - 1) if b != bit]):
        came = lax.ppermute(came, "dom", [(g, g ^ 1 << b) for g in range(doms)])
        half = kept.shape[0] // 2
        if half:
            kept, came = jnp.split(kept + came, 2)
    table, accum = call(functools.partial(update_kernel, bit), state, request_rows, table, accum, *back)
    step, rel_accum = call(
        relation_kernel,
        [((per_device, width), F32), ((1, per_device), F32)],
        kept,
        came,
        relation_accum.reshape(1, per_device),
    )
    return (table, accum.reshape(rows), step, rel_accum.reshape(per_device))


def solution(mesh):
    placed = (
        P(("dom", "shard"), None),
        P(("dom", "shard")),
        P(),
        P(("dom", "shard")),
        P(None, ("dom", "shard"), None, None),
        P(None, ("dom", "shard")),
        P(None, ("dom", "shard")),
        P(None, ("dom", "shard")),
        P(None, ("dom", "shard")),
        P(None, ("dom", "shard")),
    )
    return jax.shard_map(
        body,
        mesh=mesh,
        in_specs=placed,
        out_specs=(
            P(("dom", "shard"), None),
            P(("dom", "shard")),
            P(("dom", "shard"), None),
            P(("dom", "shard")),
        ),
        check_vma=False,
    )
```

```python
import functools

import jax
import jax.numpy as jnp
from jax import lax
from jax.experimental import pallas as pl
from jax.experimental.pallas import tpu as pltpu
from jax.sharding import PartitionSpec as P

LEARN_RATE = 0.1
LANES = 128
BF16 = jnp.bfloat16
F32 = jnp.float32
NATURAL = (((1,), (0,)), ((), ()))
LAST = (((1,), (1,)), ((), ()))
FIRST = (((0,), (0,)), ((), ()))
HBM = pl.BlockSpec(memory_space=pltpu.HBM)
VMEM = pl.BlockSpec(memory_space=pltpu.VMEM)


def dot(left, right, dims=NATURAL):
    return lax.dot_general(left, right, dims, preferred_element_type=F32)


def iota(shape, axis):
    return lax.broadcasted_iota(jnp.int32, shape, axis)


def one_hot_t(row, count):
    return (iota((count, row.shape[1]), 0) == row).astype(BF16)


def one_hot(column, count):
    return (iota((column.shape[0], count), 1) == column).astype(BF16)


def to_column(row):
    n = row.shape[1]
    return jnp.sum(jnp.where(iota((n, n), 0) == iota((n, n), 1), row, 0), axis=1, keepdims=True)


def to_row(column):
    n = column.shape[0]
    return jnp.sum(jnp.where(iota((n, n), 0) == iota((n, n), 1), column, 0), axis=0, keepdims=True)


def request_column(request_ref, r):
    ids = jnp.concatenate([request_ref[r, :, 0, :], request_ref[r, :, 1, :]], axis=0)
    pieces, slots = ids.shape
    n = pieces * slots
    spread = (iota((n, pieces), 0) // slots == iota((n, pieces), 1)).astype(F32)
    rep = dot(spread, ids.astype(F32))
    column = jnp.sum(
        jnp.where(iota((n, slots), 0) % slots == iota((n, slots), 1), rep, 0.0), axis=1, keepdims=True
    )
    return column.astype(jnp.int32)


def halves(r, shards):
    bit = (lax.axis_index("dom") >> r) & 1
    return pl.ds(bit * shards, shards), pl.ds((1 - bit) * shards, shards)


def serve(r, hot, table, out_ref):
    shards, slots = out_ref.shape[0] // 2, out_ref.shape[1]
    served = dot(hot, table.astype(BF16)).astype(BF16).reshape(2, shards, slots, table.shape[1])
    for half, value in zip(halves(r, shards), served):
        out_ref[half] = value


def first_kernel(request_hbm, table_hbm, out_ref, request_ref, table_ref, sems):
    copies = [
        pltpu.make_async_copy(request_hbm, request_ref, sems.at[0]),
        pltpu.make_async_copy(table_hbm, table_ref, sems.at[1]),
    ]
    for copy in copies:
        copy.start()
    copies[0].wait()
    hot = one_hot(request_column(request_ref, 0), table_ref.shape[0])
    copies[1].wait()
    serve(0, hot, table_ref[...], out_ref)


def row_update(r, hot_t, back_ref, table, accum):
    chunks, slots, _ = back_ref.shape
    width = table.shape[1]
    back = jnp.concatenate(
        [back_ref[half, :, :width].reshape(chunks // 2 * slots, width) for half in halves(r, chunks // 2)], axis=0
    )
    row_grad = dot(hot_t, back)
    accum = accum + jnp.mean(row_grad * row_grad, axis=1, keepdims=True)
    return table - row_grad * (LEARN_RATE / jnp.sqrt(accum)), accum


def middle_kernel(r, back_ref, table_ref, accum_ref, hot_ref, hot_t_ref, table_out, accum_out, out_ref):
    table, accum = row_update(r, hot_t_ref[r], back_ref, table_ref[...], accum_ref[...])
    serve(r + 1, hot_ref[r + 1], table, out_ref)
    table_out[...] = table
    accum_out[...] = accum


def update_kernel(r, back_ref, table_ref, accum_ref, hot_t_ref, table_out, accum_out):
    table, accum = row_update(r, hot_t_ref[r], back_ref, table_ref[...], accum_ref[...])
    table_out[...] = table
    accum_out[...] = to_row(accum)


def padded(width):
    return pl.cdiv(width, LANES) * LANES


def packed_shape(per_device, width):
    full, rest = width // LANES, width % LANES
    beside = LANES // rest
    return full, rest, beside, per_device * full + pl.cdiv(per_device, beside)


def place_relations(ids, per_device, width, shards, doms, bit):
    full, rest, beside, rows = packed_shape(per_device, width)
    owner, spot = ids // per_device, ids % per_device
    away = (owner // shards) ^ (lax.axis_index("dom") & ~(1 << bit))
    part = (away & ((1 << bit) - 1)) | (away >> (bit + 1) << bit)
    base = ((away >> bit & 1) * shards + owner % shards) * rows
    spots = jnp.concatenate(
        [base + c * per_device + spot for c in range(full)] + [base + full * per_device + spot // beside], axis=1
    )
    parts = jnp.concatenate([part] * (full + 1), axis=1)
    hots = [one_hot_t(jnp.where(parts == q, spots, -1), 2 * shards * rows) for q in range(doms // 2)]
    mask = iota((ids.shape[1], LANES), 1) // rest == to_column(spot) % beside
    return hots, mask.astype(F32)


def pack_relations(grad_rel, place_ref, mask_ref, r):
    width = grad_rel.shape[1]
    full, rest = width // LANES, width % LANES
    tail = jnp.concatenate([grad_rel[:, full * LANES :]] * (LANES // rest), axis=1) * mask_ref[r]
    values = jnp.concatenate(
        [grad_rel[:, c * LANES : (c + 1) * LANES] for c in range(full)] + [tail], axis=0
    ).astype(BF16)
    return [dot(place_ref[r, q], values) for q in range(place_ref.shape[1])]


def index_kernel(
    bit,
    doms,
    per_device,
    request_ref,
    head_ref,
    tail_ref,
    rel_ref,
    own_neg_ref,
    far_neg_ref,
    relations_ref,
    row_accum_ref,
    relation_accum_ref,
    hots_out,
    hots_t_out,
    scales_out,
    scales_t_out,
    rel_out,
    request_out,
    request_t_out,
    place_out,
    mask_out,
    row_accum_out,
    relation_accum_out,
):
    rounds, _, edges, touched = hots_out.shape
    negatives = own_neg_ref.shape[1]
    rows, shards = request_out.shape[2], request_ref.shape[1]
    relations, width = relations_ref.shape
    for r in range(rounds):
        row = slice(r, r + 1)
        for side, (slot_ref, neg_ref) in enumerate(((head_ref, own_neg_ref), (tail_ref, far_neg_ref))):
            hots_out[r, side] = one_hot(to_column(slot_ref[row]), touched)
            hots_t_out[r, side] = one_hot_t(slot_ref[row], touched)
            hit = iota((touched, negatives), 0) == neg_ref[row]
            scale = jnp.sum(jnp.where(hit, 1.0 / negatives, 0.0), axis=1, keepdims=True)
            scales_t_out[r, side] = jnp.broadcast_to(scale, (touched, edges))
            scales_out[r, side] = jnp.broadcast_to(to_row(scale), (edges, touched))
        ids = rel_ref[row]
        rel_out[r] = dot(one_hot(to_column(ids), relations), relations_ref[...])
        column = request_column(request_ref, r)
        request_out[r] = one_hot(column, rows)
        request_t_out[r] = one_hot_t(to_row(column), rows)
        hots, mask = place_relations(ids, per_device, width, shards, doms, bit)
        for q, hot in enumerate(hots):
            place_out[r, q] = hot
        mask_out[r] = mask
    row_accum_out[...] = to_column(row_accum_ref[...])
    relation_accum_out[...] = to_column(relation_accum_ref[...])


def edge_kernel(r, rec_ref, hots_ref, hots_t_ref, scales_ref, scales_t_ref, rel_ref, *rest):
    last = len(rest) == 4
    out_ref = rest[-1] if last else rest[0]
    chunks, slots, width = rec_ref.shape
    shards = chunks // 2
    own_half, far_half = halves(r, shards)
    own = rec_ref[own_half].reshape(shards * slots, width)
    far = rec_ref[far_half].reshape(shards * slots, width)
    head = dot(hots_ref[r, 0], own)
    tail = dot(hots_ref[r, 1], far)
    rel = rel_ref[r]
    query_tail = (head * rel).astype(BF16)
    query_head = (tail * rel).astype(BF16)

    def weights(rows, columns, scale_ref, side):
        return (jax.nn.sigmoid(dot(rows, columns, LAST)) * scale_ref[r, side]).astype(BF16)

    back_tail = dot(weights(query_tail, far, scales_ref, 1), far)
    back_head = dot(weights(query_head, own, scales_ref, 0), own)
    positive = jnp.sum(head * rel * tail, axis=1, keepdims=True)
    coeff = -jax.nn.sigmoid(-positive)
    toward_head = coeff * tail + back_tail
    grad_head = (rel * toward_head).astype(BF16)
    grad_tail = (rel * (coeff * head + back_head)).astype(BF16)
    grad_rel = head * toward_head + tail * back_head
    if last:
        place_ref, mask_ref, sum_ref, _ = rest
        for q, value in enumerate(pack_relations(grad_rel, place_ref, mask_ref, r)):
            value = (value + sum_ref[q]).astype(BF16).reshape(chunks, slots, LANES)
            out_ref[:, :, pl.ds(padded(width) + q * LANES, LANES)] = value
    else:
        rest[1][...] = grad_rel
    own_weights = weights(own, query_head, scales_t_ref, 0)
    far_weights = weights(far, query_tail, scales_t_ref, 1)
    own_grad = dot(
        jnp.concatenate([hots_t_ref[r, 0], own_weights], axis=1), jnp.concatenate([grad_head, query_head], axis=0)
    )
    far_grad = dot(
        jnp.concatenate([hots_t_ref[r, 1], far_weights], axis=1), jnp.concatenate([grad_tail, query_tail], axis=0)
    )
    out_ref[own_half, :, :width] = own_grad.astype(BF16).reshape(shards, slots, width)
    out_ref[far_half, :, :width] = far_grad.astype(BF16).reshape(shards, slots, width)


def pack_kernel(r, grad_ref, place_ref, mask_ref, *rest):
    out_ref = rest[-1]
    for q, value in enumerate(pack_relations(grad_ref[...], place_ref, mask_ref, r)):
        out_ref[q] = value + rest[0][q] if len(rest) == 2 else value


def relation_sum_kernel(parts_ref, kept_out, sent_out):
    half = kept_out.shape[0]
    for q in range(2 * half):
        value = parts_ref[:, :, pl.ds(parts_ref.shape[2] - (2 * half - q) * LANES, LANES)]
        out = kept_out if q < half else sent_out
        out[q % half] = jnp.sum(value.astype(F32), axis=0)


def last_kernel(
    table_ref, row_accum_ref, kept_ref, came_ref, accum_ref, table_out, row_accum_out, step_out, accum_out, *scratch
):
    step_ref, new_accum_ref, sems = scratch
    copies = [
        pltpu.make_async_copy(source, target, sems.at[i])
        for i, (source, target) in enumerate(
            (
                (table_ref, table_out),
                (row_accum_ref, row_accum_out),
                (step_ref, step_out),
                (new_accum_ref, accum_out),
            )
        )
    ]
    copies[0].start()
    copies[1].start()
    per_device, width = step_ref.shape
    full, rest, beside, rows = packed_shape(per_device, width)
    total = kept_ref[0] + came_ref[0]
    tails = [
        total[full * per_device + i // beside :][:1, i % beside * rest : (i % beside + 1) * rest]
        for i in range(per_device)
    ]
    grad = jnp.concatenate(
        [total[c * per_device : (c + 1) * per_device] for c in range(full)] + [jnp.concatenate(tails, axis=0)], axis=1
    )
    accum = accum_ref[...] + jnp.mean(grad * grad, axis=1, keepdims=True)
    step_ref[...] = grad * (-LEARN_RATE / jnp.sqrt(accum))
    new_accum_ref[...] = to_row(accum)
    copies[2].start()
    copies[3].start()
    for copy in copies:
        copy.wait()


def call(kernel, outs, *args, **kwargs):
    return pl.pallas_call(
        kernel,
        out_shape=[jax.ShapeDtypeStruct(shape, kind) for shape, kind in outs],
        compiler_params=pltpu.CompilerParams(vmem_limit_bytes=48 * 2**20),
        **kwargs,
    )(*args)


def swap_pair(value, r):
    doms, shards = lax.axis_size("dom"), lax.axis_size("shard")
    groups = [
        [g * shards + s for g in (low, low ^ (1 << r)) for s in range(shards)]
        for low in range(doms)
        if not low >> r & 1
    ]
    return lax.all_to_all(
        value, ("dom", "shard"), split_axis=0, concat_axis=0, axis_index_groups=groups, tiled=True
    )


def body(
    embeddings,
    row_accum,
    relations,
    relation_accum,
    request_rows,
    head_slots,
    tail_slots,
    relation_ids,
    own_negatives,
    far_negatives,
):
    rows, width = embeddings.shape
    doms, shards = lax.axis_size("dom"), lax.axis_size("shard")
    rounds, slots = request_rows.shape[0], request_rows.shape[-1]
    edges, touched, requests = head_slots.shape[1], shards * slots, 2 * shards * slots
    bit = rounds - 1
    parts = doms // 2
    per_device = relation_accum.shape[0]
    full, _, _, packed = packed_shape(per_device, width)
    assert packed == slots
    chunks = ((2 * shards, slots, width), BF16)
    wide = ((2 * shards, slots, padded(width) + parts * LANES), BF16)
    (outgoing,) = call(
        first_kernel,
        [chunks],
        request_rows,
        embeddings,
        in_specs=[HBM, HBM],
        scratch_shapes=[
            pltpu.VMEM(request_rows.shape, jnp.int32),
            pltpu.VMEM(embeddings.shape, F32),
            pltpu.SemaphoreType.DMA((2,)),
        ],
    )
    hots, hots_t, scales, scales_t, rel, request, request_t, place, mask, accum, relation_accum = call(
        functools.partial(index_kernel, bit, doms, per_device),
        [
            ((rounds, 2, edges, touched), BF16),
            ((rounds, 2, touched, edges), BF16),
            ((rounds, 2, edges, touched), F32),
            ((rounds, 2, touched, edges), F32),
            ((rounds, edges, width), F32),
            ((rounds, requests, rows), BF16),
            ((rounds, rows, requests), BF16),
            ((rounds, parts, 2 * shards * packed, (full + 1) * edges), BF16),
            ((rounds, edges, LANES), F32),
            ((rows, 1), F32),
            ((per_device, 1), F32),
        ],
        request_rows,
        head_slots,
        tail_slots,
        relation_ids,
        own_negatives,
        far_negatives,
        relations,
        row_accum.reshape(1, rows),
        relation_accum.reshape(1, per_device),
    )
    table = embeddings
    sums = []
    for r in range(rounds):
        received = swap_pair(outgoing, r)
        edge_args = (received, hots, hots_t, scales, scales_t, rel)
        if r < bit:
            grads, grad_rel = call(
                functools.partial(edge_kernel, r), [chunks, ((edges, width), F32)], *edge_args
            )
            sums = call(
                functools.partial(pack_kernel, r),
                [((parts, 2 * shards * packed, LANES), F32)],
                grad_rel,
                place,
                mask,
                *sums,
            )
            back = swap_pair(grads, r)
            table, accum, outgoing = call(
                functools.partial(middle_kernel, r),
                [((rows, width), F32), ((rows, 1), F32), chunks],
                back,
                table,
                accum,
                request,
                request_t,
            )
        else:
            (grads,) = call(functools.partial(edge_kernel, r), [wide], *edge_args, place, mask, *sums)
            back = swap_pair(grads, r)
    kept, came = call(relation_sum_kernel, [((parts // 2, packed, LANES), F32)] * 2, back)
    for b in reversed([b for b in range(doms.bit_length() - 1) if b != bit]):
        came = lax.ppermute(came, "dom", [(g, g ^ 1 << b) for g in range(doms)])
        if kept.shape[0] > 1:
            kept, came = jnp.split(kept + came, 2)
    table, accum = call(
        functools.partial(update_kernel, bit), [((rows, width), F32), ((1, rows), F32)], back, table, accum, request_t
    )
    table, accum, step, relation_accum = call(
        last_kernel,
        [((rows, width), F32), ((1, rows), F32), ((per_device, width), F32), ((1, per_device), F32)],
        table,
        accum,
        kept,
        came,
        relation_accum,
        in_specs=[VMEM] * 5,
        out_specs=[HBM] * 4,
        scratch_shapes=[
            pltpu.VMEM((per_device, width), F32),
            pltpu.VMEM((1, per_device), F32),
            pltpu.SemaphoreType.DMA((4,)),
        ],
    )
    return (table, accum.reshape(rows), step, relation_accum.reshape(per_device))


def solution(mesh):
    placed = (
        P(("dom", "shard"), None),
        P(("dom", "shard")),
        P(),
        P(("dom", "shard")),
        P(None, ("dom", "shard"), None, None),
        P(None, ("dom", "shard")),
        P(None, ("dom", "shard")),
        P(None, ("dom", "shard")),
        P(None, ("dom", "shard")),
        P(None, ("dom", "shard")),
    )
    return jax.shard_map(
        body,
        mesh=mesh,
        in_specs=placed,
        out_specs=(
            P(("dom", "shard"), None),
            P(("dom", "shard")),
            P(("dom", "shard"), None),
            P(("dom", "shard")),
        ),
        check_vma=False,
    )
```

```python
import functools

import jax
import jax.numpy as jnp
from jax import lax
from jax.experimental import pallas as pl
from jax.experimental.pallas import tpu as pltpu
from jax.sharding import PartitionSpec as P

LEARN_RATE = 0.1
LANES = 128
VMEM_LIMIT = 48 * 2**20
BF16 = jnp.bfloat16
F32 = jnp.float32
NATURAL = (((1,), (0,)), ((), ()))
LAST = (((1,), (1,)), ((), ()))
FIRST = (((0,), (0,)), ((), ()))
HBM = pl.BlockSpec(memory_space=pltpu.HBM)
VMEM = pl.BlockSpec(memory_space=pltpu.VMEM)


def dot(left, right, dims=NATURAL):
    return lax.dot_general(left, right, dims, preferred_element_type=F32)


def iota(shape, axis):
    return lax.broadcasted_iota(jnp.int32, shape, axis)


def one_hot_t(row, count):
    return (iota((count, row.shape[1]), 0) == row).astype(BF16)


def one_hot(column, count):
    return (iota((column.shape[0], count), 1) == column).astype(BF16)


def to_column(row):
    n = row.shape[1]
    return jnp.sum(jnp.where(iota((n, n), 0) == iota((n, n), 1), row, 0), axis=1, keepdims=True)


def to_row(column):
    n = column.shape[0]
    return jnp.sum(jnp.where(iota((n, n), 0) == iota((n, n), 1), column, 0), axis=0, keepdims=True)


def request_column(request_ref, r):
    ids = jnp.concatenate([request_ref[r, :, 0, :], request_ref[r, :, 1, :]], axis=0)
    pieces, slots = ids.shape
    n = pieces * slots
    spread = (iota((n, pieces), 0) // slots == iota((n, pieces), 1)).astype(F32)
    rep = dot(spread, ids.astype(F32))
    column = jnp.sum(
        jnp.where(iota((n, slots), 0) % slots == iota((n, slots), 1), rep, 0.0), axis=1, keepdims=True
    )
    return column.astype(jnp.int32)


def halves(r, shards):
    bit = (lax.axis_index("dom") >> r) & 1
    return pl.ds(bit * shards, shards), pl.ds((1 - bit) * shards, shards)


def serve(r, hot, table, out_ref):
    shards, slots = out_ref.shape[0] // 2, out_ref.shape[1]
    served = dot(hot, table.astype(BF16)).astype(BF16).reshape(2, shards, slots, table.shape[1])
    for half, value in zip(halves(r, shards), served):
        out_ref[half] = value


def first_kernel(request_ref, table_ref, out_ref):
    serve(0, one_hot(request_column(request_ref, 0), table_ref.shape[0]), table_ref[...], out_ref)


def row_update(r, request_ref, back_ref, table, accum):
    chunks, slots, _ = back_ref.shape
    rows, width = table.shape
    back = jnp.concatenate(
        [back_ref[half, :, :width].reshape(chunks // 2 * slots, width) for half in halves(r, chunks // 2)], axis=0
    )
    row_grad = dot(one_hot(request_column(request_ref, r), rows), back, FIRST)
    accum = accum + jnp.mean(row_grad * row_grad, axis=1, keepdims=True)
    return table - row_grad * (LEARN_RATE / jnp.sqrt(accum)), accum


def middle_kernel(r, request_ref, back_ref, table_ref, accum_ref, table_out, accum_out, out_ref):
    table, accum = row_update(r, request_ref, back_ref, table_ref[...], accum_ref[...])
    serve(r + 1, one_hot(request_column(request_ref, r + 1), table.shape[0]), table, out_ref)
    table_out[...] = table
    accum_out[...] = accum


def update_kernel(r, request_ref, back_ref, table_ref, accum_ref, table_out, accum_out):
    table, accum = row_update(r, request_ref, back_ref, table_ref[...], accum_ref[...])
    table_out[...] = table
    accum_out[...] = to_row(accum)


def padded(width):
    return pl.cdiv(width, LANES) * LANES


def packed_shape(per_device, width):
    full, rest = width // LANES, width % LANES
    beside = LANES // rest
    return full, rest, beside, per_device * full + pl.cdiv(per_device, beside)


def pack_relations(grad_rel, ids, per_device, shards, doms, bit):
    edges, width = grad_rel.shape
    full, rest, beside, rows = packed_shape(per_device, width)
    owner, spot = ids // per_device, ids % per_device
    away = (owner // shards) ^ (lax.axis_index("dom") & ~(1 << bit))
    part = (away & ((1 << bit) - 1)) | (away >> (bit + 1) << bit)
    base = ((away >> bit & 1) * shards + owner % shards) * rows
    places = jnp.concatenate(
        [base + c * per_device + spot for c in range(full)] + [base + full * per_device + spot // beside], axis=1
    )
    group = to_column(part * beside + spot % beside)
    lane = iota((edges, doms // 2 * LANES), 1)
    tail = jnp.concatenate([grad_rel[:, full * LANES :]] * (beside * doms // 2), axis=1)
    here = lane // LANES == group // beside
    values = [
        jnp.where(here, jnp.concatenate([grad_rel[:, c * LANES : (c + 1) * LANES]] * (doms // 2), axis=1), 0.0)
        for c in range(full)
    ] + [jnp.where(lane // rest == group, tail, 0.0)]
    return dot(one_hot_t(places, 2 * shards * rows), jnp.concatenate(values, axis=0).astype(BF16))


def edge_kernel(
    r,
    bit,
    doms,
    per_device,
    rec_ref,
    head_ref,
    tail_ref,
    rel_ref,
    own_neg_ref,
    far_neg_ref,
    relations_ref,
    *refs,
):
    last = r == bit
    out_ref = refs[-1] if last else refs[-2]
    chunks, slots, width = rec_ref.shape
    shards = chunks // 2
    touched = shards * slots
    negatives = own_neg_ref.shape[1]
    own_half, far_half = halves(r, shards)
    own = rec_ref[own_half].reshape(touched, width)
    far = rec_ref[far_half].reshape(touched, width)
    row = slice(r, r + 1)
    ids = rel_ref[row]
    hot_head = one_hot_t(head_ref[row], touched)
    hot_tail = one_hot_t(tail_ref[row], touched)
    head = dot(hot_head, own, FIRST)
    tail = dot(hot_tail, far, FIRST)
    rel = dot(one_hot_t(ids, relations_ref.shape[0]), relations_ref[...], FIRST)
    query_tail = (head * rel).astype(BF16)
    query_head = (tail * rel).astype(BF16)

    def weights(rows, query, neg_ref):
        hit = iota((touched, negatives), 0) == neg_ref[row]
        scale = jnp.sum(jnp.where(hit, 1.0 / negatives, 0.0), axis=1, keepdims=True)
        return (jax.nn.sigmoid(dot(rows, query, LAST)) * scale).astype(BF16)

    weight_tail = weights(far, query_tail, far_neg_ref)
    weight_head = weights(own, query_head, own_neg_ref)
    positive = jnp.sum(head * rel * tail, axis=1, keepdims=True)
    coeff = -jax.nn.sigmoid(-positive)
    back_tail = dot(weight_tail, far, FIRST)
    back_head = dot(weight_head, own, FIRST)
    toward_head = coeff * tail + back_tail
    grad_head = (rel * toward_head).astype(BF16)
    grad_tail = (rel * (coeff * head + back_head)).astype(BF16)
    grad_rel = head * toward_head + tail * back_head
    own_grad = dot(
        jnp.concatenate([hot_head, weight_head], axis=1), jnp.concatenate([grad_head, query_head], axis=0)
    )
    far_grad = dot(
        jnp.concatenate([hot_tail, weight_tail], axis=1), jnp.concatenate([grad_tail, query_tail], axis=0)
    )
    out_ref[own_half, :, :width] = own_grad.astype(BF16).reshape(shards, slots, width)
    out_ref[far_half, :, :width] = far_grad.astype(BF16).reshape(shards, slots, width)
    sums = pack_relations(grad_rel, ids, per_device, shards, doms, bit)
    if last:
        sums = (sums + refs[0][...]).astype(BF16)
        out_ref[:, :, pl.ds(padded(width), sums.shape[1])] = sums.reshape(chunks, slots, sums.shape[1])
    elif r:
        refs[-1][...] = sums + refs[0][...]
    else:
        refs[-1][...] = sums


def first_edge_kernel(*refs):
    *edge_args, row_accum_ref, accum_ref, out_ref, sum_out, row_accum_out, accum_out = refs[4:]
    row_accum_out[...] = to_column(row_accum_ref[...])
    accum_out[...] = to_column(accum_ref[...])
    edge_kernel(*refs[:4], *edge_args, out_ref, sum_out)


def relation_sum_kernel(parts_ref, kept_out, sent_out):
    half = kept_out.shape[0]
    for q in range(2 * half):
        value = parts_ref[:, :, pl.ds(parts_ref.shape[2] - (2 * half - q) * LANES, LANES)]
        out = kept_out if q < half else sent_out
        out[q % half] = jnp.sum(value.astype(F32), axis=0)


def last_kernel(
    table_ref, row_accum_ref, kept_ref, came_ref, accum_ref, table_out, row_accum_out, step_out, accum_out, *scratch
):
    step_ref, new_accum_ref, sems = scratch
    copies = [
        pltpu.make_async_copy(source, target, sems.at[i])
        for i, (source, target) in enumerate(
            (
                (table_ref, table_out),
                (row_accum_ref, row_accum_out),
                (step_ref, step_out),
                (new_accum_ref, accum_out),
            )
        )
    ]
    copies[0].start()
    copies[1].start()
    per_device, width = step_ref.shape
    full, rest, beside, rows = packed_shape(per_device, width)
    total = kept_ref[0] + came_ref[0]
    tails = [
        total[full * per_device + i // beside :][:1, i % beside * rest : (i % beside + 1) * rest]
        for i in range(per_device)
    ]
    grad = jnp.concatenate(
        [total[c * per_device : (c + 1) * per_device] for c in range(full)] + [jnp.concatenate(tails, axis=0)], axis=1
    )
    accum = accum_ref[...] + jnp.mean(grad * grad, axis=1, keepdims=True)
    step_ref[...] = grad * (-LEARN_RATE / jnp.sqrt(accum))
    new_accum_ref[...] = to_row(accum)
    copies[2].start()
    copies[3].start()
    for copy in copies:
        copy.wait()


def call(kernel, outs, *args, **kwargs):
    return pl.pallas_call(
        kernel,
        out_shape=[jax.ShapeDtypeStruct(shape, kind) for shape, kind in outs],
        compiler_params=pltpu.CompilerParams(vmem_limit_bytes=VMEM_LIMIT),
        **kwargs,
    )(*args)


def swap_pair(value, r):
    doms, shards = lax.axis_size("dom"), lax.axis_size("shard")
    groups = [
        [g * shards + s for g in (low, low ^ (1 << r)) for s in range(shards)]
        for low in range(doms)
        if not low >> r & 1
    ]
    return lax.all_to_all(
        value, ("dom", "shard"), split_axis=0, concat_axis=0, axis_index_groups=groups, tiled=True
    )


def body(
    embeddings,
    row_accum,
    relations,
    relation_accum,
    request_rows,
    head_slots,
    tail_slots,
    relation_ids,
    own_negatives,
    far_negatives,
):
    rows, width = embeddings.shape
    doms, shards = lax.axis_size("dom"), lax.axis_size("shard")
    rounds, slots = request_rows.shape[0], request_rows.shape[-1]
    bit = rounds - 1
    parts = doms // 2
    per_device = relation_accum.shape[0]
    packed = packed_shape(per_device, width)[3]
    assert packed == slots
    chunks = ((2 * shards, slots, width), BF16)
    wide = ((2 * shards, slots, padded(width) + parts * LANES), BF16)
    sums = ((2 * shards * packed, parts * LANES), F32)
    columns = [((rows, 1), F32), ((per_device, 1), F32)]
    (outgoing,) = call(first_kernel, [chunks], request_rows, embeddings)
    table = embeddings
    edges = (head_slots, tail_slots, relation_ids, own_negatives, far_negatives, relations)
    before = []
    for r in range(rounds):
        received = swap_pair(outgoing, r)
        if r == 0:
            grads, total, accum, relation_accum = call(
                functools.partial(first_edge_kernel, r, bit, doms, per_device),
                [chunks, sums] + columns,
                received,
                *edges,
                row_accum.reshape(1, rows),
                relation_accum.reshape(1, per_device),
            )
            before = [total]
        else:
            grads, *before = call(
                functools.partial(edge_kernel, r, bit, doms, per_device),
                [wide] if r == bit else [chunks, sums],
                received,
                *edges,
                *before,
            )
        back = swap_pair(grads, r)
        if r < bit:
            table, accum, outgoing = call(
                functools.partial(middle_kernel, r),
                [((rows, width), F32), ((rows, 1), F32), chunks],
                request_rows,
                back,
                table,
                accum,
            )
    kept, came = call(relation_sum_kernel, [((parts // 2, packed, LANES), F32)] * 2, back)
    for b in reversed([b for b in range(doms.bit_length() - 1) if b != bit]):
        came = lax.ppermute(came, "dom", [(g, g ^ 1 << b) for g in range(doms)])
        if kept.shape[0] > 1:
            kept, came = jnp.split(kept + came, 2)
    table, accum = call(
        functools.partial(update_kernel, bit), [((rows, width), F32), ((1, rows), F32)], request_rows, back, table, accum
    )
    table, accum, step, relation_accum = call(
        last_kernel,
        [((rows, width), F32), ((1, rows), F32), ((per_device, width), F32), ((1, per_device), F32)],
        table,
        accum,
        kept,
        came,
        relation_accum,
        in_specs=[VMEM] * 5,
        out_specs=[HBM] * 4,
        scratch_shapes=[
            pltpu.VMEM((per_device, width), F32),
            pltpu.VMEM((1, per_device), F32),
            pltpu.SemaphoreType.DMA((4,)),
        ],
    )
    return (table, accum.reshape(rows), step, relation_accum.reshape(per_device))


def solution(mesh):
    placed = (
        P(("dom", "shard"), None),
        P(("dom", "shard")),
        P(),
        P(("dom", "shard")),
        P(None, ("dom", "shard"), None, None),
        P(None, ("dom", "shard")),
        P(None, ("dom", "shard")),
        P(None, ("dom", "shard")),
        P(None, ("dom", "shard")),
        P(None, ("dom", "shard")),
    )
    return jax.shard_map(
        body,
        mesh=mesh,
        in_specs=placed,
        out_specs=(
            P(("dom", "shard"), None),
            P(("dom", "shard")),
            P(("dom", "shard"), None),
            P(("dom", "shard")),
        ),
        check_vma=False,
    )
```

```python
import functools

import jax
import jax.numpy as jnp
from jax import lax
from jax.experimental import pallas as pl
from jax.experimental.pallas import tpu as pltpu
from jax.sharding import PartitionSpec as P

LEARN_RATE = 0.1
LANES = 128
VMEM_LIMIT = 48 * 2**20
BF16 = jnp.bfloat16
F32 = jnp.float32
NATURAL = (((1,), (0,)), ((), ()))
LAST = (((1,), (1,)), ((), ()))
FIRST = (((0,), (0,)), ((), ()))
HBM = pl.BlockSpec(memory_space=pltpu.HBM)
VMEM = pl.BlockSpec(memory_space=pltpu.VMEM)


def dot(left, right, dims=NATURAL):
    return lax.dot_general(left, right, dims, preferred_element_type=F32)


def iota(shape, axis):
    return lax.broadcasted_iota(jnp.int32, shape, axis)


def one_hot_t(row, count):
    return (iota((count, row.shape[1]), 0) == row).astype(BF16)


def one_hot(column, count):
    return (iota((column.shape[0], count), 1) == column).astype(BF16)


def to_column(row):
    n = row.shape[1]
    return jnp.sum(jnp.where(iota((n, n), 0) == iota((n, n), 1), row, 0), axis=1, keepdims=True)


def to_row(column):
    n = column.shape[0]
    return jnp.sum(jnp.where(iota((n, n), 0) == iota((n, n), 1), column, 0), axis=0, keepdims=True)


def request_column(request_ref, r):
    ids = jnp.concatenate([request_ref[r, :, 0, :], request_ref[r, :, 1, :]], axis=0)
    pieces, slots = ids.shape
    n = pieces * slots
    spread = (iota((n, pieces), 0) // slots == iota((n, pieces), 1)).astype(F32)
    rep = dot(spread, ids.astype(F32))
    column = jnp.sum(
        jnp.where(iota((n, slots), 0) % slots == iota((n, slots), 1), rep, 0.0), axis=1, keepdims=True
    )
    return column.astype(jnp.int32)


def halves(r, shards):
    bit = (lax.axis_index("dom") >> r) & 1
    return pl.ds(bit * shards, shards), pl.ds((1 - bit) * shards, shards)


def serve(r, hot, table, out_ref):
    shards, slots = out_ref.shape[0] // 2, out_ref.shape[1]
    served = dot(hot, table.astype(BF16)).astype(BF16).reshape(2, shards, slots, table.shape[1])
    for half, value in zip(halves(r, shards), served):
        out_ref[half] = value


def first_kernel(request_ref, state_ref, out_ref):
    table = state_ref[: state_ref.shape[0] - 2]
    serve(0, one_hot(request_column(request_ref, 0), table.shape[0]), table, out_ref)


def row_update(r, request_ref, back_ref, state_ref):
    chunks, slots, _ = back_ref.shape
    rows, width = state_ref.shape[0] - 2, state_ref.shape[1]
    back = jnp.concatenate(
        [back_ref[half, :, :width].reshape(chunks // 2 * slots, width) for half in halves(r, chunks // 2)], axis=0
    )
    row_grad = dot(one_hot(request_column(request_ref, r), rows), back, FIRST)
    accum = to_column(state_ref[rows : rows + 1, :rows]) + jnp.mean(row_grad * row_grad, axis=1, keepdims=True)
    return state_ref[:rows] - row_grad * (LEARN_RATE / jnp.sqrt(accum)), to_row(accum)


def middle_kernel(r, request_ref, back_ref, state_ref, state_out, out_ref):
    table, accum = row_update(r, request_ref, back_ref, state_ref)
    rows = table.shape[0]
    serve(r + 1, one_hot(request_column(request_ref, r + 1), rows), table, out_ref)
    state_out[:rows] = table
    state_out[rows:] = state_ref[rows:]
    state_out[rows : rows + 1, :rows] = accum


def update_kernel(r, request_ref, back_ref, state_ref, table_out, accum_out, relation_accum_out):
    table, accum_out[...] = row_update(r, request_ref, back_ref, state_ref)
    table_out[...] = table
    per_device = relation_accum_out.shape[0]
    relation_accum_out[...] = to_column(state_ref[table.shape[0] + 1 :, :per_device])


def padded(width):
    return pl.cdiv(width, LANES) * LANES


def packed_shape(per_device, width):
    full, rest = width // LANES, width % LANES
    beside = LANES // rest
    return full, rest, beside, per_device * full + pl.cdiv(per_device, beside)


def pack_relations(grad_rel, ids, per_device, shards, doms, bit):
    edges, width = grad_rel.shape
    full, rest, beside, rows = packed_shape(per_device, width)
    owner, spot = ids // per_device, ids % per_device
    away = (owner // shards) ^ (lax.axis_index("dom") & ~(1 << bit))
    part = (away & ((1 << bit) - 1)) | (away >> (bit + 1) << bit)
    base = ((away >> bit & 1) * shards + owner % shards) * rows
    places = jnp.concatenate(
        [base + c * per_device + spot for c in range(full)] + [base + full * per_device + spot // beside], axis=1
    )
    group = to_column(part * beside + spot % beside)
    lane = iota((edges, doms // 2 * LANES), 1)
    tail = jnp.concatenate([grad_rel[:, full * LANES :]] * (beside * doms // 2), axis=1)
    here = lane // LANES == group // beside
    values = [
        jnp.where(here, jnp.concatenate([grad_rel[:, c * LANES : (c + 1) * LANES]] * (doms // 2), axis=1), 0.0)
        for c in range(full)
    ] + [jnp.where(lane // rest == group, tail, 0.0)]
    return dot(one_hot_t(places, 2 * shards * rows), jnp.concatenate(values, axis=0).astype(BF16))


def edge_kernel(
    r,
    bit,
    doms,
    per_device,
    rec_ref,
    head_ref,
    tail_ref,
    rel_ref,
    own_neg_ref,
    far_neg_ref,
    relations_ref,
    *refs,
):
    last = r == bit
    out_ref = refs[-1] if last else refs[-2]
    chunks, slots, width = rec_ref.shape
    shards = chunks // 2
    touched = shards * slots
    negatives = own_neg_ref.shape[1]
    own_half, far_half = halves(r, shards)
    own = rec_ref[own_half].reshape(touched, width)
    far = rec_ref[far_half].reshape(touched, width)
    row = slice(r, r + 1)
    ids = rel_ref[row]
    hot_head = one_hot_t(head_ref[row], touched)
    hot_tail = one_hot_t(tail_ref[row], touched)
    head = dot(hot_head, own, FIRST)
    tail = dot(hot_tail, far, FIRST)
    rel = dot(one_hot_t(ids, relations_ref.shape[0]), relations_ref[...], FIRST)
    query_tail = (head * rel).astype(BF16)
    query_head = (tail * rel).astype(BF16)

    def weights(rows, query, neg_ref):
        hit = iota((touched, negatives), 0) == neg_ref[row]
        scale = jnp.sum(jnp.where(hit, 1.0 / negatives, 0.0), axis=1, keepdims=True)
        return (jax.nn.sigmoid(dot(rows, query, LAST)) * scale).astype(BF16)

    weight_tail = weights(far, query_tail, far_neg_ref)
    weight_head = weights(own, query_head, own_neg_ref)
    positive = jnp.sum(head * rel * tail, axis=1, keepdims=True)
    coeff = -jax.nn.sigmoid(-positive)
    back_tail = dot(weight_tail, far, FIRST)
    back_head = dot(weight_head, own, FIRST)
    toward_head = coeff * tail + back_tail
    grad_head = (rel * toward_head).astype(BF16)
    grad_tail = (rel * (coeff * head + back_head)).astype(BF16)
    grad_rel = head * toward_head + tail * back_head
    own_grad = dot(
        jnp.concatenate([hot_head, weight_head], axis=1), jnp.concatenate([grad_head, query_head], axis=0)
    )
    far_grad = dot(
        jnp.concatenate([hot_tail, weight_tail], axis=1), jnp.concatenate([grad_tail, query_tail], axis=0)
    )
    out_ref[own_half, :, :width] = own_grad.astype(BF16).reshape(shards, slots, width)
    out_ref[far_half, :, :width] = far_grad.astype(BF16).reshape(shards, slots, width)
    sums = pack_relations(grad_rel, ids, per_device, shards, doms, bit)
    if last:
        sums = (sums + refs[0][...]).astype(BF16)
        out_ref[:, :, pl.ds(padded(width), sums.shape[1])] = sums.reshape(chunks, slots, sums.shape[1])
    elif r:
        refs[-1][...] = sums + refs[0][...]
    else:
        refs[-1][...] = sums


def relation_sum_kernel(parts_ref, kept_out, sent_out):
    half = kept_out.shape[0]
    for q in range(2 * half):
        value = parts_ref[:, :, pl.ds(parts_ref.shape[2] - (2 * half - q) * LANES, LANES)]
        out = kept_out if q < half else sent_out
        out[q % half] = jnp.sum(value.astype(F32), axis=0)


def last_kernel(
    table_ref, row_accum_ref, kept_ref, came_ref, accum_ref, table_out, row_accum_out, step_out, accum_out, *scratch
):
    step_ref, new_accum_ref, sems = scratch
    copies = [
        pltpu.make_async_copy(source, target, sems.at[i])
        for i, (source, target) in enumerate(
            (
                (table_ref, table_out),
                (row_accum_ref, row_accum_out),
                (step_ref, step_out),
                (new_accum_ref, accum_out),
            )
        )
    ]
    copies[0].start()
    copies[1].start()
    per_device, width = step_ref.shape
    full, rest, beside, rows = packed_shape(per_device, width)
    total = kept_ref[0] + came_ref[0]
    tails = [
        total[full * per_device + i // beside :][:1, i % beside * rest : (i % beside + 1) * rest]
        for i in range(per_device)
    ]
    grad = jnp.concatenate(
        [total[c * per_device : (c + 1) * per_device] for c in range(full)] + [jnp.concatenate(tails, axis=0)], axis=1
    )
    accum = accum_ref[...] + jnp.mean(grad * grad, axis=1, keepdims=True)
    step_ref[...] = grad * (-LEARN_RATE / jnp.sqrt(accum))
    new_accum_ref[...] = to_row(accum)
    copies[2].start()
    copies[3].start()
    for copy in copies:
        copy.wait()


def call(kernel, outs, *args, **kwargs):
    return pl.pallas_call(
        kernel,
        out_shape=[jax.ShapeDtypeStruct(shape, kind) for shape, kind in outs],
        compiler_params=pltpu.CompilerParams(vmem_limit_bytes=VMEM_LIMIT),
        **kwargs,
    )(*args)


def swap_pair(value, r):
    doms, shards = lax.axis_size("dom"), lax.axis_size("shard")
    groups = [
        [g * shards + s for g in (low, low ^ (1 << r)) for s in range(shards)]
        for low in range(doms)
        if not low >> r & 1
    ]
    return lax.all_to_all(
        value, ("dom", "shard"), split_axis=0, concat_axis=0, axis_index_groups=groups, tiled=True
    )


def body(
    embeddings,
    row_accum,
    relations,
    relation_accum,
    request_rows,
    head_slots,
    tail_slots,
    relation_ids,
    own_negatives,
    far_negatives,
):
    rows, width = embeddings.shape
    doms, shards = lax.axis_size("dom"), lax.axis_size("shard")
    rounds, slots = request_rows.shape[0], request_rows.shape[-1]
    bit = rounds - 1
    parts = doms // 2
    per_device = relation_accum.shape[0]
    packed = packed_shape(per_device, width)[3]
    assert packed == slots
    chunks = ((2 * shards, slots, width), BF16)
    wide = ((2 * shards, slots, padded(width) + parts * LANES), BF16)
    sums = ((2 * shards * packed, parts * LANES), F32)
    state = (
        jnp.pad(embeddings, ((0, 2), (0, 0)))
        + jnp.pad(row_accum[None], ((rows, 1), (0, width - rows)))
        + jnp.pad(relation_accum[None], ((rows + 1, 0), (0, width - per_device)))
    )
    (outgoing,) = call(first_kernel, [chunks], request_rows, state)
    edges = (head_slots, tail_slots, relation_ids, own_negatives, far_negatives, relations)
    before = []
    for r in range(rounds):
        received = swap_pair(outgoing, r)
        grads, *before = call(
            functools.partial(edge_kernel, r, bit, doms, per_device),
            [wide] if r == bit else [chunks, sums],
            received,
            *edges,
            *before,
        )
        back = swap_pair(grads, r)
        if r < bit:
            state, outgoing = call(
                functools.partial(middle_kernel, r), [(state.shape, F32), chunks], request_rows, back, state
            )
    kept, came = call(relation_sum_kernel, [((parts // 2, packed, LANES), F32)] * 2, back)
    for b in reversed([b for b in range(doms.bit_length() - 1) if b != bit]):
        came = lax.ppermute(came, "dom", [(g, g ^ 1 << b) for g in range(doms)])
        if kept.shape[0] > 1:
            kept, came = jnp.split(kept + came, 2)
    table, accum, relation_accum = call(
        functools.partial(update_kernel, bit),
        [((rows, width), F32), ((1, rows), F32), ((per_device, 1), F32)],
        request_rows,
        back,
        state,
    )
    table, accum, step, relation_accum = call(
        last_kernel,
        [((rows, width), F32), ((1, rows), F32), ((per_device, width), F32), ((1, per_device), F32)],
        table,
        accum,
        kept,
        came,
        relation_accum,
        in_specs=[VMEM] * 5,
        out_specs=[HBM] * 4,
        scratch_shapes=[
            pltpu.VMEM((per_device, width), F32),
            pltpu.VMEM((1, per_device), F32),
            pltpu.SemaphoreType.DMA((4,)),
        ],
    )
    return (table, accum.reshape(rows), step, relation_accum.reshape(per_device))


def solution(mesh):
    placed = (
        P(("dom", "shard"), None),
        P(("dom", "shard")),
        P(),
        P(("dom", "shard")),
        P(None, ("dom", "shard"), None, None),
        P(None, ("dom", "shard")),
        P(None, ("dom", "shard")),
        P(None, ("dom", "shard")),
        P(None, ("dom", "shard")),
        P(None, ("dom", "shard")),
    )
    return jax.shard_map(
        body,
        mesh=mesh,
        in_specs=placed,
        out_specs=(
            P(("dom", "shard"), None),
            P(("dom", "shard")),
            P(("dom", "shard"), None),
            P(("dom", "shard")),
        ),
        check_vma=False,
    )
```

```python
import functools

import jax
import jax.numpy as jnp
from jax import lax
from jax.experimental import pallas as pl
from jax.experimental.pallas import tpu as pltpu
from jax.sharding import PartitionSpec as P

LEARN_RATE = 0.1
LANES = 128
VMEM_LIMIT = 48 * 2**20
BF16 = jnp.bfloat16
F32 = jnp.float32
NATURAL = (((1,), (0,)), ((), ()))
LAST = (((1,), (1,)), ((), ()))
FIRST = (((0,), (0,)), ((), ()))
HBM = pl.BlockSpec(memory_space=pltpu.HBM)
VMEM = pl.BlockSpec(memory_space=pltpu.VMEM)


def dot(left, right, dims=NATURAL):
    return lax.dot_general(left, right, dims, preferred_element_type=F32)


def iota(shape, axis):
    return lax.broadcasted_iota(jnp.int32, shape, axis)


def one_hot_t(row, count):
    return (iota((count, row.shape[1]), 0) == row).astype(BF16)


def one_hot(column, count):
    return (iota((column.shape[0], count), 1) == column).astype(BF16)


def to_column(row):
    n = row.shape[1]
    return jnp.sum(jnp.where(iota((n, n), 0) == iota((n, n), 1), row, 0), axis=1, keepdims=True)


def to_row(column):
    n = column.shape[0]
    return jnp.sum(jnp.where(iota((n, n), 0) == iota((n, n), 1), column, 0), axis=0, keepdims=True)


def request_column(request_ref, r):
    ids = jnp.concatenate([request_ref[r, :, 0, :], request_ref[r, :, 1, :]], axis=0)
    pieces, slots = ids.shape
    n = pieces * slots
    spread = (iota((n, pieces), 0) // slots == iota((n, pieces), 1)).astype(F32)
    rep = dot(spread, ids.astype(F32))
    column = jnp.sum(
        jnp.where(iota((n, slots), 0) % slots == iota((n, slots), 1), rep, 0.0), axis=1, keepdims=True
    )
    return column.astype(jnp.int32)


def spread_order(shards):
    bits = shards.bit_length() - 1
    return [sum((s >> b & 1) << (bits - 1 - b) for b in range(bits)) for s in range(shards)]


def halves(r, shards):
    bit = (lax.axis_index("dom") >> r) & 1
    return bit * shards, (1 - bit) * shards


def put_chunks(ref, first, value):
    slots = ref.shape[1]
    order = spread_order(ref.shape[0] // 2)
    for s, place in enumerate(order):
        ref[first + place, :, : value.shape[1]] = value[s * slots : (s + 1) * slots]


def get_chunks(ref, first, width):
    return jnp.concatenate([ref[first + place, :, :width] for place in spread_order(ref.shape[0] // 2)], axis=0)


def serve(r, hot, table, out_ref):
    shards = out_ref.shape[0] // 2
    served = dot(hot, table.astype(BF16)).astype(BF16)
    half = served.shape[0] // 2
    for side, first in enumerate(halves(r, shards)):
        put_chunks(out_ref, first, served[side * half : (side + 1) * half])


def first_kernel(request_ref, state_ref, out_ref):
    table = state_ref[: state_ref.shape[0] - 2]
    serve(0, one_hot(request_column(request_ref, 0), table.shape[0]), table, out_ref)


def row_update(r, request_ref, back_ref, state_ref):
    chunks = back_ref.shape[0]
    rows, width = state_ref.shape[0] - 2, state_ref.shape[1]
    back = jnp.concatenate([get_chunks(back_ref, first, width) for first in halves(r, chunks // 2)], axis=0)
    row_grad = dot(one_hot(request_column(request_ref, r), rows), back, FIRST)
    accum = to_column(state_ref[rows : rows + 1, :rows]) + jnp.mean(row_grad * row_grad, axis=1, keepdims=True)
    return state_ref[:rows] - row_grad * (LEARN_RATE / jnp.sqrt(accum)), to_row(accum)


def middle_kernel(r, request_ref, back_ref, state_ref, state_out, out_ref):
    table, accum = row_update(r, request_ref, back_ref, state_ref)
    rows = table.shape[0]
    serve(r + 1, one_hot(request_column(request_ref, r + 1), rows), table, out_ref)
    state_out[:rows] = table
    state_out[rows:] = state_ref[rows:]
    state_out[rows : rows + 1, :rows] = accum


def update_kernel(r, request_ref, back_ref, state_ref, table_out, accum_out, relation_accum_out):
    table, accum_out[...] = row_update(r, request_ref, back_ref, state_ref)
    table_out[...] = table
    per_device = relation_accum_out.shape[0]
    relation_accum_out[...] = to_column(state_ref[table.shape[0] + 1 :, :per_device])


def padded(width):
    return pl.cdiv(width, LANES) * LANES


def packed_shape(per_device, width):
    full, rest = width // LANES, width % LANES
    beside = LANES // rest
    return full, rest, beside, per_device * full + pl.cdiv(per_device, beside)


def pack_relations(grad_rel, ids, per_device, shards, doms, bit):
    edges, width = grad_rel.shape
    full, rest, beside, rows = packed_shape(per_device, width)
    owner, spot = ids // per_device, ids % per_device
    away = (owner // shards) ^ (lax.axis_index("dom") & ~(1 << bit))
    part = (away & ((1 << bit) - 1)) | (away >> (bit + 1) << bit)
    shard = owner % shards
    place = sum(jnp.where(shard == s, p, 0) for s, p in enumerate(spread_order(shards)))
    base = ((away >> bit & 1) * shards + place) * rows
    places = jnp.concatenate(
        [base + c * per_device + spot for c in range(full)] + [base + full * per_device + spot // beside], axis=1
    )
    group = to_column(part * beside + spot % beside)
    lane = iota((edges, doms // 2 * LANES), 1)
    tail = jnp.concatenate([grad_rel[:, full * LANES :]] * (beside * doms // 2), axis=1)
    here = lane // LANES == group // beside
    values = [
        jnp.where(here, jnp.concatenate([grad_rel[:, c * LANES : (c + 1) * LANES]] * (doms // 2), axis=1), 0.0)
        for c in range(full)
    ] + [jnp.where(lane // rest == group, tail, 0.0)]
    return dot(one_hot_t(places, 2 * shards * rows), jnp.concatenate(values, axis=0).astype(BF16))


def edge_kernel(
    r,
    bit,
    doms,
    per_device,
    rec_ref,
    head_ref,
    tail_ref,
    rel_ref,
    own_neg_ref,
    far_neg_ref,
    relations_ref,
    *refs,
):
    last = r == bit
    out_ref = refs[-1] if last else refs[-2]
    chunks, slots, width = rec_ref.shape
    shards = chunks // 2
    touched = shards * slots
    negatives = own_neg_ref.shape[1]
    own_half, far_half = halves(r, shards)
    own = get_chunks(rec_ref, own_half, width)
    far = get_chunks(rec_ref, far_half, width)
    row = slice(r, r + 1)
    ids = rel_ref[row]
    hot_head = one_hot_t(head_ref[row], touched)
    hot_tail = one_hot_t(tail_ref[row], touched)
    head = dot(hot_head, own, FIRST)
    tail = dot(hot_tail, far, FIRST)
    rel = dot(one_hot_t(ids, relations_ref.shape[0]), relations_ref[...], FIRST)
    query_tail = (head * rel).astype(BF16)
    query_head = (tail * rel).astype(BF16)

    def weights(rows, query, neg_ref):
        hit = iota((touched, negatives), 0) == neg_ref[row]
        scale = jnp.sum(jnp.where(hit, 1.0 / negatives, 0.0), axis=1, keepdims=True)
        return (jax.nn.sigmoid(dot(rows, query, LAST)) * scale).astype(BF16)

    weight_tail = weights(far, query_tail, far_neg_ref)
    weight_head = weights(own, query_head, own_neg_ref)
    positive = jnp.sum(head * rel * tail, axis=1, keepdims=True)
    coeff = -jax.nn.sigmoid(-positive)
    back_tail = dot(weight_tail, far, FIRST)
    back_head = dot(weight_head, own, FIRST)
    toward_head = coeff * tail + back_tail
    grad_head = (rel * toward_head).astype(BF16)
    grad_tail = (rel * (coeff * head + back_head)).astype(BF16)
    grad_rel = head * toward_head + tail * back_head
    own_grad = dot(
        jnp.concatenate([hot_head, weight_head], axis=1), jnp.concatenate([grad_head, query_head], axis=0)
    )
    far_grad = dot(
        jnp.concatenate([hot_tail, weight_tail], axis=1), jnp.concatenate([grad_tail, query_tail], axis=0)
    )
    put_chunks(out_ref, own_half, own_grad.astype(BF16))
    put_chunks(out_ref, far_half, far_grad.astype(BF16))
    sums = pack_relations(grad_rel, ids, per_device, shards, doms, bit)
    if last:
        sums = (sums + refs[0][...]).astype(BF16)
        out_ref[:, :, pl.ds(padded(width), sums.shape[1])] = sums.reshape(chunks, slots, sums.shape[1])
    elif r:
        refs[-1][...] = sums + refs[0][...]
    else:
        refs[-1][...] = sums


def relation_sum_kernel(parts_ref, kept_out, sent_out):
    half = kept_out.shape[0]
    for q in range(2 * half):
        value = parts_ref[:, :, pl.ds(parts_ref.shape[2] - (2 * half - q) * LANES, LANES)]
        out = kept_out if q < half else sent_out
        out[q % half] = jnp.sum(value.astype(F32), axis=0)


def last_kernel(
    table_ref, row_accum_ref, kept_ref, came_ref, accum_ref, table_out, row_accum_out, step_out, accum_out, *scratch
):
    step_ref, new_accum_ref, sems = scratch
    copies = [
        pltpu.make_async_copy(source, target, sems.at[i])
        for i, (source, target) in enumerate(
            (
                (table_ref, table_out),
                (row_accum_ref, row_accum_out),
                (step_ref, step_out),
                (new_accum_ref, accum_out),
            )
        )
    ]
    copies[0].start()
    copies[1].start()
    per_device, width = step_ref.shape
    full, rest, beside, rows = packed_shape(per_device, width)
    total = kept_ref[0] + came_ref[0]
    tails = [
        total[full * per_device + i // beside :][:1, i % beside * rest : (i % beside + 1) * rest]
        for i in range(per_device)
    ]
    grad = jnp.concatenate(
        [total[c * per_device : (c + 1) * per_device] for c in range(full)] + [jnp.concatenate(tails, axis=0)], axis=1
    )
    accum = accum_ref[...] + jnp.mean(grad * grad, axis=1, keepdims=True)
    step_ref[...] = grad * (-LEARN_RATE / jnp.sqrt(accum))
    new_accum_ref[...] = to_row(accum)
    copies[2].start()
    copies[3].start()
    for copy in copies:
        copy.wait()


def call(kernel, outs, *args, **kwargs):
    return pl.pallas_call(
        kernel,
        out_shape=[jax.ShapeDtypeStruct(shape, kind) for shape, kind in outs],
        compiler_params=pltpu.CompilerParams(vmem_limit_bytes=VMEM_LIMIT),
        **kwargs,
    )(*args)


def swap_pair(value, r):
    doms, shards = lax.axis_size("dom"), lax.axis_size("shard")
    order = spread_order(shards)
    groups = [
        [g * shards + s for g in (low, low ^ (1 << r)) for s in sorted(range(shards), key=order.__getitem__)]
        for low in range(doms)
        if not low >> r & 1
    ]
    return lax.all_to_all(
        value, ("dom", "shard"), split_axis=0, concat_axis=0, axis_index_groups=groups, tiled=True
    )


def body(
    embeddings,
    row_accum,
    relations,
    relation_accum,
    request_rows,
    head_slots,
    tail_slots,
    relation_ids,
    own_negatives,
    far_negatives,
):
    rows, width = embeddings.shape
    doms, shards = lax.axis_size("dom"), lax.axis_size("shard")
    rounds, slots = request_rows.shape[0], request_rows.shape[-1]
    bit = rounds - 1
    parts = doms // 2
    per_device = relation_accum.shape[0]
    packed = packed_shape(per_device, width)[3]
    assert packed == slots
    chunks = ((2 * shards, slots, width), BF16)
    wide = ((2 * shards, slots, padded(width) + parts * LANES), BF16)
    sums = ((2 * shards * packed, parts * LANES), F32)
    state = (
        jnp.pad(embeddings, ((0, 2), (0, 0)))
        + jnp.pad(row_accum[None], ((rows, 1), (0, width - rows)))
        + jnp.pad(relation_accum[None], ((rows + 1, 0), (0, width - per_device)))
    )
    (outgoing,) = call(first_kernel, [chunks], request_rows, state)
    edges = (head_slots, tail_slots, relation_ids, own_negatives, far_negatives, relations)
    before = []
    for r in range(rounds):
        received = swap_pair(outgoing, r)
        grads, *before = call(
            functools.partial(edge_kernel, r, bit, doms, per_device),
            [wide] if r == bit else [chunks, sums],
            received,
            *edges,
            *before,
        )
        back = swap_pair(grads, r)
        if r < bit:
            state, outgoing = call(
                functools.partial(middle_kernel, r), [(state.shape, F32), chunks], request_rows, back, state
            )
    kept, came = call(relation_sum_kernel, [((parts // 2, packed, LANES), F32)] * 2, back)
    for b in reversed([b for b in range(doms.bit_length() - 1) if b != bit]):
        came = lax.ppermute(came, "dom", [(g, g ^ 1 << b) for g in range(doms)])
        if kept.shape[0] > 1:
            kept, came = jnp.split(kept + came, 2)
    table, accum, relation_accum = call(
        functools.partial(update_kernel, bit),
        [((rows, width), F32), ((1, rows), F32), ((per_device, 1), F32)],
        request_rows,
        back,
        state,
    )
    table, accum, step, relation_accum = call(
        last_kernel,
        [((rows, width), F32), ((1, rows), F32), ((per_device, width), F32), ((1, per_device), F32)],
        table,
        accum,
        kept,
        came,
        relation_accum,
        in_specs=[VMEM] * 5,
        out_specs=[HBM] * 4,
        scratch_shapes=[
            pltpu.VMEM((per_device, width), F32),
            pltpu.VMEM((1, per_device), F32),
            pltpu.SemaphoreType.DMA((4,)),
        ],
    )
    return (table, accum.reshape(rows), step, relation_accum.reshape(per_device))


def solution(mesh):
    placed = (
        P(("dom", "shard"), None),
        P(("dom", "shard")),
        P(),
        P(("dom", "shard")),
        P(None, ("dom", "shard"), None, None),
        P(None, ("dom", "shard")),
        P(None, ("dom", "shard")),
        P(None, ("dom", "shard")),
        P(None, ("dom", "shard")),
        P(None, ("dom", "shard")),
    )
    return jax.shard_map(
        body,
        mesh=mesh,
        in_specs=placed,
        out_specs=(
            P(("dom", "shard"), None),
            P(("dom", "shard")),
            P(("dom", "shard"), None),
            P(("dom", "shard")),
        ),
        check_vma=False,
    )
```

```python
import functools

import jax
import jax.numpy as jnp
from jax import lax
from jax.experimental import pallas as pl
from jax.experimental.pallas import tpu as pltpu
from jax.sharding import PartitionSpec as P

LEARN_RATE = 0.1
LANES = 128
VMEM_LIMIT = 48 * 2**20
BF16 = jnp.bfloat16
F32 = jnp.float32
NATURAL = (((1,), (0,)), ((), ()))
LAST = (((1,), (1,)), ((), ()))
FIRST = (((0,), (0,)), ((), ()))
HBM = pl.BlockSpec(memory_space=pltpu.HBM)
VMEM = pl.BlockSpec(memory_space=pltpu.VMEM)


def dot(left, right, dims=NATURAL):
    return lax.dot_general(left, right, dims, preferred_element_type=F32)


def iota(shape, axis):
    return lax.broadcasted_iota(jnp.int32, shape, axis)


def one_hot_t(row, count):
    return (iota((count, row.shape[1]), 0) == row).astype(BF16)


def one_hot(column, count):
    return (iota((column.shape[0], count), 1) == column).astype(BF16)


def to_column(row):
    n = row.shape[1]
    return jnp.sum(jnp.where(iota((n, n), 0) == iota((n, n), 1), row, 0), axis=1, keepdims=True)


def to_row(column):
    n = column.shape[0]
    return jnp.sum(jnp.where(iota((n, n), 0) == iota((n, n), 1), column, 0), axis=0, keepdims=True)


def reverse(index, count):
    bits = count.bit_length() - 1
    return sum((index >> b & 1) << (bits - 1 - b) for b in range(bits))


def spread_order(shards):
    return [reverse(s, shards) for s in range(shards)]


def group_bit(r):
    return (lax.axis_index("dom") >> r) & 1


def renumber(slot, shards, slots):
    half = slots // 2
    return (slot // half % 2) * (shards * half) + reverse(slot // slots, shards) * half + slot % half


def halves(ref, r):
    rows, bit = ref.shape[0] // 2, group_bit(r)
    return [pl.ds(pl.multiple_of(side * rows, rows), rows) for side in (bit, 1 - bit)]


def unfold(value, width):
    return jnp.concatenate([value[:, :width], value[:, width : 2 * width]], axis=0)


def fold(value):
    n = value.shape[0] // 2
    return jnp.concatenate([value[:n], value[n:]], axis=1)


def request_columns(request_ref, r):
    ids = jnp.concatenate([request_ref[r, :, 0, :], request_ref[r, :, 1, :]], axis=0)
    pieces, slots = ids.shape
    shards, half = pieces // 2, slots // 2
    n = pieces * half
    chunk = iota((n, pieces), 0) // half
    piece = (chunk // shards ^ group_bit(r)) * shards + reverse(chunk % shards, shards)
    rep = dot((piece == iota((n, pieces), 1)).astype(F32), ids.astype(F32))
    lane, inside = iota((n, slots), 1), iota((n, slots), 0) % half
    return [
        jnp.sum(jnp.where(lane == side * half + inside, rep, 0.0), axis=1, keepdims=True).astype(jnp.int32)
        for side in range(2)
    ]


def serve(request_ref, r, table, out_ref):
    rows, width = table.shape
    table = table.astype(BF16)
    hot = jnp.concatenate([one_hot(column, rows) for column in request_columns(request_ref, r)], axis=1)
    blank = jnp.zeros((rows, width), BF16)
    both = jnp.concatenate(
        [jnp.concatenate([table, blank], axis=1), jnp.concatenate([blank, table], axis=1)], axis=0
    )
    out_ref[...] = dot(hot, both).astype(BF16)


def first_kernel(request_ref, state_ref, out_ref):
    table = state_ref[: state_ref.shape[0] - 2]
    serve(request_ref, 0, table, out_ref)


def row_update(r, request_ref, back_ref, state_ref):
    rows, width = state_ref.shape[0] - 2, state_ref.shape[1]
    hot = jnp.concatenate([one_hot(column, rows) for column in request_columns(request_ref, r)], axis=0)
    row_grad = dot(hot, unfold(back_ref[:, : 2 * width], width), FIRST)
    accum = to_column(state_ref[rows : rows + 1, :rows]) + jnp.mean(row_grad * row_grad, axis=1, keepdims=True)
    return state_ref[:rows] - row_grad * (LEARN_RATE / jnp.sqrt(accum)), to_row(accum)


def middle_kernel(r, request_ref, back_ref, state_ref, state_out, out_ref):
    table, accum = row_update(r, request_ref, back_ref, state_ref)
    rows = table.shape[0]
    serve(request_ref, r + 1, table, out_ref)
    state_out[:rows] = table
    state_out[rows:] = state_ref[rows:]
    state_out[rows : rows + 1, :rows] = accum


def update_kernel(r, request_ref, back_ref, state_ref, table_out, accum_out, relation_accum_out):
    table, accum_out[...] = row_update(r, request_ref, back_ref, state_ref)
    table_out[...] = table
    per_device = relation_accum_out.shape[0]
    relation_accum_out[...] = to_column(state_ref[table.shape[0] + 1 :, :per_device])


def padded(width):
    return pl.cdiv(width, LANES) * LANES


def packed_shape(per_device, width):
    full, rest = width // LANES, width % LANES
    beside = LANES // rest
    return full, rest, beside, per_device * full + pl.cdiv(per_device, beside)


def pack_relations(grad_rel, ids, per_device, shards, doms, bit):
    edges, width = grad_rel.shape
    full, rest, beside, rows = packed_shape(per_device, width)
    half = rows // 2

    def places(index):
        owner, spot = index // per_device, index % per_device
        away = (owner // shards) ^ (lax.axis_index("dom") & ~(1 << bit))
        part = (away & ((1 << bit) - 1)) | (away >> (bit + 1) << bit)
        chunk = (away >> bit & 1) * shards + reverse(owner % shards, shards)
        packed = [c * per_device + spot for c in range(full)] + [full * per_device + spot // beside]
        return [chunk * half + row % half for row in packed], [part * 2 + row // half for row in packed], spot % beside

    hot = one_hot_t(jnp.concatenate(places(ids)[0], axis=1), 2 * shards * half)
    _, tiles, turn = places(to_column(ids))
    lane = iota((edges, doms * LANES), 1)
    pieces = [grad_rel[:, c * LANES : (c + 1) * LANES] for c in range(full)]
    tail = jnp.concatenate([grad_rel[:, full * LANES :]] * beside, axis=1)
    pieces.append(jnp.where(iota((edges, LANES), 1) // rest == turn, tail, 0.0))
    values = [
        jnp.where(lane // LANES == tile, jnp.concatenate([piece] * doms, axis=1), 0.0)
        for tile, piece in zip(tiles, pieces)
    ]
    return dot(hot, jnp.concatenate(values, axis=0).astype(BF16))


def slots_of(ref):
    return 2 * ref.shape[0] // (2 * lax.axis_size("shard"))


def edge_kernel(
    r,
    bit,
    doms,
    per_device,
    rec_ref,
    head_ref,
    tail_ref,
    rel_ref,
    own_neg_ref,
    far_neg_ref,
    relations_ref,
    *refs,
):
    last = r == bit
    out_ref = refs[-1] if last else refs[-2]
    width = relations_ref.shape[1]
    shards, slots = lax.axis_size("shard"), slots_of(rec_ref)
    touched = shards * slots
    negatives = own_neg_ref.shape[1]
    own_half, far_half = halves(rec_ref, r)
    own = unfold(rec_ref[own_half], width)
    far = unfold(rec_ref[far_half], width)
    row = slice(r, r + 1)
    ids = rel_ref[row]
    hot_head = one_hot_t(renumber(head_ref[row], shards, slots), touched)
    hot_tail = one_hot_t(renumber(tail_ref[row], shards, slots), touched)
    head = dot(hot_head, own, FIRST)
    tail = dot(hot_tail, far, FIRST)
    rel = dot(one_hot_t(ids, relations_ref.shape[0]), relations_ref[...], FIRST)
    query_tail = (head * rel).astype(BF16)
    query_head = (tail * rel).astype(BF16)

    def weights(rows, query, neg_ref):
        hit = iota((touched, negatives), 0) == renumber(neg_ref[row], shards, slots)
        scale = jnp.sum(jnp.where(hit, 1.0 / negatives, 0.0), axis=1, keepdims=True)
        return (jax.nn.sigmoid(dot(rows, query, LAST)) * scale).astype(BF16)

    weight_tail = weights(far, query_tail, far_neg_ref)
    weight_head = weights(own, query_head, own_neg_ref)
    positive = jnp.sum(head * rel * tail, axis=1, keepdims=True)
    coeff = -jax.nn.sigmoid(-positive)
    back_tail = dot(weight_tail, far, FIRST)
    back_head = dot(weight_head, own, FIRST)
    toward_head = coeff * tail + back_tail
    grad_head = (rel * toward_head).astype(BF16)
    grad_tail = (rel * (coeff * head + back_head)).astype(BF16)
    grad_rel = head * toward_head + tail * back_head
    own_grad = dot(
        jnp.concatenate([hot_head, weight_head], axis=1), jnp.concatenate([grad_head, query_head], axis=0)
    )
    far_grad = dot(
        jnp.concatenate([hot_tail, weight_tail], axis=1), jnp.concatenate([grad_tail, query_tail], axis=0)
    )
    out_ref[own_half, : 2 * width] = fold(own_grad.astype(BF16))
    out_ref[far_half, : 2 * width] = fold(far_grad.astype(BF16))
    sums = pack_relations(grad_rel, ids, per_device, shards, doms, bit)
    if last:
        sums = (sums + refs[0][...]).astype(BF16)
        out_ref[:, pl.ds(padded(2 * width), sums.shape[1])] = sums
    elif r:
        refs[-1][...] = sums + refs[0][...]
    else:
        refs[-1][...] = sums


def relation_sum_kernel(parts_ref, kept_out, sent_out):
    half = kept_out.shape[0]
    rows, lanes = kept_out.shape[1:]
    for q in range(2 * half):
        value = parts_ref[:, pl.ds(parts_ref.shape[1] - (2 * half - q) * lanes, lanes)].astype(F32)
        out = kept_out if q < half else sent_out
        out[q % half] = jnp.sum(value.reshape(value.shape[0] // rows, rows, lanes), axis=0)


def last_kernel(
    table_ref, row_accum_ref, kept_ref, came_ref, accum_ref, table_out, row_accum_out, step_out, accum_out, *scratch
):
    step_ref, new_accum_ref, sems = scratch
    copies = [
        pltpu.make_async_copy(source, target, sems.at[i])
        for i, (source, target) in enumerate(
            (
                (table_ref, table_out),
                (row_accum_ref, row_accum_out),
                (step_ref, step_out),
                (new_accum_ref, accum_out),
            )
        )
    ]
    copies[0].start()
    copies[1].start()
    per_device, width = step_ref.shape
    full, rest, beside, rows = packed_shape(per_device, width)
    total = unfold(kept_ref[0] + came_ref[0], LANES)
    tails = [
        total[full * per_device + i // beside :][:1, i % beside * rest : (i % beside + 1) * rest]
        for i in range(per_device)
    ]
    grad = jnp.concatenate(
        [total[c * per_device : (c + 1) * per_device] for c in range(full)] + [jnp.concatenate(tails, axis=0)], axis=1
    )
    accum = accum_ref[...] + jnp.mean(grad * grad, axis=1, keepdims=True)
    step_ref[...] = grad * (-LEARN_RATE / jnp.sqrt(accum))
    new_accum_ref[...] = to_row(accum)
    copies[2].start()
    copies[3].start()
    for copy in copies:
        copy.wait()


def call(kernel, outs, *args, **kwargs):
    return pl.pallas_call(
        kernel,
        out_shape=[jax.ShapeDtypeStruct(shape, kind) for shape, kind in outs],
        compiler_params=pltpu.CompilerParams(vmem_limit_bytes=VMEM_LIMIT),
        **kwargs,
    )(*args)


def swap_pair(value, r):
    doms, shards = lax.axis_size("dom"), lax.axis_size("shard")
    order = spread_order(shards)
    groups = [
        [g * shards + s for g in (low, low ^ (1 << r)) for s in sorted(range(shards), key=order.__getitem__)]
        for low in range(doms)
        if not low >> r & 1
    ]
    return lax.all_to_all(
        value, ("dom", "shard"), split_axis=0, concat_axis=0, axis_index_groups=groups, tiled=True
    )


def body(
    embeddings,
    row_accum,
    relations,
    relation_accum,
    request_rows,
    head_slots,
    tail_slots,
    relation_ids,
    own_negatives,
    far_negatives,
):
    rows, width = embeddings.shape
    doms, shards = lax.axis_size("dom"), lax.axis_size("shard")
    rounds, slots = request_rows.shape[0], request_rows.shape[-1]
    bit = rounds - 1
    parts = doms // 2
    per_device = relation_accum.shape[0]
    packed = packed_shape(per_device, width)[3]
    assert packed == slots
    chunks = ((shards * slots, 2 * width), BF16)
    wide = ((shards * slots, padded(2 * width) + doms * LANES), BF16)
    sums = ((shards * slots, doms * LANES), F32)
    state = (
        jnp.pad(embeddings, ((0, 2), (0, 0)))
        + jnp.pad(row_accum[None], ((rows, 1), (0, width - rows)))
        + jnp.pad(relation_accum[None], ((rows + 1, 0), (0, width - per_device)))
    )
    (outgoing,) = call(first_kernel, [chunks], request_rows, state)
    edges = (head_slots, tail_slots, relation_ids, own_negatives, far_negatives, relations)
    before = []
    for r in range(rounds):
        received = swap_pair(outgoing, r)
        grads, *before = call(
            functools.partial(edge_kernel, r, bit, doms, per_device),
            [wide] if r == bit else [chunks, sums],
            received,
            *edges,
            *before,
        )
        back = swap_pair(grads, r)
        if r < bit:
            state, outgoing = call(
                functools.partial(middle_kernel, r), [(state.shape, F32), chunks], request_rows, back, state
            )
    kept, came = call(relation_sum_kernel, [((parts // 2, packed // 2, 2 * LANES), F32)] * 2, back)
    for b in reversed([b for b in range(doms.bit_length() - 1) if b != bit]):
        came = lax.ppermute(came, "dom", [(g, g ^ 1 << b) for g in range(doms)])
        if kept.shape[0] > 1:
            kept, came = jnp.split(kept + came, 2)
    table, accum, relation_accum = call(
        functools.partial(update_kernel, bit),
        [((rows, width), F32), ((1, rows), F32), ((per_device, 1), F32)],
        request_rows,
        back,
        state,
    )
    table, accum, step, relation_accum = call(
        last_kernel,
        [((rows, width), F32), ((1, rows), F32), ((per_device, width), F32), ((1, per_device), F32)],
        table,
        accum,
        kept,
        came,
        relation_accum,
        in_specs=[VMEM] * 5,
        out_specs=[HBM] * 4,
        scratch_shapes=[
            pltpu.VMEM((per_device, width), F32),
            pltpu.VMEM((1, per_device), F32),
            pltpu.SemaphoreType.DMA((4,)),
        ],
    )
    return (table, accum.reshape(rows), step, relation_accum.reshape(per_device))


def solution(mesh):
    placed = (
        P(("dom", "shard"), None),
        P(("dom", "shard")),
        P(),
        P(("dom", "shard")),
        P(None, ("dom", "shard"), None, None),
        P(None, ("dom", "shard")),
        P(None, ("dom", "shard")),
        P(None, ("dom", "shard")),
        P(None, ("dom", "shard")),
        P(None, ("dom", "shard")),
    )
    return jax.shard_map(
        body,
        mesh=mesh,
        in_specs=placed,
        out_specs=(
            P(("dom", "shard"), None),
            P(("dom", "shard")),
            P(("dom", "shard"), None),
            P(("dom", "shard")),
        ),
        check_vma=False,
    )
```

```python
import functools

import jax
import jax.numpy as jnp
from jax import lax
from jax.experimental import pallas as pl
from jax.experimental.pallas import tpu as pltpu
from jax.sharding import PartitionSpec as P

LEARN_RATE = 0.1
BASE = 64
DIGITS = 16
VMEM_LIMIT = 48 * 2**20
BF16 = jnp.bfloat16
F32 = jnp.float32
NATURAL = (((1,), (0,)), ((), ()))
LAST = (((1,), (1,)), ((), ()))
FIRST = (((0,), (0,)), ((), ()))
HBM = pl.BlockSpec(memory_space=pltpu.HBM)
VMEM = pl.BlockSpec(memory_space=pltpu.VMEM)


def dot(left, right, dims=NATURAL):
    return lax.dot_general(left, right, dims, preferred_element_type=F32)


def iota(shape, axis):
    return lax.broadcasted_iota(jnp.int32, shape, axis)


def one_hot_t(row, count):
    return (iota((count, row.shape[1]), 0) == row).astype(BF16)


def one_hot(column, count):
    return (iota((column.shape[0], count), 1) == column).astype(BF16)


def to_column(row):
    n = row.shape[1]
    return jnp.sum(jnp.where(iota((n, n), 0) == iota((n, n), 1), row, 0), axis=1, keepdims=True)


def to_row(column):
    n = column.shape[0]
    return jnp.sum(jnp.where(iota((n, n), 0) == iota((n, n), 1), column, 0), axis=0, keepdims=True)


def reverse(index, count):
    bits = count.bit_length() - 1
    return sum((index >> b & 1) << (bits - 1 - b) for b in range(bits))


def spread_order(shards):
    return [reverse(s, shards) for s in range(shards)]


def group_bit(r):
    return (lax.axis_index("dom") >> r) & 1


def renumber(slot, shards, slots):
    half = slots // 2
    return (slot // half % 2) * (shards * half) + reverse(slot // slots, shards) * half + slot % half


def halves(ref, r):
    rows, bit = ref.shape[0] // 2, group_bit(r)
    return [pl.ds(pl.multiple_of(side * rows, rows), rows) for side in (bit, 1 - bit)]


def unfold(value, width):
    return jnp.concatenate([value[:, :width], value[:, width : 2 * width]], axis=0)


def fold(value):
    n = value.shape[0] // 2
    return jnp.concatenate([value[:n], value[n:]], axis=1)


def request_columns(request_ref, r):
    ids = jnp.concatenate([request_ref[r, :, 0, :], request_ref[r, :, 1, :]], axis=0)
    pieces, slots = ids.shape
    shards, half = pieces // 2, slots // 2
    n = pieces * half
    chunk = iota((n, pieces), 0) // half
    piece = (chunk // shards ^ group_bit(r)) * shards + reverse(chunk % shards, shards)
    rep = dot((piece == iota((n, pieces), 1)).astype(F32), ids.astype(F32))
    lane, inside = iota((n, slots), 1), iota((n, slots), 0) % half
    return [
        jnp.sum(jnp.where(lane == side * half + inside, rep, 0.0), axis=1, keepdims=True).astype(jnp.int32)
        for side in range(2)
    ]


def serve(request_ref, r, table, out_ref):
    rows, width = table.shape
    table = table.astype(BF16)
    hot = jnp.concatenate([one_hot(column, rows) for column in request_columns(request_ref, r)], axis=1)
    blank = jnp.zeros((rows, width), BF16)
    both = jnp.concatenate(
        [jnp.concatenate([table, blank], axis=1), jnp.concatenate([blank, table], axis=1)], axis=0
    )
    out_ref[...] = dot(hot, both).astype(BF16)


def first_kernel(request_ref, state_ref, *refs):
    out_ref = refs[-1]
    table = state_ref[: state_ref.shape[0] - 2]
    serve(request_ref, 0, table, out_ref)


def row_update(r, request_ref, back_ref, state_ref):
    rows, width = state_ref.shape[0] - 2, state_ref.shape[1]
    hot = jnp.concatenate([one_hot(column, rows) for column in request_columns(request_ref, r)], axis=0)
    row_grad = dot(hot, unfold(back_ref[:, : 2 * width], width), FIRST)
    accum = to_column(state_ref[rows : rows + 1, :rows]) + jnp.mean(row_grad * row_grad, axis=1, keepdims=True)
    return state_ref[:rows] - row_grad * (LEARN_RATE / jnp.sqrt(accum)), to_row(accum)


def middle_kernel(r, request_ref, back_ref, state_ref, state_out, out_ref):
    table, accum = row_update(r, request_ref, back_ref, state_ref)
    rows = table.shape[0]
    serve(request_ref, r + 1, table, out_ref)
    state_out[:rows] = table
    state_out[rows:] = state_ref[rows:]
    state_out[rows : rows + 1, :rows] = accum


def slots_of(ref):
    return 2 * ref.shape[0] // (2 * lax.axis_size("shard"))


def edge_kernel(
    r,
    rec_ref,
    head_ref,
    tail_ref,
    rel_ref,
    own_neg_ref,
    far_neg_ref,
    relations_ref,
    left_out,
    right_out,
    swap_out,
):
    width = relations_ref.shape[1]
    shards, slots = lax.axis_size("shard"), slots_of(rec_ref)
    touched = shards * slots
    edges, negatives = head_ref.shape[1], own_neg_ref.shape[1]
    own_half, far_half = halves(rec_ref, r)
    own = unfold(rec_ref[own_half], width)
    far = unfold(rec_ref[far_half], width)
    row = slice(r, r + 1)
    ids = rel_ref[row]
    hot_head = one_hot_t(renumber(head_ref[row], shards, slots), touched)
    hot_tail = one_hot_t(renumber(tail_ref[row], shards, slots), touched)
    head = dot(hot_head, own, FIRST)
    tail = dot(hot_tail, far, FIRST)
    rel = dot(one_hot_t(ids, relations_ref.shape[0]), relations_ref[...], FIRST)
    query_tail = (head * rel).astype(BF16)
    query_head = (tail * rel).astype(BF16)

    def weights(rows, query, neg_ref):
        hit = iota((touched, negatives), 0) == renumber(neg_ref[row], shards, slots)
        scale = jnp.sum(jnp.where(hit, 1.0 / negatives, 0.0), axis=1, keepdims=True)
        return (jax.nn.sigmoid(dot(rows, query, LAST)) * scale).astype(BF16)

    weight_tail = weights(far, query_tail, far_neg_ref)
    weight_head = weights(own, query_head, own_neg_ref)
    positive = jnp.sum(head * rel * tail, axis=1, keepdims=True)
    coeff = -jax.nn.sigmoid(-positive)
    back_tail = dot(weight_tail, far, FIRST)
    back_head = dot(weight_head, own, FIRST)
    toward_head = coeff * tail + back_tail
    grad_rel = head * toward_head + tail * back_head
    swap_out[:edges] = grad_rel.astype(BF16)
    line = iota((DIGITS, edges), 0)
    digits = jnp.where(line == 0, ids // BASE, jnp.where(line == 1, ids % BASE, 0)).astype(F32)
    swap_out[edges:] = jnp.concatenate([digits, jnp.zeros((DIGITS, width - edges), F32)], axis=1).astype(BF16)
    left_out[0] = jnp.concatenate([hot_head, weight_head], axis=1)
    left_out[1] = jnp.concatenate([hot_tail, weight_tail], axis=1)
    right_out[0, :edges] = (rel * toward_head).astype(BF16)
    right_out[0, edges:] = query_head
    right_out[1, :edges] = (rel * (coeff * head + back_head)).astype(BF16)
    right_out[1, edges:] = query_tail


def grad_kernel(r, left_ref, right_ref, out_ref):
    width = right_ref.shape[2]
    for side, half in enumerate(halves(out_ref, r)):
        out_ref[half, : 2 * width] = fold(dot(left_ref[side], right_ref[side]).astype(BF16))


def relation_kernel(bit, per_device, grads_ref, *refs):
    *swap_refs, out_ref = refs
    width = swap_refs[0].shape[1]
    edges = swap_refs[0].shape[0] - DIGITS
    shards = lax.axis_size("shard")
    half = out_ref.shape[0] // (2 * shards)
    places, values = [], []
    for ref in swap_refs:
        digits = ref[edges:, :edges].astype(F32)
        ids = (digits[:1] * BASE + digits[1:2]).astype(jnp.int32)
        owner = ids // per_device
        dom = owner // shards
        chunk = (dom >> bit & 1) * shards + reverse(owner % shards, shards)
        mine = (dom ^ lax.axis_index("dom")) & ~(1 << bit) == 0
        places.append(jnp.where(mine, chunk * half + ids % per_device, -1))
        values.append(ref[:edges])
    hot = one_hot_t(jnp.concatenate(places, axis=1), out_ref.shape[0])
    total = dot(hot, jnp.concatenate(values, axis=0)).astype(BF16)
    out_ref[:, : 2 * width] = grads_ref[:, : 2 * width]
    out_ref[:, 2 * width :] = total


def last_kernel(
    r, request_ref, back_ref, state_ref, table_out, row_accum_out, step_out, accum_out, *scratch
):
    table_ref, row_accum_ref, step_ref, new_accum_ref, sems = scratch
    pairs = (
        (table_ref, table_out),
        (row_accum_ref, row_accum_out),
        (step_ref, step_out),
        (new_accum_ref, accum_out),
    )
    copies = [pltpu.make_async_copy(source, target, sems.at[i]) for i, (source, target) in enumerate(pairs)]
    table, accum = row_update(r, request_ref, back_ref, state_ref)
    table_ref[...] = table
    copies[0].start()
    row_accum_ref[...] = accum
    copies[1].start()
    per_device, width = step_ref.shape
    rows = slots_of(back_ref) // 2
    parts = back_ref[:, 2 * width :].astype(F32)
    grad = jnp.sum(parts.reshape(parts.shape[0] // rows, rows, width), axis=0)[:per_device]
    accum = to_column(state_ref[table.shape[0] + 1 :, :per_device]) + jnp.mean(grad * grad, axis=1, keepdims=True)
    step_ref[...] = grad * (-LEARN_RATE / jnp.sqrt(accum))
    copies[2].start()
    new_accum_ref[...] = to_row(accum)
    copies[3].start()
    for copy in copies:
        copy.wait()


def call(kernel, outs, *args, **kwargs):
    return pl.pallas_call(
        kernel,
        out_shape=[jax.ShapeDtypeStruct(shape, kind) for shape, kind in outs],
        compiler_params=pltpu.CompilerParams(vmem_limit_bytes=VMEM_LIMIT),
        **kwargs,
    )(*args)


def swap_pair(value, r):
    doms, shards = lax.axis_size("dom"), lax.axis_size("shard")
    order = spread_order(shards)
    groups = [
        [g * shards + s for g in (low, low ^ (1 << r)) for s in sorted(range(shards), key=order.__getitem__)]
        for low in range(doms)
        if not low >> r & 1
    ]
    return lax.all_to_all(
        value, ("dom", "shard"), split_axis=0, concat_axis=0, axis_index_groups=groups, tiled=True
    )


def body(
    embeddings,
    row_accum,
    relations,
    relation_accum,
    request_rows,
    head_slots,
    tail_slots,
    relation_ids,
    own_negatives,
    far_negatives,
):
    rows, width = embeddings.shape
    doms, shards = lax.axis_size("dom"), lax.axis_size("shard")
    rounds, slots = request_rows.shape[0], request_rows.shape[-1]
    bit = rounds - 1
    per_device = relation_accum.shape[0]
    count, touched = head_slots.shape[1], shards * slots
    assert per_device <= slots // 2
    chunks = ((touched, 2 * width), BF16)
    edge_outs = [((2, touched, 2 * count), BF16), ((2, 2 * count, width), BF16), ((count + DIGITS, width), BF16)]
    state = (
        jnp.pad(embeddings, ((0, 2), (0, 0)))
        + jnp.pad(row_accum[None], ((rows, 1), (0, width - rows)))
        + jnp.pad(relation_accum[None], ((rows + 1, 0), (0, width - per_device)))
    )
    edges = (head_slots, tail_slots, relation_ids, own_negatives, far_negatives, relations)
    (outgoing,) = call(first_kernel, [chunks], request_rows, state, *edges)
    swapped = []
    for r in range(rounds):
        received = swap_pair(outgoing, r)
        left, right, swap = call(functools.partial(edge_kernel, r), edge_outs, received, *edges)
        swapped.append(swap)
        for mask in range(1, doms):
            if not mask >> bit & 1:
                swapped.append(lax.ppermute(swap, "dom", [(g, g ^ mask) for g in range(doms)]))
        (grads,) = call(functools.partial(grad_kernel, r), [chunks], left, right)
        if r < bit:
            back = swap_pair(grads, r)
            state, outgoing = call(
                functools.partial(middle_kernel, r), [(state.shape, F32), chunks], request_rows, back, state
            )
    (grads,) = call(
        functools.partial(relation_kernel, bit, per_device), [((touched, 3 * width), BF16)], grads, *swapped
    )
    back = swap_pair(grads, bit)
    outs = [((rows, width), F32), ((1, rows), F32), ((per_device, width), F32), ((1, per_device), F32)]
    table, accum, step, relation_accum = call(
        functools.partial(last_kernel, bit),
        outs,
        request_rows,
        back,
        state,
        in_specs=[VMEM] * 3,
        out_specs=[HBM] * 4,
        scratch_shapes=[pltpu.VMEM(*out) for out in outs] + [pltpu.SemaphoreType.DMA((4,))],
    )
    return (table, accum.reshape(rows), step, relation_accum.reshape(per_device))


def solution(mesh):
    placed = (
        P(("dom", "shard"), None),
        P(("dom", "shard")),
        P(),
        P(("dom", "shard")),
        P(None, ("dom", "shard"), None, None),
        P(None, ("dom", "shard")),
        P(None, ("dom", "shard")),
        P(None, ("dom", "shard")),
        P(None, ("dom", "shard")),
        P(None, ("dom", "shard")),
    )
    return jax.shard_map(
        body,
        mesh=mesh,
        in_specs=placed,
        out_specs=(
            P(("dom", "shard"), None),
            P(("dom", "shard")),
            P(("dom", "shard"), None),
            P(("dom", "shard")),
        ),
        check_vma=False,
    )
```

```python
import functools

import jax
import jax.numpy as jnp
from jax import lax
from jax.experimental import pallas as pl
from jax.experimental.pallas import tpu as pltpu
from jax.sharding import PartitionSpec as P

LEARN_RATE = 0.1
VMEM_LIMIT = 48 * 2**20
BF16 = jnp.bfloat16
F32 = jnp.float32
NATURAL = (((1,), (0,)), ((), ()))
LAST = (((1,), (1,)), ((), ()))
FIRST = (((0,), (0,)), ((), ()))
HBM = pl.BlockSpec(memory_space=pltpu.HBM)
VMEM = pl.BlockSpec(memory_space=pltpu.VMEM)


def dot(left, right, dims=NATURAL):
    return lax.dot_general(left, right, dims, preferred_element_type=F32)


def iota(shape, axis):
    return lax.broadcasted_iota(jnp.int32, shape, axis)


def one_hot_t(row, count):
    return (iota((count, row.shape[1]), 0) == row).astype(BF16)


def one_hot(column, count):
    return (iota((column.shape[0], count), 1) == column).astype(BF16)


def to_column(row):
    n = row.shape[1]
    return jnp.sum(jnp.where(iota((n, n), 0) == iota((n, n), 1), row, 0), axis=1, keepdims=True)


def to_row(column):
    n = column.shape[0]
    return jnp.sum(jnp.where(iota((n, n), 0) == iota((n, n), 1), column, 0), axis=0, keepdims=True)


def reverse(index, count):
    bits = count.bit_length() - 1
    return sum((index >> b & 1) << (bits - 1 - b) for b in range(bits))


def spread_order(shards):
    return [reverse(s, shards) for s in range(shards)]


def group_bit(r):
    return (lax.axis_index("dom") >> r) & 1


def renumber(slot, shards, slots):
    half = slots // 2
    return (slot // half % 2) * (shards * half) + reverse(slot // slots, shards) * half + slot % half


def halves(ref, r):
    rows, bit = ref.shape[0] // 2, group_bit(r)
    return [pl.ds(pl.multiple_of(side * rows, rows), rows) for side in (bit, 1 - bit)]


def unfold(value, width):
    return jnp.concatenate([value[:, :width], value[:, width : 2 * width]], axis=0)


def fold(value):
    n = value.shape[0] // 2
    return jnp.concatenate([value[:n], value[n:]], axis=1)


def request_columns(request_ref, r):
    ids = jnp.concatenate([request_ref[r, :, 0, :], request_ref[r, :, 1, :]], axis=0)
    pieces, slots = ids.shape
    shards, half = pieces // 2, slots // 2
    n = pieces * half
    chunk = iota((n, pieces), 0) // half
    piece = (chunk // shards ^ group_bit(r)) * shards + reverse(chunk % shards, shards)
    rep = dot((piece == iota((n, pieces), 1)).astype(F32), ids.astype(F32))
    lane, inside = iota((n, slots), 1), iota((n, slots), 0) % half
    return [
        jnp.sum(jnp.where(lane == side * half + inside, rep, 0.0), axis=1, keepdims=True).astype(jnp.int32)
        for side in range(2)
    ]


def serve(request_ref, r, table, out_ref):
    rows, width = table.shape
    table = table.astype(BF16)
    hot = jnp.concatenate([one_hot(column, rows) for column in request_columns(request_ref, r)], axis=1)
    blank = jnp.zeros((rows, width), BF16)
    both = jnp.concatenate(
        [jnp.concatenate([table, blank], axis=1), jnp.concatenate([blank, table], axis=1)], axis=0
    )
    out_ref[...] = dot(hot, both).astype(BF16)


def first_kernel(request_ref, state_ref, *refs):
    out_ref = refs[-1]
    table = state_ref[: state_ref.shape[0] - 2]
    serve(request_ref, 0, table, out_ref)


def row_update(r, request_ref, back_ref, state_ref):
    rows, width = state_ref.shape[0] - 2, state_ref.shape[1]
    hot = jnp.concatenate([one_hot(column, rows) for column in request_columns(request_ref, r)], axis=0)
    row_grad = dot(hot, unfold(back_ref[:, : 2 * width], width), FIRST)
    accum = to_column(state_ref[rows : rows + 1, :rows]) + jnp.mean(row_grad * row_grad, axis=1, keepdims=True)
    return state_ref[:rows] - row_grad * (LEARN_RATE / jnp.sqrt(accum)), to_row(accum)


def middle_kernel(r, request_ref, back_ref, state_ref, state_out, out_ref):
    table, accum = row_update(r, request_ref, back_ref, state_ref)
    rows = table.shape[0]
    serve(request_ref, r + 1, table, out_ref)
    state_out[:rows] = table
    state_out[rows:] = state_ref[rows:]
    state_out[rows : rows + 1, :rows] = accum


def slots_of(ref):
    return 2 * ref.shape[0] // (2 * lax.axis_size("shard"))


def edge_kernel(
    r,
    bit,
    per_device,
    rec_ref,
    head_ref,
    tail_ref,
    rel_ref,
    own_neg_ref,
    far_neg_ref,
    relations_ref,
    *refs,
):
    width = relations_ref.shape[1]
    shards, slots = lax.axis_size("shard"), slots_of(rec_ref)
    touched = shards * slots
    edges, negatives = head_ref.shape[1], own_neg_ref.shape[1]
    own_half, far_half = halves(rec_ref, r)
    own = unfold(rec_ref[own_half], width)
    far = unfold(rec_ref[far_half], width)
    row = slice(r, r + 1)
    ids = rel_ref[row]
    hot_head = one_hot_t(renumber(head_ref[row], shards, slots), touched)
    hot_tail = one_hot_t(renumber(tail_ref[row], shards, slots), touched)
    head = dot(hot_head, own, FIRST)
    tail = dot(hot_tail, far, FIRST)
    rel = dot(one_hot_t(ids, relations_ref.shape[0]), relations_ref[...], FIRST)
    query_tail = (head * rel).astype(BF16)
    query_head = (tail * rel).astype(BF16)

    def weights(rows, query, neg_ref):
        hit = iota((touched, negatives), 0) == renumber(neg_ref[row], shards, slots)
        scale = jnp.sum(jnp.where(hit, 1.0 / negatives, 0.0), axis=1, keepdims=True)
        return (jax.nn.sigmoid(dot(rows, query, LAST)) * scale).astype(BF16)

    weight_tail = weights(far, query_tail, far_neg_ref)
    weight_head = weights(own, query_head, own_neg_ref)
    positive = jnp.sum(head * rel * tail, axis=1, keepdims=True)
    coeff = -jax.nn.sigmoid(-positive)
    back_tail = dot(weight_tail, far, FIRST)
    back_head = dot(weight_head, own, FIRST)
    toward_head = coeff * tail + back_tail
    grad_rel = (head * toward_head + tail * back_head).astype(BF16)
    left = [
        jnp.concatenate([hot_head, weight_head], axis=1),
        jnp.concatenate([hot_tail, weight_tail], axis=1),
    ]
    right = [
        jnp.concatenate([(rel * toward_head).astype(BF16), query_head], axis=0),
        jnp.concatenate([(rel * (coeff * head + back_head)).astype(BF16), query_tail], axis=0),
    ]
    if r < bit:
        out_ref, grad_rel_out = refs
        for side, half in enumerate((own_half, far_half)):
            out_ref[half] = fold(dot(left[side], right[side]).astype(BF16))
        grad_rel_out[...] = grad_rel
    else:
        *before_refs, left_out, right_out, values_out, sums_out = refs
        for side in range(2):
            left_out[side], right_out[side] = left[side], right[side]
        values = jnp.concatenate([ref[...] for ref in before_refs] + [grad_rel], axis=0)
        values_out[...] = values
        masks = other_doms(bit)
        for i, mask in enumerate(masks):
            sums_out[i] = relation_sums(rel_ref, values, bit, per_device, mask, rec_ref.shape[0]).astype(BF16)


def other_doms(bit):
    return [mask for mask in range(1, lax.axis_size("dom")) if not mask >> bit & 1]


def relation_sums(rel_ref, values, bit, per_device, mask, rows):
    shards = lax.axis_size("shard")
    ids = jnp.concatenate([rel_ref[r : r + 1] for r in range(rel_ref.shape[0])], axis=1)
    owner = ids // per_device
    dom = owner // shards
    chunk = (dom >> bit & 1) * shards + reverse(owner % shards, shards)
    meant = (dom ^ lax.axis_index("dom") ^ mask) & ~(1 << bit) == 0
    place = jnp.where(meant, chunk * (rows // (2 * shards)) + ids % per_device, -1)
    return dot(one_hot_t(place, rows), values)


def grad_kernel(bit, per_device, rel_ref, left_ref, right_ref, values_ref, out_ref, sums_out):
    for side, half in enumerate(halves(out_ref, bit)):
        out_ref[half] = fold(dot(left_ref[side], right_ref[side]).astype(BF16))
    sums_out[...] = relation_sums(rel_ref, values_ref[...], bit, per_device, 0, out_ref.shape[0])


def join_kernel(grads_ref, sums_ref, *refs):
    *came_refs, out_ref = refs
    width = sums_ref.shape[1]
    total = sums_ref[...]
    for ref in came_refs:
        total = total + ref[...].astype(F32)
    out_ref[:, : 2 * width] = grads_ref[...]
    out_ref[:, 2 * width :] = total.astype(BF16)


def last_kernel(
    r, request_ref, back_ref, state_ref, table_out, row_accum_out, step_out, accum_out, *scratch
):
    table_ref, row_accum_ref, step_ref, new_accum_ref, sems = scratch
    pairs = (
        (table_ref, table_out),
        (row_accum_ref, row_accum_out),
        (step_ref, step_out),
        (new_accum_ref, accum_out),
    )
    copies = [pltpu.make_async_copy(source, target, sems.at[i]) for i, (source, target) in enumerate(pairs)]
    table, accum = row_update(r, request_ref, back_ref, state_ref)
    table_ref[...] = table
    copies[0].start()
    row_accum_ref[...] = accum
    copies[1].start()
    per_device, width = step_ref.shape
    rows = slots_of(back_ref) // 2
    parts = back_ref[:, 2 * width :].astype(F32)
    grad = jnp.sum(parts.reshape(parts.shape[0] // rows, rows, width), axis=0)[:per_device]
    accum = to_column(state_ref[table.shape[0] + 1 :, :per_device]) + jnp.mean(grad * grad, axis=1, keepdims=True)
    step_ref[...] = grad * (-LEARN_RATE / jnp.sqrt(accum))
    copies[2].start()
    new_accum_ref[...] = to_row(accum)
    copies[3].start()
    for copy in copies:
        copy.wait()


def call(kernel, outs, *args, **kwargs):
    return pl.pallas_call(
        kernel,
        out_shape=[jax.ShapeDtypeStruct(shape, kind) for shape, kind in outs],
        compiler_params=pltpu.CompilerParams(vmem_limit_bytes=VMEM_LIMIT),
        **kwargs,
    )(*args)


def swap_pair(value, r):
    doms, shards = lax.axis_size("dom"), lax.axis_size("shard")
    order = spread_order(shards)
    groups = [
        [g * shards + s for g in (low, low ^ (1 << r)) for s in sorted(range(shards), key=order.__getitem__)]
        for low in range(doms)
        if not low >> r & 1
    ]
    return lax.all_to_all(
        value, ("dom", "shard"), split_axis=0, concat_axis=0, axis_index_groups=groups, tiled=True
    )


def body(
    embeddings,
    row_accum,
    relations,
    relation_accum,
    request_rows,
    head_slots,
    tail_slots,
    relation_ids,
    own_negatives,
    far_negatives,
):
    rows, width = embeddings.shape
    doms, shards = lax.axis_size("dom"), lax.axis_size("shard")
    rounds, slots = request_rows.shape[0], request_rows.shape[-1]
    bit = rounds - 1
    per_device = relation_accum.shape[0]
    count, touched = head_slots.shape[1], shards * slots
    assert per_device <= slots // 2
    chunks = ((touched, 2 * width), BF16)
    state = (
        jnp.pad(embeddings, ((0, 2), (0, 0)))
        + jnp.pad(row_accum[None], ((rows, 1), (0, width - rows)))
        + jnp.pad(relation_accum[None], ((rows + 1, 0), (0, width - per_device)))
    )
    edges = (head_slots, tail_slots, relation_ids, own_negatives, far_negatives, relations)
    (outgoing,) = call(first_kernel, [chunks], request_rows, state, *edges)
    before = []
    for r in range(bit):
        received = swap_pair(outgoing, r)
        grads, grad_rel = call(
            functools.partial(edge_kernel, r, bit, per_device), [chunks, ((count, width), BF16)], received, *edges
        )
        before.append(grad_rel)
        back = swap_pair(grads, r)
        state, outgoing = call(
            functools.partial(middle_kernel, r), [(state.shape, F32), chunks], request_rows, back, state
        )
    received = swap_pair(outgoing, bit)
    masks = other_doms(bit)
    left, right, values, sums = call(
        functools.partial(edge_kernel, bit, bit, per_device),
        [
            ((2, touched, 2 * count), BF16),
            ((2, 2 * count, width), BF16),
            ((rounds * count, width), BF16),
            ((len(masks), touched, width), BF16),
        ],
        received,
        *edges,
        *before,
    )
    came = [lax.ppermute(sums[i], "dom", [(g, g ^ mask) for g in range(doms)]) for i, mask in enumerate(masks)]
    grads, sums = call(
        functools.partial(grad_kernel, bit, per_device),
        [chunks, ((touched, width), F32)],
        relation_ids,
        left,
        right,
        values,
    )
    (grads,) = call(join_kernel, [((touched, 3 * width), BF16)], grads, sums, *came)
    back = swap_pair(grads, bit)
    outs = [((rows, width), F32), ((1, rows), F32), ((per_device, width), F32), ((1, per_device), F32)]
    table, accum, step, relation_accum = call(
        functools.partial(last_kernel, bit),
        outs,
        request_rows,
        back,
        state,
        in_specs=[VMEM] * 3,
        out_specs=[HBM] * 4,
        scratch_shapes=[pltpu.VMEM(*out) for out in outs] + [pltpu.SemaphoreType.DMA((4,))],
    )
    return (table, accum.reshape(rows), step, relation_accum.reshape(per_device))


def solution(mesh):
    placed = (
        P(("dom", "shard"), None),
        P(("dom", "shard")),
        P(),
        P(("dom", "shard")),
        P(None, ("dom", "shard"), None, None),
        P(None, ("dom", "shard")),
        P(None, ("dom", "shard")),
        P(None, ("dom", "shard")),
        P(None, ("dom", "shard")),
        P(None, ("dom", "shard")),
    )
    return jax.shard_map(
        body,
        mesh=mesh,
        in_specs=placed,
        out_specs=(
            P(("dom", "shard"), None),
            P(("dom", "shard")),
            P(("dom", "shard"), None),
            P(("dom", "shard")),
        ),
        check_vma=False,
    )
```

```python
import functools

import jax
import jax.numpy as jnp
from jax import lax
from jax.experimental import pallas as pl
from jax.experimental.pallas import tpu as pltpu
from jax.sharding import PartitionSpec as P

LEARN_RATE = 0.1
LANES = 128
VMEM_LIMIT = 48 * 2**20
BF16 = jnp.bfloat16
F32 = jnp.float32
NATURAL = (((1,), (0,)), ((), ()))
LAST = (((1,), (1,)), ((), ()))
FIRST = (((0,), (0,)), ((), ()))
HBM = pl.BlockSpec(memory_space=pltpu.HBM)
VMEM = pl.BlockSpec(memory_space=pltpu.VMEM)


def dot(left, right, dims=NATURAL):
    return lax.dot_general(left, right, dims, preferred_element_type=F32)


def iota(shape, axis):
    return lax.broadcasted_iota(jnp.int32, shape, axis)


def one_hot_t(row, count):
    return (iota((count, row.shape[1]), 0) == row).astype(BF16)


def one_hot(column, count):
    return (iota((column.shape[0], count), 1) == column).astype(BF16)


def to_column(row):
    n = row.shape[1]
    return jnp.sum(jnp.where(iota((n, n), 0) == iota((n, n), 1), row, 0), axis=1, keepdims=True)


def to_row(column):
    n = column.shape[0]
    return jnp.sum(jnp.where(iota((n, n), 0) == iota((n, n), 1), column, 0), axis=0, keepdims=True)


def reverse(index, count):
    bits = count.bit_length() - 1
    return sum((index >> b & 1) << (bits - 1 - b) for b in range(bits))


def spread_order(shards):
    return [reverse(s, shards) for s in range(shards)]


def group_bit(r):
    return (lax.axis_index("dom") >> r) & 1


def renumber(slot, shards, slots):
    half = slots // 2
    return (slot // half % 2) * (shards * half) + reverse(slot // slots, shards) * half + slot % half


def halves(ref, r):
    rows, bit = ref.shape[0] // 2, group_bit(r)
    return [pl.ds(pl.multiple_of(side * rows, rows), rows) for side in (bit, 1 - bit)]


def whole(width):
    return width // LANES * LANES


def unfold(value, width):
    tiles, rest = whole(width), width - whole(width)
    return jnp.concatenate(
        [
            jnp.concatenate(
                [value[:, side * tiles : (side + 1) * tiles], value[:, 2 * tiles + side * rest :][:, :rest]], axis=1
            )
            for side in range(2)
        ],
        axis=0,
    )


def beside(left, right):
    tiles = whole(left.shape[1])
    return jnp.concatenate([left[:, :tiles], right[:, :tiles], left[:, tiles:], right[:, tiles:]], axis=1)


def fold(value):
    n = value.shape[0] // 2
    return beside(value[:n], value[n:])


def request_columns(request_ref, r):
    ids = jnp.concatenate([request_ref[r, :, 0, :], request_ref[r, :, 1, :]], axis=0)
    pieces, slots = ids.shape
    shards, half = pieces // 2, slots // 2
    n = pieces * half
    chunk = iota((n, pieces), 0) // half
    piece = (chunk // shards ^ group_bit(r)) * shards + reverse(chunk % shards, shards)
    rep = dot((piece == iota((n, pieces), 1)).astype(F32), ids.astype(F32))
    lane, inside = iota((n, slots), 1), iota((n, slots), 0) % half
    return [
        jnp.sum(jnp.where(lane == side * half + inside, rep, 0.0), axis=1, keepdims=True).astype(jnp.int32)
        for side in range(2)
    ]


def serve(request_ref, r, table, out_ref):
    rows, width = table.shape
    table = table.astype(BF16)
    hot = jnp.concatenate([one_hot(column, rows) for column in request_columns(request_ref, r)], axis=1)
    blank = jnp.zeros((rows, width), BF16)
    both = jnp.concatenate([beside(table, blank), beside(blank, table)], axis=0)
    out_ref[...] = dot(hot, both).astype(BF16)


def first_kernel(request_ref, state_ref, *refs):
    out_ref = refs[-1]
    table = state_ref[: state_ref.shape[0] - 2]
    serve(request_ref, 0, table, out_ref)


def request_hot(request_ref, r, rows):
    return jnp.concatenate([one_hot(column, rows) for column in request_columns(request_ref, r)], axis=0)


def row_update(hot, back_ref, state_ref):
    rows, width = state_ref.shape[0] - 2, state_ref.shape[1]
    row_grad = dot(hot, unfold(back_ref[:, : 2 * width], width), FIRST)
    accum = to_column(state_ref[rows : rows + 1, :rows]) + jnp.mean(row_grad * row_grad, axis=1, keepdims=True)
    return state_ref[:rows] - row_grad * (LEARN_RATE / jnp.sqrt(accum)), to_row(accum)


def middle_kernel(r, request_ref, back_ref, state_ref, state_out, out_ref):
    rows = state_ref.shape[0] - 2
    table, accum = row_update(request_hot(request_ref, r, rows), back_ref, state_ref)
    serve(request_ref, r + 1, table, out_ref)
    state_out[:rows] = table
    state_out[rows:] = state_ref[rows:]
    state_out[rows : rows + 1, :rows] = accum


def slots_of(ref):
    return 2 * ref.shape[0] // (2 * lax.axis_size("shard"))


def edge_kernel(
    r,
    bit,
    per_device,
    rec_ref,
    head_ref,
    tail_ref,
    rel_ref,
    own_neg_ref,
    far_neg_ref,
    relations_ref,
    *refs,
):
    width = relations_ref.shape[1]
    shards, slots = lax.axis_size("shard"), slots_of(rec_ref)
    touched = shards * slots
    edges, negatives = head_ref.shape[1], own_neg_ref.shape[1]
    own_half, far_half = halves(rec_ref, r)
    own = unfold(rec_ref[own_half], width)
    far = unfold(rec_ref[far_half], width)
    row = slice(r, r + 1)
    ids = rel_ref[row]
    heads, tails = renumber(head_ref[row], shards, slots), renumber(tail_ref[row], shards, slots)
    head = dot(one_hot(to_column(heads), touched), own)
    tail = dot(one_hot(to_column(tails), touched), far)
    rel = dot(one_hot(to_column(ids), relations_ref.shape[0]), relations_ref[...])
    query_tail = (head * rel).astype(BF16)
    query_head = (tail * rel).astype(BF16)

    def weights(query, rows, neg_ref):
        hit = iota((touched, negatives), 0) == renumber(neg_ref[row], shards, slots)
        scale = jnp.sum(jnp.where(hit, 1.0 / negatives, 0.0), axis=1, keepdims=True)
        return jax.nn.sigmoid(dot(query, rows, LAST)) * to_row(scale)

    weight_tail = weights(query_tail, far, far_neg_ref)
    weight_head = weights(query_head, own, own_neg_ref)
    positive = jnp.sum(head * rel * tail, axis=1, keepdims=True)
    coeff = -jax.nn.sigmoid(-positive)
    back_tail = dot(weight_tail.astype(BF16), far)
    back_head = dot(weight_head.astype(BF16), own)
    toward_head = coeff * tail + back_tail
    grad_rel = (head * toward_head + tail * back_head).astype(BF16)
    left = [
        jnp.concatenate([one_hot_t(slot, touched), weight.T.astype(BF16)], axis=1)
        for slot, weight in ((heads, weight_head), (tails, weight_tail))
    ]
    right = [
        jnp.concatenate([(rel * toward_head).astype(BF16), query_head], axis=0),
        jnp.concatenate([(rel * (coeff * head + back_head)).astype(BF16), query_tail], axis=0),
    ]
    if r < bit:
        out_ref, grad_rel_out = refs
        for side, half in enumerate((own_half, far_half)):
            out_ref[half] = fold(dot(left[side], right[side]).astype(BF16))
        grad_rel_out[...] = grad_rel
    else:
        *before_refs, left_out, right_out, values_out, sums_out = refs
        for side in range(2):
            left_out[side], right_out[side] = left[side], right[side]
        values = jnp.concatenate([ref[...] for ref in before_refs] + [grad_rel], axis=0)
        values_out[...] = values
        masks = other_doms(bit)
        for i, mask in enumerate(masks):
            sums_out[i] = relation_sums(rel_ref, values, bit, per_device, mask, rec_ref.shape[0]).astype(BF16)


def other_doms(bit):
    return [mask for mask in range(1, lax.axis_size("dom")) if not mask >> bit & 1]


def relation_sums(rel_ref, values, bit, per_device, mask, rows):
    shards = lax.axis_size("shard")
    ids = jnp.concatenate([rel_ref[r : r + 1] for r in range(rel_ref.shape[0])], axis=1)
    owner = ids // per_device
    dom = owner // shards
    chunk = (dom >> bit & 1) * shards + reverse(owner % shards, shards)
    meant = (dom ^ lax.axis_index("dom") ^ mask) & ~(1 << bit) == 0
    place = jnp.where(meant, chunk * (rows // (2 * shards)) + ids % per_device, -1)
    return dot(one_hot_t(place, rows), values)


def grad_kernel(
    bit, per_device, request_ref, rel_ref, left_ref, right_ref, values_ref, out_ref, sums_out, hot_out
):
    for side, half in enumerate(halves(out_ref, bit)):
        out_ref[half] = fold(dot(left_ref[side], right_ref[side]).astype(BF16))
    sums_out[...] = relation_sums(rel_ref, values_ref[...], bit, per_device, 0, out_ref.shape[0])
    hot_out[...] = request_hot(request_ref, bit, hot_out.shape[1])


def wide(width):
    return 3 * whole(width) + LANES


def join_kernel(grads_ref, sums_ref, *refs):
    *came_refs, out_ref = refs
    width = sums_ref.shape[1]
    tiles, rest = whole(width), width - whole(width)
    total = sums_ref[...]
    for ref in came_refs:
        total = total + ref[...].astype(F32)
    total = total.astype(BF16)
    out_ref[:, : 2 * tiles] = grads_ref[:, : 2 * tiles]
    blank = jnp.zeros((total.shape[0], LANES - 3 * rest), BF16)
    out_ref[:, 2 * tiles : 2 * tiles + LANES] = jnp.concatenate(
        [grads_ref[:, 2 * tiles :], total[:, tiles:], blank], axis=1
    )
    out_ref[:, 2 * tiles + LANES :] = total[:, :tiles]


def last_kernel(hot_ref, back_ref, state_ref, table_out, row_accum_out, step_out, accum_out, *scratch):
    table_ref, row_accum_ref, step_ref, new_accum_ref, sems = scratch
    pairs = (
        (table_ref, table_out),
        (row_accum_ref, row_accum_out),
        (step_ref, step_out),
        (new_accum_ref, accum_out),
    )
    copies = [pltpu.make_async_copy(source, target, sems.at[i]) for i, (source, target) in enumerate(pairs)]
    table, accum = row_update(hot_ref[...], back_ref, state_ref)
    table_ref[...] = table
    copies[0].start()
    row_accum_ref[...] = accum
    copies[1].start()
    per_device, width = step_ref.shape
    rows = slots_of(back_ref) // 2
    tiles, rest = whole(width), width - whole(width)
    parts = jnp.concatenate(
        [back_ref[:, 2 * tiles + LANES :], back_ref[:, 2 * tiles + 2 * rest : 2 * tiles + 3 * rest]], axis=1
    ).astype(F32)
    grad = jnp.sum(parts.reshape(parts.shape[0] // rows, rows, width), axis=0)[:per_device]
    accum = to_column(state_ref[table.shape[0] + 1 :, :per_device]) + jnp.mean(grad * grad, axis=1, keepdims=True)
    step_ref[...] = grad * (-LEARN_RATE / jnp.sqrt(accum))
    copies[2].start()
    new_accum_ref[...] = to_row(accum)
    copies[3].start()
    for copy in copies:
        copy.wait()


def call(kernel, outs, *args, **kwargs):
    return pl.pallas_call(
        kernel,
        out_shape=[jax.ShapeDtypeStruct(shape, kind) for shape, kind in outs],
        compiler_params=pltpu.CompilerParams(vmem_limit_bytes=VMEM_LIMIT),
        **kwargs,
    )(*args)


def swap_pair(value, r):
    doms, shards = lax.axis_size("dom"), lax.axis_size("shard")
    order = spread_order(shards)
    groups = [
        [g * shards + s for g in (low, low ^ (1 << r)) for s in sorted(range(shards), key=order.__getitem__)]
        for low in range(doms)
        if not low >> r & 1
    ]
    return lax.all_to_all(
        value, ("dom", "shard"), split_axis=0, concat_axis=0, axis_index_groups=groups, tiled=True
    )


def body(
    embeddings,
    row_accum,
    relations,
    relation_accum,
    request_rows,
    head_slots,
    tail_slots,
    relation_ids,
    own_negatives,
    far_negatives,
):
    rows, width = embeddings.shape
    doms, shards = lax.axis_size("dom"), lax.axis_size("shard")
    rounds, slots = request_rows.shape[0], request_rows.shape[-1]
    bit = rounds - 1
    per_device = relation_accum.shape[0]
    assert 3 * (width % LANES) <= LANES
    count, touched = head_slots.shape[1], shards * slots
    assert per_device <= slots // 2
    chunks = ((touched, 2 * width), BF16)
    state = (
        jnp.pad(embeddings, ((0, 2), (0, 0)))
        + jnp.pad(row_accum[None], ((rows, 1), (0, width - rows)))
        + jnp.pad(relation_accum[None], ((rows + 1, 0), (0, width - per_device)))
    )
    edges = (head_slots, tail_slots, relation_ids, own_negatives, far_negatives, relations)
    (outgoing,) = call(first_kernel, [chunks], request_rows, state, *edges)
    before = []
    for r in range(bit):
        received = swap_pair(outgoing, r)
        grads, grad_rel = call(
            functools.partial(edge_kernel, r, bit, per_device), [chunks, ((count, width), BF16)], received, *edges
        )
        before.append(grad_rel)
        back = swap_pair(grads, r)
        state, outgoing = call(
            functools.partial(middle_kernel, r), [(state.shape, F32), chunks], request_rows, back, state
        )
    received = swap_pair(outgoing, bit)
    masks = other_doms(bit)
    left, right, values, sums = call(
        functools.partial(edge_kernel, bit, bit, per_device),
        [
            ((2, touched, 2 * count), BF16),
            ((2, 2 * count, width), BF16),
            ((rounds * count, width), BF16),
            ((len(masks), touched, width), BF16),
        ],
        received,
        *edges,
        *before,
    )
    came = [lax.ppermute(sums[i], "dom", [(g, g ^ mask) for g in range(doms)]) for i, mask in enumerate(masks)]
    grads, sums, hot = call(
        functools.partial(grad_kernel, bit, per_device),
        [chunks, ((touched, width), F32), ((2 * touched, rows), BF16)],
        request_rows,
        relation_ids,
        left,
        right,
        values,
    )
    (grads,) = call(join_kernel, [((touched, wide(width)), BF16)], grads, sums, *came)
    back = swap_pair(grads, bit)
    outs = [((rows, width), F32), ((1, rows), F32), ((per_device, width), F32), ((1, per_device), F32)]
    table, accum, step, relation_accum = call(
        last_kernel,
        outs,
        hot,
        back,
        state,
        in_specs=[VMEM] * 3,
        out_specs=[HBM] * 4,
        scratch_shapes=[pltpu.VMEM(*out) for out in outs] + [pltpu.SemaphoreType.DMA((4,))],
    )
    return (table, accum.reshape(rows), step, relation_accum.reshape(per_device))


def solution(mesh):
    placed = (
        P(("dom", "shard"), None),
        P(("dom", "shard")),
        P(),
        P(("dom", "shard")),
        P(None, ("dom", "shard"), None, None),
        P(None, ("dom", "shard")),
        P(None, ("dom", "shard")),
        P(None, ("dom", "shard")),
        P(None, ("dom", "shard")),
        P(None, ("dom", "shard")),
    )
    return jax.shard_map(
        body,
        mesh=mesh,
        in_specs=placed,
        out_specs=(
            P(("dom", "shard"), None),
            P(("dom", "shard")),
            P(("dom", "shard"), None),
            P(("dom", "shard")),
        ),
        check_vma=False,
    )
```

```python
import functools

import jax
import jax.numpy as jnp
from jax import lax
from jax.experimental import pallas as pl
from jax.experimental.pallas import tpu as pltpu
from jax.sharding import PartitionSpec as P

LEARN_RATE = 0.1
LANES = 128
VMEM_LIMIT = 48 * 2**20
BF16 = jnp.bfloat16
F32 = jnp.float32
NATURAL = (((1,), (0,)), ((), ()))
LAST = (((1,), (1,)), ((), ()))
FIRST = (((0,), (0,)), ((), ()))
HBM = pl.BlockSpec(memory_space=pltpu.HBM)
VMEM = pl.BlockSpec(memory_space=pltpu.VMEM)


def dot(left, right, dims=NATURAL):
    return lax.dot_general(left, right, dims, preferred_element_type=F32)


def iota(shape, axis):
    return lax.broadcasted_iota(jnp.int32, shape, axis)


def one_hot_t(row, count):
    return (iota((count, row.shape[1]), 0) == row).astype(BF16)


def one_hot(column, count):
    return (iota((column.shape[0], count), 1) == column).astype(BF16)


def to_column(row):
    n = row.shape[1]
    return jnp.sum(jnp.where(iota((n, n), 0) == iota((n, n), 1), row, 0), axis=1, keepdims=True)


def to_row(column):
    n = column.shape[0]
    return jnp.sum(jnp.where(iota((n, n), 0) == iota((n, n), 1), column, 0), axis=0, keepdims=True)


def reverse(index, count):
    bits = count.bit_length() - 1
    return sum((index >> b & 1) << (bits - 1 - b) for b in range(bits))


def spread_order(shards):
    return [reverse(s, shards) for s in range(shards)]


def group_bit(r):
    return (lax.axis_index("dom") >> r) & 1


def renumber(slot, shards, slots):
    half = slots // 2
    return (slot // half % 2) * (shards * half) + reverse(slot // slots, shards) * half + slot % half


def halves(ref, r):
    rows, bit = ref.shape[0] // 2, group_bit(r)
    return [pl.ds(pl.multiple_of(side * rows, rows), rows) for side in (bit, 1 - bit)]


def whole(width):
    return width // LANES * LANES


def unfold(value, width):
    tiles, rest = whole(width), width - whole(width)
    return jnp.concatenate(
        [
            jnp.concatenate(
                [value[:, side * tiles : (side + 1) * tiles], value[:, 2 * tiles + side * rest :][:, :rest]], axis=1
            )
            for side in range(2)
        ],
        axis=0,
    )


def beside(left, right):
    tiles = whole(left.shape[1])
    return jnp.concatenate([left[:, :tiles], right[:, :tiles], left[:, tiles:], right[:, tiles:]], axis=1)


def fold(value):
    n = value.shape[0] // 2
    return beside(value[:n], value[n:])


def request_columns(request_ref, r):
    _, shards, _, slots = request_ref.shape
    half = slots // 2
    sides = [request_ref[r, :, k, :] for k in range(2)]
    flip = group_bit(r) == 1
    rep = jnp.concatenate(
        [
            jnp.broadcast_to(ids[reverse(place, shards)][None], (half, slots))
            for ids in (jnp.where(flip, sides[1], sides[0]), jnp.where(flip, sides[0], sides[1]))
            for place in range(shards)
        ],
        axis=0,
    )
    n = rep.shape[0]
    lane, inside = iota((n, slots), 1), iota((n, slots), 0) % half
    return [
        jnp.sum(jnp.where(lane == side * half + inside, rep, 0), axis=1, keepdims=True) for side in range(2)
    ]


def serve(request_ref, r, table, out_ref):
    rows, width = table.shape
    table = table.astype(BF16)
    hot = jnp.concatenate([one_hot(column, rows) for column in request_columns(request_ref, r)], axis=1)
    blank = jnp.zeros((rows, width), BF16)
    both = jnp.concatenate([beside(table, blank), beside(blank, table)], axis=0)
    out_ref[...] = dot(hot, both).astype(BF16)


def first_kernel(request_ref, state_ref, *refs):
    out_ref = refs[-1]
    table = state_ref[: state_ref.shape[0] - 2]
    serve(request_ref, 0, table, out_ref)


def request_hot(request_ref, r, rows):
    return jnp.concatenate([one_hot(column, rows) for column in request_columns(request_ref, r)], axis=0)


def row_update(hot, back_ref, state_ref):
    rows, width = state_ref.shape[0] - 2, state_ref.shape[1]
    row_grad = dot(hot, unfold(back_ref[:, : 2 * width], width), FIRST)
    accum = to_column(state_ref[rows : rows + 1, :rows]) + jnp.mean(row_grad * row_grad, axis=1, keepdims=True)
    return state_ref[:rows] - row_grad * (LEARN_RATE / jnp.sqrt(accum)), to_row(accum)


def middle_kernel(r, request_ref, back_ref, state_ref, state_out, out_ref):
    rows = state_ref.shape[0] - 2
    table, accum = row_update(request_hot(request_ref, r, rows), back_ref, state_ref)
    serve(request_ref, r + 1, table, out_ref)
    state_out[:rows] = table
    state_out[rows:] = state_ref[rows:]
    state_out[rows : rows + 1, :rows] = accum


def slots_of(ref):
    return 2 * ref.shape[0] // (2 * lax.axis_size("shard"))


def by_blocks(function, *arrays):
    step = 16
    parts = [function(*[x[i : i + step] for x in arrays]) for i in range(0, arrays[0].shape[0], step)]
    return [jnp.concatenate(column, axis=0) for column in zip(*parts)]


def query_block(head, tail, rel):
    tail_query = head * rel
    positive = jnp.sum(tail_query * tail, axis=1, keepdims=True)
    return tail_query.astype(BF16), (tail * rel).astype(BF16), -jax.nn.sigmoid(-positive)


def grad_block(head, tail, rel, coeff, back_tail, back_head):
    toward_head = coeff * tail + back_tail
    grad_rel = head * toward_head + tail * back_head
    return (
        (rel * toward_head).astype(BF16),
        (rel * (coeff * head + back_head)).astype(BF16),
        grad_rel.astype(BF16),
    )


def edge_kernel(
    r,
    bit,
    per_device,
    rec_ref,
    head_ref,
    tail_ref,
    rel_ref,
    own_neg_ref,
    far_neg_ref,
    relations_ref,
    *refs,
):
    width = relations_ref.shape[1]
    shards, slots = lax.axis_size("shard"), slots_of(rec_ref)
    touched = shards * slots
    edges, negatives = head_ref.shape[1], own_neg_ref.shape[1]
    own_half, far_half = halves(rec_ref, r)
    own = unfold(rec_ref[own_half], width)
    far = unfold(rec_ref[far_half], width)
    row = slice(r, r + 1)
    ids = rel_ref[row]
    heads, tails = renumber(head_ref[row], shards, slots), renumber(tail_ref[row], shards, slots)
    head = dot(one_hot(to_column(heads), touched), own)
    tail = dot(one_hot(to_column(tails), touched), far)
    rel = dot(one_hot(to_column(ids), relations_ref.shape[0]), relations_ref[...])
    query_tail, query_head, coeff = by_blocks(query_block, head, tail, rel)

    def weights(query, rows, neg_ref):
        hit = iota((touched, negatives), 0) == renumber(neg_ref[row], shards, slots)
        scale = jnp.sum(jnp.where(hit, 1.0 / negatives, 0.0), axis=1, keepdims=True)
        return jax.nn.sigmoid(dot(query, rows, LAST)) * to_row(scale)

    weight_tail = weights(query_tail, far, far_neg_ref)
    weight_head = weights(query_head, own, own_neg_ref)
    back_tail = dot(weight_tail.astype(BF16), far)
    back_head = dot(weight_head.astype(BF16), own)
    grad_head, grad_tail, grad_rel = by_blocks(grad_block, head, tail, rel, coeff, back_tail, back_head)
    left = [
        jnp.concatenate([one_hot_t(slot, touched), weight.T.astype(BF16)], axis=1)
        for slot, weight in ((heads, weight_head), (tails, weight_tail))
    ]
    right = [
        jnp.concatenate([grad_head, query_head], axis=0),
        jnp.concatenate([grad_tail, query_tail], axis=0),
    ]
    if r < bit:
        out_ref, grad_rel_out = refs
        for side, half in enumerate((own_half, far_half)):
            out_ref[half] = fold(dot(left[side], right[side]).astype(BF16))
        grad_rel_out[...] = grad_rel
    else:
        *before_refs, left_out, right_out, values_out, sums_out = refs
        for side in range(2):
            left_out[side], right_out[side] = left[side], right[side]
        values = jnp.concatenate([ref[...] for ref in before_refs] + [grad_rel], axis=0)
        values_out[...] = values
        masks = other_doms(bit)
        for i, mask in enumerate(masks):
            sums_out[i] = relation_sums(rel_ref, values, bit, per_device, mask, rec_ref.shape[0]).astype(BF16)


def other_doms(bit):
    return [mask for mask in range(1, lax.axis_size("dom")) if not mask >> bit & 1]


def relation_sums(rel_ref, values, bit, per_device, mask, rows):
    shards = lax.axis_size("shard")
    ids = jnp.concatenate([rel_ref[r : r + 1] for r in range(rel_ref.shape[0])], axis=1)
    owner = ids // per_device
    dom = owner // shards
    chunk = (dom >> bit & 1) * shards + reverse(owner % shards, shards)
    meant = (dom ^ lax.axis_index("dom") ^ mask) & ~(1 << bit) == 0
    place = jnp.where(meant, chunk * (rows // (2 * shards)) + ids % per_device, -1)
    return dot(one_hot_t(place, rows), values)


def grad_kernel(
    bit, per_device, request_ref, rel_ref, left_ref, right_ref, values_ref, out_ref, sums_out, hot_out
):
    for side, half in enumerate(halves(out_ref, bit)):
        out_ref[half] = fold(dot(left_ref[side], right_ref[side]).astype(BF16))
    sums_out[...] = relation_sums(rel_ref, values_ref[...], bit, per_device, 0, out_ref.shape[0])
    hot_out[...] = request_hot(request_ref, bit, hot_out.shape[1])


def wide(width):
    return 3 * whole(width) + LANES


def join_kernel(grads_ref, sums_ref, *refs):
    *came_refs, out_ref = refs
    width = sums_ref.shape[1]
    tiles, rest = whole(width), width - whole(width)
    total = sums_ref[...]
    for ref in came_refs:
        total = total + ref[...].astype(F32)
    total = total.astype(BF16)
    out_ref[:, : 2 * tiles] = grads_ref[:, : 2 * tiles]
    blank = jnp.zeros((total.shape[0], LANES - 3 * rest), BF16)
    out_ref[:, 2 * tiles : 2 * tiles + LANES] = jnp.concatenate(
        [grads_ref[:, 2 * tiles :], total[:, tiles:], blank], axis=1
    )
    out_ref[:, 2 * tiles + LANES :] = total[:, :tiles]


def last_kernel(hot_ref, back_ref, state_ref, table_out, row_accum_out, step_out, accum_out, *scratch):
    table_ref, row_accum_ref, step_ref, new_accum_ref, sems = scratch
    pairs = (
        (table_ref, table_out),
        (row_accum_ref, row_accum_out),
        (step_ref, step_out),
        (new_accum_ref, accum_out),
    )
    copies = [pltpu.make_async_copy(source, target, sems.at[i]) for i, (source, target) in enumerate(pairs)]
    table, accum = row_update(hot_ref[...], back_ref, state_ref)
    table_ref[...] = table
    copies[0].start()
    row_accum_ref[...] = accum
    copies[1].start()
    per_device, width = step_ref.shape
    rows = slots_of(back_ref) // 2
    tiles, rest = whole(width), width - whole(width)
    parts = jnp.concatenate(
        [back_ref[:, 2 * tiles + LANES :], back_ref[:, 2 * tiles + 2 * rest : 2 * tiles + 3 * rest]], axis=1
    ).astype(F32)
    grad = jnp.sum(parts.reshape(parts.shape[0] // rows, rows, width), axis=0)[:per_device]
    accum = to_column(state_ref[table.shape[0] + 1 :, :per_device]) + jnp.mean(grad * grad, axis=1, keepdims=True)
    step_ref[...] = grad * (-LEARN_RATE / jnp.sqrt(accum))
    copies[2].start()
    new_accum_ref[...] = to_row(accum)
    copies[3].start()
    for copy in copies:
        copy.wait()


def call(kernel, outs, *args, **kwargs):
    return pl.pallas_call(
        kernel,
        out_shape=[jax.ShapeDtypeStruct(shape, kind) for shape, kind in outs],
        compiler_params=pltpu.CompilerParams(vmem_limit_bytes=VMEM_LIMIT),
        **kwargs,
    )(*args)


def swap_pair(value, r):
    doms, shards = lax.axis_size("dom"), lax.axis_size("shard")
    order = spread_order(shards)
    groups = [
        [g * shards + s for g in (low, low ^ (1 << r)) for s in sorted(range(shards), key=order.__getitem__)]
        for low in range(doms)
        if not low >> r & 1
    ]
    return lax.all_to_all(
        value, ("dom", "shard"), split_axis=0, concat_axis=0, axis_index_groups=groups, tiled=True
    )


def body(
    embeddings,
    row_accum,
    relations,
    relation_accum,
    request_rows,
    head_slots,
    tail_slots,
    relation_ids,
    own_negatives,
    far_negatives,
):
    rows, width = embeddings.shape
    doms, shards = lax.axis_size("dom"), lax.axis_size("shard")
    rounds, slots = request_rows.shape[0], request_rows.shape[-1]
    bit = rounds - 1
    per_device = relation_accum.shape[0]
    assert 3 * (width % LANES) <= LANES
    count, touched = head_slots.shape[1], shards * slots
    assert per_device <= slots // 2
    chunks = ((touched, 2 * width), BF16)
    state = (
        jnp.pad(embeddings, ((0, 2), (0, 0)))
        + jnp.pad(row_accum[None], ((rows, 1), (0, width - rows)))
        + jnp.pad(relation_accum[None], ((rows + 1, 0), (0, width - per_device)))
    )
    edges = (head_slots, tail_slots, relation_ids, own_negatives, far_negatives, relations)
    (outgoing,) = call(first_kernel, [chunks], request_rows, state, *edges)
    before = []
    for r in range(bit):
        received = swap_pair(outgoing, r)
        grads, grad_rel = call(
            functools.partial(edge_kernel, r, bit, per_device), [chunks, ((count, width), BF16)], received, *edges
        )
        before.append(grad_rel)
        back = swap_pair(grads, r)
        state, outgoing = call(
            functools.partial(middle_kernel, r), [(state.shape, F32), chunks], request_rows, back, state
        )
    received = swap_pair(outgoing, bit)
    masks = other_doms(bit)
    left, right, values, sums = call(
        functools.partial(edge_kernel, bit, bit, per_device),
        [
            ((2, touched, 2 * count), BF16),
            ((2, 2 * count, width), BF16),
            ((rounds * count, width), BF16),
            ((len(masks), touched, width), BF16),
        ],
        received,
        *edges,
        *before,
    )
    came = [lax.ppermute(sums[i], "dom", [(g, g ^ mask) for g in range(doms)]) for i, mask in enumerate(masks)]
    grads, sums, hot = call(
        functools.partial(grad_kernel, bit, per_device),
        [chunks, ((touched, width), F32), ((2 * touched, rows), BF16)],
        request_rows,
        relation_ids,
        left,
        right,
        values,
    )
    (grads,) = call(join_kernel, [((touched, wide(width)), BF16)], grads, sums, *came)
    back = swap_pair(grads, bit)
    outs = [((rows, width), F32), ((1, rows), F32), ((per_device, width), F32), ((1, per_device), F32)]
    table, accum, step, relation_accum = call(
        last_kernel,
        outs,
        hot,
        back,
        state,
        in_specs=[VMEM] * 3,
        out_specs=[HBM] * 4,
        scratch_shapes=[pltpu.VMEM(*out) for out in outs] + [pltpu.SemaphoreType.DMA((4,))],
    )
    return (table, accum.reshape(rows), step, relation_accum.reshape(per_device))


def solution(mesh):
    placed = (
        P(("dom", "shard"), None),
        P(("dom", "shard")),
        P(),
        P(("dom", "shard")),
        P(None, ("dom", "shard"), None, None),
        P(None, ("dom", "shard")),
        P(None, ("dom", "shard")),
        P(None, ("dom", "shard")),
        P(None, ("dom", "shard")),
        P(None, ("dom", "shard")),
    )
    return jax.shard_map(
        body,
        mesh=mesh,
        in_specs=placed,
        out_specs=(
            P(("dom", "shard"), None),
            P(("dom", "shard")),
            P(("dom", "shard"), None),
            P(("dom", "shard")),
        ),
        check_vma=False,
    )
```

```python
import functools

import jax
import jax.numpy as jnp
from jax import lax
from jax.experimental import pallas as pl
from jax.experimental.pallas import tpu as pltpu
from jax.sharding import PartitionSpec as P

LEARN_RATE = 0.1
LANES = 128
VMEM_LIMIT = 48 * 2**20
BF16 = jnp.bfloat16
F32 = jnp.float32
NATURAL = (((1,), (0,)), ((), ()))
LAST = (((1,), (1,)), ((), ()))
FIRST = (((0,), (0,)), ((), ()))
HBM = pl.BlockSpec(memory_space=pltpu.HBM)
VMEM = pl.BlockSpec(memory_space=pltpu.VMEM)


def dot(left, right, dims=NATURAL):
    return lax.dot_general(left, right, dims, preferred_element_type=F32)


def iota(shape, axis):
    return lax.broadcasted_iota(jnp.int32, shape, axis)


def one_hot_t(row, count):
    return (iota((count, row.shape[1]), 0) == row).astype(BF16)


def one_hot(column, count):
    return (iota((column.shape[0], count), 1) == column).astype(BF16)


def to_column(row):
    n = row.shape[1]
    return jnp.sum(jnp.where(iota((n, n), 0) == iota((n, n), 1), row, 0), axis=1, keepdims=True)


def to_row(column):
    n = column.shape[0]
    return jnp.sum(jnp.where(iota((n, n), 0) == iota((n, n), 1), column, 0), axis=0, keepdims=True)


def reverse(index, count):
    bits = count.bit_length() - 1
    return sum((index >> b & 1) << (bits - 1 - b) for b in range(bits))


def spread_order(shards):
    return [reverse(s, shards) for s in range(shards)]


def group_bit(r):
    return (lax.axis_index("dom") >> r) & 1


def renumber(slot, shards, slots):
    half = slots // 2
    return (slot // half % 2) * (shards * half) + reverse(slot // slots, shards) * half + slot % half


def halves(ref, r):
    rows, bit = ref.shape[0] // 2, group_bit(r)
    return [pl.ds(pl.multiple_of(side * rows, rows), rows) for side in (bit, 1 - bit)]


def whole(width):
    return width // LANES * LANES


def unfold(value, width):
    tiles, rest = whole(width), width - whole(width)
    return jnp.concatenate(
        [
            jnp.concatenate(
                [value[:, side * tiles : (side + 1) * tiles], value[:, 2 * tiles + side * rest :][:, :rest]], axis=1
            )
            for side in range(2)
        ],
        axis=0,
    )


def beside(left, right):
    tiles = whole(left.shape[1])
    return jnp.concatenate([left[:, :tiles], right[:, :tiles], left[:, tiles:], right[:, tiles:]], axis=1)


def fold(value):
    n = value.shape[0] // 2
    return beside(value[:n], value[n:])


def request_columns(request_ref, r):
    _, shards, _, slots = request_ref.shape
    half = slots // 2
    sides = [request_ref[r, :, k, :] for k in range(2)]
    flip = group_bit(r) == 1
    rep = jnp.concatenate(
        [
            jnp.broadcast_to(ids[reverse(place, shards)][None], (half, slots))
            for ids in (jnp.where(flip, sides[1], sides[0]), jnp.where(flip, sides[0], sides[1]))
            for place in range(shards)
        ],
        axis=0,
    )
    n = rep.shape[0]
    lane, inside = iota((n, slots), 1), iota((n, slots), 0) % half
    return [
        jnp.sum(jnp.where(lane == side * half + inside, rep, 0), axis=1, keepdims=True) for side in range(2)
    ]


def serve(request_ref, r, table, out_ref):
    rows, width = table.shape
    table = table.astype(BF16)
    hot = jnp.concatenate([one_hot(column, rows) for column in request_columns(request_ref, r)], axis=1)
    blank = jnp.zeros((rows, width), BF16)
    both = jnp.concatenate([beside(table, blank), beside(blank, table)], axis=0)
    out_ref[...] = dot(hot, both).astype(BF16)


def first_kernel(request_ref, state_ref, *refs):
    out_ref = refs[-1]
    table = state_ref[: state_ref.shape[0] - 2]
    serve(request_ref, 0, table, out_ref)


def request_hot(request_ref, r, rows):
    return jnp.concatenate([one_hot(column, rows) for column in request_columns(request_ref, r)], axis=0)


def row_update(hot, back_ref, state_ref):
    rows, width = state_ref.shape[0] - 2, state_ref.shape[1]
    row_grad = dot(hot, unfold(back_ref[:, : 2 * width], width), FIRST)
    accum = to_column(state_ref[rows : rows + 1, :rows]) + jnp.mean(row_grad * row_grad, axis=1, keepdims=True)
    return state_ref[:rows] - row_grad * (LEARN_RATE / jnp.sqrt(accum)), to_row(accum)


def middle_kernel(r, request_ref, back_ref, state_ref, state_out, out_ref):
    rows = state_ref.shape[0] - 2
    table, accum = row_update(request_hot(request_ref, r, rows), back_ref, state_ref)
    serve(request_ref, r + 1, table, out_ref)
    state_out[:rows] = table
    state_out[rows:] = state_ref[rows:]
    state_out[rows : rows + 1, :rows] = accum


def slots_of(ref):
    return 2 * ref.shape[0] // (2 * lax.axis_size("shard"))


def by_blocks(function, *arrays):
    step = 16
    parts = [function(*[x[i : i + step] for x in arrays]) for i in range(0, arrays[0].shape[0], step)]
    return [jnp.concatenate(column, axis=0) for column in zip(*parts)]


def query_block(head, tail, rel):
    tail_query = head * rel
    positive = jnp.sum(tail_query * tail, axis=1, keepdims=True)
    return tail_query.astype(BF16), (tail * rel).astype(BF16), -jax.nn.sigmoid(-positive)


def grad_block(head, tail, rel, coeff, back_tail, back_head):
    toward_head = coeff * tail + back_tail
    grad_rel = head * toward_head + tail * back_head
    return (
        (rel * toward_head).astype(BF16),
        (rel * (coeff * head + back_head)).astype(BF16),
        grad_rel.astype(BF16),
    )


def edge_kernel(
    r,
    bit,
    per_device,
    rec_ref,
    head_ref,
    tail_ref,
    rel_ref,
    own_neg_ref,
    far_neg_ref,
    relations_ref,
    *refs,
):
    width = relations_ref.shape[1]
    shards, slots = lax.axis_size("shard"), slots_of(rec_ref)
    touched = shards * slots
    edges, negatives = head_ref.shape[1], own_neg_ref.shape[1]
    own_half, far_half = halves(rec_ref, r)
    own = unfold(rec_ref[own_half], width)
    far = unfold(rec_ref[far_half], width)
    row = slice(r, r + 1)
    ids = rel_ref[row]
    heads, tails = renumber(head_ref[row], shards, slots), renumber(tail_ref[row], shards, slots)
    head = dot(one_hot(to_column(heads), touched), own)
    tail = dot(one_hot(to_column(tails), touched), far)
    rel = dot(one_hot(to_column(ids), relations_ref.shape[0]), relations_ref[...])
    query_tail, query_head, coeff = by_blocks(query_block, head, tail, rel)

    def weights(query, rows, neg_ref):
        hit = iota((touched, negatives), 0) == renumber(neg_ref[row], shards, slots)
        scale = jnp.sum(jnp.where(hit, 1.0 / negatives, 0.0), axis=1, keepdims=True)
        return jax.nn.sigmoid(dot(query, rows, LAST)) * to_row(scale)

    weight_tail = weights(query_tail, far, far_neg_ref)
    weight_head = weights(query_head, own, own_neg_ref)
    back_tail = dot(weight_tail.astype(BF16), far)
    back_head = dot(weight_head.astype(BF16), own)
    grad_head, grad_tail, grad_rel = by_blocks(grad_block, head, tail, rel, coeff, back_tail, back_head)
    left = [
        jnp.concatenate([one_hot_t(slot, touched), weight.T.astype(BF16)], axis=1)
        for slot, weight in ((heads, weight_head), (tails, weight_tail))
    ]
    right = [
        jnp.concatenate([grad_head, query_head], axis=0),
        jnp.concatenate([grad_tail, query_tail], axis=0),
    ]
    *before_refs, out_ref, values_out = refs[: len(refs) - (r == bit)]
    for side, half in enumerate((own_half, far_half)):
        out_ref[half] = fold(dot(left[side], right[side]).astype(BF16))
    values = jnp.concatenate([ref[...] for ref in before_refs] + [grad_rel], axis=0)
    values_out[...] = values
    if r == bit:
        refs[-1][...] = relation_sums(rel_ref, values, per_device, slots // 2, 1).astype(BF16)


def device_bits():
    doms, shards = lax.axis_size("dom"), lax.axis_size("shard")
    return [shards << b for b in range(doms.bit_length() - 1)] + [1 << b for b in range(shards.bit_length() - 1)]


def relation_sums(rel_ref, values, per_device, rows, side):
    shards = lax.axis_size("shard")
    ids = jnp.concatenate([rel_ref[r : r + 1] for r in range(rel_ref.shape[0])], axis=1)
    away = ids // per_device ^ (lax.axis_index("dom") * shards + lax.axis_index("shard"))
    bits = device_bits()
    place = sum(jnp.where(away & bit != 0, 1 << (len(bits) - 1 - i), 0) for i, bit in enumerate(bits))
    half = 1 << (len(bits) - 1)
    spot = jnp.where(place // half == side, place % half * rows + ids % per_device, -1)
    return dot(one_hot_t(spot, half * rows), values)


def keep_kernel(per_device, rows, rel_ref, values_ref, sums_out):
    sums_out[...] = relation_sums(rel_ref, values_ref[...], per_device, rows, 0)


def hot_kernel(r, request_ref, hot_out):
    hot_out[...] = request_hot(request_ref, r, hot_out.shape[1])


def add_kernel(kept_ref, came_ref, kept_out, send_out):
    total = kept_ref[...] + came_ref[...].astype(F32)
    half = kept_out.shape[0]
    kept_out[...] = total[:half]
    send_out[...] = total[half:].astype(send_out.dtype)


def relation_kernel(kept_ref, came_ref, state_ref, step_out, accum_out):
    per_device, width = step_out.shape
    grad = (kept_ref[...] + came_ref[...].astype(F32))[:per_device]
    accum = to_column(state_ref[state_ref.shape[0] - 1 :, :per_device]) + jnp.mean(grad * grad, axis=1, keepdims=True)
    step_out[...] = grad * (-LEARN_RATE / jnp.sqrt(accum))
    accum_out[...] = to_row(accum)


def last_kernel(hot_ref, back_ref, state_ref, table_out, accum_out):
    table_out[...], accum_out[...] = row_update(hot_ref[...], back_ref, state_ref)


def call(kernel, outs, *args, **kwargs):
    return pl.pallas_call(
        kernel,
        out_shape=[jax.ShapeDtypeStruct(shape, kind) for shape, kind in outs],
        compiler_params=pltpu.CompilerParams(vmem_limit_bytes=VMEM_LIMIT),
        **kwargs,
    )(*args)


def swap_pair(value, r):
    doms, shards = lax.axis_size("dom"), lax.axis_size("shard")
    order = spread_order(shards)
    groups = [
        [g * shards + s for g in (low, low ^ (1 << r)) for s in sorted(range(shards), key=order.__getitem__)]
        for low in range(doms)
        if not low >> r & 1
    ]
    return lax.all_to_all(
        value, ("dom", "shard"), split_axis=0, concat_axis=0, axis_index_groups=groups, tiled=True
    )


def body(
    embeddings,
    row_accum,
    relations,
    relation_accum,
    request_rows,
    head_slots,
    tail_slots,
    relation_ids,
    own_negatives,
    far_negatives,
):
    rows, width = embeddings.shape
    doms, shards = lax.axis_size("dom"), lax.axis_size("shard")
    rounds, slots = request_rows.shape[0], request_rows.shape[-1]
    bit = rounds - 1
    per_device = relation_accum.shape[0]
    count, touched = head_slots.shape[1], shards * slots
    assert per_device <= slots // 2
    chunks = ((touched, 2 * width), BF16)
    half_sums = (doms * shards // 2 * (slots // 2), width)
    state = (
        jnp.pad(embeddings, ((0, 2), (0, 0)))
        + jnp.pad(row_accum[None], ((rows, 1), (0, width - rows)))
        + jnp.pad(relation_accum[None], ((rows + 1, 0), (0, width - per_device)))
    )
    edges = (head_slots, tail_slots, relation_ids, own_negatives, far_negatives, relations)
    (outgoing,) = call(first_kernel, [chunks], request_rows, state, *edges)
    before = []
    for r in range(rounds):
        received = swap_pair(outgoing, r)
        outs = [chunks, (((len(before) + 1) * count, width), BF16)]
        if r == bit:
            outs.append((half_sums, BF16))
        grads, values, *send = call(
            functools.partial(edge_kernel, r, bit, per_device), outs, received, *edges, *before
        )
        before = [values]
        back = swap_pair(grads, r)
        if r < bit:
            state, outgoing = call(
                functools.partial(middle_kernel, r), [(state.shape, F32), chunks], request_rows, back, state
            )
    (kept,) = call(
        functools.partial(keep_kernel, per_device, slots // 2), [(half_sums, F32)], relation_ids, values
    )
    (hot,) = call(functools.partial(hot_kernel, bit), [((2 * touched, rows), BF16)], request_rows)
    (send,) = send
    for flip in device_bits():
        came = lax.ppermute(send, ("dom", "shard"), [(i, i ^ flip) for i in range(doms * shards)])
        left = kept.shape[0] // 2
        if left >= slots // 2:
            kept, send = call(
                add_kernel, [((left, width), F32), ((left, width), BF16 if left > 32 else F32)], kept, came
            )
    step, relation_accum = call(
        relation_kernel, [((per_device, width), F32), ((1, per_device), F32)], kept, came, state
    )
    table, accum = call(last_kernel, [((rows, width), F32), ((1, rows), F32)], hot, back, state)
    return (table, accum.reshape(rows), step, relation_accum.reshape(per_device))


def solution(mesh):
    placed = (
        P(("dom", "shard"), None),
        P(("dom", "shard")),
        P(),
        P(("dom", "shard")),
        P(None, ("dom", "shard"), None, None),
        P(None, ("dom", "shard")),
        P(None, ("dom", "shard")),
        P(None, ("dom", "shard")),
        P(None, ("dom", "shard")),
        P(None, ("dom", "shard")),
    )
    return jax.shard_map(
        body,
        mesh=mesh,
        in_specs=placed,
        out_specs=(
            P(("dom", "shard"), None),
            P(("dom", "shard")),
            P(("dom", "shard"), None),
            P(("dom", "shard")),
        ),
        check_vma=False,
    )
```

```python
import functools

import jax
import jax.numpy as jnp
from jax import lax
from jax.experimental import pallas as pl
from jax.experimental.pallas import tpu as pltpu
from jax.sharding import PartitionSpec as P

LEARN_RATE = 0.1
LANES = 128
VMEM_LIMIT = 48 * 2**20
BF16 = jnp.bfloat16
F32 = jnp.float32
NATURAL = (((1,), (0,)), ((), ()))
LAST = (((1,), (1,)), ((), ()))
FIRST = (((0,), (0,)), ((), ()))
HBM = pl.BlockSpec(memory_space=pltpu.HBM)
VMEM = pl.BlockSpec(memory_space=pltpu.VMEM)


def dot(left, right, dims=NATURAL):
    return lax.dot_general(left, right, dims, preferred_element_type=F32)


def iota(shape, axis):
    return lax.broadcasted_iota(jnp.int32, shape, axis)


def one_hot_t(row, count):
    return (iota((count, row.shape[1]), 0) == row).astype(BF16)


def one_hot(column, count):
    return (iota((column.shape[0], count), 1) == column.astype(jnp.int32)).astype(BF16)


def to_column(row):
    n = row.shape[1]
    same = iota((n, n), 0) == iota((n, n), 1)
    return jnp.sum(jnp.where(same, row.astype(F32), 0.0), axis=1, keepdims=True)


def to_row(column):
    n = column.shape[0]
    return jnp.sum(jnp.where(iota((n, n), 0) == iota((n, n), 1), column, 0.0), axis=0, keepdims=True)


def reverse(index, count):
    bits = count.bit_length() - 1
    return sum((index >> b & 1) << (bits - 1 - b) for b in range(bits))


def spread_order(shards):
    return [reverse(s, shards) for s in range(shards)]


def group_bit(r):
    return (lax.axis_index("dom") >> r) & 1


def renumber(slot, shards, slots):
    half = slots // 2
    return (slot // half % 2) * (shards * half) + reverse(slot // slots, shards) * half + slot % half


def halves(ref, r):
    rows, bit = ref.shape[0] // 2, group_bit(r)
    return [pl.ds(pl.multiple_of(side * rows, rows), rows) for side in (bit, 1 - bit)]


def whole(width):
    return width // LANES * LANES


def unfold(value, width):
    tiles, rest = whole(width), width - whole(width)
    return jnp.concatenate(
        [
            jnp.concatenate(
                [value[:, side * tiles : (side + 1) * tiles], value[:, 2 * tiles + side * rest :][:, :rest]], axis=1
            )
            for side in range(2)
        ],
        axis=0,
    )


def beside(left, right):
    tiles = whole(left.shape[1])
    return jnp.concatenate([left[:, :tiles], right[:, :tiles], left[:, tiles:], right[:, tiles:]], axis=1)


def fold(value):
    n = value.shape[0] // 2
    return beside(value[:n], value[n:])


def request_columns(request_ref, r):
    _, shards, _, slots = request_ref.shape
    half = slots // 2
    sides = [request_ref[r, :, k, :].astype(F32) for k in range(2)]
    flip = group_bit(r) == 1
    rep = jnp.concatenate(
        [
            jnp.broadcast_to(ids[reverse(place, shards)][None], (half, slots))
            for ids in (jnp.where(flip, sides[1], sides[0]), jnp.where(flip, sides[0], sides[1]))
            for place in range(shards)
        ],
        axis=0,
    )
    n = rep.shape[0]
    lane, inside = iota((n, slots), 1), iota((n, slots), 0) % half
    return [
        jnp.sum(jnp.where(lane == side * half + inside, rep, 0.0), axis=1, keepdims=True) for side in range(2)
    ]


def serve(request_ref, r, table, out_ref):
    rows, width = table.shape
    table = table.astype(BF16)
    hot = jnp.concatenate([one_hot(column, rows) for column in request_columns(request_ref, r)], axis=1)
    blank = jnp.zeros((rows, width), BF16)
    both = jnp.concatenate([beside(table, blank), beside(blank, table)], axis=0)
    out_ref[...] = dot(hot, both).astype(BF16)


def first_kernel(request_ref, state_ref, *refs):
    out_ref = refs[-1]
    table = state_ref[: state_ref.shape[0] - 2]
    serve(request_ref, 0, table, out_ref)


def request_hot(request_ref, r, rows):
    return jnp.concatenate([one_hot(column, rows) for column in request_columns(request_ref, r)], axis=0)


def row_update(hot, back_ref, state_ref, dims=FIRST):
    rows, width = state_ref.shape[0] - 2, state_ref.shape[1]
    row_grad = dot(hot, unfold(back_ref[:, : 2 * width], width), dims)
    accum = to_column(state_ref[rows : rows + 1, :rows]) + jnp.mean(row_grad * row_grad, axis=1, keepdims=True)
    return state_ref[:rows] - row_grad * (LEARN_RATE * lax.rsqrt(accum)), to_row(accum)


def middle_kernel(r, request_ref, back_ref, state_ref, state_out, out_ref):
    rows = state_ref.shape[0] - 2
    table, accum = row_update(request_hot(request_ref, r, rows), back_ref, state_ref)
    serve(request_ref, r + 1, table, out_ref)
    state_out[:rows] = table
    state_out[rows:] = state_ref[rows:]
    state_out[rows : rows + 1, :rows] = accum


def slots_of(ref):
    return 2 * ref.shape[0] // (2 * lax.axis_size("shard"))


def by_blocks(function, *arrays):
    step = 16
    parts = [function(*[x[i : i + step] for x in arrays]) for i in range(0, arrays[0].shape[0], step)]
    return [jnp.concatenate(column, axis=0) for column in zip(*parts)]


def query_block(head, tail, rel):
    tail_query = head * rel
    positive = jnp.sum(tail_query * tail, axis=1, keepdims=True)
    return tail_query.astype(BF16), (tail * rel).astype(BF16), -jax.nn.sigmoid(-positive)


def grad_block(head, tail, rel, coeff, back_tail, back_head):
    toward_head = coeff * tail + back_tail
    grad_rel = head * toward_head + tail * back_head
    return (
        (rel * toward_head).astype(BF16),
        (rel * (coeff * head + back_head)).astype(BF16),
        grad_rel.astype(BF16),
    )


def edge_kernel(
    r,
    bit,
    per_device,
    rec_ref,
    head_ref,
    tail_ref,
    rel_ref,
    own_neg_ref,
    far_neg_ref,
    relations_ref,
    *refs,
):
    width = relations_ref.shape[1]
    shards, slots = lax.axis_size("shard"), slots_of(rec_ref)
    touched = shards * slots
    edges, negatives = head_ref.shape[1], own_neg_ref.shape[1]
    own_half, far_half = halves(rec_ref, r)
    own = unfold(rec_ref[own_half], width)
    far = unfold(rec_ref[far_half], width)
    row = slice(r, r + 1)
    ids = rel_ref[row]
    heads, tails = renumber(head_ref[row], shards, slots), renumber(tail_ref[row], shards, slots)
    head = dot(one_hot(to_column(heads), touched), own)
    tail = dot(one_hot(to_column(tails), touched), far)
    rel = dot(one_hot(to_column(ids), relations_ref.shape[0]), relations_ref[...])
    query_tail, query_head, coeff = by_blocks(query_block, head, tail, rel)

    def weights(query, rows, neg_ref):
        hit = iota((touched, negatives), 0) == renumber(neg_ref[row], shards, slots)
        scale = jnp.sum(jnp.where(hit, 1.0 / negatives, 0.0), axis=1, keepdims=True)
        return jax.nn.sigmoid(dot(query, rows, LAST)) * to_row(scale)

    weight_tail = weights(query_tail, far, far_neg_ref)
    weight_head = weights(query_head, own, own_neg_ref)
    back_tail = dot(weight_tail.astype(BF16), far)
    back_head = dot(weight_head.astype(BF16), own)
    grad_head, grad_tail, grad_rel = by_blocks(grad_block, head, tail, rel, coeff, back_tail, back_head)
    right = [
        jnp.concatenate([grad_head, query_head], axis=0),
        jnp.concatenate([grad_tail, query_tail], axis=0),
    ]
    if r < bit:
        out_ref, grad_rel_out = refs
        sides = (own_half, heads, weight_head), (far_half, tails, weight_tail)
        for (half, slot, weight), grads in zip(sides, right):
            out_ref[half] = row_grads(slot, weight, grads)
        grad_rel_out[...] = grad_rel
    else:
        *before_refs, weights_out, right_out, values_out, sums_out = refs
        for side, weight in enumerate((weight_head, weight_tail)):
            weights_out[side], right_out[side] = weight.astype(BF16), right[side]
        values = jnp.concatenate([ref[...] for ref in before_refs] + [grad_rel], axis=0)
        values_out[...] = values
        masks = other_doms(bit)
        for i, mask in enumerate(masks):
            sums_out[i] = relation_sums(rel_ref, values, bit, per_device, mask, rec_ref.shape[0]).astype(BF16)


def other_doms(bit):
    return [mask for mask in range(1, lax.axis_size("dom")) if not mask >> bit & 1]


def relation_sums(rel_ref, values, bit, per_device, mask, rows):
    shards = lax.axis_size("shard")
    ids = jnp.concatenate([rel_ref[r : r + 1] for r in range(rel_ref.shape[0])], axis=1)
    owner = ids // per_device
    dom = owner // shards
    chunk = (dom >> bit & 1) * shards + reverse(owner % shards, shards)
    meant = (dom ^ lax.axis_index("dom") ^ mask) & ~(1 << bit) == 0
    place = jnp.where(meant, chunk * (rows // (2 * shards)) + ids % per_device, -1)
    return dot(one_hot_t(place, rows), values)


def row_grads(slot, weight, grads):
    left = jnp.concatenate([one_hot_t(slot, weight.shape[1]), weight.T.astype(BF16)], axis=1)
    return fold(dot(left, grads).astype(BF16))


def grad_kernel(
    bit,
    per_device,
    request_ref,
    head_ref,
    tail_ref,
    rel_ref,
    weights_ref,
    right_ref,
    values_ref,
    out_ref,
    sums_out,
    hot_out,
):
    shards, slots = lax.axis_size("shard"), slots_of(out_ref)
    for side, (half, slot_ref) in enumerate(zip(halves(out_ref, bit), (head_ref, tail_ref))):
        slot = renumber(slot_ref[bit : bit + 1], shards, slots)
        out_ref[half] = row_grads(slot, weights_ref[side].astype(F32), right_ref[side])
    sums_out[...] = relation_sums(rel_ref, values_ref[...], bit, per_device, 0, out_ref.shape[0])
    hot_out[...] = request_hot(request_ref, bit, hot_out.shape[0]).astype(F32).T.astype(BF16)


def wide(width):
    return 3 * whole(width) + LANES


def join_kernel(grads_ref, sums_ref, *refs):
    *came_refs, out_ref = refs
    width = sums_ref.shape[1]
    tiles, rest = whole(width), width - whole(width)
    total = sums_ref[...]
    for ref in came_refs:
        total = total + ref[...].astype(F32)
    total = total.astype(BF16)
    out_ref[:, : 2 * tiles] = grads_ref[:, : 2 * tiles]
    blank = jnp.zeros((total.shape[0], LANES - 3 * rest), BF16)
    out_ref[:, 2 * tiles : 2 * tiles + LANES] = jnp.concatenate(
        [grads_ref[:, 2 * tiles :], total[:, tiles:], blank], axis=1
    )
    out_ref[:, 2 * tiles + LANES :] = total[:, :tiles]


def last_kernel(hot_ref, back_ref, state_ref, table_out, row_accum_out, step_out, accum_out, *scratch):
    table_ref, row_accum_ref, step_ref, new_accum_ref, sems = scratch
    pairs = (
        (table_ref, table_out),
        (row_accum_ref, row_accum_out),
        (step_ref, step_out),
        (new_accum_ref, accum_out),
    )
    copies = [pltpu.make_async_copy(source, target, sems.at[i]) for i, (source, target) in enumerate(pairs)]
    table, accum = row_update(hot_ref[...], back_ref, state_ref, NATURAL)
    table_ref[...] = table
    copies[0].start()
    row_accum_ref[...] = accum
    copies[1].start()
    per_device, width = step_ref.shape
    rows = slots_of(back_ref) // 2
    tiles, rest = whole(width), width - whole(width)
    parts = jnp.concatenate(
        [back_ref[:, 2 * tiles + LANES :], back_ref[:, 2 * tiles + 2 * rest : 2 * tiles + 3 * rest]], axis=1
    ).astype(F32)
    grad = jnp.sum(parts.reshape(parts.shape[0] // rows, rows, width), axis=0)[:per_device]
    accum = to_column(state_ref[table.shape[0] + 1 :, :per_device]) + jnp.mean(grad * grad, axis=1, keepdims=True)
    step_ref[...] = grad * (-LEARN_RATE * lax.rsqrt(accum))
    copies[2].start()
    new_accum_ref[...] = to_row(accum)
    copies[3].start()
    for copy in copies:
        copy.wait()


def call(kernel, outs, *args, **kwargs):
    return pl.pallas_call(
        kernel,
        out_shape=[jax.ShapeDtypeStruct(shape, kind) for shape, kind in outs],
        compiler_params=pltpu.CompilerParams(vmem_limit_bytes=VMEM_LIMIT),
        **kwargs,
    )(*args)


def swap_pair(value, r):
    doms, shards = lax.axis_size("dom"), lax.axis_size("shard")
    order = spread_order(shards)
    groups = [
        [g * shards + s for g in (low, low ^ (1 << r)) for s in sorted(range(shards), key=order.__getitem__)]
        for low in range(doms)
        if not low >> r & 1
    ]
    return lax.all_to_all(
        value, ("dom", "shard"), split_axis=0, concat_axis=0, axis_index_groups=groups, tiled=True
    )


def body(
    embeddings,
    row_accum,
    relations,
    relation_accum,
    request_rows,
    head_slots,
    tail_slots,
    relation_ids,
    own_negatives,
    far_negatives,
):
    rows, width = embeddings.shape
    doms, shards = lax.axis_size("dom"), lax.axis_size("shard")
    rounds, slots = request_rows.shape[0], request_rows.shape[-1]
    bit = rounds - 1
    per_device = relation_accum.shape[0]
    assert 3 * (width % LANES) <= LANES
    count, touched = head_slots.shape[1], shards * slots
    assert per_device <= slots // 2
    chunks = ((touched, 2 * width), BF16)
    state = (
        jnp.pad(embeddings, ((0, 2), (0, 0)))
        + jnp.pad(row_accum[None], ((rows, 1), (0, width - rows)))
        + jnp.pad(relation_accum[None], ((rows + 1, 0), (0, width - per_device)))
    )
    edges = (head_slots, tail_slots, relation_ids, own_negatives, far_negatives, relations)
    (outgoing,) = call(first_kernel, [chunks], request_rows, state, *edges)
    before = []
    for r in range(bit):
        received = swap_pair(outgoing, r)
        grads, grad_rel = call(
            functools.partial(edge_kernel, r, bit, per_device), [chunks, ((count, width), BF16)], received, *edges
        )
        before.append(grad_rel)
        back = swap_pair(grads, r)
        state, outgoing = call(
            functools.partial(middle_kernel, r), [(state.shape, F32), chunks], request_rows, back, state
        )
    received = swap_pair(outgoing, bit)
    masks = other_doms(bit)
    weights, right, values, sums = call(
        functools.partial(edge_kernel, bit, bit, per_device),
        [
            ((2, count, touched), BF16),
            ((2, 2 * count, width), BF16),
            ((rounds * count, width), BF16),
            ((len(masks), touched, width), BF16),
        ],
        received,
        *edges,
        *before,
    )
    came = [lax.ppermute(sums[i], "dom", [(g, g ^ mask) for g in range(doms)]) for i, mask in enumerate(masks)]
    grads, sums, hot = call(
        functools.partial(grad_kernel, bit, per_device),
        [chunks, ((touched, width), F32), ((rows, 2 * touched), BF16)],
        request_rows,
        head_slots,
        tail_slots,
        relation_ids,
        weights,
        right,
        values,
    )
    (grads,) = call(join_kernel, [((touched, wide(width)), BF16)], grads, sums, *came)
    back = swap_pair(grads, bit)
    outs = [((rows, width), F32), ((1, rows), F32), ((per_device, width), F32), ((1, per_device), F32)]
    table, accum, step, relation_accum = call(
        last_kernel,
        outs,
        hot,
        back,
        state,
        in_specs=[VMEM] * 3,
        out_specs=[HBM] * 4,
        scratch_shapes=[pltpu.VMEM(*out) for out in outs] + [pltpu.SemaphoreType.DMA((4,))],
    )
    return (table, accum.reshape(rows), step, relation_accum.reshape(per_device))


def solution(mesh):
    placed = (
        P(("dom", "shard"), None),
        P(("dom", "shard")),
        P(),
        P(("dom", "shard")),
        P(None, ("dom", "shard"), None, None),
        P(None, ("dom", "shard")),
        P(None, ("dom", "shard")),
        P(None, ("dom", "shard")),
        P(None, ("dom", "shard")),
        P(None, ("dom", "shard")),
    )
    return jax.shard_map(
        body,
        mesh=mesh,
        in_specs=placed,
        out_specs=(
            P(("dom", "shard"), None),
            P(("dom", "shard")),
            P(("dom", "shard"), None),
            P(("dom", "shard")),
        ),
        check_vma=False,
    )
```

```python
import functools

import jax
import jax.numpy as jnp
from jax import lax
from jax.experimental import pallas as pl
from jax.experimental.pallas import tpu as pltpu
from jax.sharding import PartitionSpec as P

LEARN_RATE = 0.1
LANES = 128
VMEM_LIMIT = 48 * 2**20
BF16 = jnp.bfloat16
F32 = jnp.float32
NATURAL = (((1,), (0,)), ((), ()))
LAST = (((1,), (1,)), ((), ()))
FIRST = (((0,), (0,)), ((), ()))
HBM = pl.BlockSpec(memory_space=pltpu.HBM)
VMEM = pl.BlockSpec(memory_space=pltpu.VMEM)


def dot(left, right, dims=NATURAL):
    return lax.dot_general(left, right, dims, preferred_element_type=F32)


def iota(shape, axis):
    return lax.broadcasted_iota(jnp.int32, shape, axis)


def one_hot_t(row, count):
    return (iota((count, row.shape[1]), 0) == row).astype(BF16)


def one_hot(column, count):
    return (iota((column.shape[0], count), 1) == column.astype(jnp.int32)).astype(BF16)


def to_column(row):
    n = row.shape[1]
    same = iota((n, n), 0) == iota((n, n), 1)
    return jnp.sum(jnp.where(same, row.astype(F32), 0.0), axis=1, keepdims=True)


def to_row(column):
    n = column.shape[0]
    return jnp.sum(jnp.where(iota((n, n), 0) == iota((n, n), 1), column, 0.0), axis=0, keepdims=True)


def reverse(index, count):
    bits = count.bit_length() - 1
    return (count - 1) ^ sum((index >> b & 1) << (bits - 1 - b) for b in range(bits))


def spread_order(shards):
    return [reverse(s, shards) for s in range(shards)]


def group_bit(r):
    return 1 - ((lax.axis_index("dom") >> r) & 1)


def renumber(slot, shards, slots):
    half = slots // 2
    return (slot // half % 2) * (shards * half) + reverse(slot // slots, shards) * half + slot % half


def halves(ref, r):
    rows, bit = ref.shape[0] // 2, group_bit(r)
    return [pl.ds(pl.multiple_of(side * rows, rows), rows) for side in (bit, 1 - bit)]


def whole(width):
    return width // LANES * LANES


def unfold(value, width):
    tiles, rest = whole(width), width - whole(width)
    return jnp.concatenate(
        [
            jnp.concatenate(
                [value[:, side * tiles : (side + 1) * tiles], value[:, 2 * tiles + side * rest :][:, :rest]], axis=1
            )
            for side in range(2)
        ],
        axis=0,
    )


def beside(left, right):
    tiles = whole(left.shape[1])
    return jnp.concatenate([left[:, :tiles], right[:, :tiles], left[:, tiles:], right[:, tiles:]], axis=1)


def fold(value):
    n = value.shape[0] // 2
    return beside(value[:n], value[n:])


def request_columns(request_ref, r):
    _, shards, _, slots = request_ref.shape
    half = slots // 2
    sides = [request_ref[r, :, k, :].astype(F32) for k in range(2)]
    flip = group_bit(r) == 1
    rep = jnp.concatenate(
        [
            jnp.broadcast_to(ids[reverse(place, shards)][None], (half, slots))
            for ids in (jnp.where(flip, sides[1], sides[0]), jnp.where(flip, sides[0], sides[1]))
            for place in range(shards)
        ],
        axis=0,
    )
    n = rep.shape[0]
    lane, inside = iota((n, slots), 1), iota((n, slots), 0) % half
    return [
        jnp.sum(jnp.where(lane == side * half + inside, rep, 0.0), axis=1, keepdims=True) for side in range(2)
    ]


def serve(request_ref, r, table, out_ref):
    rows, width = table.shape
    table = table.astype(BF16)
    hot = jnp.concatenate([one_hot(column, rows) for column in request_columns(request_ref, r)], axis=1)
    blank = jnp.zeros((rows, width), BF16)
    both = jnp.concatenate([beside(table, blank), beside(blank, table)], axis=0)
    out_ref[...] = dot(hot, both).astype(BF16)


def first_kernel(request_ref, state_ref, *refs):
    out_ref = refs[-1]
    table = state_ref[: state_ref.shape[0] - 2]
    serve(request_ref, 0, table, out_ref)


def request_hot(request_ref, r, rows):
    return jnp.concatenate([one_hot(column, rows) for column in request_columns(request_ref, r)], axis=0)


def row_update(hot, back_ref, state_ref, dims=FIRST):
    rows, width = state_ref.shape[0] - 2, state_ref.shape[1]
    row_grad = dot(hot, unfold(back_ref[:, : 2 * width], width), dims)
    accum = to_column(state_ref[rows : rows + 1, :rows]) + jnp.mean(row_grad * row_grad, axis=1, keepdims=True)
    return state_ref[:rows] - row_grad * (LEARN_RATE * lax.rsqrt(accum)), to_row(accum)


def middle_kernel(r, request_ref, back_ref, state_ref, state_out, out_ref):
    rows = state_ref.shape[0] - 2
    table, accum = row_update(request_hot(request_ref, r, rows), back_ref, state_ref)
    serve(request_ref, r + 1, table, out_ref)
    state_out[:rows] = table
    state_out[rows:] = state_ref[rows:]
    state_out[rows : rows + 1, :rows] = accum


def slots_of(ref):
    return 2 * ref.shape[0] // (2 * lax.axis_size("shard"))


def by_blocks(function, *arrays):
    step = 16
    parts = [function(*[x[i : i + step] for x in arrays]) for i in range(0, arrays[0].shape[0], step)]
    return [jnp.concatenate(column, axis=0) for column in zip(*parts)]


def query_block(head, tail, rel):
    tail_query = head * rel
    positive = jnp.sum(tail_query * tail, axis=1, keepdims=True)
    return tail_query.astype(BF16), (tail * rel).astype(BF16), -jax.nn.sigmoid(-positive)


def grad_block(head, tail, rel, coeff, back_tail, back_head):
    toward_head = coeff * tail + back_tail
    grad_rel = head * toward_head + tail * back_head
    return (
        (rel * toward_head).astype(BF16),
        (rel * (coeff * head + back_head)).astype(BF16),
        grad_rel.astype(BF16),
    )


def edge_kernel(
    r,
    bit,
    per_device,
    rec_ref,
    head_ref,
    tail_ref,
    rel_ref,
    own_neg_ref,
    far_neg_ref,
    relations_ref,
    *refs,
):
    width = relations_ref.shape[1]
    shards, slots = lax.axis_size("shard"), slots_of(rec_ref)
    touched = shards * slots
    edges, negatives = head_ref.shape[1], own_neg_ref.shape[1]
    own_half, far_half = halves(rec_ref, r)
    own = unfold(rec_ref[own_half], width)
    far = unfold(rec_ref[far_half], width)
    row = slice(r, r + 1)
    ids = rel_ref[row]
    heads, tails = renumber(head_ref[row], shards, slots), renumber(tail_ref[row], shards, slots)
    head = dot(one_hot(to_column(heads), touched), own)
    tail = dot(one_hot(to_column(tails), touched), far)
    rel = dot(one_hot(to_column(ids), relations_ref.shape[0]), relations_ref[...])
    query_tail, query_head, coeff = by_blocks(query_block, head, tail, rel)

    def weights(query, rows, neg_ref):
        hit = iota((touched, negatives), 0) == renumber(neg_ref[row], shards, slots)
        scale = jnp.sum(jnp.where(hit, 1.0 / negatives, 0.0), axis=1, keepdims=True)
        return jax.nn.sigmoid(dot(query, rows, LAST)) * to_row(scale)

    weight_tail = weights(query_tail, far, far_neg_ref)
    weight_head = weights(query_head, own, own_neg_ref)
    back_tail = dot(weight_tail.astype(BF16), far)
    back_head = dot(weight_head.astype(BF16), own)
    grad_head, grad_tail, grad_rel = by_blocks(grad_block, head, tail, rel, coeff, back_tail, back_head)
    right = [
        jnp.concatenate([grad_head, query_head], axis=0),
        jnp.concatenate([grad_tail, query_tail], axis=0),
    ]
    if r < bit:
        out_ref, grad_rel_out = refs
        sides = (own_half, heads, weight_head), (far_half, tails, weight_tail)
        for (half, slot, weight), grads in zip(sides, right):
            out_ref[half] = row_grads(slot, weight, grads)
        grad_rel_out[...] = grad_rel
    else:
        *before_refs, weights_out, right_out, values_out, sums_out = refs
        for side, weight in enumerate((weight_head, weight_tail)):
            weights_out[side], right_out[side] = weight.astype(BF16), right[side]
        values = jnp.concatenate([ref[...] for ref in before_refs] + [grad_rel], axis=0)
        values_out[...] = values
        masks = other_doms(bit)
        for i, mask in enumerate(masks):
            sums_out[i] = relation_sums(rel_ref, values, bit, per_device, mask, rec_ref.shape[0]).astype(BF16)


def other_doms(bit):
    return [mask for mask in range(1, lax.axis_size("dom")) if not mask >> bit & 1]


def relation_sums(rel_ref, values, bit, per_device, mask, rows):
    shards = lax.axis_size("shard")
    ids = jnp.concatenate([rel_ref[r : r + 1] for r in range(rel_ref.shape[0])], axis=1)
    owner = ids // per_device
    dom = owner // shards
    chunk = (1 - (dom >> bit & 1)) * shards + reverse(owner % shards, shards)
    meant = (dom ^ lax.axis_index("dom") ^ mask) & ~(1 << bit) == 0
    place = jnp.where(meant, chunk * (rows // (2 * shards)) + ids % per_device, -1)
    return dot(one_hot_t(place, rows), values)


def row_grads(slot, weight, grads):
    left = jnp.concatenate([one_hot_t(slot, weight.shape[1]), weight.T.astype(BF16)], axis=1)
    return fold(dot(left, grads).astype(BF16))


def grad_kernel(
    bit,
    per_device,
    request_ref,
    head_ref,
    tail_ref,
    rel_ref,
    weights_ref,
    right_ref,
    values_ref,
    out_ref,
    sums_out,
    hot_out,
):
    shards, slots = lax.axis_size("shard"), slots_of(out_ref)
    for side, (half, slot_ref) in enumerate(zip(halves(out_ref, bit), (head_ref, tail_ref))):
        slot = renumber(slot_ref[bit : bit + 1], shards, slots)
        out_ref[half] = row_grads(slot, weights_ref[side].astype(F32), right_ref[side])
    sums_out[...] = relation_sums(rel_ref, values_ref[...], bit, per_device, 0, out_ref.shape[0])
    hot_out[...] = request_hot(request_ref, bit, hot_out.shape[0]).astype(F32).T.astype(BF16)


def wide(width):
    return 3 * whole(width) + LANES


def join_kernel(grads_ref, sums_ref, *refs):
    *came_refs, out_ref = refs
    width = sums_ref.shape[1]
    tiles, rest = whole(width), width - whole(width)
    total = sums_ref[...]
    for ref in came_refs:
        total = total + ref[...].astype(F32)
    total = total.astype(BF16)
    out_ref[:, : 2 * tiles] = grads_ref[:, : 2 * tiles]
    blank = jnp.zeros((total.shape[0], LANES - 3 * rest), BF16)
    out_ref[:, 2 * tiles : 2 * tiles + LANES] = jnp.concatenate(
        [grads_ref[:, 2 * tiles :], total[:, tiles:], blank], axis=1
    )
    out_ref[:, 2 * tiles + LANES :] = total[:, :tiles]


def last_kernel(hot_ref, back_ref, state_ref, table_out, row_accum_out, step_out, accum_out, *scratch):
    table_ref, row_accum_ref, step_ref, new_accum_ref, sems = scratch
    pairs = (
        (table_ref, table_out),
        (row_accum_ref, row_accum_out),
        (step_ref, step_out),
        (new_accum_ref, accum_out),
    )
    copies = [pltpu.make_async_copy(source, target, sems.at[i]) for i, (source, target) in enumerate(pairs)]
    table, accum = row_update(hot_ref[...], back_ref, state_ref, NATURAL)
    table_ref[...] = table
    copies[0].start()
    row_accum_ref[...] = accum
    copies[1].start()
    per_device, width = step_ref.shape
    rows = slots_of(back_ref) // 2
    tiles, rest = whole(width), width - whole(width)
    parts = jnp.concatenate(
        [back_ref[:, 2 * tiles + LANES :], back_ref[:, 2 * tiles + 2 * rest : 2 * tiles + 3 * rest]], axis=1
    ).astype(F32)
    grad = jnp.sum(parts.reshape(parts.shape[0] // rows, rows, width), axis=0)[:per_device]
    accum = to_column(state_ref[table.shape[0] + 1 :, :per_device]) + jnp.mean(grad * grad, axis=1, keepdims=True)
    step_ref[...] = grad * (-LEARN_RATE * lax.rsqrt(accum))
    copies[2].start()
    new_accum_ref[...] = to_row(accum)
    copies[3].start()
    for copy in copies:
        copy.wait()


def call(kernel, outs, *args, **kwargs):
    return pl.pallas_call(
        kernel,
        out_shape=[jax.ShapeDtypeStruct(shape, kind) for shape, kind in outs],
        compiler_params=pltpu.CompilerParams(vmem_limit_bytes=VMEM_LIMIT),
        **kwargs,
    )(*args)


def swap_pair(value, r):
    doms, shards = lax.axis_size("dom"), lax.axis_size("shard")
    order = spread_order(shards)
    groups = [
        [g * shards + s for g in (low ^ (1 << r), low) for s in sorted(range(shards), key=order.__getitem__)]
        for low in range(doms)
        if not low >> r & 1
    ]
    return lax.all_to_all(
        value, ("dom", "shard"), split_axis=0, concat_axis=0, axis_index_groups=groups, tiled=True
    )


def body(
    embeddings,
    row_accum,
    relations,
    relation_accum,
    request_rows,
    head_slots,
    tail_slots,
    relation_ids,
    own_negatives,
    far_negatives,
):
    rows, width = embeddings.shape
    doms, shards = lax.axis_size("dom"), lax.axis_size("shard")
    rounds, slots = request_rows.shape[0], request_rows.shape[-1]
    bit = rounds - 1
    per_device = relation_accum.shape[0]
    assert 3 * (width % LANES) <= LANES
    count, touched = head_slots.shape[1], shards * slots
    assert per_device <= slots // 2
    chunks = ((touched, 2 * width), BF16)
    state = (
        jnp.pad(embeddings, ((0, 2), (0, 0)))
        + jnp.pad(row_accum[None], ((rows, 1), (0, width - rows)))
        + jnp.pad(relation_accum[None], ((rows + 1, 0), (0, width - per_device)))
    )
    edges = (head_slots, tail_slots, relation_ids, own_negatives, far_negatives, relations)
    (outgoing,) = call(first_kernel, [chunks], request_rows, state, *edges)
    before = []
    for r in range(bit):
        received = swap_pair(outgoing, r)
        grads, grad_rel = call(
            functools.partial(edge_kernel, r, bit, per_device), [chunks, ((count, width), BF16)], received, *edges
        )
        before.append(grad_rel)
        back = swap_pair(grads, r)
        state, outgoing = call(
            functools.partial(middle_kernel, r), [(state.shape, F32), chunks], request_rows, back, state
        )
    received = swap_pair(outgoing, bit)
    masks = other_doms(bit)
    weights, right, values, sums = call(
        functools.partial(edge_kernel, bit, bit, per_device),
        [
            ((2, count, touched), BF16),
            ((2, 2 * count, width), BF16),
            ((rounds * count, width), BF16),
            ((len(masks), touched, width), BF16),
        ],
        received,
        *edges,
        *before,
    )
    came = [lax.ppermute(sums[i], "dom", [(g, g ^ mask) for g in range(doms)]) for i, mask in enumerate(masks)]
    grads, sums, hot = call(
        functools.partial(grad_kernel, bit, per_device),
        [chunks, ((touched, width), F32), ((rows, 2 * touched), BF16)],
        request_rows,
        head_slots,
        tail_slots,
        relation_ids,
        weights,
        right,
        values,
    )
    (grads,) = call(join_kernel, [((touched, wide(width)), BF16)], grads, sums, *came)
    back = swap_pair(grads, bit)
    outs = [((rows, width), F32), ((1, rows), F32), ((per_device, width), F32), ((1, per_device), F32)]
    table, accum, step, relation_accum = call(
        last_kernel,
        outs,
        hot,
        back,
        state,
        in_specs=[VMEM] * 3,
        out_specs=[HBM] * 4,
        scratch_shapes=[pltpu.VMEM(*out) for out in outs] + [pltpu.SemaphoreType.DMA((4,))],
    )
    return (table, accum.reshape(rows), step, relation_accum.reshape(per_device))


def solution(mesh):
    placed = (
        P(("dom", "shard"), None),
        P(("dom", "shard")),
        P(),
        P(("dom", "shard")),
        P(None, ("dom", "shard"), None, None),
        P(None, ("dom", "shard")),
        P(None, ("dom", "shard")),
        P(None, ("dom", "shard")),
        P(None, ("dom", "shard")),
        P(None, ("dom", "shard")),
    )
    return jax.shard_map(
        body,
        mesh=mesh,
        in_specs=placed,
        out_specs=(
            P(("dom", "shard"), None),
            P(("dom", "shard")),
            P(("dom", "shard"), None),
            P(("dom", "shard")),
        ),
        check_vma=False,
    )
```

```python
import functools

import jax
import jax.numpy as jnp
from jax import lax
from jax.experimental import pallas as pl
from jax.experimental.pallas import tpu as pltpu
from jax.sharding import PartitionSpec as P

LEARN_RATE = 0.1
LANES = 128
VMEM_LIMIT = 48 * 2**20
BF16 = jnp.bfloat16
F32 = jnp.float32
NATURAL = (((1,), (0,)), ((), ()))
LAST = (((1,), (1,)), ((), ()))
FIRST = (((0,), (0,)), ((), ()))
HBM = pl.BlockSpec(memory_space=pltpu.HBM)
VMEM = pl.BlockSpec(memory_space=pltpu.VMEM)


def dot(left, right, dims=NATURAL):
    return lax.dot_general(left, right, dims, preferred_element_type=F32)


def iota(shape, axis):
    return lax.broadcasted_iota(jnp.int32, shape, axis)


def one_hot_t(row, count):
    return (iota((count, row.shape[1]), 0) == row).astype(BF16)


def one_hot(column, count):
    return (iota((column.shape[0], count), 1) == column.astype(jnp.int32)).astype(BF16)


def to_column(row):
    n = row.shape[1]
    same = iota((n, n), 0) == iota((n, n), 1)
    return jnp.sum(jnp.where(same, row.astype(F32), 0.0), axis=1, keepdims=True)


def to_row(column):
    n = column.shape[0]
    return jnp.sum(jnp.where(iota((n, n), 0) == iota((n, n), 1), column, 0.0), axis=0, keepdims=True)


def reverse(index, count):
    return (count - 1) ^ index


def spread_order(shards):
    return [reverse(s, shards) for s in range(shards)]


def group_bit(r):
    return 1 - ((lax.axis_index("dom") >> r) & 1)


def renumber(slot, shards, slots):
    half = slots // 2
    return (slot // half % 2) * (shards * half) + reverse(slot // slots, shards) * half + slot % half


def halves(ref, r):
    rows, bit = ref.shape[0] // 2, group_bit(r)
    return [pl.ds(pl.multiple_of(side * rows, rows), rows) for side in (bit, 1 - bit)]


def whole(width):
    return width // LANES * LANES


def unfold(value, width):
    tiles, rest = whole(width), width - whole(width)
    return jnp.concatenate(
        [
            jnp.concatenate(
                [value[:, side * tiles : (side + 1) * tiles], value[:, 2 * tiles + side * rest :][:, :rest]], axis=1
            )
            for side in range(2)
        ],
        axis=0,
    )


def beside(left, right):
    tiles = whole(left.shape[1])
    return jnp.concatenate([left[:, :tiles], right[:, :tiles], left[:, tiles:], right[:, tiles:]], axis=1)


def fold(value):
    n = value.shape[0] // 2
    return beside(value[:n], value[n:])


def request_columns(request_ref, r):
    _, shards, _, slots = request_ref.shape
    half = slots // 2
    sides = [request_ref[r, :, k, :].astype(F32) for k in range(2)]
    flip = group_bit(r) == 1
    rep = jnp.concatenate(
        [
            jnp.broadcast_to(ids[reverse(place, shards)][None], (half, slots))
            for ids in (jnp.where(flip, sides[1], sides[0]), jnp.where(flip, sides[0], sides[1]))
            for place in range(shards)
        ],
        axis=0,
    )
    n = rep.shape[0]
    lane, inside = iota((n, slots), 1), iota((n, slots), 0) % half
    return [
        jnp.sum(jnp.where(lane == side * half + inside, rep, 0.0), axis=1, keepdims=True) for side in range(2)
    ]


def serve(request_ref, r, table, out_ref):
    rows, width = table.shape
    table = table.astype(BF16)
    hot = jnp.concatenate([one_hot(column, rows) for column in request_columns(request_ref, r)], axis=1)
    blank = jnp.zeros((rows, width), BF16)
    both = jnp.concatenate([beside(table, blank), beside(blank, table)], axis=0)
    out_ref[...] = dot(hot, both).astype(BF16)


def first_kernel(request_ref, state_ref, *refs):
    out_ref = refs[-1]
    table = state_ref[: state_ref.shape[0] - 2]
    serve(request_ref, 0, table, out_ref)


def request_hot(request_ref, r, rows):
    return jnp.concatenate([one_hot(column, rows) for column in request_columns(request_ref, r)], axis=0)


def row_update(hot, back_ref, state_ref, dims=FIRST):
    rows, width = state_ref.shape[0] - 2, state_ref.shape[1]
    row_grad = dot(hot, unfold(back_ref[:, : 2 * width], width), dims)
    accum = to_column(state_ref[rows : rows + 1, :rows]) + jnp.mean(row_grad * row_grad, axis=1, keepdims=True)
    return state_ref[:rows] - row_grad * (LEARN_RATE * lax.rsqrt(accum)), to_row(accum)


def middle_kernel(r, request_ref, back_ref, state_ref, state_out, out_ref):
    rows = state_ref.shape[0] - 2
    table, accum = row_update(request_hot(request_ref, r, rows), back_ref, state_ref)
    serve(request_ref, r + 1, table, out_ref)
    state_out[:rows] = table
    state_out[rows:] = state_ref[rows:]
    state_out[rows : rows + 1, :rows] = accum


def slots_of(ref):
    return 2 * ref.shape[0] // (2 * lax.axis_size("shard"))


def by_blocks(function, *arrays):
    step = 16
    parts = [function(*[x[i : i + step] for x in arrays]) for i in range(0, arrays[0].shape[0], step)]
    return [jnp.concatenate(column, axis=0) for column in zip(*parts)]


def query_block(head, tail, rel):
    tail_query = head * rel
    positive = jnp.sum(tail_query * tail, axis=1, keepdims=True)
    return tail_query.astype(BF16), (tail * rel).astype(BF16), -jax.nn.sigmoid(-positive)


def grad_block(head, tail, rel, coeff, back_tail, back_head):
    toward_head = coeff * tail + back_tail
    grad_rel = head * toward_head + tail * back_head
    return (
        (rel * toward_head).astype(BF16),
        (rel * (coeff * head + back_head)).astype(BF16),
        grad_rel.astype(BF16),
    )


def edge_kernel(
    r,
    bit,
    per_device,
    rec_ref,
    head_ref,
    tail_ref,
    rel_ref,
    own_neg_ref,
    far_neg_ref,
    relations_ref,
    *refs,
):
    width = relations_ref.shape[1]
    shards, slots = lax.axis_size("shard"), slots_of(rec_ref)
    touched = shards * slots
    edges, negatives = head_ref.shape[1], own_neg_ref.shape[1]
    own_half, far_half = halves(rec_ref, r)
    own = unfold(rec_ref[own_half], width)
    far = unfold(rec_ref[far_half], width)
    row = slice(r, r + 1)
    ids = rel_ref[row]
    heads, tails = renumber(head_ref[row], shards, slots), renumber(tail_ref[row], shards, slots)
    head = dot(one_hot(to_column(heads), touched), own)
    tail = dot(one_hot(to_column(tails), touched), far)
    rel = dot(one_hot(to_column(ids), relations_ref.shape[0]), relations_ref[...])
    query_tail, query_head, coeff = by_blocks(query_block, head, tail, rel)

    def weights(query, rows, neg_ref):
        hit = iota((touched, negatives), 0) == renumber(neg_ref[row], shards, slots)
        scale = jnp.sum(jnp.where(hit, 1.0 / negatives, 0.0), axis=1, keepdims=True)
        return jax.nn.sigmoid(dot(query, rows, LAST)) * to_row(scale)

    weight_tail = weights(query_tail, far, far_neg_ref)
    weight_head = weights(query_head, own, own_neg_ref)
    back_tail = dot(weight_tail.astype(BF16), far)
    back_head = dot(weight_head.astype(BF16), own)
    grad_head, grad_tail, grad_rel = by_blocks(grad_block, head, tail, rel, coeff, back_tail, back_head)
    right = [
        jnp.concatenate([grad_head, query_head], axis=0),
        jnp.concatenate([grad_tail, query_tail], axis=0),
    ]
    if r < bit:
        out_ref, grad_rel_out = refs
        sides = (own_half, heads, weight_head), (far_half, tails, weight_tail)
        for (half, slot, weight), grads in zip(sides, right):
            out_ref[half] = row_grads(slot, weight, grads)
        grad_rel_out[...] = grad_rel
    else:
        *before_refs, weights_out, right_out, values_out, sums_out = refs
        for side, weight in enumerate((weight_head, weight_tail)):
            weights_out[side], right_out[side] = weight.astype(BF16), right[side]
        values = jnp.concatenate([ref[...] for ref in before_refs] + [grad_rel], axis=0)
        values_out[...] = values
        masks = other_doms(bit)
        for i, mask in enumerate(masks):
            sums_out[i] = relation_sums(rel_ref, values, bit, per_device, mask, rec_ref.shape[0]).astype(BF16)


def other_doms(bit):
    return [mask for mask in range(1, lax.axis_size("dom")) if not mask >> bit & 1]


def relation_sums(rel_ref, values, bit, per_device, mask, rows):
    shards = lax.axis_size("shard")
    ids = jnp.concatenate([rel_ref[r : r + 1] for r in range(rel_ref.shape[0])], axis=1)
    owner = ids // per_device
    dom = owner // shards
    chunk = (1 - (dom >> bit & 1)) * shards + reverse(owner % shards, shards)
    meant = (dom ^ lax.axis_index("dom") ^ mask) & ~(1 << bit) == 0
    place = jnp.where(meant, chunk * (rows // (2 * shards)) + ids % per_device, -1)
    return dot(one_hot_t(place, rows), values)


def row_grads(slot, weight, grads):
    left = jnp.concatenate([one_hot_t(slot, weight.shape[1]), weight.T.astype(BF16)], axis=1)
    return fold(dot(left, grads).astype(BF16))


def grad_kernel(
    bit,
    per_device,
    request_ref,
    head_ref,
    tail_ref,
    rel_ref,
    weights_ref,
    right_ref,
    values_ref,
    out_ref,
    sums_out,
    hot_out,
):
    shards, slots = lax.axis_size("shard"), slots_of(out_ref)
    for side, (half, slot_ref) in enumerate(zip(halves(out_ref, bit), (head_ref, tail_ref))):
        slot = renumber(slot_ref[bit : bit + 1], shards, slots)
        out_ref[half] = row_grads(slot, weights_ref[side].astype(F32), right_ref[side])
    sums_out[...] = relation_sums(rel_ref, values_ref[...], bit, per_device, 0, out_ref.shape[0])
    hot_out[...] = request_hot(request_ref, bit, hot_out.shape[0]).astype(F32).T.astype(BF16)


def wide(width):
    return 3 * whole(width) + LANES


def join_kernel(grads_ref, sums_ref, *refs):
    *came_refs, out_ref = refs
    width = sums_ref.shape[1]
    tiles, rest = whole(width), width - whole(width)
    total = sums_ref[...]
    for ref in came_refs:
        total = total + ref[...].astype(F32)
    total = total.astype(BF16)
    out_ref[:, : 2 * tiles] = grads_ref[:, : 2 * tiles]
    blank = jnp.zeros((total.shape[0], LANES - 3 * rest), BF16)
    out_ref[:, 2 * tiles : 2 * tiles + LANES] = jnp.concatenate(
        [grads_ref[:, 2 * tiles :], total[:, tiles:], blank], axis=1
    )
    out_ref[:, 2 * tiles + LANES :] = total[:, :tiles]


def last_kernel(hot_ref, back_ref, state_ref, table_out, row_accum_out, step_out, accum_out, *scratch):
    table_ref, row_accum_ref, step_ref, new_accum_ref, sems = scratch
    pairs = (
        (table_ref, table_out),
        (row_accum_ref, row_accum_out),
        (step_ref, step_out),
        (new_accum_ref, accum_out),
    )
    copies = [pltpu.make_async_copy(source, target, sems.at[i]) for i, (source, target) in enumerate(pairs)]
    table, accum = row_update(hot_ref[...], back_ref, state_ref, NATURAL)
    table_ref[...] = table
    copies[0].start()
    row_accum_ref[...] = accum
    copies[1].start()
    per_device, width = step_ref.shape
    rows = slots_of(back_ref) // 2
    tiles, rest = whole(width), width - whole(width)
    parts = jnp.concatenate(
        [back_ref[:, 2 * tiles + LANES :], back_ref[:, 2 * tiles + 2 * rest : 2 * tiles + 3 * rest]], axis=1
    ).astype(F32)
    grad = jnp.sum(parts.reshape(parts.shape[0] // rows, rows, width), axis=0)[:per_device]
    accum = to_column(state_ref[table.shape[0] + 1 :, :per_device]) + jnp.mean(grad * grad, axis=1, keepdims=True)
    step_ref[...] = grad * (-LEARN_RATE * lax.rsqrt(accum))
    copies[2].start()
    new_accum_ref[...] = to_row(accum)
    copies[3].start()
    for copy in copies:
        copy.wait()


def call(kernel, outs, *args, **kwargs):
    return pl.pallas_call(
        kernel,
        out_shape=[jax.ShapeDtypeStruct(shape, kind) for shape, kind in outs],
        compiler_params=pltpu.CompilerParams(vmem_limit_bytes=VMEM_LIMIT),
        **kwargs,
    )(*args)


def swap_pair(value, r):
    doms, shards = lax.axis_size("dom"), lax.axis_size("shard")
    order = spread_order(shards)
    groups = [
        [g * shards + s for g in (low ^ (1 << r), low) for s in sorted(range(shards), key=order.__getitem__)]
        for low in range(doms)
        if not low >> r & 1
    ]
    return lax.all_to_all(
        value, ("dom", "shard"), split_axis=0, concat_axis=0, axis_index_groups=groups, tiled=True
    )


def body(
    embeddings,
    row_accum,
    relations,
    relation_accum,
    request_rows,
    head_slots,
    tail_slots,
    relation_ids,
    own_negatives,
    far_negatives,
):
    rows, width = embeddings.shape
    doms, shards = lax.axis_size("dom"), lax.axis_size("shard")
    rounds, slots = request_rows.shape[0], request_rows.shape[-1]
    bit = rounds - 1
    per_device = relation_accum.shape[0]
    assert 3 * (width % LANES) <= LANES
    count, touched = head_slots.shape[1], shards * slots
    assert per_device <= slots // 2
    chunks = ((touched, 2 * width), BF16)
    state = (
        jnp.pad(embeddings, ((0, 2), (0, 0)))
        + jnp.pad(row_accum[None], ((rows, 1), (0, width - rows)))
        + jnp.pad(relation_accum[None], ((rows + 1, 0), (0, width - per_device)))
    )
    edges = (head_slots, tail_slots, relation_ids, own_negatives, far_negatives, relations)
    (outgoing,) = call(first_kernel, [chunks], request_rows, state, *edges)
    before = []
    for r in range(bit):
        received = swap_pair(outgoing, r)
        grads, grad_rel = call(
            functools.partial(edge_kernel, r, bit, per_device), [chunks, ((count, width), BF16)], received, *edges
        )
        before.append(grad_rel)
        back = swap_pair(grads, r)
        state, outgoing = call(
            functools.partial(middle_kernel, r), [(state.shape, F32), chunks], request_rows, back, state
        )
    received = swap_pair(outgoing, bit)
    masks = other_doms(bit)
    weights, right, values, sums = call(
        functools.partial(edge_kernel, bit, bit, per_device),
        [
            ((2, count, touched), BF16),
            ((2, 2 * count, width), BF16),
            ((rounds * count, width), BF16),
            ((len(masks), touched, width), BF16),
        ],
        received,
        *edges,
        *before,
    )
    came = [lax.ppermute(sums[i], "dom", [(g, g ^ mask) for g in range(doms)]) for i, mask in enumerate(masks)]
    grads, sums, hot = call(
        functools.partial(grad_kernel, bit, per_device),
        [chunks, ((touched, width), F32), ((rows, 2 * touched), BF16)],
        request_rows,
        head_slots,
        tail_slots,
        relation_ids,
        weights,
        right,
        values,
    )
    (grads,) = call(join_kernel, [((touched, wide(width)), BF16)], grads, sums, *came)
    back = swap_pair(grads, bit)
    outs = [((rows, width), F32), ((1, rows), F32), ((per_device, width), F32), ((1, per_device), F32)]
    table, accum, step, relation_accum = call(
        last_kernel,
        outs,
        hot,
        back,
        state,
        in_specs=[VMEM] * 3,
        out_specs=[HBM] * 4,
        scratch_shapes=[pltpu.VMEM(*out) for out in outs] + [pltpu.SemaphoreType.DMA((4,))],
    )
    return (table, accum.reshape(rows), step, relation_accum.reshape(per_device))


def solution(mesh):
    placed = (
        P(("dom", "shard"), None),
        P(("dom", "shard")),
        P(),
        P(("dom", "shard")),
        P(None, ("dom", "shard"), None, None),
        P(None, ("dom", "shard")),
        P(None, ("dom", "shard")),
        P(None, ("dom", "shard")),
        P(None, ("dom", "shard")),
        P(None, ("dom", "shard")),
    )
    return jax.shard_map(
        body,
        mesh=mesh,
        in_specs=placed,
        out_specs=(
            P(("dom", "shard"), None),
            P(("dom", "shard")),
            P(("dom", "shard"), None),
            P(("dom", "shard")),
        ),
        check_vma=False,
    )
```

```python
import functools

import jax
import jax.numpy as jnp
from jax import lax
from jax.experimental import pallas as pl
from jax.experimental.pallas import tpu as pltpu
from jax.sharding import PartitionSpec as P

LEARN_RATE = 0.1
LANES = 128
VMEM_LIMIT = 48 * 2**20
BF16 = jnp.bfloat16
F32 = jnp.float32
NATURAL = (((1,), (0,)), ((), ()))
LAST = (((1,), (1,)), ((), ()))
FIRST = (((0,), (0,)), ((), ()))
HBM = pl.BlockSpec(memory_space=pltpu.HBM)
VMEM = pl.BlockSpec(memory_space=pltpu.VMEM)


def dot(left, right, dims=NATURAL):
    return lax.dot_general(left, right, dims, preferred_element_type=F32)


def iota(shape, axis):
    return lax.broadcasted_iota(jnp.int32, shape, axis)


def one_hot_t(row, count):
    return (iota((count, row.shape[1]), 0) == row).astype(BF16)


def one_hot(column, count):
    return (iota((column.shape[0], count), 1) == column.astype(jnp.int32)).astype(BF16)


def to_column(row):
    n = row.shape[1]
    same = iota((n, n), 0) == iota((n, n), 1)
    return jnp.sum(jnp.where(same, row.astype(F32), 0.0), axis=1, keepdims=True)


def to_row(column):
    n = column.shape[0]
    return jnp.sum(jnp.where(iota((n, n), 0) == iota((n, n), 1), column, 0.0), axis=0, keepdims=True)


def reverse(index, count):
    return (count - 1) ^ index


def group_bit(r):
    return 1 - ((lax.axis_index("dom") >> r) & 1)


def renumber(slot, shards, slots):
    half = slots // 2
    return (slot // half % 2) * (shards * half) + reverse(slot // slots, shards) * half + slot % half


def pieces(ref, r, side):
    rows = slots_of(ref)
    half = group_bit(r) if side == 0 else 1 - group_bit(r)
    return [
        pl.ds(pl.multiple_of((2 * pair + half) * rows, rows), rows) for pair in range(lax.axis_size("shard") // 2)
    ]


def get_side(ref, r, side):
    return jnp.concatenate([ref[piece] for piece in pieces(ref, r, side)], axis=0)


def put_side(ref, r, side, value):
    rows = slots_of(ref)
    for i, piece in enumerate(pieces(ref, r, side)):
        ref[piece] = value[i * rows : (i + 1) * rows]


def whole(width):
    return width // LANES * LANES


def unfold(value, width):
    tiles, rest = whole(width), width - whole(width)
    return jnp.concatenate(
        [
            jnp.concatenate(
                [value[:, side * tiles : (side + 1) * tiles], value[:, 2 * tiles + side * rest :][:, :rest]], axis=1
            )
            for side in range(2)
        ],
        axis=0,
    )


def beside(left, right):
    tiles = whole(left.shape[1])
    return jnp.concatenate([left[:, :tiles], right[:, :tiles], left[:, tiles:], right[:, tiles:]], axis=1)


def fold(value):
    n = value.shape[0] // 2
    return beside(value[:n], value[n:])


def request_columns(request_ref, r):
    _, shards, _, slots = request_ref.shape
    half = slots // 2
    sides = [request_ref[r, :, k, :].astype(F32) for k in range(2)]
    flip = group_bit(r) == 1
    rep = jnp.concatenate(
        [
            jnp.broadcast_to(ids[reverse(place, shards)][None], (half, slots))
            for pair in range(shards // 2)
            for ids in (jnp.where(flip, sides[1], sides[0]), jnp.where(flip, sides[0], sides[1]))
            for place in (2 * pair, 2 * pair + 1)
        ],
        axis=0,
    )
    n = rep.shape[0]
    lane, inside = iota((n, slots), 1), iota((n, slots), 0) % half
    return [
        jnp.sum(jnp.where(lane == side * half + inside, rep, 0.0), axis=1, keepdims=True) for side in range(2)
    ]


def serve(request_ref, r, table, out_ref):
    rows, width = table.shape
    table = table.astype(BF16)
    hot = jnp.concatenate([one_hot(column, rows) for column in request_columns(request_ref, r)], axis=1)
    blank = jnp.zeros((rows, width), BF16)
    both = jnp.concatenate([beside(table, blank), beside(blank, table)], axis=0)
    out_ref[...] = dot(hot, both).astype(BF16)


def first_kernel(request_ref, state_ref, *refs):
    out_ref = refs[-1]
    table = state_ref[: state_ref.shape[0] - 2]
    serve(request_ref, 0, table, out_ref)


def request_hot(request_ref, r, rows):
    return jnp.concatenate([one_hot(column, rows) for column in request_columns(request_ref, r)], axis=0)


def row_update(hot, back_ref, state_ref, dims=FIRST):
    rows, width = state_ref.shape[0] - 2, state_ref.shape[1]
    row_grad = dot(hot, unfold(back_ref[:, : 2 * width], width), dims)
    accum = to_column(state_ref[rows : rows + 1, :rows]) + jnp.mean(row_grad * row_grad, axis=1, keepdims=True)
    return state_ref[:rows] - row_grad * (LEARN_RATE * lax.rsqrt(accum)), to_row(accum)


def middle_kernel(r, request_ref, back_ref, state_ref, state_out, out_ref):
    rows = state_ref.shape[0] - 2
    table, accum = row_update(request_hot(request_ref, r, rows), back_ref, state_ref)
    serve(request_ref, r + 1, table, out_ref)
    state_out[:rows] = table
    state_out[rows:] = state_ref[rows:]
    state_out[rows : rows + 1, :rows] = accum


def slots_of(ref):
    return 2 * ref.shape[0] // (2 * lax.axis_size("shard"))


def by_blocks(function, *arrays):
    step = 16
    parts = [function(*[x[i : i + step] for x in arrays]) for i in range(0, arrays[0].shape[0], step)]
    return [jnp.concatenate(column, axis=0) for column in zip(*parts)]


def query_block(head, tail, rel):
    tail_query = head * rel
    positive = jnp.sum(tail_query * tail, axis=1, keepdims=True)
    return tail_query.astype(BF16), (tail * rel).astype(BF16), -jax.nn.sigmoid(-positive)


def grad_block(head, tail, rel, coeff, back_tail, back_head):
    toward_head = coeff * tail + back_tail
    grad_rel = head * toward_head + tail * back_head
    return (
        (rel * toward_head).astype(BF16),
        (rel * (coeff * head + back_head)).astype(BF16),
        grad_rel.astype(BF16),
    )


def edge_kernel(
    r,
    bit,
    per_device,
    rec_ref,
    head_ref,
    tail_ref,
    rel_ref,
    own_neg_ref,
    far_neg_ref,
    relations_ref,
    *refs,
):
    width = relations_ref.shape[1]
    shards, slots = lax.axis_size("shard"), slots_of(rec_ref)
    touched = shards * slots
    edges, negatives = head_ref.shape[1], own_neg_ref.shape[1]
    own = unfold(get_side(rec_ref, r, 0), width)
    far = unfold(get_side(rec_ref, r, 1), width)
    row = slice(r, r + 1)
    ids = rel_ref[row]
    heads, tails = renumber(head_ref[row], shards, slots), renumber(tail_ref[row], shards, slots)
    head = dot(one_hot(to_column(heads), touched), own)
    tail = dot(one_hot(to_column(tails), touched), far)
    rel = dot(one_hot(to_column(ids), relations_ref.shape[0]), relations_ref[...])
    query_tail, query_head, coeff = by_blocks(query_block, head, tail, rel)

    def weights(query, rows, neg_ref):
        hit = iota((touched, negatives), 0) == renumber(neg_ref[row], shards, slots)
        scale = jnp.sum(jnp.where(hit, 1.0 / negatives, 0.0), axis=1, keepdims=True)
        return jax.nn.sigmoid(dot(query, rows, LAST)) * to_row(scale)

    weight_tail = weights(query_tail, far, far_neg_ref)
    weight_head = weights(query_head, own, own_neg_ref)
    back_tail = dot(weight_tail.astype(BF16), far)
    back_head = dot(weight_head.astype(BF16), own)
    grad_head, grad_tail, grad_rel = by_blocks(grad_block, head, tail, rel, coeff, back_tail, back_head)
    right = [
        jnp.concatenate([grad_head, query_head], axis=0),
        jnp.concatenate([grad_tail, query_tail], axis=0),
    ]
    if r < bit:
        out_ref, grad_rel_out = refs
        for side, (slot, weight) in enumerate(((heads, weight_head), (tails, weight_tail))):
            put_side(out_ref, r, side, row_grads(slot, weight, right[side]))
        grad_rel_out[...] = grad_rel
    else:
        *before_refs, weights_out, right_out, values_out, sums_out = refs
        for side, weight in enumerate((weight_head, weight_tail)):
            weights_out[side], right_out[side] = weight.astype(BF16), right[side]
        values = jnp.concatenate([ref[...] for ref in before_refs] + [grad_rel], axis=0)
        values_out[...] = values
        masks = other_doms(bit)
        for i, mask in enumerate(masks):
            sums_out[i] = relation_sums(rel_ref, values, bit, per_device, mask, rec_ref.shape[0]).astype(BF16)


def other_doms(bit):
    return [mask for mask in range(1, lax.axis_size("dom")) if not mask >> bit & 1]


def relation_sums(rel_ref, values, bit, per_device, mask, rows):
    shards = lax.axis_size("shard")
    ids = jnp.concatenate([rel_ref[r : r + 1] for r in range(rel_ref.shape[0])], axis=1)
    owner = ids // per_device
    dom = owner // shards
    place = reverse(owner % shards, shards)
    chunk = place // 2 * 4 + (1 - (dom >> bit & 1)) * 2 + place % 2
    meant = (dom ^ lax.axis_index("dom") ^ mask) & ~(1 << bit) == 0
    spot = jnp.where(meant, chunk * (rows // (2 * shards)) + ids % per_device, -1)
    return dot(one_hot_t(spot, rows), values)


def row_grads(slot, weight, grads):
    left = jnp.concatenate([one_hot_t(slot, weight.shape[1]), weight.T.astype(BF16)], axis=1)
    return fold(dot(left, grads).astype(BF16))


def grad_kernel(
    bit,
    per_device,
    request_ref,
    head_ref,
    tail_ref,
    rel_ref,
    weights_ref,
    right_ref,
    values_ref,
    out_ref,
    sums_out,
    hot_out,
):
    shards, slots = lax.axis_size("shard"), slots_of(out_ref)
    for side, slot_ref in enumerate((head_ref, tail_ref)):
        slot = renumber(slot_ref[bit : bit + 1], shards, slots)
        put_side(out_ref, bit, side, row_grads(slot, weights_ref[side].astype(F32), right_ref[side]))
    sums_out[...] = relation_sums(rel_ref, values_ref[...], bit, per_device, 0, out_ref.shape[0])
    hot_out[...] = request_hot(request_ref, bit, hot_out.shape[0]).astype(F32).T.astype(BF16)


def wide(width):
    return 3 * whole(width) + LANES


def join_kernel(grads_ref, sums_ref, *refs):
    *came_refs, out_ref = refs
    width = sums_ref.shape[1]
    tiles, rest = whole(width), width - whole(width)
    total = sums_ref[...]
    for ref in came_refs:
        total = total + ref[...].astype(F32)
    total = total.astype(BF16)
    out_ref[:, : 2 * tiles] = grads_ref[:, : 2 * tiles]
    blank = jnp.zeros((total.shape[0], LANES - 3 * rest), BF16)
    out_ref[:, 2 * tiles : 2 * tiles + LANES] = jnp.concatenate(
        [grads_ref[:, 2 * tiles :], total[:, tiles:], blank], axis=1
    )
    out_ref[:, 2 * tiles + LANES :] = total[:, :tiles]


def last_kernel(hot_ref, back_ref, state_ref, table_out, row_accum_out, step_out, accum_out, *scratch):
    table_ref, row_accum_ref, step_ref, new_accum_ref, sems = scratch
    pairs = (
        (table_ref, table_out),
        (row_accum_ref, row_accum_out),
        (step_ref, step_out),
        (new_accum_ref, accum_out),
    )
    copies = [pltpu.make_async_copy(source, target, sems.at[i]) for i, (source, target) in enumerate(pairs)]
    table, accum = row_update(hot_ref[...], back_ref, state_ref, NATURAL)
    table_ref[...] = table
    copies[0].start()
    row_accum_ref[...] = accum
    copies[1].start()
    per_device, width = step_ref.shape
    rows = slots_of(back_ref) // 2
    tiles, rest = whole(width), width - whole(width)
    parts = jnp.concatenate(
        [back_ref[:, 2 * tiles + LANES :], back_ref[:, 2 * tiles + 2 * rest : 2 * tiles + 3 * rest]], axis=1
    ).astype(F32)
    grad = jnp.sum(parts.reshape(parts.shape[0] // rows, rows, width), axis=0)[:per_device]
    accum = to_column(state_ref[table.shape[0] + 1 :, :per_device]) + jnp.mean(grad * grad, axis=1, keepdims=True)
    step_ref[...] = grad * (-LEARN_RATE * lax.rsqrt(accum))
    copies[2].start()
    new_accum_ref[...] = to_row(accum)
    copies[3].start()
    for copy in copies:
        copy.wait()


def call(kernel, outs, *args, **kwargs):
    return pl.pallas_call(
        kernel,
        out_shape=[jax.ShapeDtypeStruct(shape, kind) for shape, kind in outs],
        compiler_params=pltpu.CompilerParams(vmem_limit_bytes=VMEM_LIMIT),
        **kwargs,
    )(*args)


def swap_pair(value, r):
    doms, shards = lax.axis_size("dom"), lax.axis_size("shard")
    groups = [
        [
            g * shards + reverse(place, shards)
            for pair in range(shards // 2)
            for g in (low ^ (1 << r), low)
            for place in (2 * pair, 2 * pair + 1)
        ]
        for low in range(doms)
        if not low >> r & 1
    ]
    return lax.all_to_all(
        value, ("dom", "shard"), split_axis=0, concat_axis=0, axis_index_groups=groups, tiled=True
    )


def body(
    embeddings,
    row_accum,
    relations,
    relation_accum,
    request_rows,
    head_slots,
    tail_slots,
    relation_ids,
    own_negatives,
    far_negatives,
):
    rows, width = embeddings.shape
    doms, shards = lax.axis_size("dom"), lax.axis_size("shard")
    rounds, slots = request_rows.shape[0], request_rows.shape[-1]
    bit = rounds - 1
    per_device = relation_accum.shape[0]
    assert 3 * (width % LANES) <= LANES
    count, touched = head_slots.shape[1], shards * slots
    assert per_device <= slots // 2
    chunks = ((touched, 2 * width), BF16)
    state = (
        jnp.pad(embeddings, ((0, 2), (0, 0)))
        + jnp.pad(row_accum[None], ((rows, 1), (0, width - rows)))
        + jnp.pad(relation_accum[None], ((rows + 1, 0), (0, width - per_device)))
    )
    edges = (head_slots, tail_slots, relation_ids, own_negatives, far_negatives, relations)
    (outgoing,) = call(first_kernel, [chunks], request_rows, state, *edges)
    before = []
    for r in range(bit):
        received = swap_pair(outgoing, r)
        grads, grad_rel = call(
            functools.partial(edge_kernel, r, bit, per_device), [chunks, ((count, width), BF16)], received, *edges
        )
        before.append(grad_rel)
        back = swap_pair(grads, r)
        state, outgoing = call(
            functools.partial(middle_kernel, r), [(state.shape, F32), chunks], request_rows, back, state
        )
    received = swap_pair(outgoing, bit)
    masks = other_doms(bit)
    weights, right, values, sums = call(
        functools.partial(edge_kernel, bit, bit, per_device),
        [
            ((2, count, touched), BF16),
            ((2, 2 * count, width), BF16),
            ((rounds * count, width), BF16),
            ((len(masks), touched, width), BF16),
        ],
        received,
        *edges,
        *before,
    )
    came = [lax.ppermute(sums[i], "dom", [(g, g ^ mask) for g in range(doms)]) for i, mask in enumerate(masks)]
    grads, sums, hot = call(
        functools.partial(grad_kernel, bit, per_device),
        [chunks, ((touched, width), F32), ((rows, 2 * touched), BF16)],
        request_rows,
        head_slots,
        tail_slots,
        relation_ids,
        weights,
        right,
        values,
    )
    (grads,) = call(join_kernel, [((touched, wide(width)), BF16)], grads, sums, *came)
    back = swap_pair(grads, bit)
    outs = [((rows, width), F32), ((1, rows), F32), ((per_device, width), F32), ((1, per_device), F32)]
    table, accum, step, relation_accum = call(
        last_kernel,
        outs,
        hot,
        back,
        state,
        in_specs=[VMEM] * 3,
        out_specs=[HBM] * 4,
        scratch_shapes=[pltpu.VMEM(*out) for out in outs] + [pltpu.SemaphoreType.DMA((4,))],
    )
    return (table, accum.reshape(rows), step, relation_accum.reshape(per_device))


def solution(mesh):
    placed = (
        P(("dom", "shard"), None),
        P(("dom", "shard")),
        P(),
        P(("dom", "shard")),
        P(None, ("dom", "shard"), None, None),
        P(None, ("dom", "shard")),
        P(None, ("dom", "shard")),
        P(None, ("dom", "shard")),
        P(None, ("dom", "shard")),
        P(None, ("dom", "shard")),
    )
    return jax.shard_map(
        body,
        mesh=mesh,
        in_specs=placed,
        out_specs=(
            P(("dom", "shard"), None),
            P(("dom", "shard")),
            P(("dom", "shard"), None),
            P(("dom", "shard")),
        ),
        check_vma=False,
    )
```

```python
import functools

import jax
import jax.numpy as jnp
from jax import lax
from jax.experimental import pallas as pl
from jax.experimental.pallas import tpu as pltpu
from jax.sharding import PartitionSpec as P

LEARN_RATE = 0.1
LANES = 128
VMEM_LIMIT = 48 * 2**20
BF16 = jnp.bfloat16
F32 = jnp.float32
NATURAL = (((1,), (0,)), ((), ()))
LAST = (((1,), (1,)), ((), ()))
FIRST = (((0,), (0,)), ((), ()))
HBM = pl.BlockSpec(memory_space=pltpu.HBM)
VMEM = pl.BlockSpec(memory_space=pltpu.VMEM)


def dot(left, right, dims=NATURAL):
    return lax.dot_general(left, right, dims, preferred_element_type=F32)


def iota(shape, axis):
    return lax.broadcasted_iota(jnp.int32, shape, axis)


def one_hot_t(row, count):
    return (iota((count, row.shape[1]), 0) == row).astype(BF16)


def one_hot(column, count):
    return (iota((column.shape[0], count), 1) == column.astype(jnp.int32)).astype(BF16)


def to_column(row):
    n = row.shape[1]
    same = iota((n, n), 0) == iota((n, n), 1)
    return jnp.sum(jnp.where(same, row.astype(F32), 0.0), axis=1, keepdims=True)


def to_row(column):
    n = column.shape[0]
    return jnp.sum(jnp.where(iota((n, n), 0) == iota((n, n), 1), column, 0.0), axis=0, keepdims=True)


def ascending(r, mask=0):
    return (lax.axis_index("dom") ^ mask) & 1 if r else 0


def turn(index, count, r, mask=0):
    return index ^ (1 - ascending(r, mask)) * (count - 1)


def group_bit(r):
    return (1 - ((lax.axis_index("dom") >> r) & 1)) ^ ascending(r)


def renumber(slot, shards, slots, r):
    half = slots // 2
    return (slot // half % 2) * (shards * half) + turn(slot // slots, shards, r) * half + slot % half


def halves(ref, r):
    rows, bit = ref.shape[0] // 2, group_bit(r)
    return [pl.ds(pl.multiple_of(side * rows, rows), rows) for side in (bit, 1 - bit)]


def whole(width):
    return width // LANES * LANES


def unfold(value, width):
    tiles, rest = whole(width), width - whole(width)
    return jnp.concatenate(
        [
            jnp.concatenate(
                [value[:, side * tiles : (side + 1) * tiles], value[:, 2 * tiles + side * rest :][:, :rest]], axis=1
            )
            for side in range(2)
        ],
        axis=0,
    )


def beside(left, right):
    tiles = whole(left.shape[1])
    return jnp.concatenate([left[:, :tiles], right[:, :tiles], left[:, tiles:], right[:, tiles:]], axis=1)


def fold(value):
    n = value.shape[0] // 2
    return beside(value[:n], value[n:])


def request_columns(request_ref, r):
    _, shards, _, slots = request_ref.shape
    half = slots // 2
    sides = [request_ref[r, :, k, :].astype(F32) for k in range(2)]
    flip, up = group_bit(r) == 1, ascending(r) == 1
    rep = jnp.concatenate(
        [
            jnp.broadcast_to(jnp.where(up, ids[place], ids[shards - 1 - place])[None], (half, slots))
            for ids in (jnp.where(flip, sides[1], sides[0]), jnp.where(flip, sides[0], sides[1]))
            for place in range(shards)
        ],
        axis=0,
    )
    n = rep.shape[0]
    lane, inside = iota((n, slots), 1), iota((n, slots), 0) % half
    return [
        jnp.sum(jnp.where(lane == side * half + inside, rep, 0.0), axis=1, keepdims=True) for side in range(2)
    ]


def serve(request_ref, r, table, out_ref):
    rows, width = table.shape
    table = table.astype(BF16)
    hot = jnp.concatenate([one_hot(column, rows) for column in request_columns(request_ref, r)], axis=1)
    blank = jnp.zeros((rows, width), BF16)
    both = jnp.concatenate([beside(table, blank), beside(blank, table)], axis=0)
    out_ref[...] = dot(hot, both).astype(BF16)


def first_kernel(request_ref, state_ref, *refs):
    out_ref = refs[-1]
    table = state_ref[: state_ref.shape[0] - 2]
    serve(request_ref, 0, table, out_ref)


def request_hot(request_ref, r, rows):
    return jnp.concatenate([one_hot(column, rows) for column in request_columns(request_ref, r)], axis=0)


def row_update(hot, back_ref, state_ref, dims=FIRST):
    rows, width = state_ref.shape[0] - 2, state_ref.shape[1]
    row_grad = dot(hot, unfold(back_ref[:, : 2 * width], width), dims)
    accum = to_column(state_ref[rows : rows + 1, :rows]) + jnp.mean(row_grad * row_grad, axis=1, keepdims=True)
    return state_ref[:rows] - row_grad * (LEARN_RATE * lax.rsqrt(accum)), to_row(accum)


def middle_kernel(r, request_ref, back_ref, state_ref, state_out, out_ref):
    rows = state_ref.shape[0] - 2
    table, accum = row_update(request_hot(request_ref, r, rows), back_ref, state_ref)
    serve(request_ref, r + 1, table, out_ref)
    state_out[:rows] = table
    state_out[rows:] = state_ref[rows:]
    state_out[rows : rows + 1, :rows] = accum


def slots_of(ref):
    return 2 * ref.shape[0] // (2 * lax.axis_size("shard"))


def by_blocks(function, *arrays):
    step = 16
    parts = [function(*[x[i : i + step] for x in arrays]) for i in range(0, arrays[0].shape[0], step)]
    return [jnp.concatenate(column, axis=0) for column in zip(*parts)]


def query_block(head, tail, rel):
    tail_query = head * rel
    positive = jnp.sum(tail_query * tail, axis=1, keepdims=True)
    return tail_query.astype(BF16), (tail * rel).astype(BF16), -jax.nn.sigmoid(-positive)


def grad_block(head, tail, rel, coeff, back_tail, back_head):
    toward_head = coeff * tail + back_tail
    grad_rel = head * toward_head + tail * back_head
    return (
        (rel * toward_head).astype(BF16),
        (rel * (coeff * head + back_head)).astype(BF16),
        grad_rel.astype(BF16),
    )


def edge_kernel(
    r,
    bit,
    per_device,
    rec_ref,
    head_ref,
    tail_ref,
    rel_ref,
    own_neg_ref,
    far_neg_ref,
    relations_ref,
    *refs,
):
    width = relations_ref.shape[1]
    shards, slots = lax.axis_size("shard"), slots_of(rec_ref)
    touched = shards * slots
    edges, negatives = head_ref.shape[1], own_neg_ref.shape[1]
    own_half, far_half = halves(rec_ref, r)
    own = unfold(rec_ref[own_half], width)
    far = unfold(rec_ref[far_half], width)
    row = slice(r, r + 1)
    ids = rel_ref[row]
    heads, tails = renumber(head_ref[row], shards, slots, r), renumber(tail_ref[row], shards, slots, r)
    head = dot(one_hot(to_column(heads), touched), own)
    tail = dot(one_hot(to_column(tails), touched), far)
    rel = dot(one_hot(to_column(ids), relations_ref.shape[0]), relations_ref[...])
    query_tail, query_head, coeff = by_blocks(query_block, head, tail, rel)

    def weights(query, rows, neg_ref):
        hit = iota((touched, negatives), 0) == renumber(neg_ref[row], shards, slots, r)
        scale = jnp.sum(jnp.where(hit, 1.0 / negatives, 0.0), axis=1, keepdims=True)
        return jax.nn.sigmoid(dot(query, rows, LAST)) * to_row(scale)

    weight_tail = weights(query_tail, far, far_neg_ref)
    weight_head = weights(query_head, own, own_neg_ref)
    back_tail = dot(weight_tail.astype(BF16), far)
    back_head = dot(weight_head.astype(BF16), own)
    grad_head, grad_tail, grad_rel = by_blocks(grad_block, head, tail, rel, coeff, back_tail, back_head)
    right = [
        jnp.concatenate([grad_head, query_head], axis=0),
        jnp.concatenate([grad_tail, query_tail], axis=0),
    ]
    if r < bit:
        out_ref, grad_rel_out = refs
        sides = (own_half, heads, weight_head), (far_half, tails, weight_tail)
        for (half, slot, weight), grads in zip(sides, right):
            out_ref[half] = row_grads(slot, weight, grads)
        grad_rel_out[...] = grad_rel
    else:
        *before_refs, weights_out, right_out, values_out, sums_out = refs
        for side, weight in enumerate((weight_head, weight_tail)):
            weights_out[side], right_out[side] = weight.astype(BF16), right[side]
        values = jnp.concatenate([ref[...] for ref in before_refs] + [grad_rel], axis=0)
        values_out[...] = values
        masks = other_doms(bit)
        for i, mask in enumerate(masks):
            sums_out[i] = relation_sums(rel_ref, values, bit, per_device, mask, rec_ref.shape[0]).astype(BF16)


def other_doms(bit):
    return [mask for mask in range(1, lax.axis_size("dom")) if not mask >> bit & 1]


def relation_sums(rel_ref, values, bit, per_device, mask, rows):
    shards = lax.axis_size("shard")
    ids = jnp.concatenate([rel_ref[r : r + 1] for r in range(rel_ref.shape[0])], axis=1)
    owner = ids // per_device
    dom = owner // shards
    chunk = ((1 - (dom >> bit & 1)) ^ ascending(bit, mask)) * shards + turn(owner % shards, shards, bit, mask)
    meant = (dom ^ lax.axis_index("dom") ^ mask) & ~(1 << bit) == 0
    place = jnp.where(meant, chunk * (rows // (2 * shards)) + ids % per_device, -1)
    return dot(one_hot_t(place, rows), values)


def row_grads(slot, weight, grads):
    left = jnp.concatenate([one_hot_t(slot, weight.shape[1]), weight.T.astype(BF16)], axis=1)
    return fold(dot(left, grads).astype(BF16))


def grad_kernel(
    bit,
    per_device,
    request_ref,
    head_ref,
    tail_ref,
    rel_ref,
    weights_ref,
    right_ref,
    values_ref,
    out_ref,
    sums_out,
    hot_out,
):
    shards, slots = lax.axis_size("shard"), slots_of(out_ref)
    for side, (half, slot_ref) in enumerate(zip(halves(out_ref, bit), (head_ref, tail_ref))):
        slot = renumber(slot_ref[bit : bit + 1], shards, slots, bit)
        out_ref[half] = row_grads(slot, weights_ref[side].astype(F32), right_ref[side])
    sums_out[...] = relation_sums(rel_ref, values_ref[...], bit, per_device, 0, out_ref.shape[0])
    hot_out[...] = request_hot(request_ref, bit, hot_out.shape[0]).astype(F32).T.astype(BF16)


def wide(width):
    return 3 * whole(width) + LANES


def join_kernel(grads_ref, sums_ref, *refs):
    *came_refs, out_ref = refs
    width = sums_ref.shape[1]
    tiles, rest = whole(width), width - whole(width)
    total = sums_ref[...]
    for ref in came_refs:
        total = total + ref[...].astype(F32)
    total = total.astype(BF16)
    out_ref[:, : 2 * tiles] = grads_ref[:, : 2 * tiles]
    blank = jnp.zeros((total.shape[0], LANES - 3 * rest), BF16)
    out_ref[:, 2 * tiles : 2 * tiles + LANES] = jnp.concatenate(
        [grads_ref[:, 2 * tiles :], total[:, tiles:], blank], axis=1
    )
    out_ref[:, 2 * tiles + LANES :] = total[:, :tiles]


def last_kernel(hot_ref, back_ref, state_ref, table_out, row_accum_out, step_out, accum_out, *scratch):
    table_ref, row_accum_ref, step_ref, new_accum_ref, sems = scratch
    pairs = (
        (table_ref, table_out),
        (row_accum_ref, row_accum_out),
        (step_ref, step_out),
        (new_accum_ref, accum_out),
    )
    copies = [pltpu.make_async_copy(source, target, sems.at[i]) for i, (source, target) in enumerate(pairs)]
    table, accum = row_update(hot_ref[...], back_ref, state_ref, NATURAL)
    table_ref[...] = table
    copies[0].start()
    row_accum_ref[...] = accum
    copies[1].start()
    per_device, width = step_ref.shape
    rows = slots_of(back_ref) // 2
    tiles, rest = whole(width), width - whole(width)
    parts = jnp.concatenate(
        [back_ref[:, 2 * tiles + LANES :], back_ref[:, 2 * tiles + 2 * rest : 2 * tiles + 3 * rest]], axis=1
    ).astype(F32)
    grad = jnp.sum(parts.reshape(parts.shape[0] // rows, rows, width), axis=0)[:per_device]
    accum = to_column(state_ref[table.shape[0] + 1 :, :per_device]) + jnp.mean(grad * grad, axis=1, keepdims=True)
    step_ref[...] = grad * (-LEARN_RATE * lax.rsqrt(accum))
    copies[2].start()
    new_accum_ref[...] = to_row(accum)
    copies[3].start()
    for copy in copies:
        copy.wait()


def call(kernel, outs, *args, **kwargs):
    return pl.pallas_call(
        kernel,
        out_shape=[jax.ShapeDtypeStruct(shape, kind) for shape, kind in outs],
        compiler_params=pltpu.CompilerParams(vmem_limit_bytes=VMEM_LIMIT),
        **kwargs,
    )(*args)


def swap_pair(value, r):
    doms, shards = lax.axis_size("dom"), lax.axis_size("shard")
    groups = [
        [g * shards + s for g in (low, low ^ (1 << r)) for s in range(shards)] for low in range(doms) if not low >> r & 1
    ]
    groups = [group if r and group[0] // shards & 1 else group[::-1] for group in groups]
    return lax.all_to_all(
        value, ("dom", "shard"), split_axis=0, concat_axis=0, axis_index_groups=groups, tiled=True
    )


def body(
    embeddings,
    row_accum,
    relations,
    relation_accum,
    request_rows,
    head_slots,
    tail_slots,
    relation_ids,
    own_negatives,
    far_negatives,
):
    rows, width = embeddings.shape
    doms, shards = lax.axis_size("dom"), lax.axis_size("shard")
    rounds, slots = request_rows.shape[0], request_rows.shape[-1]
    bit = rounds - 1
    per_device = relation_accum.shape[0]
    assert 3 * (width % LANES) <= LANES
    count, touched = head_slots.shape[1], shards * slots
    assert per_device <= slots // 2
    chunks = ((touched, 2 * width), BF16)
    state = (
        jnp.pad(embeddings, ((0, 2), (0, 0)))
        + jnp.pad(row_accum[None], ((rows, 1), (0, width - rows)))
        + jnp.pad(relation_accum[None], ((rows + 1, 0), (0, width - per_device)))
    )
    edges = (head_slots, tail_slots, relation_ids, own_negatives, far_negatives, relations)
    (outgoing,) = call(first_kernel, [chunks], request_rows, state, *edges)
    before = []
    for r in range(bit):
        received = swap_pair(outgoing, r)
        grads, grad_rel = call(
            functools.partial(edge_kernel, r, bit, per_device), [chunks, ((count, width), BF16)], received, *edges
        )
        before.append(grad_rel)
        back = swap_pair(grads, r)
        state, outgoing = call(
            functools.partial(middle_kernel, r), [(state.shape, F32), chunks], request_rows, back, state
        )
    received = swap_pair(outgoing, bit)
    masks = other_doms(bit)
    weights, right, values, sums = call(
        functools.partial(edge_kernel, bit, bit, per_device),
        [
            ((2, count, touched), BF16),
            ((2, 2 * count, width), BF16),
            ((rounds * count, width), BF16),
            ((len(masks), touched, width), BF16),
        ],
        received,
        *edges,
        *before,
    )
    came = [lax.ppermute(sums[i], "dom", [(g, g ^ mask) for g in range(doms)]) for i, mask in enumerate(masks)]
    grads, sums, hot = call(
        functools.partial(grad_kernel, bit, per_device),
        [chunks, ((touched, width), F32), ((rows, 2 * touched), BF16)],
        request_rows,
        head_slots,
        tail_slots,
        relation_ids,
        weights,
        right,
        values,
    )
    (grads,) = call(join_kernel, [((touched, wide(width)), BF16)], grads, sums, *came)
    back = swap_pair(grads, bit)
    outs = [((rows, width), F32), ((1, rows), F32), ((per_device, width), F32), ((1, per_device), F32)]
    table, accum, step, relation_accum = call(
        last_kernel,
        outs,
        hot,
        back,
        state,
        in_specs=[VMEM] * 3,
        out_specs=[HBM] * 4,
        scratch_shapes=[pltpu.VMEM(*out) for out in outs] + [pltpu.SemaphoreType.DMA((4,))],
    )
    return (table, accum.reshape(rows), step, relation_accum.reshape(per_device))


def solution(mesh):
    placed = (
        P(("dom", "shard"), None),
        P(("dom", "shard")),
        P(),
        P(("dom", "shard")),
        P(None, ("dom", "shard"), None, None),
        P(None, ("dom", "shard")),
        P(None, ("dom", "shard")),
        P(None, ("dom", "shard")),
        P(None, ("dom", "shard")),
        P(None, ("dom", "shard")),
    )
    return jax.shard_map(
        body,
        mesh=mesh,
        in_specs=placed,
        out_specs=(
            P(("dom", "shard"), None),
            P(("dom", "shard")),
            P(("dom", "shard"), None),
            P(("dom", "shard")),
        ),
        check_vma=False,
    )
```

```python
import functools

import jax
import jax.numpy as jnp
from jax import lax
from jax.experimental import pallas as pl
from jax.experimental.pallas import tpu as pltpu
from jax.sharding import PartitionSpec as P

LEARN_RATE = 0.1
LANES = 128
VMEM_LIMIT = 48 * 2**20
BF16 = jnp.bfloat16
F32 = jnp.float32
NATURAL = (((1,), (0,)), ((), ()))
LAST = (((1,), (1,)), ((), ()))
FIRST = (((0,), (0,)), ((), ()))
HBM = pl.BlockSpec(memory_space=pltpu.HBM)
VMEM = pl.BlockSpec(memory_space=pltpu.VMEM)


def dot(left, right, dims=NATURAL):
    return lax.dot_general(left, right, dims, preferred_element_type=F32)


def iota(shape, axis):
    return lax.broadcasted_iota(jnp.int32, shape, axis)


def one_hot_t(row, count):
    return (iota((count, row.shape[1]), 0) == row).astype(BF16)


def one_hot(column, count):
    return (iota((column.shape[0], count), 1) == column.astype(jnp.int32)).astype(BF16)


def to_column(row):
    n = row.shape[1]
    same = iota((n, n), 0) == iota((n, n), 1)
    return jnp.sum(jnp.where(same, row.astype(F32), 0.0), axis=1, keepdims=True)


def to_row(column):
    n = column.shape[0]
    return jnp.sum(jnp.where(iota((n, n), 0) == iota((n, n), 1), column, 0.0), axis=0, keepdims=True)


def reverse(index, count):
    return (count - 1) ^ index


def spread_order(shards):
    return [reverse(s, shards) for s in range(shards)]


def group_bit(r):
    return (lax.axis_index("dom") >> r) & 1


def renumber(slot, shards, slots):
    half = slots // 2
    return (slot // half % 2) * (shards * half) + reverse(slot // slots, shards) * half + slot % half


def halves(ref, r):
    rows, bit = ref.shape[0] // 2, group_bit(r)
    return [pl.ds(pl.multiple_of(side * rows, rows), rows) for side in (bit, 1 - bit)]


def whole(width):
    return width // LANES * LANES


def unfold(value, width):
    tiles, rest = whole(width), width - whole(width)
    return jnp.concatenate(
        [
            jnp.concatenate(
                [value[:, side * tiles : (side + 1) * tiles], value[:, 2 * tiles + side * rest :][:, :rest]], axis=1
            )
            for side in range(2)
        ],
        axis=0,
    )


def beside(left, right):
    tiles = whole(left.shape[1])
    return jnp.concatenate([left[:, :tiles], right[:, :tiles], left[:, tiles:], right[:, tiles:]], axis=1)


def fold(value):
    n = value.shape[0] // 2
    return beside(value[:n], value[n:])


def request_columns(request_ref, r):
    _, shards, _, slots = request_ref.shape
    half = slots // 2
    sides = [request_ref[r, :, k, :].astype(F32) for k in range(2)]
    flip = group_bit(r) == 1
    rep = jnp.concatenate(
        [
            jnp.broadcast_to(ids[reverse(place, shards)][None], (half, slots))
            for ids in (jnp.where(flip, sides[1], sides[0]), jnp.where(flip, sides[0], sides[1]))
            for place in range(shards)
        ],
        axis=0,
    )
    n = rep.shape[0]
    lane, inside = iota((n, slots), 1), iota((n, slots), 0) % half
    return [
        jnp.sum(jnp.where(lane == side * half + inside, rep, 0.0), axis=1, keepdims=True) for side in range(2)
    ]


def serve(request_ref, r, table, out_ref):
    rows, width = table.shape
    table = table.astype(BF16)
    hot = jnp.concatenate([one_hot(column, rows) for column in request_columns(request_ref, r)], axis=1)
    blank = jnp.zeros((rows, width), BF16)
    both = jnp.concatenate([beside(table, blank), beside(blank, table)], axis=0)
    out_ref[...] = dot(hot, both).astype(BF16)


def first_kernel(request_ref, state_ref, *refs):
    out_ref = refs[-1]
    table = state_ref[: state_ref.shape[0] - 2]
    serve(request_ref, 0, table, out_ref)


def request_hot(request_ref, r, rows):
    return jnp.concatenate([one_hot(column, rows) for column in request_columns(request_ref, r)], axis=0)


def row_update(hot, back_ref, state_ref, dims=FIRST):
    rows, width = state_ref.shape[0] - 2, state_ref.shape[1]
    row_grad = dot(hot, unfold(back_ref[:, : 2 * width], width), dims)
    accum = to_column(state_ref[rows : rows + 1, :rows]) + jnp.mean(row_grad * row_grad, axis=1, keepdims=True)
    return state_ref[:rows] - row_grad * (LEARN_RATE * lax.rsqrt(accum)), to_row(accum)


def middle_kernel(r, request_ref, back_ref, state_ref, state_out, out_ref):
    rows = state_ref.shape[0] - 2
    table, accum = row_update(request_hot(request_ref, r, rows), back_ref, state_ref)
    serve(request_ref, r + 1, table, out_ref)
    state_out[:rows] = table
    state_out[rows:] = state_ref[rows:]
    state_out[rows : rows + 1, :rows] = accum


def slots_of(ref):
    return 2 * ref.shape[0] // (2 * lax.axis_size("shard"))


def by_blocks(function, *arrays):
    step = 16
    parts = [function(*[x[i : i + step] for x in arrays]) for i in range(0, arrays[0].shape[0], step)]
    return [jnp.concatenate(column, axis=0) for column in zip(*parts)]


def query_block(head, tail, rel):
    tail_query = head * rel
    positive = jnp.sum(tail_query * tail, axis=1, keepdims=True)
    return tail_query.astype(BF16), (tail * rel).astype(BF16), -jax.nn.sigmoid(-positive)


def grad_block(head, tail, rel, coeff, back_tail, back_head):
    toward_head = coeff * tail + back_tail
    grad_rel = head * toward_head + tail * back_head
    return (
        (rel * toward_head).astype(BF16),
        (rel * (coeff * head + back_head)).astype(BF16),
        grad_rel.astype(BF16),
    )


def edge_kernel(
    r,
    bit,
    per_device,
    rec_ref,
    head_ref,
    tail_ref,
    rel_ref,
    own_neg_ref,
    far_neg_ref,
    relations_ref,
    *refs,
):
    width = relations_ref.shape[1]
    shards, slots = lax.axis_size("shard"), slots_of(rec_ref)
    touched = shards * slots
    edges, negatives = head_ref.shape[1], own_neg_ref.shape[1]
    own_half, far_half = halves(rec_ref, r)
    own = unfold(rec_ref[own_half], width)
    far = unfold(rec_ref[far_half], width)
    row = slice(r, r + 1)
    ids = rel_ref[row]
    heads, tails = renumber(head_ref[row], shards, slots), renumber(tail_ref[row], shards, slots)
    head = dot(one_hot(to_column(heads), touched), own)
    tail = dot(one_hot(to_column(tails), touched), far)
    rel = dot(one_hot(to_column(ids), relations_ref.shape[0]), relations_ref[...])
    query_tail, query_head, coeff = by_blocks(query_block, head, tail, rel)

    def weights(query, rows, neg_ref):
        hit = iota((touched, negatives), 0) == renumber(neg_ref[row], shards, slots)
        scale = jnp.sum(jnp.where(hit, 1.0 / negatives, 0.0), axis=1, keepdims=True)
        return jax.nn.sigmoid(dot(query, rows, LAST)) * to_row(scale)

    weight_tail = weights(query_tail, far, far_neg_ref)
    weight_head = weights(query_head, own, own_neg_ref)
    back_tail = dot(weight_tail.astype(BF16), far)
    back_head = dot(weight_head.astype(BF16), own)
    grad_head, grad_tail, grad_rel = by_blocks(grad_block, head, tail, rel, coeff, back_tail, back_head)
    right = [
        jnp.concatenate([grad_head, query_head], axis=0),
        jnp.concatenate([grad_tail, query_tail], axis=0),
    ]
    if r < bit:
        out_ref, grad_rel_out = refs
        sides = (own_half, heads, weight_head), (far_half, tails, weight_tail)
        for (half, slot, weight), grads in zip(sides, right):
            out_ref[half] = row_grads(slot, weight, grads)
        grad_rel_out[...] = grad_rel
    else:
        *before_refs, weights_out, right_out, values_out, sums_out = refs
        for side, weight in enumerate((weight_head, weight_tail)):
            weights_out[side], right_out[side] = weight.astype(BF16), right[side]
        values = jnp.concatenate([ref[...] for ref in before_refs] + [grad_rel], axis=0)
        values_out[...] = values
        masks = other_doms(bit)
        for i, mask in enumerate(masks):
            sums_out[i] = relation_sums(rel_ref, values, bit, per_device, mask, rec_ref.shape[0]).astype(BF16)


def other_doms(bit):
    return [mask for mask in range(1, lax.axis_size("dom")) if not mask >> bit & 1]


def relation_sums(rel_ref, values, bit, per_device, mask, rows):
    shards = lax.axis_size("shard")
    ids = jnp.concatenate([rel_ref[r : r + 1] for r in range(rel_ref.shape[0])], axis=1)
    owner = ids // per_device
    dom = owner // shards
    chunk = (dom >> bit & 1) * shards + reverse(owner % shards, shards)
    meant = (dom ^ lax.axis_index("dom") ^ mask) & ~(1 << bit) == 0
    place = jnp.where(meant, chunk * (rows // (2 * shards)) + ids % per_device, -1)
    return dot(one_hot_t(place, rows), values)


def row_grads(slot, weight, grads):
    left = jnp.concatenate([one_hot_t(slot, weight.shape[1]), weight.T.astype(BF16)], axis=1)
    return fold(dot(left, grads).astype(BF16))


def grad_kernel(
    bit,
    per_device,
    request_ref,
    head_ref,
    tail_ref,
    rel_ref,
    weights_ref,
    right_ref,
    values_ref,
    out_ref,
    sums_out,
    hot_out,
):
    shards, slots = lax.axis_size("shard"), slots_of(out_ref)
    for side, (half, slot_ref) in enumerate(zip(halves(out_ref, bit), (head_ref, tail_ref))):
        slot = renumber(slot_ref[bit : bit + 1], shards, slots)
        out_ref[half] = row_grads(slot, weights_ref[side].astype(F32), right_ref[side])
    sums_out[...] = relation_sums(rel_ref, values_ref[...], bit, per_device, 0, out_ref.shape[0])
    hot_out[...] = request_hot(request_ref, bit, hot_out.shape[0]).astype(F32).T.astype(BF16)


def wide(width):
    return 3 * whole(width) + LANES


def join_kernel(grads_ref, sums_ref, *refs):
    *came_refs, out_ref = refs
    width = sums_ref.shape[1]
    tiles, rest = whole(width), width - whole(width)
    total = sums_ref[...]
    for ref in came_refs:
        total = total + ref[...].astype(F32)
    total = total.astype(BF16)
    out_ref[:, : 2 * tiles] = grads_ref[:, : 2 * tiles]
    blank = jnp.zeros((total.shape[0], LANES - 3 * rest), BF16)
    out_ref[:, 2 * tiles : 2 * tiles + LANES] = jnp.concatenate(
        [grads_ref[:, 2 * tiles :], total[:, tiles:], blank], axis=1
    )
    out_ref[:, 2 * tiles + LANES :] = total[:, :tiles]


def last_kernel(hot_ref, back_ref, state_ref, table_out, row_accum_out, step_out, accum_out, *scratch):
    table_ref, row_accum_ref, step_ref, new_accum_ref, sems = scratch
    pairs = (
        (table_ref, table_out),
        (row_accum_ref, row_accum_out),
        (step_ref, step_out),
        (new_accum_ref, accum_out),
    )
    copies = [pltpu.make_async_copy(source, target, sems.at[i]) for i, (source, target) in enumerate(pairs)]
    table, accum = row_update(hot_ref[...], back_ref, state_ref, NATURAL)
    table_ref[...] = table
    copies[0].start()
    row_accum_ref[...] = accum
    copies[1].start()
    per_device, width = step_ref.shape
    rows = slots_of(back_ref) // 2
    tiles, rest = whole(width), width - whole(width)
    parts = jnp.concatenate(
        [back_ref[:, 2 * tiles + LANES :], back_ref[:, 2 * tiles + 2 * rest : 2 * tiles + 3 * rest]], axis=1
    ).astype(F32)
    grad = jnp.sum(parts.reshape(parts.shape[0] // rows, rows, width), axis=0)[:per_device]
    accum = to_column(state_ref[table.shape[0] + 1 :, :per_device]) + jnp.mean(grad * grad, axis=1, keepdims=True)
    step_ref[...] = grad * (-LEARN_RATE * lax.rsqrt(accum))
    copies[2].start()
    new_accum_ref[...] = to_row(accum)
    copies[3].start()
    for copy in copies:
        copy.wait()


def call(kernel, outs, *args, **kwargs):
    return pl.pallas_call(
        kernel,
        out_shape=[jax.ShapeDtypeStruct(shape, kind) for shape, kind in outs],
        compiler_params=pltpu.CompilerParams(vmem_limit_bytes=VMEM_LIMIT),
        **kwargs,
    )(*args)


def swap_pair(value, r):
    doms, shards = lax.axis_size("dom"), lax.axis_size("shard")
    order = spread_order(shards)
    groups = [
        [g * shards + s for g in (low, low ^ (1 << r)) for s in sorted(range(shards), key=order.__getitem__)]
        for low in range(doms)
        if not low >> r & 1
    ]
    return lax.all_to_all(
        value, ("dom", "shard"), split_axis=0, concat_axis=0, axis_index_groups=groups, tiled=True
    )


def body(
    embeddings,
    row_accum,
    relations,
    relation_accum,
    request_rows,
    head_slots,
    tail_slots,
    relation_ids,
    own_negatives,
    far_negatives,
):
    rows, width = embeddings.shape
    doms, shards = lax.axis_size("dom"), lax.axis_size("shard")
    rounds, slots = request_rows.shape[0], request_rows.shape[-1]
    bit = rounds - 1
    per_device = relation_accum.shape[0]
    assert 3 * (width % LANES) <= LANES
    count, touched = head_slots.shape[1], shards * slots
    assert per_device <= slots // 2
    chunks = ((touched, 2 * width), BF16)
    state = (
        jnp.pad(embeddings, ((0, 2), (0, 0)))
        + jnp.pad(row_accum[None], ((rows, 1), (0, width - rows)))
        + jnp.pad(relation_accum[None], ((rows + 1, 0), (0, width - per_device)))
    )
    edges = (head_slots, tail_slots, relation_ids, own_negatives, far_negatives, relations)
    (outgoing,) = call(first_kernel, [chunks], request_rows, state, *edges)
    before = []
    for r in range(bit):
        received = swap_pair(outgoing, r)
        grads, grad_rel = call(
            functools.partial(edge_kernel, r, bit, per_device), [chunks, ((count, width), BF16)], received, *edges
        )
        before.append(grad_rel)
        back = swap_pair(grads, r)
        state, outgoing = call(
            functools.partial(middle_kernel, r), [(state.shape, F32), chunks], request_rows, back, state
        )
    received = swap_pair(outgoing, bit)
    masks = other_doms(bit)
    weights, right, values, sums = call(
        functools.partial(edge_kernel, bit, bit, per_device),
        [
            ((2, count, touched), BF16),
            ((2, 2 * count, width), BF16),
            ((rounds * count, width), BF16),
            ((len(masks), touched, width), BF16),
        ],
        received,
        *edges,
        *before,
    )
    came = [lax.ppermute(sums[i], "dom", [(g, g ^ mask) for g in range(doms)]) for i, mask in enumerate(masks)]
    grads, sums, hot = call(
        functools.partial(grad_kernel, bit, per_device),
        [chunks, ((touched, width), F32), ((rows, 2 * touched), BF16)],
        request_rows,
        head_slots,
        tail_slots,
        relation_ids,
        weights,
        right,
        values,
    )
    (grads,) = call(join_kernel, [((touched, wide(width)), BF16)], grads, sums, *came)
    back = swap_pair(grads, bit)
    outs = [((rows, width), F32), ((1, rows), F32), ((per_device, width), F32), ((1, per_device), F32)]
    table, accum, step, relation_accum = call(
        last_kernel,
        outs,
        hot,
        back,
        state,
        in_specs=[VMEM] * 3,
        out_specs=[HBM] * 4,
        scratch_shapes=[pltpu.VMEM(*out) for out in outs] + [pltpu.SemaphoreType.DMA((4,))],
    )
    return (table, accum.reshape(rows), step, relation_accum.reshape(per_device))


def solution(mesh):
    placed = (
        P(("dom", "shard"), None),
        P(("dom", "shard")),
        P(),
        P(("dom", "shard")),
        P(None, ("dom", "shard"), None, None),
        P(None, ("dom", "shard")),
        P(None, ("dom", "shard")),
        P(None, ("dom", "shard")),
        P(None, ("dom", "shard")),
        P(None, ("dom", "shard")),
    )
    return jax.shard_map(
        body,
        mesh=mesh,
        in_specs=placed,
        out_specs=(
            P(("dom", "shard"), None),
            P(("dom", "shard")),
            P(("dom", "shard"), None),
            P(("dom", "shard")),
        ),
        check_vma=False,
    )
```

```python
import functools

import jax
import jax.numpy as jnp
from jax import lax
from jax.experimental import pallas as pl
from jax.experimental.pallas import tpu as pltpu
from jax.sharding import PartitionSpec as P

LEARN_RATE = 0.1
LANES = 128
VMEM_LIMIT = 48 * 2**20
BF16 = jnp.bfloat16
F32 = jnp.float32
NATURAL = (((1,), (0,)), ((), ()))
LAST = (((1,), (1,)), ((), ()))
FIRST = (((0,), (0,)), ((), ()))
HBM = pl.BlockSpec(memory_space=pltpu.HBM)
VMEM = pl.BlockSpec(memory_space=pltpu.VMEM)


def dot(left, right, dims=NATURAL):
    return lax.dot_general(left, right, dims, preferred_element_type=F32)


def iota(shape, axis):
    return lax.broadcasted_iota(jnp.int32, shape, axis)


def one_hot_t(row, count):
    return (iota((count, row.shape[1]), 0) == row).astype(BF16)


def one_hot(column, count):
    return (iota((column.shape[0], count), 1) == column.astype(jnp.int32)).astype(BF16)


def to_column(row):
    n = row.shape[1]
    same = iota((n, n), 0) == iota((n, n), 1)
    return jnp.sum(jnp.where(same, row.astype(F32), 0.0), axis=1, keepdims=True)


def to_row(column):
    n = column.shape[0]
    return jnp.sum(jnp.where(iota((n, n), 0) == iota((n, n), 1), column, 0.0), axis=0, keepdims=True)


def reverse(index, count):
    return index


def spread_order(shards):
    return [reverse(s, shards) for s in range(shards)]


def group_bit(r):
    return 1 - ((lax.axis_index("dom") >> r) & 1)


def renumber(slot, shards, slots):
    half = slots // 2
    return (slot // half % 2) * (shards * half) + reverse(slot // slots, shards) * half + slot % half


def halves(ref, r):
    rows, bit = ref.shape[0] // 2, group_bit(r)
    return [pl.ds(pl.multiple_of(side * rows, rows), rows) for side in (bit, 1 - bit)]


def whole(width):
    return width // LANES * LANES


def unfold(value, width):
    tiles, rest = whole(width), width - whole(width)
    return jnp.concatenate(
        [
            jnp.concatenate(
                [value[:, side * tiles : (side + 1) * tiles], value[:, 2 * tiles + side * rest :][:, :rest]], axis=1
            )
            for side in range(2)
        ],
        axis=0,
    )


def beside(left, right):
    tiles = whole(left.shape[1])
    return jnp.concatenate([left[:, :tiles], right[:, :tiles], left[:, tiles:], right[:, tiles:]], axis=1)


def fold(value):
    n = value.shape[0] // 2
    return beside(value[:n], value[n:])


def request_columns(request_ref, r):
    _, shards, _, slots = request_ref.shape
    half = slots // 2
    sides = [request_ref[r, :, k, :].astype(F32) for k in range(2)]
    flip = group_bit(r) == 1
    rep = jnp.concatenate(
        [
            jnp.broadcast_to(ids[reverse(place, shards)][None], (half, slots))
            for ids in (jnp.where(flip, sides[1], sides[0]), jnp.where(flip, sides[0], sides[1]))
            for place in range(shards)
        ],
        axis=0,
    )
    n = rep.shape[0]
    lane, inside = iota((n, slots), 1), iota((n, slots), 0) % half
    return [
        jnp.sum(jnp.where(lane == side * half + inside, rep, 0.0), axis=1, keepdims=True) for side in range(2)
    ]


def serve(request_ref, r, table, out_ref):
    rows, width = table.shape
    table = table.astype(BF16)
    hot = jnp.concatenate([one_hot(column, rows) for column in request_columns(request_ref, r)], axis=1)
    blank = jnp.zeros((rows, width), BF16)
    both = jnp.concatenate([beside(table, blank), beside(blank, table)], axis=0)
    out_ref[...] = dot(hot, both).astype(BF16)


def first_kernel(request_ref, state_ref, *refs):
    out_ref = refs[-1]
    table = state_ref[: state_ref.shape[0] - 2]
    serve(request_ref, 0, table, out_ref)


def request_hot(request_ref, r, rows):
    return jnp.concatenate([one_hot(column, rows) for column in request_columns(request_ref, r)], axis=0)


def row_update(hot, back_ref, state_ref, dims=FIRST):
    rows, width = state_ref.shape[0] - 2, state_ref.shape[1]
    row_grad = dot(hot, unfold(back_ref[:, : 2 * width], width), dims)
    accum = to_column(state_ref[rows : rows + 1, :rows]) + jnp.mean(row_grad * row_grad, axis=1, keepdims=True)
    return state_ref[:rows] - row_grad * (LEARN_RATE * lax.rsqrt(accum)), to_row(accum)


def middle_kernel(r, request_ref, back_ref, state_ref, state_out, out_ref):
    rows = state_ref.shape[0] - 2
    table, accum = row_update(request_hot(request_ref, r, rows), back_ref, state_ref)
    serve(request_ref, r + 1, table, out_ref)
    state_out[:rows] = table
    state_out[rows:] = state_ref[rows:]
    state_out[rows : rows + 1, :rows] = accum


def slots_of(ref):
    return 2 * ref.shape[0] // (2 * lax.axis_size("shard"))


def by_blocks(function, *arrays):
    step = 16
    parts = [function(*[x[i : i + step] for x in arrays]) for i in range(0, arrays[0].shape[0], step)]
    return [jnp.concatenate(column, axis=0) for column in zip(*parts)]


def query_block(head, tail, rel):
    tail_query = head * rel
    positive = jnp.sum(tail_query * tail, axis=1, keepdims=True)
    return tail_query.astype(BF16), (tail * rel).astype(BF16), -jax.nn.sigmoid(-positive)


def grad_block(head, tail, rel, coeff, back_tail, back_head):
    toward_head = coeff * tail + back_tail
    grad_rel = head * toward_head + tail * back_head
    return (
        (rel * toward_head).astype(BF16),
        (rel * (coeff * head + back_head)).astype(BF16),
        grad_rel.astype(BF16),
    )


def edge_kernel(
    r,
    bit,
    per_device,
    rec_ref,
    head_ref,
    tail_ref,
    rel_ref,
    own_neg_ref,
    far_neg_ref,
    relations_ref,
    *refs,
):
    width = relations_ref.shape[1]
    shards, slots = lax.axis_size("shard"), slots_of(rec_ref)
    touched = shards * slots
    edges, negatives = head_ref.shape[1], own_neg_ref.shape[1]
    own_half, far_half = halves(rec_ref, r)
    own = unfold(rec_ref[own_half], width)
    far = unfold(rec_ref[far_half], width)
    row = slice(r, r + 1)
    ids = rel_ref[row]
    heads, tails = renumber(head_ref[row], shards, slots), renumber(tail_ref[row], shards, slots)
    head = dot(one_hot(to_column(heads), touched), own)
    tail = dot(one_hot(to_column(tails), touched), far)
    rel = dot(one_hot(to_column(ids), relations_ref.shape[0]), relations_ref[...])
    query_tail, query_head, coeff = by_blocks(query_block, head, tail, rel)

    def weights(query, rows, neg_ref):
        hit = iota((touched, negatives), 0) == renumber(neg_ref[row], shards, slots)
        scale = jnp.sum(jnp.where(hit, 1.0 / negatives, 0.0), axis=1, keepdims=True)
        return jax.nn.sigmoid(dot(query, rows, LAST)) * to_row(scale)

    weight_tail = weights(query_tail, far, far_neg_ref)
    weight_head = weights(query_head, own, own_neg_ref)
    back_tail = dot(weight_tail.astype(BF16), far)
    back_head = dot(weight_head.astype(BF16), own)
    grad_head, grad_tail, grad_rel = by_blocks(grad_block, head, tail, rel, coeff, back_tail, back_head)
    right = [
        jnp.concatenate([grad_head, query_head], axis=0),
        jnp.concatenate([grad_tail, query_tail], axis=0),
    ]
    if r < bit:
        out_ref, grad_rel_out = refs
        sides = (own_half, heads, weight_head), (far_half, tails, weight_tail)
        for (half, slot, weight), grads in zip(sides, right):
            out_ref[half] = row_grads(slot, weight, grads)
        grad_rel_out[...] = grad_rel
    else:
        *before_refs, weights_out, right_out, values_out, sums_out = refs
        for side, weight in enumerate((weight_head, weight_tail)):
            weights_out[side], right_out[side] = weight.astype(BF16), right[side]
        values = jnp.concatenate([ref[...] for ref in before_refs] + [grad_rel], axis=0)
        values_out[...] = values
        masks = other_doms(bit)
        for i, mask in enumerate(masks):
            sums_out[i] = relation_sums(rel_ref, values, bit, per_device, mask, rec_ref.shape[0]).astype(BF16)


def other_doms(bit):
    return [mask for mask in range(1, lax.axis_size("dom")) if not mask >> bit & 1]


def relation_sums(rel_ref, values, bit, per_device, mask, rows):
    shards = lax.axis_size("shard")
    ids = jnp.concatenate([rel_ref[r : r + 1] for r in range(rel_ref.shape[0])], axis=1)
    owner = ids // per_device
    dom = owner // shards
    chunk = (1 - (dom >> bit & 1)) * shards + reverse(owner % shards, shards)
    meant = (dom ^ lax.axis_index("dom") ^ mask) & ~(1 << bit) == 0
    place = jnp.where(meant, chunk * (rows // (2 * shards)) + ids % per_device, -1)
    return dot(one_hot_t(place, rows), values)


def row_grads(slot, weight, grads):
    left = jnp.concatenate([one_hot_t(slot, weight.shape[1]), weight.T.astype(BF16)], axis=1)
    return fold(dot(left, grads).astype(BF16))


def grad_kernel(
    bit,
    per_device,
    request_ref,
    head_ref,
    tail_ref,
    rel_ref,
    weights_ref,
    right_ref,
    values_ref,
    out_ref,
    sums_out,
    hot_out,
):
    shards, slots = lax.axis_size("shard"), slots_of(out_ref)
    for side, (half, slot_ref) in enumerate(zip(halves(out_ref, bit), (head_ref, tail_ref))):
        slot = renumber(slot_ref[bit : bit + 1], shards, slots)
        out_ref[half] = row_grads(slot, weights_ref[side].astype(F32), right_ref[side])
    sums_out[...] = relation_sums(rel_ref, values_ref[...], bit, per_device, 0, out_ref.shape[0])
    hot_out[...] = request_hot(request_ref, bit, hot_out.shape[0]).astype(F32).T.astype(BF16)


def wide(width):
    return 3 * whole(width) + LANES


def join_kernel(grads_ref, sums_ref, *refs):
    *came_refs, out_ref = refs
    width = sums_ref.shape[1]
    tiles, rest = whole(width), width - whole(width)
    total = sums_ref[...]
    for ref in came_refs:
        total = total + ref[...].astype(F32)
    total = total.astype(BF16)
    out_ref[:, : 2 * tiles] = grads_ref[:, : 2 * tiles]
    blank = jnp.zeros((total.shape[0], LANES - 3 * rest), BF16)
    out_ref[:, 2 * tiles : 2 * tiles + LANES] = jnp.concatenate(
        [grads_ref[:, 2 * tiles :], total[:, tiles:], blank], axis=1
    )
    out_ref[:, 2 * tiles + LANES :] = total[:, :tiles]


def last_kernel(hot_ref, back_ref, state_ref, table_out, row_accum_out, step_out, accum_out, *scratch):
    table_ref, row_accum_ref, step_ref, new_accum_ref, sems = scratch
    pairs = (
        (table_ref, table_out),
        (row_accum_ref, row_accum_out),
        (step_ref, step_out),
        (new_accum_ref, accum_out),
    )
    copies = [pltpu.make_async_copy(source, target, sems.at[i]) for i, (source, target) in enumerate(pairs)]
    table, accum = row_update(hot_ref[...], back_ref, state_ref, NATURAL)
    table_ref[...] = table
    copies[0].start()
    row_accum_ref[...] = accum
    copies[1].start()
    per_device, width = step_ref.shape
    rows = slots_of(back_ref) // 2
    tiles, rest = whole(width), width - whole(width)
    parts = jnp.concatenate(
        [back_ref[:, 2 * tiles + LANES :], back_ref[:, 2 * tiles + 2 * rest : 2 * tiles + 3 * rest]], axis=1
    ).astype(F32)
    grad = jnp.sum(parts.reshape(parts.shape[0] // rows, rows, width), axis=0)[:per_device]
    accum = to_column(state_ref[table.shape[0] + 1 :, :per_device]) + jnp.mean(grad * grad, axis=1, keepdims=True)
    step_ref[...] = grad * (-LEARN_RATE * lax.rsqrt(accum))
    copies[2].start()
    new_accum_ref[...] = to_row(accum)
    copies[3].start()
    for copy in copies:
        copy.wait()


def call(kernel, outs, *args, **kwargs):
    return pl.pallas_call(
        kernel,
        out_shape=[jax.ShapeDtypeStruct(shape, kind) for shape, kind in outs],
        compiler_params=pltpu.CompilerParams(vmem_limit_bytes=VMEM_LIMIT),
        **kwargs,
    )(*args)


def swap_pair(value, r):
    doms, shards = lax.axis_size("dom"), lax.axis_size("shard")
    order = spread_order(shards)
    groups = [
        [g * shards + s for g in (low ^ (1 << r), low) for s in sorted(range(shards), key=order.__getitem__)]
        for low in range(doms)
        if not low >> r & 1
    ]
    return lax.all_to_all(
        value, ("dom", "shard"), split_axis=0, concat_axis=0, axis_index_groups=groups, tiled=True
    )


def body(
    embeddings,
    row_accum,
    relations,
    relation_accum,
    request_rows,
    head_slots,
    tail_slots,
    relation_ids,
    own_negatives,
    far_negatives,
):
    rows, width = embeddings.shape
    doms, shards = lax.axis_size("dom"), lax.axis_size("shard")
    rounds, slots = request_rows.shape[0], request_rows.shape[-1]
    bit = rounds - 1
    per_device = relation_accum.shape[0]
    assert 3 * (width % LANES) <= LANES
    count, touched = head_slots.shape[1], shards * slots
    assert per_device <= slots // 2
    chunks = ((touched, 2 * width), BF16)
    state = (
        jnp.pad(embeddings, ((0, 2), (0, 0)))
        + jnp.pad(row_accum[None], ((rows, 1), (0, width - rows)))
        + jnp.pad(relation_accum[None], ((rows + 1, 0), (0, width - per_device)))
    )
    edges = (head_slots, tail_slots, relation_ids, own_negatives, far_negatives, relations)
    (outgoing,) = call(first_kernel, [chunks], request_rows, state, *edges)
    before = []
    for r in range(bit):
        received = swap_pair(outgoing, r)
        grads, grad_rel = call(
            functools.partial(edge_kernel, r, bit, per_device), [chunks, ((count, width), BF16)], received, *edges
        )
        before.append(grad_rel)
        back = swap_pair(grads, r)
        state, outgoing = call(
            functools.partial(middle_kernel, r), [(state.shape, F32), chunks], request_rows, back, state
        )
    received = swap_pair(outgoing, bit)
    masks = other_doms(bit)
    weights, right, values, sums = call(
        functools.partial(edge_kernel, bit, bit, per_device),
        [
            ((2, count, touched), BF16),
            ((2, 2 * count, width), BF16),
            ((rounds * count, width), BF16),
            ((len(masks), touched, width), BF16),
        ],
        received,
        *edges,
        *before,
    )
    came = [lax.ppermute(sums[i], "dom", [(g, g ^ mask) for g in range(doms)]) for i, mask in enumerate(masks)]
    grads, sums, hot = call(
        functools.partial(grad_kernel, bit, per_device),
        [chunks, ((touched, width), F32), ((rows, 2 * touched), BF16)],
        request_rows,
        head_slots,
        tail_slots,
        relation_ids,
        weights,
        right,
        values,
    )
    (grads,) = call(join_kernel, [((touched, wide(width)), BF16)], grads, sums, *came)
    back = swap_pair(grads, bit)
    outs = [((rows, width), F32), ((1, rows), F32), ((per_device, width), F32), ((1, per_device), F32)]
    table, accum, step, relation_accum = call(
        last_kernel,
        outs,
        hot,
        back,
        state,
        in_specs=[VMEM] * 3,
        out_specs=[HBM] * 4,
        scratch_shapes=[pltpu.VMEM(*out) for out in outs] + [pltpu.SemaphoreType.DMA((4,))],
    )
    return (table, accum.reshape(rows), step, relation_accum.reshape(per_device))


def solution(mesh):
    placed = (
        P(("dom", "shard"), None),
        P(("dom", "shard")),
        P(),
        P(("dom", "shard")),
        P(None, ("dom", "shard"), None, None),
        P(None, ("dom", "shard")),
        P(None, ("dom", "shard")),
        P(None, ("dom", "shard")),
        P(None, ("dom", "shard")),
        P(None, ("dom", "shard")),
    )
    return jax.shard_map(
        body,
        mesh=mesh,
        in_specs=placed,
        out_specs=(
            P(("dom", "shard"), None),
            P(("dom", "shard")),
            P(("dom", "shard"), None),
            P(("dom", "shard")),
        ),
        check_vma=False,
    )
```

```python
import functools

import jax
import jax.numpy as jnp
from jax import lax
from jax.experimental import pallas as pl
from jax.experimental.pallas import tpu as pltpu
from jax.sharding import PartitionSpec as P

LEARN_RATE = 0.1
LANES = 128
VMEM_LIMIT = 48 * 2**20
BF16 = jnp.bfloat16
F32 = jnp.float32
NATURAL = (((1,), (0,)), ((), ()))
LAST = (((1,), (1,)), ((), ()))
FIRST = (((0,), (0,)), ((), ()))
HBM = pl.BlockSpec(memory_space=pltpu.HBM)
VMEM = pl.BlockSpec(memory_space=pltpu.VMEM)


def dot(left, right, dims=NATURAL):
    return lax.dot_general(left, right, dims, preferred_element_type=F32)


def iota(shape, axis):
    return lax.broadcasted_iota(jnp.int32, shape, axis)


def one_hot_t(row, count):
    return (iota((count, row.shape[1]), 0) == row).astype(BF16)


def one_hot(column, count):
    return (iota((column.shape[0], count), 1) == column.astype(jnp.int32)).astype(BF16)


def to_column(row):
    n = row.shape[1]
    same = iota((n, n), 0) == iota((n, n), 1)
    return jnp.sum(jnp.where(same, row.astype(F32), 0.0), axis=1, keepdims=True)


def to_row(column):
    n = column.shape[0]
    return jnp.sum(jnp.where(iota((n, n), 0) == iota((n, n), 1), column, 0.0), axis=0, keepdims=True)


def reverse(index, count):
    swap = (index >> 1 ^ index >> 2) & 1 if count >= 8 else 0
    return (count - 1) ^ index ^ swap * 6


def spread_order(shards):
    return [reverse(s, shards) for s in range(shards)]


def group_bit(r):
    return 1 - ((lax.axis_index("dom") >> r) & 1)


def renumber(slot, shards, slots):
    half = slots // 2
    return (slot // half % 2) * (shards * half) + reverse(slot // slots, shards) * half + slot % half


def halves(ref, r):
    rows, bit = ref.shape[0] // 2, group_bit(r)
    return [pl.ds(pl.multiple_of(side * rows, rows), rows) for side in (bit, 1 - bit)]


def whole(width):
    return width // LANES * LANES


def unfold(value, width):
    tiles, rest = whole(width), width - whole(width)
    return jnp.concatenate(
        [
            jnp.concatenate(
                [value[:, side * tiles : (side + 1) * tiles], value[:, 2 * tiles + side * rest :][:, :rest]], axis=1
            )
            for side in range(2)
        ],
        axis=0,
    )


def beside(left, right):
    tiles = whole(left.shape[1])
    return jnp.concatenate([left[:, :tiles], right[:, :tiles], left[:, tiles:], right[:, tiles:]], axis=1)


def fold(value):
    n = value.shape[0] // 2
    return beside(value[:n], value[n:])


def request_columns(request_ref, r):
    _, shards, _, slots = request_ref.shape
    half = slots // 2
    sides = [request_ref[r, :, k, :].astype(F32) for k in range(2)]
    flip = group_bit(r) == 1
    rep = jnp.concatenate(
        [
            jnp.broadcast_to(ids[reverse(place, shards)][None], (half, slots))
            for ids in (jnp.where(flip, sides[1], sides[0]), jnp.where(flip, sides[0], sides[1]))
            for place in range(shards)
        ],
        axis=0,
    )
    n = rep.shape[0]
    lane, inside = iota((n, slots), 1), iota((n, slots), 0) % half
    return [
        jnp.sum(jnp.where(lane == side * half + inside, rep, 0.0), axis=1, keepdims=True) for side in range(2)
    ]


def serve(request_ref, r, table, out_ref):
    rows, width = table.shape
    table = table.astype(BF16)
    hot = jnp.concatenate([one_hot(column, rows) for column in request_columns(request_ref, r)], axis=1)
    blank = jnp.zeros((rows, width), BF16)
    both = jnp.concatenate([beside(table, blank), beside(blank, table)], axis=0)
    out_ref[...] = dot(hot, both).astype(BF16)


def first_kernel(request_ref, state_ref, *refs):
    out_ref = refs[-1]
    table = state_ref[: state_ref.shape[0] - 2]
    serve(request_ref, 0, table, out_ref)


def request_hot(request_ref, r, rows):
    return jnp.concatenate([one_hot(column, rows) for column in request_columns(request_ref, r)], axis=0)


def row_update(hot, back_ref, state_ref, dims=FIRST):
    rows, width = state_ref.shape[0] - 2, state_ref.shape[1]
    row_grad = dot(hot, unfold(back_ref[:, : 2 * width], width), dims)
    accum = to_column(state_ref[rows : rows + 1, :rows]) + jnp.mean(row_grad * row_grad, axis=1, keepdims=True)
    return state_ref[:rows] - row_grad * (LEARN_RATE * lax.rsqrt(accum)), to_row(accum)


def middle_kernel(r, request_ref, back_ref, state_ref, state_out, out_ref):
    rows = state_ref.shape[0] - 2
    table, accum = row_update(request_hot(request_ref, r, rows), back_ref, state_ref)
    serve(request_ref, r + 1, table, out_ref)
    state_out[:rows] = table
    state_out[rows:] = state_ref[rows:]
    state_out[rows : rows + 1, :rows] = accum


def slots_of(ref):
    return 2 * ref.shape[0] // (2 * lax.axis_size("shard"))


def by_blocks(function, *arrays):
    step = 16
    parts = [function(*[x[i : i + step] for x in arrays]) for i in range(0, arrays[0].shape[0], step)]
    return [jnp.concatenate(column, axis=0) for column in zip(*parts)]


def query_block(head, tail, rel):
    tail_query = head * rel
    positive = jnp.sum(tail_query * tail, axis=1, keepdims=True)
    return tail_query.astype(BF16), (tail * rel).astype(BF16), -jax.nn.sigmoid(-positive)


def grad_block(head, tail, rel, coeff, back_tail, back_head):
    toward_head = coeff * tail + back_tail
    grad_rel = head * toward_head + tail * back_head
    return (
        (rel * toward_head).astype(BF16),
        (rel * (coeff * head + back_head)).astype(BF16),
        grad_rel.astype(BF16),
    )


def edge_kernel(
    r,
    bit,
    per_device,
    rec_ref,
    head_ref,
    tail_ref,
    rel_ref,
    own_neg_ref,
    far_neg_ref,
    relations_ref,
    *refs,
):
    width = relations_ref.shape[1]
    shards, slots = lax.axis_size("shard"), slots_of(rec_ref)
    touched = shards * slots
    edges, negatives = head_ref.shape[1], own_neg_ref.shape[1]
    own_half, far_half = halves(rec_ref, r)
    own = unfold(rec_ref[own_half], width)
    far = unfold(rec_ref[far_half], width)
    row = slice(r, r + 1)
    ids = rel_ref[row]
    heads, tails = renumber(head_ref[row], shards, slots), renumber(tail_ref[row], shards, slots)
    head = dot(one_hot(to_column(heads), touched), own)
    tail = dot(one_hot(to_column(tails), touched), far)
    rel = dot(one_hot(to_column(ids), relations_ref.shape[0]), relations_ref[...])
    query_tail, query_head, coeff = by_blocks(query_block, head, tail, rel)

    def weights(query, rows, neg_ref):
        hit = iota((touched, negatives), 0) == renumber(neg_ref[row], shards, slots)
        scale = jnp.sum(jnp.where(hit, 1.0 / negatives, 0.0), axis=1, keepdims=True)
        return jax.nn.sigmoid(dot(query, rows, LAST)) * to_row(scale)

    weight_tail = weights(query_tail, far, far_neg_ref)
    weight_head = weights(query_head, own, own_neg_ref)
    back_tail = dot(weight_tail.astype(BF16), far)
    back_head = dot(weight_head.astype(BF16), own)
    grad_head, grad_tail, grad_rel = by_blocks(grad_block, head, tail, rel, coeff, back_tail, back_head)
    right = [
        jnp.concatenate([grad_head, query_head], axis=0),
        jnp.concatenate([grad_tail, query_tail], axis=0),
    ]
    if r < bit:
        out_ref, grad_rel_out = refs
        sides = (own_half, heads, weight_head), (far_half, tails, weight_tail)
        for (half, slot, weight), grads in zip(sides, right):
            out_ref[half] = row_grads(slot, weight, grads)
        grad_rel_out[...] = grad_rel
    else:
        *before_refs, weights_out, right_out, values_out, sums_out = refs
        for side, weight in enumerate((weight_head, weight_tail)):
            weights_out[side], right_out[side] = weight.astype(BF16), right[side]
        values = jnp.concatenate([ref[...] for ref in before_refs] + [grad_rel], axis=0)
        values_out[...] = values
        masks = other_doms(bit)
        for i, mask in enumerate(masks):
            sums_out[i] = relation_sums(rel_ref, values, bit, per_device, mask, rec_ref.shape[0]).astype(BF16)


def other_doms(bit):
    return [mask for mask in range(1, lax.axis_size("dom")) if not mask >> bit & 1]


def relation_sums(rel_ref, values, bit, per_device, mask, rows):
    shards = lax.axis_size("shard")
    ids = jnp.concatenate([rel_ref[r : r + 1] for r in range(rel_ref.shape[0])], axis=1)
    owner = ids // per_device
    dom = owner // shards
    chunk = (1 - (dom >> bit & 1)) * shards + reverse(owner % shards, shards)
    meant = (dom ^ lax.axis_index("dom") ^ mask) & ~(1 << bit) == 0
    place = jnp.where(meant, chunk * (rows // (2 * shards)) + ids % per_device, -1)
    return dot(one_hot_t(place, rows), values)


def row_grads(slot, weight, grads):
    left = jnp.concatenate([one_hot_t(slot, weight.shape[1]), weight.T.astype(BF16)], axis=1)
    return fold(dot(left, grads).astype(BF16))


def grad_kernel(
    bit,
    per_device,
    request_ref,
    head_ref,
    tail_ref,
    rel_ref,
    weights_ref,
    right_ref,
    values_ref,
    out_ref,
    sums_out,
    hot_out,
):
    shards, slots = lax.axis_size("shard"), slots_of(out_ref)
    for side, (half, slot_ref) in enumerate(zip(halves(out_ref, bit), (head_ref, tail_ref))):
        slot = renumber(slot_ref[bit : bit + 1], shards, slots)
        out_ref[half] = row_grads(slot, weights_ref[side].astype(F32), right_ref[side])
    sums_out[...] = relation_sums(rel_ref, values_ref[...], bit, per_device, 0, out_ref.shape[0])
    hot_out[...] = request_hot(request_ref, bit, hot_out.shape[0]).astype(F32).T.astype(BF16)


def wide(width):
    return 3 * whole(width) + LANES


def join_kernel(grads_ref, sums_ref, *refs):
    *came_refs, out_ref = refs
    width = sums_ref.shape[1]
    tiles, rest = whole(width), width - whole(width)
    total = sums_ref[...]
    for ref in came_refs:
        total = total + ref[...].astype(F32)
    total = total.astype(BF16)
    out_ref[:, : 2 * tiles] = grads_ref[:, : 2 * tiles]
    blank = jnp.zeros((total.shape[0], LANES - 3 * rest), BF16)
    out_ref[:, 2 * tiles : 2 * tiles + LANES] = jnp.concatenate(
        [grads_ref[:, 2 * tiles :], total[:, tiles:], blank], axis=1
    )
    out_ref[:, 2 * tiles + LANES :] = total[:, :tiles]


def last_kernel(hot_ref, back_ref, state_ref, table_out, row_accum_out, step_out, accum_out, *scratch):
    table_ref, row_accum_ref, step_ref, new_accum_ref, sems = scratch
    pairs = (
        (table_ref, table_out),
        (row_accum_ref, row_accum_out),
        (step_ref, step_out),
        (new_accum_ref, accum_out),
    )
    copies = [pltpu.make_async_copy(source, target, sems.at[i]) for i, (source, target) in enumerate(pairs)]
    table, accum = row_update(hot_ref[...], back_ref, state_ref, NATURAL)
    table_ref[...] = table
    copies[0].start()
    row_accum_ref[...] = accum
    copies[1].start()
    per_device, width = step_ref.shape
    rows = slots_of(back_ref) // 2
    tiles, rest = whole(width), width - whole(width)
    parts = jnp.concatenate(
        [back_ref[:, 2 * tiles + LANES :], back_ref[:, 2 * tiles + 2 * rest : 2 * tiles + 3 * rest]], axis=1
    ).astype(F32)
    grad = jnp.sum(parts.reshape(parts.shape[0] // rows, rows, width), axis=0)[:per_device]
    accum = to_column(state_ref[table.shape[0] + 1 :, :per_device]) + jnp.mean(grad * grad, axis=1, keepdims=True)
    step_ref[...] = grad * (-LEARN_RATE * lax.rsqrt(accum))
    copies[2].start()
    new_accum_ref[...] = to_row(accum)
    copies[3].start()
    for copy in copies:
        copy.wait()


def call(kernel, outs, *args, **kwargs):
    return pl.pallas_call(
        kernel,
        out_shape=[jax.ShapeDtypeStruct(shape, kind) for shape, kind in outs],
        compiler_params=pltpu.CompilerParams(vmem_limit_bytes=VMEM_LIMIT),
        **kwargs,
    )(*args)


def swap_pair(value, r):
    doms, shards = lax.axis_size("dom"), lax.axis_size("shard")
    order = spread_order(shards)
    groups = [
        [g * shards + s for g in (low ^ (1 << r), low) for s in sorted(range(shards), key=order.__getitem__)]
        for low in range(doms)
        if not low >> r & 1
    ]
    return lax.all_to_all(
        value, ("dom", "shard"), split_axis=0, concat_axis=0, axis_index_groups=groups, tiled=True
    )


def body(
    embeddings,
    row_accum,
    relations,
    relation_accum,
    request_rows,
    head_slots,
    tail_slots,
    relation_ids,
    own_negatives,
    far_negatives,
):
    rows, width = embeddings.shape
    doms, shards = lax.axis_size("dom"), lax.axis_size("shard")
    rounds, slots = request_rows.shape[0], request_rows.shape[-1]
    bit = rounds - 1
    per_device = relation_accum.shape[0]
    assert 3 * (width % LANES) <= LANES
    count, touched = head_slots.shape[1], shards * slots
    assert per_device <= slots // 2
    chunks = ((touched, 2 * width), BF16)
    state = (
        jnp.pad(embeddings, ((0, 2), (0, 0)))
        + jnp.pad(row_accum[None], ((rows, 1), (0, width - rows)))
        + jnp.pad(relation_accum[None], ((rows + 1, 0), (0, width - per_device)))
    )
    edges = (head_slots, tail_slots, relation_ids, own_negatives, far_negatives, relations)
    (outgoing,) = call(first_kernel, [chunks], request_rows, state, *edges)
    before = []
    for r in range(bit):
        received = swap_pair(outgoing, r)
        grads, grad_rel = call(
            functools.partial(edge_kernel, r, bit, per_device), [chunks, ((count, width), BF16)], received, *edges
        )
        before.append(grad_rel)
        back = swap_pair(grads, r)
        state, outgoing = call(
            functools.partial(middle_kernel, r), [(state.shape, F32), chunks], request_rows, back, state
        )
    received = swap_pair(outgoing, bit)
    masks = other_doms(bit)
    weights, right, values, sums = call(
        functools.partial(edge_kernel, bit, bit, per_device),
        [
            ((2, count, touched), BF16),
            ((2, 2 * count, width), BF16),
            ((rounds * count, width), BF16),
            ((len(masks), touched, width), BF16),
        ],
        received,
        *edges,
        *before,
    )
    came = [lax.ppermute(sums[i], "dom", [(g, g ^ mask) for g in range(doms)]) for i, mask in enumerate(masks)]
    grads, sums, hot = call(
        functools.partial(grad_kernel, bit, per_device),
        [chunks, ((touched, width), F32), ((rows, 2 * touched), BF16)],
        request_rows,
        head_slots,
        tail_slots,
        relation_ids,
        weights,
        right,
        values,
    )
    (grads,) = call(join_kernel, [((touched, wide(width)), BF16)], grads, sums, *came)
    back = swap_pair(grads, bit)
    outs = [((rows, width), F32), ((1, rows), F32), ((per_device, width), F32), ((1, per_device), F32)]
    table, accum, step, relation_accum = call(
        last_kernel,
        outs,
        hot,
        back,
        state,
        in_specs=[VMEM] * 3,
        out_specs=[HBM] * 4,
        scratch_shapes=[pltpu.VMEM(*out) for out in outs] + [pltpu.SemaphoreType.DMA((4,))],
    )
    return (table, accum.reshape(rows), step, relation_accum.reshape(per_device))


def solution(mesh):
    placed = (
        P(("dom", "shard"), None),
        P(("dom", "shard")),
        P(),
        P(("dom", "shard")),
        P(None, ("dom", "shard"), None, None),
        P(None, ("dom", "shard")),
        P(None, ("dom", "shard")),
        P(None, ("dom", "shard")),
        P(None, ("dom", "shard")),
        P(None, ("dom", "shard")),
    )
    return jax.shard_map(
        body,
        mesh=mesh,
        in_specs=placed,
        out_specs=(
            P(("dom", "shard"), None),
            P(("dom", "shard")),
            P(("dom", "shard"), None),
            P(("dom", "shard")),
        ),
        check_vma=False,
    )
```

```python
import functools

import jax
import jax.numpy as jnp
from jax import lax
from jax.experimental import pallas as pl
from jax.experimental.pallas import tpu as pltpu
from jax.sharding import PartitionSpec as P

LEARN_RATE = 0.1
LANES = 128
VMEM_LIMIT = 48 * 2**20
BF16 = jnp.bfloat16
F32 = jnp.float32
NATURAL = (((1,), (0,)), ((), ()))
LAST = (((1,), (1,)), ((), ()))
FIRST = (((0,), (0,)), ((), ()))
HBM = pl.BlockSpec(memory_space=pltpu.HBM)
VMEM = pl.BlockSpec(memory_space=pltpu.VMEM)


def dot(left, right, dims=NATURAL):
    return lax.dot_general(left, right, dims, preferred_element_type=F32)


def iota(shape, axis):
    return lax.broadcasted_iota(jnp.int32, shape, axis)


def one_hot_t(row, count):
    return (iota((count, row.shape[1]), 0) == row).astype(BF16)


def one_hot(column, count):
    return (iota((column.shape[0], count), 1) == column.astype(jnp.int32)).astype(BF16)


def to_column(row):
    n = row.shape[1]
    same = iota((n, n), 0) == iota((n, n), 1)
    return jnp.sum(jnp.where(same, row.astype(F32), 0.0), axis=1, keepdims=True)


def to_row(column):
    n = column.shape[0]
    return jnp.sum(jnp.where(iota((n, n), 0) == iota((n, n), 1), column, 0.0), axis=0, keepdims=True)


def reverse(index, count):
    return (count - 1) ^ index


def spread_order(shards):
    return [reverse(s, shards) for s in range(shards)]


def half_of(dom, r):
    return (1 - (dom >> r & 1)) ^ (dom & 1 if r else 0)


def group_bit(r):
    return half_of(lax.axis_index("dom"), r)


def renumber(slot, shards, slots):
    half = slots // 2
    return (slot // half % 2) * (shards * half) + reverse(slot // slots, shards) * half + slot % half


def halves(ref, r):
    rows, bit = ref.shape[0] // 2, group_bit(r)
    return [pl.ds(pl.multiple_of(side * rows, rows), rows) for side in (bit, 1 - bit)]


def whole(width):
    return width // LANES * LANES


def unfold(value, width):
    tiles, rest = whole(width), width - whole(width)
    return jnp.concatenate(
        [
            jnp.concatenate(
                [value[:, side * tiles : (side + 1) * tiles], value[:, 2 * tiles + side * rest :][:, :rest]], axis=1
            )
            for side in range(2)
        ],
        axis=0,
    )


def beside(left, right):
    tiles = whole(left.shape[1])
    return jnp.concatenate([left[:, :tiles], right[:, :tiles], left[:, tiles:], right[:, tiles:]], axis=1)


def fold(value):
    n = value.shape[0] // 2
    return beside(value[:n], value[n:])


def request_columns(request_ref, r):
    _, shards, _, slots = request_ref.shape
    half = slots // 2
    sides = [request_ref[r, :, k, :].astype(F32) for k in range(2)]
    flip = group_bit(r) == 1
    rep = jnp.concatenate(
        [
            jnp.broadcast_to(ids[reverse(place, shards)][None], (half, slots))
            for ids in (jnp.where(flip, sides[1], sides[0]), jnp.where(flip, sides[0], sides[1]))
            for place in range(shards)
        ],
        axis=0,
    )
    n = rep.shape[0]
    lane, inside = iota((n, slots), 1), iota((n, slots), 0) % half
    return [
        jnp.sum(jnp.where(lane == side * half + inside, rep, 0.0), axis=1, keepdims=True) for side in range(2)
    ]


def serve(request_ref, r, table, out_ref):
    rows, width = table.shape
    table = table.astype(BF16)
    hot = jnp.concatenate([one_hot(column, rows) for column in request_columns(request_ref, r)], axis=1)
    blank = jnp.zeros((rows, width), BF16)
    both = jnp.concatenate([beside(table, blank), beside(blank, table)], axis=0)
    out_ref[...] = dot(hot, both).astype(BF16)


def first_kernel(request_ref, state_ref, *refs):
    out_ref = refs[-1]
    table = state_ref[: state_ref.shape[0] - 2]
    serve(request_ref, 0, table, out_ref)


def request_hot(request_ref, r, rows):
    return jnp.concatenate([one_hot(column, rows) for column in request_columns(request_ref, r)], axis=0)


def row_update(hot, back_ref, state_ref, dims=FIRST):
    rows, width = state_ref.shape[0] - 2, state_ref.shape[1]
    row_grad = dot(hot, unfold(back_ref[:, : 2 * width], width), dims)
    accum = to_column(state_ref[rows : rows + 1, :rows]) + jnp.mean(row_grad * row_grad, axis=1, keepdims=True)
    return state_ref[:rows] - row_grad * (LEARN_RATE * lax.rsqrt(accum)), to_row(accum)


def middle_kernel(r, request_ref, back_ref, state_ref, state_out, out_ref):
    rows = state_ref.shape[0] - 2
    table, accum = row_update(request_hot(request_ref, r, rows), back_ref, state_ref)
    serve(request_ref, r + 1, table, out_ref)
    state_out[:rows] = table
    state_out[rows:] = state_ref[rows:]
    state_out[rows : rows + 1, :rows] = accum


def slots_of(ref):
    return 2 * ref.shape[0] // (2 * lax.axis_size("shard"))


def by_blocks(function, *arrays):
    step = 16
    parts = [function(*[x[i : i + step] for x in arrays]) for i in range(0, arrays[0].shape[0], step)]
    return [jnp.concatenate(column, axis=0) for column in zip(*parts)]


def query_block(head, tail, rel):
    tail_query = head * rel
    positive = jnp.sum(tail_query * tail, axis=1, keepdims=True)
    return tail_query.astype(BF16), (tail * rel).astype(BF16), -jax.nn.sigmoid(-positive)


def grad_block(head, tail, rel, coeff, back_tail, back_head):
    toward_head = coeff * tail + back_tail
    grad_rel = head * toward_head + tail * back_head
    return (
        (rel * toward_head).astype(BF16),
        (rel * (coeff * head + back_head)).astype(BF16),
        grad_rel.astype(BF16),
    )


def edge_kernel(
    r,
    bit,
    per_device,
    rec_ref,
    head_ref,
    tail_ref,
    rel_ref,
    own_neg_ref,
    far_neg_ref,
    relations_ref,
    *refs,
):
    width = relations_ref.shape[1]
    shards, slots = lax.axis_size("shard"), slots_of(rec_ref)
    touched = shards * slots
    edges, negatives = head_ref.shape[1], own_neg_ref.shape[1]
    own_half, far_half = halves(rec_ref, r)
    own = unfold(rec_ref[own_half], width)
    far = unfold(rec_ref[far_half], width)
    row = slice(r, r + 1)
    ids = rel_ref[row]
    heads, tails = renumber(head_ref[row], shards, slots), renumber(tail_ref[row], shards, slots)
    head = dot(one_hot(to_column(heads), touched), own)
    tail = dot(one_hot(to_column(tails), touched), far)
    rel = dot(one_hot(to_column(ids), relations_ref.shape[0]), relations_ref[...])
    query_tail, query_head, coeff = by_blocks(query_block, head, tail, rel)

    def weights(query, rows, neg_ref):
        hit = iota((touched, negatives), 0) == renumber(neg_ref[row], shards, slots)
        scale = jnp.sum(jnp.where(hit, 1.0 / negatives, 0.0), axis=1, keepdims=True)
        return jax.nn.sigmoid(dot(query, rows, LAST)) * to_row(scale)

    weight_tail = weights(query_tail, far, far_neg_ref)
    weight_head = weights(query_head, own, own_neg_ref)
    back_tail = dot(weight_tail.astype(BF16), far)
    back_head = dot(weight_head.astype(BF16), own)
    grad_head, grad_tail, grad_rel = by_blocks(grad_block, head, tail, rel, coeff, back_tail, back_head)
    right = [
        jnp.concatenate([grad_head, query_head], axis=0),
        jnp.concatenate([grad_tail, query_tail], axis=0),
    ]
    if r < bit:
        out_ref, grad_rel_out = refs
        sides = (own_half, heads, weight_head), (far_half, tails, weight_tail)
        for (half, slot, weight), grads in zip(sides, right):
            out_ref[half] = row_grads(slot, weight, grads)
        grad_rel_out[...] = grad_rel
    else:
        *before_refs, weights_out, right_out, values_out, sums_out = refs
        for side, weight in enumerate((weight_head, weight_tail)):
            weights_out[side], right_out[side] = weight.astype(BF16), right[side]
        values = jnp.concatenate([ref[...] for ref in before_refs] + [grad_rel], axis=0)
        values_out[...] = values
        masks = other_doms(bit)
        for i, mask in enumerate(masks):
            sums_out[i] = relation_sums(rel_ref, values, bit, per_device, mask, rec_ref.shape[0]).astype(BF16)


def other_doms(bit):
    return [mask for mask in range(1, lax.axis_size("dom")) if not mask >> bit & 1]


def relation_sums(rel_ref, values, bit, per_device, mask, rows):
    shards = lax.axis_size("shard")
    ids = jnp.concatenate([rel_ref[r : r + 1] for r in range(rel_ref.shape[0])], axis=1)
    owner = ids // per_device
    dom = owner // shards
    chunk = half_of(dom, bit) * shards + reverse(owner % shards, shards)
    meant = (dom ^ lax.axis_index("dom") ^ mask) & ~(1 << bit) == 0
    place = jnp.where(meant, chunk * (rows // (2 * shards)) + ids % per_device, -1)
    return dot(one_hot_t(place, rows), values)


def row_grads(slot, weight, grads):
    left = jnp.concatenate([one_hot_t(slot, weight.shape[1]), weight.T.astype(BF16)], axis=1)
    return fold(dot(left, grads).astype(BF16))


def grad_kernel(
    bit,
    per_device,
    request_ref,
    head_ref,
    tail_ref,
    rel_ref,
    weights_ref,
    right_ref,
    values_ref,
    out_ref,
    sums_out,
    hot_out,
):
    shards, slots = lax.axis_size("shard"), slots_of(out_ref)
    for side, (half, slot_ref) in enumerate(zip(halves(out_ref, bit), (head_ref, tail_ref))):
        slot = renumber(slot_ref[bit : bit + 1], shards, slots)
        out_ref[half] = row_grads(slot, weights_ref[side].astype(F32), right_ref[side])
    sums_out[...] = relation_sums(rel_ref, values_ref[...], bit, per_device, 0, out_ref.shape[0])
    hot_out[...] = request_hot(request_ref, bit, hot_out.shape[0]).astype(F32).T.astype(BF16)


def wide(width):
    return 3 * whole(width) + LANES


def join_kernel(grads_ref, sums_ref, *refs):
    *came_refs, out_ref = refs
    width = sums_ref.shape[1]
    tiles, rest = whole(width), width - whole(width)
    total = sums_ref[...]
    for ref in came_refs:
        total = total + ref[...].astype(F32)
    total = total.astype(BF16)
    out_ref[:, : 2 * tiles] = grads_ref[:, : 2 * tiles]
    blank = jnp.zeros((total.shape[0], LANES - 3 * rest), BF16)
    out_ref[:, 2 * tiles : 2 * tiles + LANES] = jnp.concatenate(
        [grads_ref[:, 2 * tiles :], total[:, tiles:], blank], axis=1
    )
    out_ref[:, 2 * tiles + LANES :] = total[:, :tiles]


def last_kernel(hot_ref, back_ref, state_ref, table_out, row_accum_out, step_out, accum_out, *scratch):
    table_ref, row_accum_ref, step_ref, new_accum_ref, sems = scratch
    pairs = (
        (table_ref, table_out),
        (row_accum_ref, row_accum_out),
        (step_ref, step_out),
        (new_accum_ref, accum_out),
    )
    copies = [pltpu.make_async_copy(source, target, sems.at[i]) for i, (source, target) in enumerate(pairs)]
    table, accum = row_update(hot_ref[...], back_ref, state_ref, NATURAL)
    table_ref[...] = table
    copies[0].start()
    row_accum_ref[...] = accum
    copies[1].start()
    per_device, width = step_ref.shape
    rows = slots_of(back_ref) // 2
    tiles, rest = whole(width), width - whole(width)
    parts = jnp.concatenate(
        [back_ref[:, 2 * tiles + LANES :], back_ref[:, 2 * tiles + 2 * rest : 2 * tiles + 3 * rest]], axis=1
    ).astype(F32)
    grad = jnp.sum(parts.reshape(parts.shape[0] // rows, rows, width), axis=0)[:per_device]
    accum = to_column(state_ref[table.shape[0] + 1 :, :per_device]) + jnp.mean(grad * grad, axis=1, keepdims=True)
    step_ref[...] = grad * (-LEARN_RATE * lax.rsqrt(accum))
    copies[2].start()
    new_accum_ref[...] = to_row(accum)
    copies[3].start()
    for copy in copies:
        copy.wait()


def call(kernel, outs, *args, **kwargs):
    return pl.pallas_call(
        kernel,
        out_shape=[jax.ShapeDtypeStruct(shape, kind) for shape, kind in outs],
        compiler_params=pltpu.CompilerParams(vmem_limit_bytes=VMEM_LIMIT),
        **kwargs,
    )(*args)


def swap_pair(value, r):
    doms, shards = lax.axis_size("dom"), lax.axis_size("shard")
    order = spread_order(shards)
    groups = [
        [g * shards + s for g in sorted((low, low ^ (1 << r)), key=lambda g: half_of(g, r)) for s in sorted(range(shards), key=order.__getitem__)]
        for low in range(doms)
        if not low >> r & 1
    ]
    return lax.all_to_all(
        value, ("dom", "shard"), split_axis=0, concat_axis=0, axis_index_groups=groups, tiled=True
    )


def body(
    embeddings,
    row_accum,
    relations,
    relation_accum,
    request_rows,
    head_slots,
    tail_slots,
    relation_ids,
    own_negatives,
    far_negatives,
):
    rows, width = embeddings.shape
    doms, shards = lax.axis_size("dom"), lax.axis_size("shard")
    rounds, slots = request_rows.shape[0], request_rows.shape[-1]
    bit = rounds - 1
    per_device = relation_accum.shape[0]
    assert 3 * (width % LANES) <= LANES
    count, touched = head_slots.shape[1], shards * slots
    assert per_device <= slots // 2
    chunks = ((touched, 2 * width), BF16)
    state = (
        jnp.pad(embeddings, ((0, 2), (0, 0)))
        + jnp.pad(row_accum[None], ((rows, 1), (0, width - rows)))
        + jnp.pad(relation_accum[None], ((rows + 1, 0), (0, width - per_device)))
    )
    edges = (head_slots, tail_slots, relation_ids, own_negatives, far_negatives, relations)
    (outgoing,) = call(first_kernel, [chunks], request_rows, state, *edges)
    before = []
    for r in range(bit):
        received = swap_pair(outgoing, r)
        grads, grad_rel = call(
            functools.partial(edge_kernel, r, bit, per_device), [chunks, ((count, width), BF16)], received, *edges
        )
        before.append(grad_rel)
        back = swap_pair(grads, r)
        state, outgoing = call(
            functools.partial(middle_kernel, r), [(state.shape, F32), chunks], request_rows, back, state
        )
    received = swap_pair(outgoing, bit)
    masks = other_doms(bit)
    weights, right, values, sums = call(
        functools.partial(edge_kernel, bit, bit, per_device),
        [
            ((2, count, touched), BF16),
            ((2, 2 * count, width), BF16),
            ((rounds * count, width), BF16),
            ((len(masks), touched, width), BF16),
        ],
        received,
        *edges,
        *before,
    )
    came = [lax.ppermute(sums[i], "dom", [(g, g ^ mask) for g in range(doms)]) for i, mask in enumerate(masks)]
    grads, sums, hot = call(
        functools.partial(grad_kernel, bit, per_device),
        [chunks, ((touched, width), F32), ((rows, 2 * touched), BF16)],
        request_rows,
        head_slots,
        tail_slots,
        relation_ids,
        weights,
        right,
        values,
    )
    (grads,) = call(join_kernel, [((touched, wide(width)), BF16)], grads, sums, *came)
    back = swap_pair(grads, bit)
    outs = [((rows, width), F32), ((1, rows), F32), ((per_device, width), F32), ((1, per_device), F32)]
    table, accum, step, relation_accum = call(
        last_kernel,
        outs,
        hot,
        back,
        state,
        in_specs=[VMEM] * 3,
        out_specs=[HBM] * 4,
        scratch_shapes=[pltpu.VMEM(*out) for out in outs] + [pltpu.SemaphoreType.DMA((4,))],
    )
    return (table, accum.reshape(rows), step, relation_accum.reshape(per_device))


def solution(mesh):
    placed = (
        P(("dom", "shard"), None),
        P(("dom", "shard")),
        P(),
        P(("dom", "shard")),
        P(None, ("dom", "shard"), None, None),
        P(None, ("dom", "shard")),
        P(None, ("dom", "shard")),
        P(None, ("dom", "shard")),
        P(None, ("dom", "shard")),
        P(None, ("dom", "shard")),
    )
    return jax.shard_map(
        body,
        mesh=mesh,
        in_specs=placed,
        out_specs=(
            P(("dom", "shard"), None),
            P(("dom", "shard")),
            P(("dom", "shard"), None),
            P(("dom", "shard")),
        ),
        check_vma=False,
    )
```

```python
import functools

import jax
import jax.numpy as jnp
from jax import lax
from jax.experimental import pallas as pl
from jax.experimental.pallas import tpu as pltpu
from jax.sharding import PartitionSpec as P

LEARN_RATE = 0.1
LANES = 128
VMEM_LIMIT = 48 * 2**20
BF16 = jnp.bfloat16
F32 = jnp.float32
NATURAL = (((1,), (0,)), ((), ()))
LAST = (((1,), (1,)), ((), ()))
FIRST = (((0,), (0,)), ((), ()))
HBM = pl.BlockSpec(memory_space=pltpu.HBM)
VMEM = pl.BlockSpec(memory_space=pltpu.VMEM)


def dot(left, right, dims=NATURAL):
    return lax.dot_general(left, right, dims, preferred_element_type=F32)


def iota(shape, axis):
    return lax.broadcasted_iota(jnp.int32, shape, axis)


def one_hot_t(row, count):
    return (iota((count, row.shape[1]), 0) == row).astype(BF16)


def one_hot(column, count):
    return (iota((column.shape[0], count), 1) == column.astype(jnp.int32)).astype(BF16)


def to_column(row):
    n = row.shape[1]
    same = iota((n, n), 0) == iota((n, n), 1)
    return jnp.sum(jnp.where(same, row.astype(F32), 0.0), axis=1, keepdims=True)


def to_row(column):
    n = column.shape[0]
    return jnp.sum(jnp.where(iota((n, n), 0) == iota((n, n), 1), column, 0.0), axis=0, keepdims=True)


def reverse(index, count):
    return (count - 1) ^ index


def spread_order(shards):
    return [reverse(s, shards) for s in range(shards)]


def group_bit(r):
    return 1 - ((lax.axis_index("dom") >> r) & 1)


def renumber(slot, shards, slots):
    half = slots // 2
    return (slot // half % 2) * (shards * half) + reverse(slot // slots, shards) * half + slot % half


def halves(ref, r):
    rows, bit = ref.shape[0] // 2, group_bit(r)
    return [pl.ds(pl.multiple_of(side * rows, rows), rows) for side in (bit, 1 - bit)]


def whole(width):
    return width // LANES * LANES


def unfold(value, width):
    tiles, rest = whole(width), width - whole(width)
    return jnp.concatenate(
        [
            jnp.concatenate(
                [value[:, side * tiles : (side + 1) * tiles], value[:, 2 * tiles + side * rest :][:, :rest]], axis=1
            )
            for side in range(2)
        ],
        axis=0,
    )


def beside(left, right):
    tiles = whole(left.shape[1])
    return jnp.concatenate([left[:, :tiles], right[:, :tiles], left[:, tiles:], right[:, tiles:]], axis=1)


def fold(value):
    n = value.shape[0] // 2
    return beside(value[:n], value[n:])


def request_columns(request_ref, r):
    _, shards, _, slots = request_ref.shape
    half = slots // 2
    sides = [request_ref[r, :, k, :].astype(F32) for k in range(2)]
    flip = group_bit(r) == 1
    rep = jnp.concatenate(
        [
            jnp.broadcast_to(ids[reverse(place, shards)][None], (half, slots))
            for ids in (jnp.where(flip, sides[1], sides[0]), jnp.where(flip, sides[0], sides[1]))
            for place in range(shards)
        ],
        axis=0,
    )
    n = rep.shape[0]
    lane, inside = iota((n, slots), 1), iota((n, slots), 0) % half
    return [
        jnp.sum(jnp.where(lane == side * half + inside, rep, 0.0), axis=1, keepdims=True) for side in range(2)
    ]


def serve(request_ref, r, table, out_ref):
    rows, width = table.shape
    table = table.astype(BF16)
    hot = jnp.concatenate([one_hot(column, rows) for column in request_columns(request_ref, r)], axis=1)
    blank = jnp.zeros((rows, width), BF16)
    both = jnp.concatenate([beside(table, blank), beside(blank, table)], axis=0)
    out_ref[...] = dot(hot, both).astype(BF16)


def first_kernel(request_ref, state_ref, *refs):
    out_ref = refs[-1]
    table = state_ref[: state_ref.shape[0] - 2]
    serve(request_ref, 0, table, out_ref)


def request_hot(request_ref, r, rows):
    return jnp.concatenate([one_hot(column, rows) for column in request_columns(request_ref, r)], axis=0)


def row_update(hot, back_ref, state_ref, dims=FIRST):
    rows, width = state_ref.shape[0] - 2, state_ref.shape[1]
    row_grad = dot(hot, unfold(back_ref[:, : 2 * width], width), dims)
    accum = to_column(state_ref[rows : rows + 1, :rows]) + jnp.mean(row_grad * row_grad, axis=1, keepdims=True)
    return state_ref[:rows] - row_grad * (LEARN_RATE * lax.rsqrt(accum)), to_row(accum)


def middle_kernel(r, request_ref, back_ref, state_ref, state_out, out_ref):
    rows = state_ref.shape[0] - 2
    table, accum = row_update(request_hot(request_ref, r, rows), back_ref, state_ref)
    serve(request_ref, r + 1, table, out_ref)
    state_out[:rows] = table
    state_out[rows:] = state_ref[rows:]
    state_out[rows : rows + 1, :rows] = accum


def slots_of(ref):
    return 2 * ref.shape[0] // (2 * lax.axis_size("shard"))


def by_blocks(function, *arrays):
    step = 16
    parts = [function(*[x[i : i + step] for x in arrays]) for i in range(0, arrays[0].shape[0], step)]
    return [jnp.concatenate(column, axis=0) for column in zip(*parts)]


def query_block(head, tail, rel):
    tail_query = head * rel
    positive = jnp.sum(tail_query * tail, axis=1, keepdims=True)
    return tail_query.astype(BF16), (tail * rel).astype(BF16), -jax.nn.sigmoid(-positive)


def grad_block(head, tail, rel, coeff, back_tail, back_head):
    toward_head = coeff * tail + back_tail
    grad_rel = head * toward_head + tail * back_head
    return (
        (rel * toward_head).astype(BF16),
        (rel * (coeff * head + back_head)).astype(BF16),
        grad_rel.astype(BF16),
    )


def edge_kernel(
    r,
    bit,
    per_device,
    rec_ref,
    head_ref,
    tail_ref,
    rel_ref,
    own_neg_ref,
    far_neg_ref,
    relations_ref,
    *refs,
):
    width = relations_ref.shape[1]
    shards, slots = lax.axis_size("shard"), slots_of(rec_ref)
    touched = shards * slots
    edges, negatives = head_ref.shape[1], own_neg_ref.shape[1]
    own_half, far_half = halves(rec_ref, r)
    own = unfold(rec_ref[own_half], width)
    far = unfold(rec_ref[far_half], width)
    row = slice(r, r + 1)
    ids = rel_ref[row]
    heads, tails = renumber(head_ref[row], shards, slots), renumber(tail_ref[row], shards, slots)
    head = dot(one_hot(to_column(heads), touched), own)
    tail = dot(one_hot(to_column(tails), touched), far)
    rel = dot(one_hot(to_column(ids), relations_ref.shape[0]), relations_ref[...])
    query_tail, query_head, coeff = by_blocks(query_block, head, tail, rel)

    def weights(query, rows, neg_ref):
        hit = iota((touched, negatives), 0) == renumber(neg_ref[row], shards, slots)
        scale = jnp.sum(jnp.where(hit, 1.0 / negatives, 0.0), axis=1, keepdims=True)
        return jax.nn.sigmoid(dot(query, rows, LAST)) * to_row(scale)

    weight_tail = weights(query_tail, far, far_neg_ref)
    weight_head = weights(query_head, own, own_neg_ref)
    back_tail = dot(weight_tail.astype(BF16), far)
    back_head = dot(weight_head.astype(BF16), own)
    grad_head, grad_tail, grad_rel = by_blocks(grad_block, head, tail, rel, coeff, back_tail, back_head)
    right = [
        jnp.concatenate([grad_head, query_head], axis=0),
        jnp.concatenate([grad_tail, query_tail], axis=0),
    ]
    if r < bit:
        out_ref, grad_rel_out = refs
        sides = (own_half, heads, weight_head), (far_half, tails, weight_tail)
        for (half, slot, weight), grads in zip(sides, right):
            out_ref[half] = row_grads(slot, weight, grads)
        grad_rel_out[...] = grad_rel
    else:
        *before_refs, weights_out, right_out, values_out, sums_out = refs
        for side, weight in enumerate((weight_head, weight_tail)):
            weights_out[side], right_out[side] = weight.astype(BF16), right[side]
        values = jnp.concatenate([ref[...] for ref in before_refs] + [grad_rel], axis=0)
        values_out[...] = values
        masks = other_doms(bit)
        for i, mask in enumerate(masks):
            sums_out[i] = relation_sums(rel_ref, values, bit, per_device, mask, rec_ref.shape[0]).astype(BF16)


def other_doms(bit):
    return [mask for mask in range(1, lax.axis_size("dom")) if not mask >> bit & 1]


def relation_sums(rel_ref, values, bit, per_device, mask, rows):
    shards = lax.axis_size("shard")
    ids = jnp.concatenate([rel_ref[r : r + 1] for r in range(rel_ref.shape[0])], axis=1)
    owner = ids // per_device
    dom = owner // shards
    chunk = (1 - (dom >> bit & 1)) * shards + reverse(owner % shards, shards)
    meant = (dom ^ lax.axis_index("dom") ^ mask) & ~(1 << bit) == 0
    rows_each = rows // (2 * shards)
    spot, free = ids % per_device, rows_each - per_device
    hot = one_hot_t(
        jnp.concatenate(
            [
                jnp.where(meant, chunk * rows_each + spot, -1),
                jnp.where(meant, chunk * rows_each + per_device + spot % free, -1),
            ],
            axis=1,
        ),
        rows,
    )
    third = values[:, 2 * LANES : 3 * LANES].astype(F32)
    first = to_column(spot) < free
    split = [jnp.where(first, third, 0.0).astype(BF16), jnp.where(first, 0.0, third).astype(BF16)]
    right = jnp.concatenate([values[:, : 2 * LANES], jnp.concatenate(split, axis=1)], axis=0)
    rest = dot(hot[:, : values.shape[0]], values[:, 3 * LANES :])
    return jnp.concatenate([dot(hot, right), rest], axis=1)


def unpack_sums(total, per_device):
    free = total.shape[0] - per_device
    third = jnp.concatenate(
        [total[per_device:, :LANES], total[per_device : 2 * per_device - free, LANES : 2 * LANES]], axis=0
    )
    return jnp.concatenate([total[:per_device, : 2 * LANES], third, total[:per_device, 2 * LANES :]], axis=1)


def row_grads(slot, weight, grads):
    left = jnp.concatenate([one_hot_t(slot, weight.shape[1]), weight.T.astype(BF16)], axis=1)
    return fold(dot(left, grads).astype(BF16))


def grad_kernel(
    bit,
    per_device,
    request_ref,
    head_ref,
    tail_ref,
    rel_ref,
    weights_ref,
    right_ref,
    values_ref,
    out_ref,
    sums_out,
    hot_out,
):
    shards, slots = lax.axis_size("shard"), slots_of(out_ref)
    for side, (half, slot_ref) in enumerate(zip(halves(out_ref, bit), (head_ref, tail_ref))):
        slot = renumber(slot_ref[bit : bit + 1], shards, slots)
        out_ref[half] = row_grads(slot, weights_ref[side].astype(F32), right_ref[side])
    sums_out[...] = relation_sums(rel_ref, values_ref[...], bit, per_device, 0, out_ref.shape[0])
    hot_out[...] = request_hot(request_ref, bit, hot_out.shape[0]).astype(F32).T.astype(BF16)


def sums_width(width):
    return width - LANES


def wide(width):
    return 2 * whole(width) + 3 * LANES


def join_kernel(grads_ref, sums_ref, *refs):
    *came_refs, out_ref = refs
    tiles = out_ref.shape[1] - 3 * LANES
    total = sums_ref[...]
    for ref in came_refs:
        total = total + ref[...].astype(F32)
    total = total.astype(BF16)
    rests = jnp.concatenate([grads_ref[:, tiles:], total[:, 2 * LANES :]], axis=1)
    blank = jnp.zeros((total.shape[0], LANES - rests.shape[1]), BF16)
    out_ref[:, :tiles] = grads_ref[:, :tiles]
    out_ref[:, tiles : tiles + LANES] = jnp.concatenate([rests, blank], axis=1)
    out_ref[:, tiles + LANES :] = total[:, : 2 * LANES]


def last_kernel(hot_ref, back_ref, state_ref, table_out, row_accum_out, step_out, accum_out, *scratch):
    table_ref, row_accum_ref, step_ref, new_accum_ref, sems = scratch
    pairs = (
        (table_ref, table_out),
        (row_accum_ref, row_accum_out),
        (step_ref, step_out),
        (new_accum_ref, accum_out),
    )
    copies = [pltpu.make_async_copy(source, target, sems.at[i]) for i, (source, target) in enumerate(pairs)]
    table, accum = row_update(hot_ref[...], back_ref, state_ref, NATURAL)
    table_ref[...] = table
    copies[0].start()
    row_accum_ref[...] = accum
    copies[1].start()
    per_device, width = step_ref.shape
    rows = slots_of(back_ref) // 2
    tiles, rest = 2 * whole(width), width - whole(width)
    parts = jnp.concatenate(
        [back_ref[:, tiles + LANES :], back_ref[:, tiles + 2 * rest : tiles + 3 * rest]], axis=1
    ).astype(F32)
    total = jnp.sum(parts.reshape(parts.shape[0] // rows, rows, parts.shape[1]), axis=0)
    grad = unpack_sums(total, per_device)
    accum = to_column(state_ref[table.shape[0] + 1 :, :per_device]) + jnp.mean(grad * grad, axis=1, keepdims=True)
    step_ref[...] = grad * (-LEARN_RATE * lax.rsqrt(accum))
    copies[2].start()
    new_accum_ref[...] = to_row(accum)
    copies[3].start()
    for copy in copies:
        copy.wait()


def call(kernel, outs, *args, **kwargs):
    return pl.pallas_call(
        kernel,
        out_shape=[jax.ShapeDtypeStruct(shape, kind) for shape, kind in outs],
        compiler_params=pltpu.CompilerParams(vmem_limit_bytes=VMEM_LIMIT),
        **kwargs,
    )(*args)


def swap_pair(value, r):
    doms, shards = lax.axis_size("dom"), lax.axis_size("shard")
    order = spread_order(shards)
    groups = [
        [g * shards + s for g in (low ^ (1 << r), low) for s in sorted(range(shards), key=order.__getitem__)]
        for low in range(doms)
        if not low >> r & 1
    ]
    return lax.all_to_all(
        value, ("dom", "shard"), split_axis=0, concat_axis=0, axis_index_groups=groups, tiled=True
    )


def body(
    embeddings,
    row_accum,
    relations,
    relation_accum,
    request_rows,
    head_slots,
    tail_slots,
    relation_ids,
    own_negatives,
    far_negatives,
):
    rows, width = embeddings.shape
    doms, shards = lax.axis_size("dom"), lax.axis_size("shard")
    rounds, slots = request_rows.shape[0], request_rows.shape[-1]
    bit = rounds - 1
    per_device = relation_accum.shape[0]
    assert 3 * (width % LANES) <= LANES
    count, touched = head_slots.shape[1], shards * slots
    free = slots // 2 - per_device
    assert free < per_device <= 2 * free and whole(width) == 3 * LANES
    chunks = ((touched, 2 * width), BF16)
    state = (
        jnp.pad(embeddings, ((0, 2), (0, 0)))
        + jnp.pad(row_accum[None], ((rows, 1), (0, width - rows)))
        + jnp.pad(relation_accum[None], ((rows + 1, 0), (0, width - per_device)))
    )
    edges = (head_slots, tail_slots, relation_ids, own_negatives, far_negatives, relations)
    (outgoing,) = call(first_kernel, [chunks], request_rows, state, *edges)
    before = []
    for r in range(bit):
        received = swap_pair(outgoing, r)
        grads, grad_rel = call(
            functools.partial(edge_kernel, r, bit, per_device), [chunks, ((count, width), BF16)], received, *edges
        )
        before.append(grad_rel)
        back = swap_pair(grads, r)
        state, outgoing = call(
            functools.partial(middle_kernel, r), [(state.shape, F32), chunks], request_rows, back, state
        )
    received = swap_pair(outgoing, bit)
    masks = other_doms(bit)
    weights, right, values, sums = call(
        functools.partial(edge_kernel, bit, bit, per_device),
        [
            ((2, count, touched), BF16),
            ((2, 2 * count, width), BF16),
            ((rounds * count, width), BF16),
            ((len(masks), touched, sums_width(width)), BF16),
        ],
        received,
        *edges,
        *before,
    )
    came = [lax.ppermute(sums[i], "dom", [(g, g ^ mask) for g in range(doms)]) for i, mask in enumerate(masks)]
    grads, sums, hot = call(
        functools.partial(grad_kernel, bit, per_device),
        [chunks, ((touched, sums_width(width)), F32), ((rows, 2 * touched), BF16)],
        request_rows,
        head_slots,
        tail_slots,
        relation_ids,
        weights,
        right,
        values,
    )
    (grads,) = call(join_kernel, [((touched, wide(width)), BF16)], grads, sums, *came)
    back = swap_pair(grads, bit)
    outs = [((rows, width), F32), ((1, rows), F32), ((per_device, width), F32), ((1, per_device), F32)]
    table, accum, step, relation_accum = call(
        last_kernel,
        outs,
        hot,
        back,
        state,
        in_specs=[VMEM] * 3,
        out_specs=[HBM] * 4,
        scratch_shapes=[pltpu.VMEM(*out) for out in outs] + [pltpu.SemaphoreType.DMA((4,))],
    )
    return (table, accum.reshape(rows), step, relation_accum.reshape(per_device))


def solution(mesh):
    placed = (
        P(("dom", "shard"), None),
        P(("dom", "shard")),
        P(),
        P(("dom", "shard")),
        P(None, ("dom", "shard"), None, None),
        P(None, ("dom", "shard")),
        P(None, ("dom", "shard")),
        P(None, ("dom", "shard")),
        P(None, ("dom", "shard")),
        P(None, ("dom", "shard")),
    )
    return jax.shard_map(
        body,
        mesh=mesh,
        in_specs=placed,
        out_specs=(
            P(("dom", "shard"), None),
            P(("dom", "shard")),
            P(("dom", "shard"), None),
            P(("dom", "shard")),
        ),
        check_vma=False,
    )
```

```python
import functools

import jax
import jax.numpy as jnp
from jax import lax
from jax.experimental import pallas as pl
from jax.experimental.pallas import tpu as pltpu
from jax.sharding import PartitionSpec as P

LEARN_RATE = 0.1
LANES = 128
VMEM_LIMIT = 48 * 2**20
BF16 = jnp.bfloat16
F32 = jnp.float32
NATURAL = (((1,), (0,)), ((), ()))
LAST = (((1,), (1,)), ((), ()))
FIRST = (((0,), (0,)), ((), ()))
HBM = pl.BlockSpec(memory_space=pltpu.HBM)
VMEM = pl.BlockSpec(memory_space=pltpu.VMEM)


def dot(left, right, dims=NATURAL):
    return lax.dot_general(left, right, dims, preferred_element_type=F32)


def iota(shape, axis):
    return lax.broadcasted_iota(jnp.int32, shape, axis)


def one_hot_t(row, count):
    return (iota((count, row.shape[1]), 0) == row).astype(BF16)


def one_hot(column, count):
    return (iota((column.shape[0], count), 1) == column.astype(jnp.int32)).astype(BF16)


def to_column(row):
    n = row.shape[1]
    same = iota((n, n), 0) == iota((n, n), 1)
    return jnp.sum(jnp.where(same, row.astype(F32), 0.0), axis=1, keepdims=True)


def to_row(column):
    n = column.shape[0]
    return jnp.sum(jnp.where(iota((n, n), 0) == iota((n, n), 1), column, 0.0), axis=0, keepdims=True)


def reverse(index, count):
    return (count - 1) ^ index


def spread_order(shards):
    return [reverse(s, shards) for s in range(shards)]


def group_bit(r):
    return 1 - ((lax.axis_index("dom") >> r) & 1)


def renumber(slot, shards, slots):
    half = slots // 2
    return (slot // half % 2) * (shards * half) + reverse(slot // slots, shards) * half + slot % half


def halves(ref, r):
    rows, bit = ref.shape[0] // 2, group_bit(r)
    return [pl.ds(pl.multiple_of(side * rows, rows), rows) for side in (bit, 1 - bit)]


def whole(width):
    return width // LANES * LANES


def unfold(value, width):
    tiles, rest = whole(width), width - whole(width)
    return jnp.concatenate(
        [
            jnp.concatenate(
                [value[:, side * tiles : (side + 1) * tiles], value[:, 2 * tiles + side * rest :][:, :rest]], axis=1
            )
            for side in range(2)
        ],
        axis=0,
    )


def beside(left, right):
    tiles = whole(left.shape[1])
    return jnp.concatenate([left[:, :tiles], right[:, :tiles], left[:, tiles:], right[:, tiles:]], axis=1)


def fold(value):
    n = value.shape[0] // 2
    return beside(value[:n], value[n:])


def request_columns(request_ref, r):
    _, shards, _, slots = request_ref.shape
    half = slots // 2
    sides = [request_ref[r, :, k, :].astype(F32) for k in range(2)]
    flip = group_bit(r) == 1
    rep = jnp.concatenate(
        [
            jnp.broadcast_to(ids[reverse(place, shards)][None], (half, slots))
            for ids in (jnp.where(flip, sides[1], sides[0]), jnp.where(flip, sides[0], sides[1]))
            for place in range(shards)
        ],
        axis=0,
    )
    n = rep.shape[0]
    lane, inside = iota((n, slots), 1), iota((n, slots), 0) % half
    return [
        jnp.sum(jnp.where(lane == side * half + inside, rep, 0.0), axis=1, keepdims=True) for side in range(2)
    ]


def serve(request_ref, r, table, out_ref):
    rows, width = table.shape
    table = table.astype(BF16)
    hot = jnp.concatenate([one_hot(column, rows) for column in request_columns(request_ref, r)], axis=1)
    blank = jnp.zeros((rows, width), BF16)
    both = jnp.concatenate([beside(table, blank), beside(blank, table)], axis=0)
    out_ref[...] = dot(hot, both).astype(BF16)


def first_kernel(request_ref, table_ref, *refs):
    serve(request_ref, 0, table_ref[...], refs[-1])


def request_hot(request_ref, r, rows):
    return jnp.concatenate([one_hot(column, rows) for column in request_columns(request_ref, r)], axis=0)


def row_update(hot, back_ref, table_ref, accum_ref, dims=FIRST):
    table, width = table_ref[...], table_ref.shape[1]
    row_grad = dot(hot, unfold(back_ref[:, : 2 * width], width), dims)
    accum = to_column(accum_ref[...].reshape(1, table.shape[0])) + jnp.mean(row_grad * row_grad, axis=1, keepdims=True)
    return table - row_grad * (LEARN_RATE * lax.rsqrt(accum)), to_row(accum)


def middle_kernel(r, request_ref, back_ref, table_ref, accum_ref, table_out, accum_out, out_ref):
    hot = request_hot(request_ref, r, table_ref.shape[0])
    table, accum_out[...] = row_update(hot, back_ref, table_ref, accum_ref)
    serve(request_ref, r + 1, table, out_ref)
    table_out[...] = table


def slots_of(ref):
    return 2 * ref.shape[0] // (2 * lax.axis_size("shard"))


def by_blocks(function, *arrays):
    step = 16
    parts = [function(*[x[i : i + step] for x in arrays]) for i in range(0, arrays[0].shape[0], step)]
    return [jnp.concatenate(column, axis=0) for column in zip(*parts)]


def query_block(head, tail, rel):
    tail_query = head * rel
    positive = jnp.sum(tail_query * tail, axis=1, keepdims=True)
    return tail_query.astype(BF16), (tail * rel).astype(BF16), -jax.nn.sigmoid(-positive)


def grad_block(head, tail, rel, coeff, back_tail, back_head):
    toward_head = coeff * tail + back_tail
    grad_rel = head * toward_head + tail * back_head
    return (
        (rel * toward_head).astype(BF16),
        (rel * (coeff * head + back_head)).astype(BF16),
        grad_rel.astype(BF16),
    )


def edge_kernel(
    r,
    bit,
    per_device,
    rec_ref,
    head_ref,
    tail_ref,
    rel_ref,
    own_neg_ref,
    far_neg_ref,
    relations_ref,
    *refs,
):
    width = relations_ref.shape[1]
    shards, slots = lax.axis_size("shard"), slots_of(rec_ref)
    touched = shards * slots
    edges, negatives = head_ref.shape[1], own_neg_ref.shape[1]
    own_half, far_half = halves(rec_ref, r)
    own = unfold(rec_ref[own_half], width)
    far = unfold(rec_ref[far_half], width)
    row = slice(r, r + 1)
    ids = rel_ref[row]
    heads, tails = renumber(head_ref[row], shards, slots), renumber(tail_ref[row], shards, slots)
    head = dot(one_hot(to_column(heads), touched), own)
    tail = dot(one_hot(to_column(tails), touched), far)
    rel = dot(one_hot(to_column(ids), relations_ref.shape[0]), relations_ref[...])
    query_tail, query_head, coeff = by_blocks(query_block, head, tail, rel)

    def weights(query, rows, neg_ref):
        hit = iota((touched, negatives), 0) == renumber(neg_ref[row], shards, slots)
        scale = jnp.sum(jnp.where(hit, 1.0 / negatives, 0.0), axis=1, keepdims=True)
        return jax.nn.sigmoid(dot(query, rows, LAST)) * to_row(scale)

    weight_tail = weights(query_tail, far, far_neg_ref)
    weight_head = weights(query_head, own, own_neg_ref)
    back_tail = dot(weight_tail.astype(BF16), far)
    back_head = dot(weight_head.astype(BF16), own)
    grad_head, grad_tail, grad_rel = by_blocks(grad_block, head, tail, rel, coeff, back_tail, back_head)
    right = [
        jnp.concatenate([grad_head, query_head], axis=0),
        jnp.concatenate([grad_tail, query_tail], axis=0),
    ]
    if r < bit:
        out_ref, grad_rel_out = refs
        sides = (own_half, heads, weight_head), (far_half, tails, weight_tail)
        for (half, slot, weight), grads in zip(sides, right):
            out_ref[half] = row_grads(slot, weight, grads)
        grad_rel_out[...] = grad_rel
    else:
        *before_refs, weights_out, right_out, values_out, sums_out = refs
        for side, weight in enumerate((weight_head, weight_tail)):
            weights_out[side], right_out[side] = weight.astype(BF16), right[side]
        values = jnp.concatenate([ref[...] for ref in before_refs] + [grad_rel], axis=0)
        values_out[...] = values
        masks = other_doms(bit)
        for i, mask in enumerate(masks):
            sums_out[i] = relation_sums(rel_ref, values, bit, per_device, mask, rec_ref.shape[0]).astype(BF16)


def other_doms(bit):
    return [mask for mask in range(1, lax.axis_size("dom")) if not mask >> bit & 1]


def relation_sums(rel_ref, values, bit, per_device, mask, rows):
    shards = lax.axis_size("shard")
    ids = jnp.concatenate([rel_ref[r : r + 1] for r in range(rel_ref.shape[0])], axis=1)
    owner = ids // per_device
    dom = owner // shards
    chunk = (1 - (dom >> bit & 1)) * shards + reverse(owner % shards, shards)
    meant = (dom ^ lax.axis_index("dom") ^ mask) & ~(1 << bit) == 0
    rows_each = rows // (2 * shards)
    spot, free = ids % per_device, rows_each - per_device
    hot = one_hot_t(
        jnp.concatenate(
            [
                jnp.where(meant, chunk * rows_each + spot, -1),
                jnp.where(meant, chunk * rows_each + per_device + spot % free, -1),
            ],
            axis=1,
        ),
        rows,
    )
    third = values[:, 2 * LANES : 3 * LANES].astype(F32)
    first = to_column(spot) < free
    split = [jnp.where(first, third, 0.0).astype(BF16), jnp.where(first, 0.0, third).astype(BF16)]
    right = jnp.concatenate([values[:, : 2 * LANES], jnp.concatenate(split, axis=1)], axis=0)
    rest = dot(hot[:, : values.shape[0]], values[:, 3 * LANES :])
    return jnp.concatenate([dot(hot, right), rest], axis=1)


def unpack_sums(total, per_device):
    free = total.shape[0] - per_device
    third = jnp.concatenate(
        [total[per_device:, :LANES], total[per_device : 2 * per_device - free, LANES : 2 * LANES]], axis=0
    )
    return jnp.concatenate([total[:per_device, : 2 * LANES], third, total[:per_device, 2 * LANES :]], axis=1)


def row_grads(slot, weight, grads):
    left = jnp.concatenate([one_hot_t(slot, weight.shape[1]), weight.T.astype(BF16)], axis=1)
    return fold(dot(left, grads).astype(BF16))


def grad_kernel(
    bit,
    per_device,
    request_ref,
    head_ref,
    tail_ref,
    rel_ref,
    weights_ref,
    right_ref,
    values_ref,
    out_ref,
    sums_out,
    hot_out,
):
    shards, slots = lax.axis_size("shard"), slots_of(out_ref)
    for side, (half, slot_ref) in enumerate(zip(halves(out_ref, bit), (head_ref, tail_ref))):
        slot = renumber(slot_ref[bit : bit + 1], shards, slots)
        out_ref[half] = row_grads(slot, weights_ref[side].astype(F32), right_ref[side])
    sums_out[...] = relation_sums(rel_ref, values_ref[...], bit, per_device, 0, out_ref.shape[0])
    hot_out[...] = request_hot(request_ref, bit, hot_out.shape[0]).astype(F32).T.astype(BF16)


def sums_width(width):
    return width - LANES


def wide(width):
    return 2 * whole(width) + 3 * LANES


def join_kernel(grads_ref, sums_ref, *refs):
    *came_refs, out_ref = refs
    tiles = out_ref.shape[1] - 3 * LANES
    total = sums_ref[...]
    for ref in came_refs:
        total = total + ref[...].astype(F32)
    total = total.astype(BF16)
    rests = jnp.concatenate([grads_ref[:, tiles:], total[:, 2 * LANES :]], axis=1)
    blank = jnp.zeros((total.shape[0], LANES - rests.shape[1]), BF16)
    out_ref[:, :tiles] = grads_ref[:, :tiles]
    out_ref[:, tiles : tiles + LANES] = jnp.concatenate([rests, blank], axis=1)
    out_ref[:, tiles + LANES :] = total[:, : 2 * LANES]


def last_kernel(
    hot_ref, back_ref, old_ref, row_accum_in, accum_in, table_out, row_accum_out, step_out, accum_out, *scratch
):
    table_ref, row_accum_ref, step_ref, new_accum_ref, sems = scratch
    pairs = (
        (table_ref, table_out),
        (row_accum_ref, row_accum_out),
        (step_ref, step_out),
        (new_accum_ref, accum_out),
    )
    copies = [pltpu.make_async_copy(source, target, sems.at[i]) for i, (source, target) in enumerate(pairs)]
    table, accum = row_update(hot_ref[...], back_ref, old_ref, row_accum_in, NATURAL)
    table_ref[...] = table
    copies[0].start()
    row_accum_ref[...] = accum
    copies[1].start()
    per_device, width = step_ref.shape
    rows = slots_of(back_ref) // 2
    tiles, rest = 2 * whole(width), width - whole(width)
    parts = jnp.concatenate(
        [back_ref[:, tiles + LANES :], back_ref[:, tiles + 2 * rest : tiles + 3 * rest]], axis=1
    ).astype(F32)
    total = jnp.sum(parts.reshape(parts.shape[0] // rows, rows, parts.shape[1]), axis=0)
    grad = unpack_sums(total, per_device)
    accum = to_column(accum_in[...].reshape(1, per_device)) + jnp.mean(grad * grad, axis=1, keepdims=True)
    step_ref[...] = grad * (-LEARN_RATE * lax.rsqrt(accum))
    copies[2].start()
    new_accum_ref[...] = to_row(accum)
    copies[3].start()
    for copy in copies:
        copy.wait()


def call(kernel, outs, *args, **kwargs):
    return pl.pallas_call(
        kernel,
        out_shape=[jax.ShapeDtypeStruct(shape, kind) for shape, kind in outs],
        compiler_params=pltpu.CompilerParams(vmem_limit_bytes=VMEM_LIMIT),
        **kwargs,
    )(*args)


def swap_pair(value, r):
    doms, shards = lax.axis_size("dom"), lax.axis_size("shard")
    order = spread_order(shards)
    groups = [
        [g * shards + s for g in (low ^ (1 << r), low) for s in sorted(range(shards), key=order.__getitem__)]
        for low in range(doms)
        if not low >> r & 1
    ]
    return lax.all_to_all(
        value, ("dom", "shard"), split_axis=0, concat_axis=0, axis_index_groups=groups, tiled=True
    )


def body(
    embeddings,
    row_accum,
    relations,
    relation_accum,
    request_rows,
    head_slots,
    tail_slots,
    relation_ids,
    own_negatives,
    far_negatives,
):
    rows, width = embeddings.shape
    doms, shards = lax.axis_size("dom"), lax.axis_size("shard")
    rounds, slots = request_rows.shape[0], request_rows.shape[-1]
    bit = rounds - 1
    per_device = relation_accum.shape[0]
    assert 3 * (width % LANES) <= LANES
    count, touched = head_slots.shape[1], shards * slots
    free = slots // 2 - per_device
    assert free < per_device <= 2 * free and whole(width) == 3 * LANES
    chunks = ((touched, 2 * width), BF16)
    table, accum = embeddings, row_accum
    edges = (head_slots, tail_slots, relation_ids, own_negatives, far_negatives, relations)
    (outgoing,) = call(first_kernel, [chunks], request_rows, table.astype(BF16), accum, relation_accum, *edges)
    before = []
    for r in range(bit):
        received = swap_pair(outgoing, r)
        grads, grad_rel = call(
            functools.partial(edge_kernel, r, bit, per_device), [chunks, ((count, width), BF16)], received, *edges
        )
        before.append(grad_rel)
        back = swap_pair(grads, r)
        table, accum, outgoing = call(
            functools.partial(middle_kernel, r),
            [((rows, width), F32), ((1, rows), F32), chunks],
            request_rows,
            back,
            table,
            accum,
        )
    received = swap_pair(outgoing, bit)
    masks = other_doms(bit)
    weights, right, values, sums = call(
        functools.partial(edge_kernel, bit, bit, per_device),
        [
            ((2, count, touched), BF16),
            ((2, 2 * count, width), BF16),
            ((rounds * count, width), BF16),
            ((len(masks), touched, sums_width(width)), BF16),
        ],
        received,
        *edges,
        *before,
    )
    came = [lax.ppermute(sums[i], "dom", [(g, g ^ mask) for g in range(doms)]) for i, mask in enumerate(masks)]
    grads, sums, hot = call(
        functools.partial(grad_kernel, bit, per_device),
        [chunks, ((touched, sums_width(width)), F32), ((rows, 2 * touched), BF16)],
        request_rows,
        head_slots,
        tail_slots,
        relation_ids,
        weights,
        right,
        values,
    )
    (grads,) = call(join_kernel, [((touched, wide(width)), BF16)], grads, sums, *came)
    back = swap_pair(grads, bit)
    outs = [((rows, width), F32), ((1, rows), F32), ((per_device, width), F32), ((1, per_device), F32)]
    table, accum, step, relation_accum = call(
        last_kernel,
        outs,
        hot,
        back,
        table,
        accum,
        relation_accum,
        in_specs=[VMEM] * 5,
        out_specs=[HBM] * 4,
        scratch_shapes=[pltpu.VMEM(*out) for out in outs] + [pltpu.SemaphoreType.DMA((4,))],
    )
    return (table, accum.reshape(rows), step, relation_accum.reshape(per_device))


def solution(mesh):
    placed = (
        P(("dom", "shard"), None),
        P(("dom", "shard")),
        P(),
        P(("dom", "shard")),
        P(None, ("dom", "shard"), None, None),
        P(None, ("dom", "shard")),
        P(None, ("dom", "shard")),
        P(None, ("dom", "shard")),
        P(None, ("dom", "shard")),
        P(None, ("dom", "shard")),
    )
    return jax.shard_map(
        body,
        mesh=mesh,
        in_specs=placed,
        out_specs=(
            P(("dom", "shard"), None),
            P(("dom", "shard")),
            P(("dom", "shard"), None),
            P(("dom", "shard")),
        ),
        check_vma=False,
    )
```

```python
import functools

import jax
import jax.numpy as jnp
from jax import lax
from jax.experimental import pallas as pl
from jax.experimental.pallas import tpu as pltpu
from jax.sharding import PartitionSpec as P

LEARN_RATE = 0.1
LANES = 128
VMEM_LIMIT = 48 * 2**20
BF16 = jnp.bfloat16
F32 = jnp.float32
NATURAL = (((1,), (0,)), ((), ()))
LAST = (((1,), (1,)), ((), ()))
FIRST = (((0,), (0,)), ((), ()))
HBM = pl.BlockSpec(memory_space=pltpu.HBM)
VMEM = pl.BlockSpec(memory_space=pltpu.VMEM)


def dot(left, right, dims=NATURAL):
    return lax.dot_general(left, right, dims, preferred_element_type=F32)


def iota(shape, axis):
    return lax.broadcasted_iota(jnp.int32, shape, axis)


def one_hot_t(row, count):
    return (iota((count, row.shape[1]), 0) == row).astype(BF16)


def one_hot(column, count):
    return (iota((column.shape[0], count), 1) == column.astype(jnp.int32)).astype(BF16)


def to_column(row):
    n = row.shape[1]
    same = iota((n, n), 0) == iota((n, n), 1)
    return jnp.sum(jnp.where(same, row.astype(F32), 0.0), axis=1, keepdims=True)


def to_row(column):
    n = column.shape[0]
    return jnp.sum(jnp.where(iota((n, n), 0) == iota((n, n), 1), column, 0.0), axis=0, keepdims=True)


def turn(index, count, r):
    swap = (index >> 1 ^ index >> 2) & 1 if r and count >= 8 else 0
    return (count - 1) ^ index ^ swap * 6


def group_bit(r):
    return 1 - ((lax.axis_index("dom") >> r) & 1)


def renumber(slot, shards, slots, r):
    half = slots // 2
    return (slot // half % 2) * (shards * half) + turn(slot // slots, shards, r) * half + slot % half


def halves(ref, r):
    rows, bit = ref.shape[0] // 2, group_bit(r)
    return [pl.ds(pl.multiple_of(side * rows, rows), rows) for side in (bit, 1 - bit)]


def whole(width):
    return width // LANES * LANES


def unfold(value, width):
    tiles, rest = whole(width), width - whole(width)
    return jnp.concatenate(
        [
            jnp.concatenate(
                [value[:, side * tiles : (side + 1) * tiles], value[:, 2 * tiles + side * rest :][:, :rest]], axis=1
            )
            for side in range(2)
        ],
        axis=0,
    )


def beside(left, right):
    tiles = whole(left.shape[1])
    return jnp.concatenate([left[:, :tiles], right[:, :tiles], left[:, tiles:], right[:, tiles:]], axis=1)


def fold(value):
    n = value.shape[0] // 2
    return beside(value[:n], value[n:])


def request_columns(request_ref, r):
    _, shards, _, slots = request_ref.shape
    half = slots // 2
    sides = [request_ref[r, :, k, :].astype(F32) for k in range(2)]
    flip = group_bit(r) == 1
    rep = jnp.concatenate(
        [
            jnp.broadcast_to(ids[turn(place, shards, r)][None], (half, slots))
            for ids in (jnp.where(flip, sides[1], sides[0]), jnp.where(flip, sides[0], sides[1]))
            for place in range(shards)
        ],
        axis=0,
    )
    n = rep.shape[0]
    lane, inside = iota((n, slots), 1), iota((n, slots), 0) % half
    return [
        jnp.sum(jnp.where(lane == side * half + inside, rep, 0.0), axis=1, keepdims=True) for side in range(2)
    ]


def serve(request_ref, r, table, out_ref):
    rows, width = table.shape
    table = table.astype(BF16)
    hot = jnp.concatenate([one_hot(column, rows) for column in request_columns(request_ref, r)], axis=1)
    blank = jnp.zeros((rows, width), BF16)
    both = jnp.concatenate([beside(table, blank), beside(blank, table)], axis=0)
    out_ref[...] = dot(hot, both).astype(BF16)


def first_kernel(request_ref, state_ref, *refs):
    out_ref = refs[-1]
    table = state_ref[: state_ref.shape[0] - 2]
    serve(request_ref, 0, table, out_ref)


def request_hot(request_ref, r, rows):
    return jnp.concatenate([one_hot(column, rows) for column in request_columns(request_ref, r)], axis=0)


def row_update(hot, back_ref, state_ref, dims=FIRST):
    rows, width = state_ref.shape[0] - 2, state_ref.shape[1]
    row_grad = dot(hot, unfold(back_ref[:, : 2 * width], width), dims)
    accum = to_column(state_ref[rows : rows + 1, :rows]) + jnp.mean(row_grad * row_grad, axis=1, keepdims=True)
    return state_ref[:rows] - row_grad * (LEARN_RATE * lax.rsqrt(accum)), to_row(accum)


def middle_kernel(r, request_ref, back_ref, state_ref, state_out, out_ref):
    rows = state_ref.shape[0] - 2
    table, accum = row_update(request_hot(request_ref, r, rows), back_ref, state_ref)
    serve(request_ref, r + 1, table, out_ref)
    state_out[:rows] = table
    state_out[rows:] = state_ref[rows:]
    state_out[rows : rows + 1, :rows] = accum


def slots_of(ref):
    return 2 * ref.shape[0] // (2 * lax.axis_size("shard"))


def by_blocks(function, *arrays):
    step = 16
    parts = [function(*[x[i : i + step] for x in arrays]) for i in range(0, arrays[0].shape[0], step)]
    return [jnp.concatenate(column, axis=0) for column in zip(*parts)]


def query_block(head, tail, rel):
    tail_query = head * rel
    positive = jnp.sum(tail_query * tail, axis=1, keepdims=True)
    return tail_query.astype(BF16), (tail * rel).astype(BF16), -jax.nn.sigmoid(-positive)


def grad_block(head, tail, rel, coeff, back_tail, back_head):
    toward_head = coeff * tail + back_tail
    grad_rel = head * toward_head + tail * back_head
    return (
        (rel * toward_head).astype(BF16),
        (rel * (coeff * head + back_head)).astype(BF16),
        grad_rel.astype(BF16),
    )


def edge_kernel(
    r,
    bit,
    per_device,
    rec_ref,
    head_ref,
    tail_ref,
    rel_ref,
    own_neg_ref,
    far_neg_ref,
    relations_ref,
    *refs,
):
    width = relations_ref.shape[1]
    shards, slots = lax.axis_size("shard"), slots_of(rec_ref)
    touched = shards * slots
    edges, negatives = head_ref.shape[1], own_neg_ref.shape[1]
    own_half, far_half = halves(rec_ref, r)
    own = unfold(rec_ref[own_half], width)
    far = unfold(rec_ref[far_half], width)
    row = slice(r, r + 1)
    ids = rel_ref[row]
    heads, tails = renumber(head_ref[row], shards, slots, r), renumber(tail_ref[row], shards, slots, r)
    head = dot(one_hot(to_column(heads), touched), own)
    tail = dot(one_hot(to_column(tails), touched), far)
    rel = dot(one_hot(to_column(ids), relations_ref.shape[0]), relations_ref[...])
    query_tail, query_head, coeff = by_blocks(query_block, head, tail, rel)

    def weights(query, rows, neg_ref):
        hit = iota((touched, negatives), 0) == renumber(neg_ref[row], shards, slots, r)
        scale = jnp.sum(jnp.where(hit, 1.0 / negatives, 0.0), axis=1, keepdims=True)
        return jax.nn.sigmoid(dot(query, rows, LAST)) * to_row(scale)

    weight_tail = weights(query_tail, far, far_neg_ref)
    weight_head = weights(query_head, own, own_neg_ref)
    back_tail = dot(weight_tail.astype(BF16), far)
    back_head = dot(weight_head.astype(BF16), own)
    grad_head, grad_tail, grad_rel = by_blocks(grad_block, head, tail, rel, coeff, back_tail, back_head)
    right = [
        jnp.concatenate([grad_head, query_head], axis=0),
        jnp.concatenate([grad_tail, query_tail], axis=0),
    ]
    if r < bit:
        out_ref, grad_rel_out = refs
        sides = (own_half, heads, weight_head), (far_half, tails, weight_tail)
        for (half, slot, weight), grads in zip(sides, right):
            out_ref[half] = row_grads(slot, weight, grads)
        grad_rel_out[...] = grad_rel
    else:
        *before_refs, weights_out, right_out, values_out, sums_out = refs
        for side, weight in enumerate((weight_head, weight_tail)):
            weights_out[side], right_out[side] = weight.astype(BF16), right[side]
        values = jnp.concatenate([ref[...] for ref in before_refs] + [grad_rel], axis=0)
        values_out[...] = values
        masks = other_doms(bit)
        for i, mask in enumerate(masks):
            sums_out[i] = relation_sums(rel_ref, values, bit, per_device, mask, rec_ref.shape[0]).astype(BF16)


def other_doms(bit):
    return [mask for mask in range(1, lax.axis_size("dom")) if not mask >> bit & 1]


def relation_sums(rel_ref, values, bit, per_device, mask, rows):
    shards = lax.axis_size("shard")
    ids = jnp.concatenate([rel_ref[r : r + 1] for r in range(rel_ref.shape[0])], axis=1)
    owner = ids // per_device
    dom = owner // shards
    chunk = (1 - (dom >> bit & 1)) * shards + turn(owner % shards, shards, bit)
    meant = (dom ^ lax.axis_index("dom") ^ mask) & ~(1 << bit) == 0
    rows_each = rows // (2 * shards)
    spot, free = ids % per_device, rows_each - per_device
    hot = one_hot_t(
        jnp.concatenate(
            [
                jnp.where(meant, chunk * rows_each + spot, -1),
                jnp.where(meant, chunk * rows_each + per_device + spot % free, -1),
            ],
            axis=1,
        ),
        rows,
    )
    third = values[:, 2 * LANES : 3 * LANES].astype(F32)
    first = to_column(spot) < free
    split = [jnp.where(first, third, 0.0).astype(BF16), jnp.where(first, 0.0, third).astype(BF16)]
    right = jnp.concatenate([values[:, : 2 * LANES], jnp.concatenate(split, axis=1)], axis=0)
    rest = dot(hot[:, : values.shape[0]], values[:, 3 * LANES :])
    return jnp.concatenate([dot(hot, right), rest], axis=1)


def unpack_sums(total, per_device):
    free = total.shape[0] - per_device
    third = jnp.concatenate(
        [total[per_device:, :LANES], total[per_device : 2 * per_device - free, LANES : 2 * LANES]], axis=0
    )
    return jnp.concatenate([total[:per_device, : 2 * LANES], third, total[:per_device, 2 * LANES :]], axis=1)


def row_grads(slot, weight, grads):
    left = jnp.concatenate([one_hot_t(slot, weight.shape[1]), weight.T.astype(BF16)], axis=1)
    return fold(dot(left, grads).astype(BF16))


def grad_kernel(
    bit,
    per_device,
    request_ref,
    head_ref,
    tail_ref,
    rel_ref,
    weights_ref,
    right_ref,
    values_ref,
    out_ref,
    sums_out,
    hot_out,
):
    shards, slots = lax.axis_size("shard"), slots_of(out_ref)
    for side, (half, slot_ref) in enumerate(zip(halves(out_ref, bit), (head_ref, tail_ref))):
        slot = renumber(slot_ref[bit : bit + 1], shards, slots, bit)
        out_ref[half] = row_grads(slot, weights_ref[side].astype(F32), right_ref[side])
    sums_out[...] = relation_sums(rel_ref, values_ref[...], bit, per_device, 0, out_ref.shape[0])
    hot_out[...] = request_hot(request_ref, bit, hot_out.shape[0]).astype(F32).T.astype(BF16)


def sums_width(width):
    return width - LANES


def wide(width):
    return 2 * whole(width) + 3 * LANES


def join_kernel(grads_ref, sums_ref, *refs):
    *came_refs, out_ref = refs
    tiles = out_ref.shape[1] - 3 * LANES
    total = sums_ref[...]
    for ref in came_refs:
        total = total + ref[...].astype(F32)
    total = total.astype(BF16)
    rests = jnp.concatenate([grads_ref[:, tiles:], total[:, 2 * LANES :]], axis=1)
    blank = jnp.zeros((total.shape[0], LANES - rests.shape[1]), BF16)
    out_ref[:, :tiles] = grads_ref[:, :tiles]
    out_ref[:, tiles : tiles + LANES] = jnp.concatenate([rests, blank], axis=1)
    out_ref[:, tiles + LANES :] = total[:, : 2 * LANES]


def last_kernel(hot_ref, back_ref, state_ref, table_out, row_accum_out, step_out, accum_out, *scratch):
    table_ref, row_accum_ref, step_ref, new_accum_ref, sems = scratch
    pairs = (
        (table_ref, table_out),
        (row_accum_ref, row_accum_out),
        (step_ref, step_out),
        (new_accum_ref, accum_out),
    )
    copies = [pltpu.make_async_copy(source, target, sems.at[i]) for i, (source, target) in enumerate(pairs)]
    table, accum = row_update(hot_ref[...], back_ref, state_ref, NATURAL)
    table_ref[...] = table
    copies[0].start()
    row_accum_ref[...] = accum
    copies[1].start()
    per_device, width = step_ref.shape
    rows = slots_of(back_ref) // 2
    tiles, rest = 2 * whole(width), width - whole(width)
    parts = jnp.concatenate(
        [back_ref[:, tiles + LANES :], back_ref[:, tiles + 2 * rest : tiles + 3 * rest]], axis=1
    ).astype(F32)
    total = jnp.sum(parts.reshape(parts.shape[0] // rows, rows, parts.shape[1]), axis=0)
    grad = unpack_sums(total, per_device)
    accum = to_column(state_ref[table.shape[0] + 1 :, :per_device]) + jnp.mean(grad * grad, axis=1, keepdims=True)
    step_ref[...] = grad * (-LEARN_RATE * lax.rsqrt(accum))
    copies[2].start()
    new_accum_ref[...] = to_row(accum)
    copies[3].start()
    for copy in copies:
        copy.wait()


def call(kernel, outs, *args, **kwargs):
    return pl.pallas_call(
        kernel,
        out_shape=[jax.ShapeDtypeStruct(shape, kind) for shape, kind in outs],
        compiler_params=pltpu.CompilerParams(vmem_limit_bytes=VMEM_LIMIT),
        **kwargs,
    )(*args)


def swap_pair(value, r):
    doms, shards = lax.axis_size("dom"), lax.axis_size("shard")
    groups = [
        [g * shards + turn(place, shards, r) for g in (low ^ (1 << r), low) for place in range(shards)]
        for low in range(doms)
        if not low >> r & 1
    ]
    return lax.all_to_all(
        value, ("dom", "shard"), split_axis=0, concat_axis=0, axis_index_groups=groups, tiled=True
    )


def body(
    embeddings,
    row_accum,
    relations,
    relation_accum,
    request_rows,
    head_slots,
    tail_slots,
    relation_ids,
    own_negatives,
    far_negatives,
):
    rows, width = embeddings.shape
    doms, shards = lax.axis_size("dom"), lax.axis_size("shard")
    rounds, slots = request_rows.shape[0], request_rows.shape[-1]
    bit = rounds - 1
    per_device = relation_accum.shape[0]
    assert 3 * (width % LANES) <= LANES
    count, touched = head_slots.shape[1], shards * slots
    free = slots // 2 - per_device
    assert free < per_device <= 2 * free and whole(width) == 3 * LANES
    chunks = ((touched, 2 * width), BF16)
    state = (
        jnp.pad(embeddings, ((0, 2), (0, 0)))
        + jnp.pad(row_accum[None], ((rows, 1), (0, width - rows)))
        + jnp.pad(relation_accum[None], ((rows + 1, 0), (0, width - per_device)))
    )
    edges = (head_slots, tail_slots, relation_ids, own_negatives, far_negatives, relations)
    (outgoing,) = call(first_kernel, [chunks], request_rows, state, *edges)
    before = []
    for r in range(bit):
        received = swap_pair(outgoing, r)
        grads, grad_rel = call(
            functools.partial(edge_kernel, r, bit, per_device), [chunks, ((count, width), BF16)], received, *edges
        )
        before.append(grad_rel)
        back = swap_pair(grads, r)
        state, outgoing = call(
            functools.partial(middle_kernel, r), [(state.shape, F32), chunks], request_rows, back, state
        )
    received = swap_pair(outgoing, bit)
    masks = other_doms(bit)
    weights, right, values, sums = call(
        functools.partial(edge_kernel, bit, bit, per_device),
        [
            ((2, count, touched), BF16),
            ((2, 2 * count, width), BF16),
            ((rounds * count, width), BF16),
            ((len(masks), touched, sums_width(width)), BF16),
        ],
        received,
        *edges,
        *before,
    )
    came = [lax.ppermute(sums[i], "dom", [(g, g ^ mask) for g in range(doms)]) for i, mask in enumerate(masks)]
    grads, sums, hot = call(
        functools.partial(grad_kernel, bit, per_device),
        [chunks, ((touched, sums_width(width)), F32), ((rows, 2 * touched), BF16)],
        request_rows,
        head_slots,
        tail_slots,
        relation_ids,
        weights,
        right,
        values,
    )
    (grads,) = call(join_kernel, [((touched, wide(width)), BF16)], grads, sums, *came)
    back = swap_pair(grads, bit)
    outs = [((rows, width), F32), ((1, rows), F32), ((per_device, width), F32), ((1, per_device), F32)]
    table, accum, step, relation_accum = call(
        last_kernel,
        outs,
        hot,
        back,
        state,
        in_specs=[VMEM] * 3,
        out_specs=[HBM] * 4,
        scratch_shapes=[pltpu.VMEM(*out) for out in outs] + [pltpu.SemaphoreType.DMA((4,))],
    )
    return (table, accum.reshape(rows), step, relation_accum.reshape(per_device))


def solution(mesh):
    placed = (
        P(("dom", "shard"), None),
        P(("dom", "shard")),
        P(),
        P(("dom", "shard")),
        P(None, ("dom", "shard"), None, None),
        P(None, ("dom", "shard")),
        P(None, ("dom", "shard")),
        P(None, ("dom", "shard")),
        P(None, ("dom", "shard")),
        P(None, ("dom", "shard")),
    )
    return jax.shard_map(
        body,
        mesh=mesh,
        in_specs=placed,
        out_specs=(
            P(("dom", "shard"), None),
            P(("dom", "shard")),
            P(("dom", "shard"), None),
            P(("dom", "shard")),
        ),
        check_vma=False,
    )
```

```python
import functools

import jax
import jax.numpy as jnp
from jax import lax
from jax.experimental import pallas as pl
from jax.experimental.pallas import tpu as pltpu
from jax.sharding import PartitionSpec as P

LEARN_RATE = 0.1
LANES = 128
VMEM_LIMIT = 48 * 2**20
BF16 = jnp.bfloat16
F32 = jnp.float32
NATURAL = (((1,), (0,)), ((), ()))
LAST = (((1,), (1,)), ((), ()))
FIRST = (((0,), (0,)), ((), ()))
HBM = pl.BlockSpec(memory_space=pltpu.HBM)
VMEM = pl.BlockSpec(memory_space=pltpu.VMEM)


def dot(left, right, dims=NATURAL):
    return lax.dot_general(left, right, dims, preferred_element_type=F32)


def iota(shape, axis):
    return lax.broadcasted_iota(jnp.int32, shape, axis)


def one_hot_t(row, count):
    return (iota((count, row.shape[1]), 0) == row).astype(BF16)


def one_hot(column, count):
    return (iota((column.shape[0], count), 1) == column.astype(jnp.int32)).astype(BF16)


def to_column(row):
    n = row.shape[1]
    same = iota((n, n), 0) == iota((n, n), 1)
    return jnp.sum(jnp.where(same, row.astype(F32), 0.0), axis=1, keepdims=True)


def to_row(column):
    n = column.shape[0]
    return jnp.sum(jnp.where(iota((n, n), 0) == iota((n, n), 1), column, 0.0), axis=0, keepdims=True)


def reverse(index, count):
    return (count - 1) ^ index


def spread_order(shards):
    return [reverse(s, shards) for s in range(shards)]


def group_bit(r):
    return 1 - ((lax.axis_index("dom") >> r) & 1)


def renumber(slot, shards, slots):
    half = slots // 2
    return (slot // half % 2) * (shards * half) + reverse(slot // slots, shards) * half + slot % half


def halves(ref, r):
    rows, bit = ref.shape[0] // 2, group_bit(r)
    return [pl.ds(pl.multiple_of(side * rows, rows), rows) for side in (bit, 1 - bit)]


def whole(width):
    return width // LANES * LANES


def unfold(value, width):
    tiles, rest = whole(width), width - whole(width)
    return jnp.concatenate(
        [
            jnp.concatenate(
                [value[:, side * tiles : (side + 1) * tiles], value[:, 2 * tiles + side * rest :][:, :rest]], axis=1
            )
            for side in range(2)
        ],
        axis=0,
    )


def beside(left, right):
    tiles = whole(left.shape[1])
    return jnp.concatenate([left[:, :tiles], right[:, :tiles], left[:, tiles:], right[:, tiles:]], axis=1)


def fold(value):
    n = value.shape[0] // 2
    return beside(value[:n], value[n:])


def request_columns(request_ref, r):
    _, shards, _, slots = request_ref.shape
    half = slots // 2
    sides = [request_ref[r, :, k, :].astype(F32) for k in range(2)]
    flip = group_bit(r) == 1
    rep = jnp.concatenate(
        [
            jnp.broadcast_to(ids[reverse(place, shards)][None], (half, slots))
            for ids in (jnp.where(flip, sides[1], sides[0]), jnp.where(flip, sides[0], sides[1]))
            for place in range(shards)
        ],
        axis=0,
    )
    n = rep.shape[0]
    lane, inside = iota((n, slots), 1), iota((n, slots), 0) % half
    return [
        jnp.sum(jnp.where(lane == side * half + inside, rep, 0.0), axis=1, keepdims=True) for side in range(2)
    ]


def serve(request_ref, r, table, out_ref):
    rows, width = table.shape
    table = table.astype(BF16)
    hot = jnp.concatenate([one_hot(column, rows) for column in request_columns(request_ref, r)], axis=1)
    blank = jnp.zeros((rows, width), BF16)
    both = jnp.concatenate([beside(table, blank), beside(blank, table)], axis=0)
    out_ref[...] = dot(hot, both).astype(BF16)


def first_kernel(request_ref, state_ref, *refs):
    out_ref = refs[-1]
    table = state_ref[: state_ref.shape[0] - 2]
    serve(request_ref, 0, table, out_ref)


def request_hot(request_ref, r, rows):
    return jnp.concatenate([one_hot(column, rows) for column in request_columns(request_ref, r)], axis=0)


def row_update(hot, back_ref, state_ref, dims=FIRST):
    rows, width = state_ref.shape[0] - 2, state_ref.shape[1]
    row_grad = dot(hot, unfold(back_ref[:, : 2 * width], width), dims)
    accum = to_column(state_ref[rows : rows + 1, :rows]) + jnp.mean(row_grad * row_grad, axis=1, keepdims=True)
    return state_ref[:rows] - row_grad * (LEARN_RATE * lax.rsqrt(accum)), to_row(accum)


def middle_kernel(r, request_ref, back_ref, state_ref, state_out, out_ref):
    rows = state_ref.shape[0] - 2
    table, accum = row_update(request_hot(request_ref, r, rows), back_ref, state_ref)
    serve(request_ref, r + 1, table, out_ref)
    state_out[:rows] = table
    state_out[rows:] = state_ref[rows:]
    state_out[rows : rows + 1, :rows] = accum


def slots_of(ref):
    return 2 * ref.shape[0] // (2 * lax.axis_size("shard"))


def by_blocks(function, *arrays):
    step = 16
    parts = [function(*[x[i : i + step] for x in arrays]) for i in range(0, arrays[0].shape[0], step)]
    return [jnp.concatenate(column, axis=0) for column in zip(*parts)]


def query_block(head, tail, rel):
    tail_query = head * rel
    positive = jnp.sum(tail_query * tail, axis=1, keepdims=True)
    return tail_query.astype(BF16), (tail * rel).astype(BF16), -jax.nn.sigmoid(-positive)


def grad_block(head, tail, rel, coeff, back_tail, back_head):
    toward_head = coeff * tail + back_tail
    grad_rel = head * toward_head + tail * back_head
    return (
        (rel * toward_head).astype(BF16),
        (rel * (coeff * head + back_head)).astype(BF16),
        grad_rel.astype(BF16),
    )


def edge_kernel(
    r,
    bit,
    per_device,
    rec_ref,
    head_ref,
    tail_ref,
    rel_ref,
    own_neg_ref,
    far_neg_ref,
    relations_ref,
    *refs,
):
    width = relations_ref.shape[1]
    shards, slots = lax.axis_size("shard"), slots_of(rec_ref)
    touched = shards * slots
    edges, negatives = head_ref.shape[1], own_neg_ref.shape[1]
    own_half, far_half = halves(rec_ref, r)
    own = unfold(rec_ref[own_half], width)
    far = unfold(rec_ref[far_half], width)
    row = slice(r, r + 1)
    ids = rel_ref[row]
    heads, tails = renumber(head_ref[row], shards, slots), renumber(tail_ref[row], shards, slots)
    head = dot(one_hot(to_column(heads), touched), own)
    tail = dot(one_hot(to_column(tails), touched), far)
    rel = dot(one_hot(to_column(ids), relations_ref.shape[0]), relations_ref[...])
    query_tail, query_head, coeff = by_blocks(query_block, head, tail, rel)

    def weights(query, rows, neg_ref):
        hit = one_hot_t(renumber(neg_ref[row], shards, slots), touched)
        counts = dot(hit, jnp.ones((negatives, touched), BF16))
        same = iota((touched, touched), 0) == iota((touched, touched), 1)
        scale = jnp.sum(jnp.where(same, counts, 0.0), axis=0, keepdims=True) * (1.0 / negatives)
        return jax.nn.sigmoid(dot(query, rows, LAST)) * scale

    weight_tail = weights(query_tail, far, far_neg_ref)
    weight_head = weights(query_head, own, own_neg_ref)
    back_tail = dot(weight_tail.astype(BF16), far)
    back_head = dot(weight_head.astype(BF16), own)
    grad_head, grad_tail, grad_rel = by_blocks(grad_block, head, tail, rel, coeff, back_tail, back_head)
    right = [
        jnp.concatenate([grad_head, query_head], axis=0),
        jnp.concatenate([grad_tail, query_tail], axis=0),
    ]
    if r < bit:
        out_ref, grad_rel_out = refs
        sides = (own_half, heads, weight_head), (far_half, tails, weight_tail)
        for (half, slot, weight), grads in zip(sides, right):
            out_ref[half] = row_grads(slot, weight, grads)
        grad_rel_out[...] = grad_rel
    else:
        *before_refs, weights_out, right_out, values_out, sums_out = refs
        for side, weight in enumerate((weight_head, weight_tail)):
            weights_out[side], right_out[side] = weight.astype(BF16), right[side]
        values = jnp.concatenate([ref[...] for ref in before_refs] + [grad_rel], axis=0)
        values_out[...] = values
        masks = other_doms(bit)
        for i, mask in enumerate(masks):
            sums_out[i] = relation_sums(rel_ref, values, bit, per_device, mask, rec_ref.shape[0]).astype(BF16)


def other_doms(bit):
    return [mask for mask in range(1, lax.axis_size("dom")) if not mask >> bit & 1]


def relation_sums(rel_ref, values, bit, per_device, mask, rows):
    shards = lax.axis_size("shard")
    ids = jnp.concatenate([rel_ref[r : r + 1] for r in range(rel_ref.shape[0])], axis=1)
    owner = ids // per_device
    dom = owner // shards
    chunk = (1 - (dom >> bit & 1)) * shards + reverse(owner % shards, shards)
    meant = (dom ^ lax.axis_index("dom") ^ mask) & ~(1 << bit) == 0
    rows_each = rows // (2 * shards)
    spot, free = ids % per_device, rows_each - per_device
    hot = one_hot_t(
        jnp.concatenate(
            [
                jnp.where(meant, chunk * rows_each + spot, -1),
                jnp.where(meant, chunk * rows_each + per_device + spot % free, -1),
            ],
            axis=1,
        ),
        rows,
    )
    third = values[:, 2 * LANES : 3 * LANES].astype(F32)
    first = to_column(spot) < free
    split = [jnp.where(first, third, 0.0).astype(BF16), jnp.where(first, 0.0, third).astype(BF16)]
    right = jnp.concatenate([values[:, : 2 * LANES], jnp.concatenate(split, axis=1)], axis=0)
    rest = dot(hot[:, : values.shape[0]], values[:, 3 * LANES :])
    return jnp.concatenate([dot(hot, right), rest], axis=1)


def unpack_sums(total, per_device):
    free = total.shape[0] - per_device
    third = jnp.concatenate(
        [total[per_device:, :LANES], total[per_device : 2 * per_device - free, LANES : 2 * LANES]], axis=0
    )
    return jnp.concatenate([total[:per_device, : 2 * LANES], third, total[:per_device, 2 * LANES :]], axis=1)


def row_grads(slot, weight, grads):
    left = jnp.concatenate([one_hot_t(slot, weight.shape[1]), weight.T.astype(BF16)], axis=1)
    return fold(dot(left, grads).astype(BF16))


def grad_kernel(
    bit,
    per_device,
    request_ref,
    head_ref,
    tail_ref,
    rel_ref,
    weights_ref,
    right_ref,
    values_ref,
    out_ref,
    sums_out,
    hot_out,
):
    shards, slots = lax.axis_size("shard"), slots_of(out_ref)
    for side, (half, slot_ref) in enumerate(zip(halves(out_ref, bit), (head_ref, tail_ref))):
        slot = renumber(slot_ref[bit : bit + 1], shards, slots)
        out_ref[half] = row_grads(slot, weights_ref[side].astype(F32), right_ref[side])
    sums_out[...] = relation_sums(rel_ref, values_ref[...], bit, per_device, 0, out_ref.shape[0])
    hot_out[...] = request_hot(request_ref, bit, hot_out.shape[0]).astype(F32).T.astype(BF16)


def sums_width(width):
    return width - LANES


def wide(width):
    return 2 * whole(width) + 3 * LANES


def join_kernel(grads_ref, sums_ref, *refs):
    *came_refs, out_ref = refs
    tiles = out_ref.shape[1] - 3 * LANES
    total = sums_ref[...]
    for ref in came_refs:
        total = total + ref[...].astype(F32)
    total = total.astype(BF16)
    rests = jnp.concatenate([grads_ref[:, tiles:], total[:, 2 * LANES :]], axis=1)
    blank = jnp.zeros((total.shape[0], LANES - rests.shape[1]), BF16)
    out_ref[:, :tiles] = grads_ref[:, :tiles]
    out_ref[:, tiles : tiles + LANES] = jnp.concatenate([rests, blank], axis=1)
    out_ref[:, tiles + LANES :] = total[:, : 2 * LANES]


def last_kernel(hot_ref, back_ref, state_ref, table_out, row_accum_out, step_out, accum_out, *scratch):
    table_ref, row_accum_ref, step_ref, new_accum_ref, sems = scratch
    pairs = (
        (table_ref, table_out),
        (row_accum_ref, row_accum_out),
        (step_ref, step_out),
        (new_accum_ref, accum_out),
    )
    copies = [pltpu.make_async_copy(source, target, sems.at[i]) for i, (source, target) in enumerate(pairs)]
    table, accum = row_update(hot_ref[...], back_ref, state_ref, NATURAL)
    table_ref[...] = table
    copies[0].start()
    row_accum_ref[...] = accum
    copies[1].start()
    per_device, width = step_ref.shape
    rows = slots_of(back_ref) // 2
    tiles, rest = 2 * whole(width), width - whole(width)
    parts = jnp.concatenate(
        [back_ref[:, tiles + LANES :], back_ref[:, tiles + 2 * rest : tiles + 3 * rest]], axis=1
    ).astype(F32)
    total = jnp.sum(parts.reshape(parts.shape[0] // rows, rows, parts.shape[1]), axis=0)
    grad = unpack_sums(total, per_device)
    accum = to_column(state_ref[table.shape[0] + 1 :, :per_device]) + jnp.mean(grad * grad, axis=1, keepdims=True)
    step_ref[...] = grad * (-LEARN_RATE * lax.rsqrt(accum))
    copies[2].start()
    new_accum_ref[...] = to_row(accum)
    copies[3].start()
    for copy in copies:
        copy.wait()


def call(kernel, outs, *args, **kwargs):
    return pl.pallas_call(
        kernel,
        out_shape=[jax.ShapeDtypeStruct(shape, kind) for shape, kind in outs],
        compiler_params=pltpu.CompilerParams(vmem_limit_bytes=VMEM_LIMIT),
        **kwargs,
    )(*args)


def swap_pair(value, r):
    doms, shards = lax.axis_size("dom"), lax.axis_size("shard")
    order = spread_order(shards)
    groups = [
        [g * shards + s for g in (low ^ (1 << r), low) for s in sorted(range(shards), key=order.__getitem__)]
        for low in range(doms)
        if not low >> r & 1
    ]
    return lax.all_to_all(
        value, ("dom", "shard"), split_axis=0, concat_axis=0, axis_index_groups=groups, tiled=True
    )


def body(
    embeddings,
    row_accum,
    relations,
    relation_accum,
    request_rows,
    head_slots,
    tail_slots,
    relation_ids,
    own_negatives,
    far_negatives,
):
    rows, width = embeddings.shape
    doms, shards = lax.axis_size("dom"), lax.axis_size("shard")
    rounds, slots = request_rows.shape[0], request_rows.shape[-1]
    bit = rounds - 1
    per_device = relation_accum.shape[0]
    assert 3 * (width % LANES) <= LANES
    count, touched = head_slots.shape[1], shards * slots
    free = slots // 2 - per_device
    assert free < per_device <= 2 * free and whole(width) == 3 * LANES
    chunks = ((touched, 2 * width), BF16)
    state = (
        jnp.pad(embeddings, ((0, 2), (0, 0)))
        + jnp.pad(row_accum[None], ((rows, 1), (0, width - rows)))
        + jnp.pad(relation_accum[None], ((rows + 1, 0), (0, width - per_device)))
    )
    edges = (head_slots, tail_slots, relation_ids, own_negatives, far_negatives, relations)
    (outgoing,) = call(first_kernel, [chunks], request_rows, state, *edges)
    before = []
    for r in range(bit):
        received = swap_pair(outgoing, r)
        grads, grad_rel = call(
            functools.partial(edge_kernel, r, bit, per_device), [chunks, ((count, width), BF16)], received, *edges
        )
        before.append(grad_rel)
        back = swap_pair(grads, r)
        state, outgoing = call(
            functools.partial(middle_kernel, r), [(state.shape, F32), chunks], request_rows, back, state
        )
    received = swap_pair(outgoing, bit)
    masks = other_doms(bit)
    weights, right, values, sums = call(
        functools.partial(edge_kernel, bit, bit, per_device),
        [
            ((2, count, touched), BF16),
            ((2, 2 * count, width), BF16),
            ((rounds * count, width), BF16),
            ((len(masks), touched, sums_width(width)), BF16),
        ],
        received,
        *edges,
        *before,
    )
    came = [lax.ppermute(sums[i], "dom", [(g, g ^ mask) for g in range(doms)]) for i, mask in enumerate(masks)]
    grads, sums, hot = call(
        functools.partial(grad_kernel, bit, per_device),
        [chunks, ((touched, sums_width(width)), F32), ((rows, 2 * touched), BF16)],
        request_rows,
        head_slots,
        tail_slots,
        relation_ids,
        weights,
        right,
        values,
    )
    (grads,) = call(join_kernel, [((touched, wide(width)), BF16)], grads, sums, *came)
    back = swap_pair(grads, bit)
    outs = [((rows, width), F32), ((1, rows), F32), ((per_device, width), F32), ((1, per_device), F32)]
    table, accum, step, relation_accum = call(
        last_kernel,
        outs,
        hot,
        back,
        state,
        in_specs=[VMEM] * 3,
        out_specs=[HBM] * 4,
        scratch_shapes=[pltpu.VMEM(*out) for out in outs] + [pltpu.SemaphoreType.DMA((4,))],
    )
    return (table, accum.reshape(rows), step, relation_accum.reshape(per_device))


def solution(mesh):
    placed = (
        P(("dom", "shard"), None),
        P(("dom", "shard")),
        P(),
        P(("dom", "shard")),
        P(None, ("dom", "shard"), None, None),
        P(None, ("dom", "shard")),
        P(None, ("dom", "shard")),
        P(None, ("dom", "shard")),
        P(None, ("dom", "shard")),
        P(None, ("dom", "shard")),
    )
    return jax.shard_map(
        body,
        mesh=mesh,
        in_specs=placed,
        out_specs=(
            P(("dom", "shard"), None),
            P(("dom", "shard")),
            P(("dom", "shard"), None),
            P(("dom", "shard")),
        ),
        check_vma=False,
    )
```

```python
import functools

import jax
import jax.numpy as jnp
from jax import lax
from jax.experimental import pallas as pl
from jax.experimental.pallas import tpu as pltpu
from jax.sharding import PartitionSpec as P

LEARN_RATE = 0.1
LANES = 128
VMEM_LIMIT = 48 * 2**20
BF16 = jnp.bfloat16
F32 = jnp.float32
NATURAL = (((1,), (0,)), ((), ()))
LAST = (((1,), (1,)), ((), ()))
FIRST = (((0,), (0,)), ((), ()))
HBM = pl.BlockSpec(memory_space=pltpu.HBM)
VMEM = pl.BlockSpec(memory_space=pltpu.VMEM)


def dot(left, right, dims=NATURAL):
    return lax.dot_general(left, right, dims, preferred_element_type=F32)


def iota(shape, axis):
    return lax.broadcasted_iota(jnp.int32, shape, axis)


def one_hot_t(row, count):
    return (iota((count, row.shape[1]), 0) == row).astype(BF16)


def one_hot(column, count):
    return (iota((column.shape[0], count), 1) == column.astype(jnp.int32)).astype(BF16)


def to_column(row):
    n = row.shape[1]
    same = iota((n, n), 0) == iota((n, n), 1)
    return jnp.sum(jnp.where(same, row.astype(F32), 0.0), axis=1, keepdims=True)


def to_row(column):
    n = column.shape[0]
    return jnp.sum(jnp.where(iota((n, n), 0) == iota((n, n), 1), column, 0.0), axis=0, keepdims=True)


def reverse(index, count):
    return (count - 1) ^ index


def spread_order(shards):
    return [reverse(s, shards) for s in range(shards)]


def group_bit(r):
    return 1 - ((lax.axis_index("dom") >> r) & 1)


def renumber(slot, shards, slots):
    half = slots // 2
    return (slot // half % 2) * (shards * half) + reverse(slot // slots, shards) * half + slot % half


def halves(ref, r):
    rows, bit = ref.shape[0] // 2, group_bit(r)
    return [pl.ds(pl.multiple_of(side * rows, rows), rows) for side in (bit, 1 - bit)]


def whole(width):
    return width // LANES * LANES


def unfold(value, width):
    tiles, rest = whole(width), width - whole(width)
    return jnp.concatenate(
        [
            jnp.concatenate(
                [value[:, side * tiles : (side + 1) * tiles], value[:, 2 * tiles + side * rest :][:, :rest]], axis=1
            )
            for side in range(2)
        ],
        axis=0,
    )


def beside(left, right):
    tiles = whole(left.shape[1])
    return jnp.concatenate([left[:, :tiles], right[:, :tiles], left[:, tiles:], right[:, tiles:]], axis=1)


def fold(value):
    n = value.shape[0] // 2
    return beside(value[:n], value[n:])


def request_columns(request_ref, r):
    _, shards, _, slots = request_ref.shape
    half = slots // 2
    sides = [request_ref[r, :, k, :].astype(F32) for k in range(2)]
    flip = group_bit(r) == 1
    rep = jnp.concatenate(
        [
            jnp.broadcast_to(ids[reverse(place, shards)][None], (half, slots))
            for ids in (jnp.where(flip, sides[1], sides[0]), jnp.where(flip, sides[0], sides[1]))
            for place in range(shards)
        ],
        axis=0,
    )
    n = rep.shape[0]
    lane, inside = iota((n, slots), 1), iota((n, slots), 0) % half
    return [
        jnp.sum(jnp.where(lane == side * half + inside, rep, 0.0), axis=1, keepdims=True) for side in range(2)
    ]


def serve(request_ref, r, table, out_ref):
    rows, width = table.shape
    table = table.astype(BF16)
    hot = jnp.concatenate([one_hot(column, rows) for column in request_columns(request_ref, r)], axis=1)
    blank = jnp.zeros((rows, width), BF16)
    both = jnp.concatenate([beside(table, blank), beside(blank, table)], axis=0)
    out_ref[...] = dot(hot, both).astype(BF16)


def first_kernel(request_ref, state_ref, *refs):
    out_ref = refs[-1]
    table = state_ref[: state_ref.shape[0] - 2]
    serve(request_ref, 0, table, out_ref)


def request_hot(request_ref, r, rows):
    return jnp.concatenate([one_hot(column, rows) for column in request_columns(request_ref, r)], axis=0)


def row_update(hot, back_ref, state_ref, dims=FIRST):
    rows, width = state_ref.shape[0] - 2, state_ref.shape[1]
    row_grad = dot(hot, unfold(back_ref[:, : 2 * width], width), dims)
    accum = to_column(state_ref[rows : rows + 1, :rows]) + jnp.mean(row_grad * row_grad, axis=1, keepdims=True)
    return state_ref[:rows] - row_grad * (LEARN_RATE * lax.rsqrt(accum)), to_row(accum)


def middle_kernel(r, request_ref, back_ref, state_ref, state_out, out_ref):
    rows = state_ref.shape[0] - 2
    table, accum = row_update(request_hot(request_ref, r, rows), back_ref, state_ref)
    serve(request_ref, r + 1, table, out_ref)
    state_out[:rows] = table
    state_out[rows:] = state_ref[rows:]
    state_out[rows : rows + 1, :rows] = accum


def slots_of(ref):
    return 2 * ref.shape[0] // (2 * lax.axis_size("shard"))


def by_blocks(function, *arrays):
    step = 16
    parts = [function(*[x[i : i + step] for x in arrays]) for i in range(0, arrays[0].shape[0], step)]
    return [jnp.concatenate(column, axis=0) for column in zip(*parts)]


def query_block(head, tail, rel):
    tail_query = head * rel
    positive = jnp.sum(tail_query * tail, axis=1, keepdims=True)
    return tail_query.astype(BF16), (tail * rel).astype(BF16), -jax.nn.sigmoid(-positive)


def grad_block(head, tail, rel, coeff, back_tail, back_head):
    toward_head = coeff * tail + back_tail
    grad_rel = head * toward_head + tail * back_head
    return (
        (rel * toward_head).astype(BF16),
        (rel * (coeff * head + back_head)).astype(BF16),
        grad_rel.astype(BF16),
    )


def edge_kernel(
    r,
    bit,
    per_device,
    rec_ref,
    head_ref,
    tail_ref,
    rel_ref,
    own_neg_ref,
    far_neg_ref,
    relations_ref,
    *refs,
):
    width = relations_ref.shape[1]
    shards, slots = lax.axis_size("shard"), slots_of(rec_ref)
    touched = shards * slots
    edges, negatives = head_ref.shape[1], own_neg_ref.shape[1]
    own_half, far_half = halves(rec_ref, r)
    own = unfold(rec_ref[own_half], width)
    far = unfold(rec_ref[far_half], width)
    row = slice(r, r + 1)
    ids = rel_ref[row]
    heads, tails = renumber(head_ref[row], shards, slots), renumber(tail_ref[row], shards, slots)
    head = dot(one_hot(to_column(heads), touched), own)
    tail = dot(one_hot(to_column(tails), touched), far)
    rel = dot(one_hot(to_column(ids), relations_ref.shape[0]), relations_ref[...])
    query_tail, query_head, coeff = by_blocks(query_block, head, tail, rel)

    def weights(query, rows, neg_ref):
        hit = one_hot_t(renumber(neg_ref[row], shards, slots), touched)
        counts = dot(hit, jnp.ones((negatives, touched), BF16))
        same = iota((touched, touched), 0) == iota((touched, touched), 1)
        scale = jnp.sum(jnp.where(same, counts, 0.0), axis=0, keepdims=True) * (1.0 / negatives)
        return jax.nn.sigmoid(dot(query, rows, LAST)) * scale

    weight_tail = weights(query_tail, far, far_neg_ref)
    weight_head = weights(query_head, own, own_neg_ref)
    back_tail = dot(weight_tail.astype(BF16), far)
    back_head = dot(weight_head.astype(BF16), own)
    grad_head, grad_tail, grad_rel = by_blocks(grad_block, head, tail, rel, coeff, back_tail, back_head)
    right = [
        jnp.concatenate([grad_head, query_head], axis=0),
        jnp.concatenate([grad_tail, query_tail], axis=0),
    ]
    if r < bit:
        out_ref, grad_rel_out = refs
        sides = (own_half, heads, weight_head), (far_half, tails, weight_tail)
        for (half, slot, weight), grads in zip(sides, right):
            out_ref[half] = row_grads(slot, weight, grads)
        grad_rel_out[...] = grad_rel
    else:
        *before_refs, weights_out, right_out, values_out, sums_out = refs
        for side, weight in enumerate((weight_head, weight_tail)):
            weights_out[side], right_out[side] = weight.astype(BF16), right[side]
        values = jnp.concatenate([ref[...] for ref in before_refs] + [grad_rel], axis=0)
        values_out[...] = values
        masks = other_doms(bit)
        for i, mask in enumerate(masks):
            sums_out[i] = relation_sums(rel_ref, values, bit, per_device, mask, rec_ref.shape[0]).astype(BF16)


def other_doms(bit):
    return [mask for mask in range(1, lax.axis_size("dom")) if not mask >> bit & 1]


def relation_sums(rel_ref, values, bit, per_device, mask, rows):
    shards = lax.axis_size("shard")
    ids = jnp.concatenate([rel_ref[r : r + 1] for r in range(rel_ref.shape[0])], axis=1)
    owner = ids // per_device
    dom = owner // shards
    chunk = (1 - (dom >> bit & 1)) * shards + reverse(owner % shards, shards)
    meant = (dom ^ lax.axis_index("dom") ^ mask) & ~(1 << bit) == 0
    rows_each = rows // (2 * shards)
    spot, free = ids % per_device, rows_each - per_device
    hot = one_hot_t(
        jnp.concatenate(
            [
                jnp.where(meant, chunk * rows_each + spot, -1),
                jnp.where(meant, chunk * rows_each + per_device + spot % free, -1),
            ],
            axis=1,
        ),
        rows,
    )
    third = values[:, 2 * LANES : 3 * LANES].astype(F32)
    first = to_column(spot) < free
    split = [jnp.where(first, third, 0.0).astype(BF16), jnp.where(first, 0.0, third).astype(BF16)]
    right = jnp.concatenate([values[:, : 2 * LANES], jnp.concatenate(split, axis=1)], axis=0)
    rest = dot(hot[:, : values.shape[0]], values[:, 3 * LANES :])
    return jnp.concatenate([dot(hot, right), rest], axis=1)


def unpack_sums(total, per_device):
    free = total.shape[0] - per_device
    third = jnp.concatenate(
        [total[per_device:, :LANES], total[per_device : 2 * per_device - free, LANES : 2 * LANES]], axis=0
    )
    return jnp.concatenate([total[:per_device, : 2 * LANES], third, total[:per_device, 2 * LANES :]], axis=1)


def row_grads(slot, weight, grads):
    left = jnp.concatenate([one_hot_t(slot, weight.shape[1]), weight.T.astype(BF16)], axis=1)
    return fold(dot(left, grads).astype(BF16))


def grad_kernel(
    bit,
    per_device,
    request_ref,
    head_ref,
    tail_ref,
    rel_ref,
    weights_ref,
    right_ref,
    values_ref,
    out_ref,
    sums_out,
    hot_out,
):
    shards, slots = lax.axis_size("shard"), slots_of(out_ref)
    for side, (half, slot_ref) in enumerate(zip(halves(out_ref, bit), (head_ref, tail_ref))):
        slot = renumber(slot_ref[bit : bit + 1], shards, slots)
        out_ref[half] = row_grads(slot, weights_ref[side].astype(F32), right_ref[side])
    sums_out[...] = relation_sums(rel_ref, values_ref[...], bit, per_device, 0, out_ref.shape[0])
    hot_out[...] = request_hot(request_ref, bit, hot_out.shape[0]).astype(F32).T.astype(BF16)


def sums_width(width):
    return width - LANES


def wide(width):
    return 2 * whole(width) + 3 * LANES


def join_kernel(grads_ref, sums_ref, *refs):
    *came_refs, out_ref = refs
    tiles = out_ref.shape[1] - 3 * LANES
    total = sums_ref[...]
    for ref in came_refs:
        total = total + ref[...].astype(F32)
    total = total.astype(BF16)
    rests = jnp.concatenate([grads_ref[:, tiles:], total[:, 2 * LANES :]], axis=1)
    blank = jnp.zeros((total.shape[0], LANES - rests.shape[1]), BF16)
    out_ref[:, :tiles] = grads_ref[:, :tiles]
    out_ref[:, tiles : tiles + LANES] = jnp.concatenate([rests, blank], axis=1)
    out_ref[:, tiles + LANES :] = total[:, : 2 * LANES]


def last_kernel(hot_ref, back_ref, state_ref, table_out, row_accum_out, step_out, accum_out, *scratch):
    table_ref, row_accum_ref, step_ref, new_accum_ref, sems = scratch
    pairs = (
        (table_ref, table_out),
        (row_accum_ref, row_accum_out),
        (step_ref, step_out),
        (new_accum_ref, accum_out),
    )
    copies = [pltpu.make_async_copy(source, target, sems.at[i]) for i, (source, target) in enumerate(pairs)]
    table, accum = row_update(hot_ref[...], back_ref, state_ref, NATURAL)
    table_ref[...] = table
    row_accum_ref[...] = accum
    per_device, width = step_ref.shape
    rows = slots_of(back_ref) // 2
    tiles, rest = 2 * whole(width), width - whole(width)
    parts = jnp.concatenate(
        [back_ref[:, tiles + LANES :], back_ref[:, tiles + 2 * rest : tiles + 3 * rest]], axis=1
    ).astype(F32)
    total = jnp.sum(parts.reshape(parts.shape[0] // rows, rows, parts.shape[1]), axis=0)
    grad = unpack_sums(total, per_device)
    accum = to_column(state_ref[table.shape[0] + 1 :, :per_device]) + jnp.mean(grad * grad, axis=1, keepdims=True)
    step_ref[...] = grad * (-LEARN_RATE * lax.rsqrt(accum))
    new_accum_ref[...] = to_row(accum)
    for copy in copies:
        copy.start()
    for copy in copies:
        copy.wait()


def call(kernel, outs, *args, **kwargs):
    return pl.pallas_call(
        kernel,
        out_shape=[jax.ShapeDtypeStruct(shape, kind) for shape, kind in outs],
        compiler_params=pltpu.CompilerParams(vmem_limit_bytes=VMEM_LIMIT),
        **kwargs,
    )(*args)


def swap_pair(value, r):
    doms, shards = lax.axis_size("dom"), lax.axis_size("shard")
    order = spread_order(shards)
    groups = [
        [g * shards + s for g in (low ^ (1 << r), low) for s in sorted(range(shards), key=order.__getitem__)]
        for low in range(doms)
        if not low >> r & 1
    ]
    return lax.all_to_all(
        value, ("dom", "shard"), split_axis=0, concat_axis=0, axis_index_groups=groups, tiled=True
    )


def body(
    embeddings,
    row_accum,
    relations,
    relation_accum,
    request_rows,
    head_slots,
    tail_slots,
    relation_ids,
    own_negatives,
    far_negatives,
):
    rows, width = embeddings.shape
    doms, shards = lax.axis_size("dom"), lax.axis_size("shard")
    rounds, slots = request_rows.shape[0], request_rows.shape[-1]
    bit = rounds - 1
    per_device = relation_accum.shape[0]
    assert 3 * (width % LANES) <= LANES
    count, touched = head_slots.shape[1], shards * slots
    free = slots // 2 - per_device
    assert free < per_device <= 2 * free and whole(width) == 3 * LANES
    chunks = ((touched, 2 * width), BF16)
    state = (
        jnp.pad(embeddings, ((0, 2), (0, 0)))
        + jnp.pad(row_accum[None], ((rows, 1), (0, width - rows)))
        + jnp.pad(relation_accum[None], ((rows + 1, 0), (0, width - per_device)))
    )
    edges = (head_slots, tail_slots, relation_ids, own_negatives, far_negatives, relations)
    (outgoing,) = call(first_kernel, [chunks], request_rows, state, *edges)
    before = []
    for r in range(bit):
        received = swap_pair(outgoing, r)
        grads, grad_rel = call(
            functools.partial(edge_kernel, r, bit, per_device), [chunks, ((count, width), BF16)], received, *edges
        )
        before.append(grad_rel)
        back = swap_pair(grads, r)
        state, outgoing = call(
            functools.partial(middle_kernel, r), [(state.shape, F32), chunks], request_rows, back, state
        )
    received = swap_pair(outgoing, bit)
    masks = other_doms(bit)
    weights, right, values, sums = call(
        functools.partial(edge_kernel, bit, bit, per_device),
        [
            ((2, count, touched), BF16),
            ((2, 2 * count, width), BF16),
            ((rounds * count, width), BF16),
            ((len(masks), touched, sums_width(width)), BF16),
        ],
        received,
        *edges,
        *before,
    )
    came = [lax.ppermute(sums[i], "dom", [(g, g ^ mask) for g in range(doms)]) for i, mask in enumerate(masks)]
    grads, sums, hot = call(
        functools.partial(grad_kernel, bit, per_device),
        [chunks, ((touched, sums_width(width)), F32), ((rows, 2 * touched), BF16)],
        request_rows,
        head_slots,
        tail_slots,
        relation_ids,
        weights,
        right,
        values,
    )
    (grads,) = call(join_kernel, [((touched, wide(width)), BF16)], grads, sums, *came)
    back = swap_pair(grads, bit)
    outs = [((rows, width), F32), ((1, rows), F32), ((per_device, width), F32), ((1, per_device), F32)]
    table, accum, step, relation_accum = call(
        last_kernel,
        outs,
        hot,
        back,
        state,
        in_specs=[VMEM] * 3,
        out_specs=[HBM] * 4,
        scratch_shapes=[pltpu.VMEM(*out) for out in outs] + [pltpu.SemaphoreType.DMA((4,))],
    )
    return (table, accum.reshape(rows), step, relation_accum.reshape(per_device))


def solution(mesh):
    placed = (
        P(("dom", "shard"), None),
        P(("dom", "shard")),
        P(),
        P(("dom", "shard")),
        P(None, ("dom", "shard"), None, None),
        P(None, ("dom", "shard")),
        P(None, ("dom", "shard")),
        P(None, ("dom", "shard")),
        P(None, ("dom", "shard")),
        P(None, ("dom", "shard")),
    )
    return jax.shard_map(
        body,
        mesh=mesh,
        in_specs=placed,
        out_specs=(
            P(("dom", "shard"), None),
            P(("dom", "shard")),
            P(("dom", "shard"), None),
            P(("dom", "shard")),
        ),
        check_vma=False,
    )
```

```python
import functools

import jax
import jax.numpy as jnp
from jax import lax
from jax.experimental import pallas as pl
from jax.experimental.pallas import tpu as pltpu
from jax.sharding import PartitionSpec as P

LEARN_RATE = 0.1
LANES = 128
VMEM_LIMIT = 48 * 2**20
BF16 = jnp.bfloat16
F32 = jnp.float32
NATURAL = (((1,), (0,)), ((), ()))
LAST = (((1,), (1,)), ((), ()))
FIRST = (((0,), (0,)), ((), ()))
HBM = pl.BlockSpec(memory_space=pltpu.HBM)
VMEM = pl.BlockSpec(memory_space=pltpu.VMEM)


def dot(left, right, dims=NATURAL):
    return lax.dot_general(left, right, dims, preferred_element_type=F32)


def iota(shape, axis):
    return lax.broadcasted_iota(jnp.int32, shape, axis)


def one_hot_t(row, count):
    return (iota((count, row.shape[1]), 0) == row).astype(BF16)


def one_hot(column, count):
    return (iota((column.shape[0], count), 1) == column.astype(jnp.int32)).astype(BF16)


def to_column(row):
    n = row.shape[1]
    same = iota((n, n), 0) == iota((n, n), 1)
    return jnp.sum(jnp.where(same, row.astype(F32), 0.0), axis=1, keepdims=True)


def to_row(column):
    n = column.shape[0]
    return jnp.sum(jnp.where(iota((n, n), 0) == iota((n, n), 1), column, 0.0), axis=0, keepdims=True)


def reverse(index, count):
    return (count - 1) ^ index


def spread_order(shards):
    return [reverse(s, shards) for s in range(shards)]


def group_bit(r):
    return 1 - ((lax.axis_index("dom") >> r) & 1)


def renumber(slot, shards, slots):
    half = slots // 2
    return (slot // half % 2) * (shards * half) + reverse(slot // slots, shards) * half + slot % half


def halves(ref, r):
    rows, bit = ref.shape[0] // 2, group_bit(r)
    return [pl.ds(pl.multiple_of(side * rows, rows), rows) for side in (bit, 1 - bit)]


def whole(width):
    return width // LANES * LANES


def unfold(value, width):
    tiles, rest = whole(width), width - whole(width)
    return jnp.concatenate(
        [
            jnp.concatenate(
                [value[:, side * tiles : (side + 1) * tiles], value[:, 2 * tiles + side * rest :][:, :rest]], axis=1
            )
            for side in range(2)
        ],
        axis=0,
    )


def beside(left, right):
    tiles = whole(left.shape[1])
    return jnp.concatenate([left[:, :tiles], right[:, :tiles], left[:, tiles:], right[:, tiles:]], axis=1)


def fold(value):
    n = value.shape[0] // 2
    return beside(value[:n], value[n:])


def request_columns(request_ref, r):
    _, shards, _, slots = request_ref.shape
    half = slots // 2
    sides = [request_ref[r, :, k, :].astype(F32) for k in range(2)]
    flip = group_bit(r) == 1
    rep = jnp.concatenate(
        [
            jnp.broadcast_to(ids[reverse(place, shards)][None], (half, slots))
            for ids in (jnp.where(flip, sides[1], sides[0]), jnp.where(flip, sides[0], sides[1]))
            for place in range(shards)
        ],
        axis=0,
    )
    n = rep.shape[0]
    lane, inside = iota((n, slots), 1), iota((n, slots), 0) % half
    return [
        jnp.sum(jnp.where(lane == side * half + inside, rep, 0.0), axis=1, keepdims=True) for side in range(2)
    ]


def serve(request_ref, r, table, out_ref):
    rows, width = table.shape
    table = table.astype(BF16)
    hot = jnp.concatenate([one_hot(column, rows) for column in request_columns(request_ref, r)], axis=1)
    blank = jnp.zeros((rows, width), BF16)
    both = jnp.concatenate([beside(table, blank), beside(blank, table)], axis=0)
    out_ref[...] = dot(hot, both).astype(BF16)


def first_kernel(request_ref, state_ref, *refs):
    out_ref = refs[-1]
    table = state_ref[: state_ref.shape[0] - 2]
    serve(request_ref, 0, table, out_ref)


def request_hot(request_ref, r, rows):
    return jnp.concatenate([one_hot(column, rows) for column in request_columns(request_ref, r)], axis=0)


def row_update(hot, back_ref, state_ref, dims=FIRST):
    rows, width = state_ref.shape[0] - 2, state_ref.shape[1]
    row_grad = dot(hot, unfold(back_ref[:, : 2 * width], width), dims)
    accum = to_column(state_ref[rows : rows + 1, :rows]) + jnp.mean(row_grad * row_grad, axis=1, keepdims=True)
    return state_ref[:rows] - row_grad * (LEARN_RATE * lax.rsqrt(accum)), to_row(accum)


def middle_kernel(r, request_ref, back_ref, state_ref, state_out, out_ref):
    rows = state_ref.shape[0] - 2
    table, accum = row_update(request_hot(request_ref, r, rows), back_ref, state_ref)
    serve(request_ref, r + 1, table, out_ref)
    state_out[:rows] = table
    state_out[rows:] = state_ref[rows:]
    state_out[rows : rows + 1, :rows] = accum


def slots_of(ref):
    return 2 * ref.shape[0] // (2 * lax.axis_size("shard"))


def by_blocks(function, *arrays):
    step = 16
    parts = [function(*[x[i : i + step] for x in arrays]) for i in range(0, arrays[0].shape[0], step)]
    return [jnp.concatenate(column, axis=0) for column in zip(*parts)]


def query_block(head, tail, rel):
    tail_query = head * rel
    positive = jnp.sum(tail_query * tail, axis=1, keepdims=True)
    return tail_query.astype(BF16), (tail * rel).astype(BF16), -jax.nn.sigmoid(-positive)


def grad_block(head, tail, rel, coeff, back_tail, back_head):
    toward_head = coeff * tail + back_tail
    grad_rel = head * toward_head + tail * back_head
    return (
        (rel * toward_head).astype(BF16),
        (rel * (coeff * head + back_head)).astype(BF16),
        grad_rel.astype(BF16),
    )


def edge_kernel(
    r,
    bit,
    per_device,
    rec_ref,
    head_ref,
    tail_ref,
    rel_ref,
    own_neg_ref,
    far_neg_ref,
    relations_ref,
    *refs,
):
    width = relations_ref.shape[1]
    shards, slots = lax.axis_size("shard"), slots_of(rec_ref)
    touched = shards * slots
    edges, negatives = head_ref.shape[1], own_neg_ref.shape[1]
    own_half, far_half = halves(rec_ref, r)
    own = unfold(rec_ref[own_half], width)
    far = unfold(rec_ref[far_half], width)
    row = slice(r, r + 1)
    ids = rel_ref[row]
    heads, tails = renumber(head_ref[row], shards, slots), renumber(tail_ref[row], shards, slots)
    head = dot(one_hot_t(heads, touched), own, FIRST)
    tail = dot(one_hot_t(tails, touched), far, FIRST)
    rel = dot(one_hot_t(ids, relations_ref.shape[0]), relations_ref[...], FIRST)
    query_tail, query_head, coeff = by_blocks(query_block, head, tail, rel)

    def weights(query, rows, neg_ref):
        hit = one_hot_t(renumber(neg_ref[row], shards, slots), touched)
        counts = dot(hit, jnp.ones((negatives, touched), BF16))
        same = iota((touched, touched), 0) == iota((touched, touched), 1)
        scale = jnp.sum(jnp.where(same, counts, 0.0), axis=0, keepdims=True) * (1.0 / negatives)
        return jax.nn.sigmoid(dot(query, rows, LAST)) * scale

    weight_tail = weights(query_tail, far, far_neg_ref)
    weight_head = weights(query_head, own, own_neg_ref)
    back_tail = dot(weight_tail.astype(BF16), far)
    back_head = dot(weight_head.astype(BF16), own)
    grad_head, grad_tail, grad_rel = by_blocks(grad_block, head, tail, rel, coeff, back_tail, back_head)
    right = [
        jnp.concatenate([grad_head, query_head], axis=0),
        jnp.concatenate([grad_tail, query_tail], axis=0),
    ]
    if r < bit:
        out_ref, grad_rel_out = refs
        sides = (own_half, heads, weight_head), (far_half, tails, weight_tail)
        for (half, slot, weight), grads in zip(sides, right):
            out_ref[half] = row_grads(slot, weight, grads)
        grad_rel_out[...] = grad_rel
    else:
        *before_refs, weights_out, right_out, values_out, sums_out = refs
        for side, weight in enumerate((weight_head, weight_tail)):
            weights_out[side], right_out[side] = weight.astype(BF16), right[side]
        values = jnp.concatenate([ref[...] for ref in before_refs] + [grad_rel], axis=0)
        values_out[...] = values
        masks = other_doms(bit)
        for i, mask in enumerate(masks):
            sums_out[i] = relation_sums(rel_ref, values, bit, per_device, mask, rec_ref.shape[0]).astype(BF16)


def other_doms(bit):
    return [mask for mask in range(1, lax.axis_size("dom")) if not mask >> bit & 1]


def relation_sums(rel_ref, values, bit, per_device, mask, rows):
    shards = lax.axis_size("shard")
    ids = jnp.concatenate([rel_ref[r : r + 1] for r in range(rel_ref.shape[0])], axis=1)
    owner = ids // per_device
    dom = owner // shards
    chunk = (1 - (dom >> bit & 1)) * shards + reverse(owner % shards, shards)
    meant = (dom ^ lax.axis_index("dom") ^ mask) & ~(1 << bit) == 0
    rows_each = rows // (2 * shards)
    spot, free = ids % per_device, rows_each - per_device
    hot = one_hot_t(
        jnp.concatenate(
            [
                jnp.where(meant, chunk * rows_each + spot, -1),
                jnp.where(meant, chunk * rows_each + per_device + spot % free, -1),
            ],
            axis=1,
        ),
        rows,
    )
    third = values[:, 2 * LANES : 3 * LANES].astype(F32)
    first = to_column(spot) < free
    split = [jnp.where(first, third, 0.0).astype(BF16), jnp.where(first, 0.0, third).astype(BF16)]
    right = jnp.concatenate([values[:, : 2 * LANES], jnp.concatenate(split, axis=1)], axis=0)
    rest = dot(hot[:, : values.shape[0]], values[:, 3 * LANES :])
    return jnp.concatenate([dot(hot, right), rest], axis=1)


def unpack_sums(total, per_device):
    free = total.shape[0] - per_device
    third = jnp.concatenate(
        [total[per_device:, :LANES], total[per_device : 2 * per_device - free, LANES : 2 * LANES]], axis=0
    )
    return jnp.concatenate([total[:per_device, : 2 * LANES], third, total[:per_device, 2 * LANES :]], axis=1)


def row_grads(slot, weight, grads):
    left = jnp.concatenate([one_hot_t(slot, weight.shape[1]), weight.T.astype(BF16)], axis=1)
    return fold(dot(left, grads).astype(BF16))


def grad_kernel(
    bit,
    per_device,
    request_ref,
    head_ref,
    tail_ref,
    rel_ref,
    weights_ref,
    right_ref,
    values_ref,
    out_ref,
    sums_out,
    hot_out,
):
    shards, slots = lax.axis_size("shard"), slots_of(out_ref)
    for side, (half, slot_ref) in enumerate(zip(halves(out_ref, bit), (head_ref, tail_ref))):
        slot = renumber(slot_ref[bit : bit + 1], shards, slots)
        out_ref[half] = row_grads(slot, weights_ref[side].astype(F32), right_ref[side])
    sums_out[...] = relation_sums(rel_ref, values_ref[...], bit, per_device, 0, out_ref.shape[0])
    hot_out[...] = request_hot(request_ref, bit, hot_out.shape[0]).astype(F32).T.astype(BF16)


def sums_width(width):
    return width - LANES


def wide(width):
    return 2 * whole(width) + 3 * LANES


def join_kernel(grads_ref, sums_ref, *refs):
    *came_refs, out_ref = refs
    tiles = out_ref.shape[1] - 3 * LANES
    total = sums_ref[...]
    for ref in came_refs:
        total = total + ref[...].astype(F32)
    total = total.astype(BF16)
    rests = jnp.concatenate([grads_ref[:, tiles:], total[:, 2 * LANES :]], axis=1)
    blank = jnp.zeros((total.shape[0], LANES - rests.shape[1]), BF16)
    out_ref[:, :tiles] = grads_ref[:, :tiles]
    out_ref[:, tiles : tiles + LANES] = jnp.concatenate([rests, blank], axis=1)
    out_ref[:, tiles + LANES :] = total[:, : 2 * LANES]


def last_kernel(hot_ref, back_ref, state_ref, table_out, row_accum_out, step_out, accum_out, *scratch):
    table_ref, row_accum_ref, step_ref, new_accum_ref, sems = scratch
    pairs = (
        (table_ref, table_out),
        (row_accum_ref, row_accum_out),
        (step_ref, step_out),
        (new_accum_ref, accum_out),
    )
    copies = [pltpu.make_async_copy(source, target, sems.at[i]) for i, (source, target) in enumerate(pairs)]
    table, accum = row_update(hot_ref[...], back_ref, state_ref, NATURAL)
    table_ref[...] = table
    copies[0].start()
    row_accum_ref[...] = accum
    copies[1].start()
    per_device, width = step_ref.shape
    rows = slots_of(back_ref) // 2
    tiles, rest = 2 * whole(width), width - whole(width)
    parts = jnp.concatenate(
        [back_ref[:, tiles + LANES :], back_ref[:, tiles + 2 * rest : tiles + 3 * rest]], axis=1
    ).astype(F32)
    total = jnp.sum(parts.reshape(parts.shape[0] // rows, rows, parts.shape[1]), axis=0)
    grad = unpack_sums(total, per_device)
    accum = to_column(state_ref[table.shape[0] + 1 :, :per_device]) + jnp.mean(grad * grad, axis=1, keepdims=True)
    step_ref[...] = grad * (-LEARN_RATE * lax.rsqrt(accum))
    copies[2].start()
    new_accum_ref[...] = to_row(accum)
    copies[3].start()
    for copy in copies:
        copy.wait()


def call(kernel, outs, *args, **kwargs):
    return pl.pallas_call(
        kernel,
        out_shape=[jax.ShapeDtypeStruct(shape, kind) for shape, kind in outs],
        compiler_params=pltpu.CompilerParams(vmem_limit_bytes=VMEM_LIMIT),
        **kwargs,
    )(*args)


def swap_pair(value, r):
    doms, shards = lax.axis_size("dom"), lax.axis_size("shard")
    order = spread_order(shards)
    groups = [
        [g * shards + s for g in (low ^ (1 << r), low) for s in sorted(range(shards), key=order.__getitem__)]
        for low in range(doms)
        if not low >> r & 1
    ]
    return lax.all_to_all(
        value, ("dom", "shard"), split_axis=0, concat_axis=0, axis_index_groups=groups, tiled=True
    )


def body(
    embeddings,
    row_accum,
    relations,
    relation_accum,
    request_rows,
    head_slots,
    tail_slots,
    relation_ids,
    own_negatives,
    far_negatives,
):
    rows, width = embeddings.shape
    doms, shards = lax.axis_size("dom"), lax.axis_size("shard")
    rounds, slots = request_rows.shape[0], request_rows.shape[-1]
    bit = rounds - 1
    per_device = relation_accum.shape[0]
    assert 3 * (width % LANES) <= LANES
    count, touched = head_slots.shape[1], shards * slots
    free = slots // 2 - per_device
    assert free < per_device <= 2 * free and whole(width) == 3 * LANES
    chunks = ((touched, 2 * width), BF16)
    state = (
        jnp.pad(embeddings, ((0, 2), (0, 0)))
        + jnp.pad(row_accum[None], ((rows, 1), (0, width - rows)))
        + jnp.pad(relation_accum[None], ((rows + 1, 0), (0, width - per_device)))
    )
    edges = (head_slots, tail_slots, relation_ids, own_negatives, far_negatives, relations)
    (outgoing,) = call(first_kernel, [chunks], request_rows, state, *edges)
    before = []
    for r in range(bit):
        received = swap_pair(outgoing, r)
        grads, grad_rel = call(
            functools.partial(edge_kernel, r, bit, per_device), [chunks, ((count, width), BF16)], received, *edges
        )
        before.append(grad_rel)
        back = swap_pair(grads, r)
        state, outgoing = call(
            functools.partial(middle_kernel, r), [(state.shape, F32), chunks], request_rows, back, state
        )
    received = swap_pair(outgoing, bit)
    masks = other_doms(bit)
    weights, right, values, sums = call(
        functools.partial(edge_kernel, bit, bit, per_device),
        [
            ((2, count, touched), BF16),
            ((2, 2 * count, width), BF16),
            ((rounds * count, width), BF16),
            ((len(masks), touched, sums_width(width)), BF16),
        ],
        received,
        *edges,
        *before,
    )
    came = [lax.ppermute(sums[i], "dom", [(g, g ^ mask) for g in range(doms)]) for i, mask in enumerate(masks)]
    grads, sums, hot = call(
        functools.partial(grad_kernel, bit, per_device),
        [chunks, ((touched, sums_width(width)), F32), ((rows, 2 * touched), BF16)],
        request_rows,
        head_slots,
        tail_slots,
        relation_ids,
        weights,
        right,
        values,
    )
    (grads,) = call(join_kernel, [((touched, wide(width)), BF16)], grads, sums, *came)
    back = swap_pair(grads, bit)
    outs = [((rows, width), F32), ((1, rows), F32), ((per_device, width), F32), ((1, per_device), F32)]
    table, accum, step, relation_accum = call(
        last_kernel,
        outs,
        hot,
        back,
        state,
        in_specs=[VMEM] * 3,
        out_specs=[HBM] * 4,
        scratch_shapes=[pltpu.VMEM(*out) for out in outs] + [pltpu.SemaphoreType.DMA((4,))],
    )
    return (table, accum.reshape(rows), step, relation_accum.reshape(per_device))


def solution(mesh):
    placed = (
        P(("dom", "shard"), None),
        P(("dom", "shard")),
        P(),
        P(("dom", "shard")),
        P(None, ("dom", "shard"), None, None),
        P(None, ("dom", "shard")),
        P(None, ("dom", "shard")),
        P(None, ("dom", "shard")),
        P(None, ("dom", "shard")),
        P(None, ("dom", "shard")),
    )
    return jax.shard_map(
        body,
        mesh=mesh,
        in_specs=placed,
        out_specs=(
            P(("dom", "shard"), None),
            P(("dom", "shard")),
            P(("dom", "shard"), None),
            P(("dom", "shard")),
        ),
        check_vma=False,
    )
```
